32 devices in a mesh: ctx: 16 (over z, y, x), wsh: 2 (over core).
Axes of the slice: x: 2, y: 2, z: 4, core: 2. Of those that a mesh axis runs over, the one named last changes fastest.
Arguments:
- tokens: bfloat16 [2, 2, 8192, 768], P(None, 'wsh', 'ctx'), may hold values from -6 to 6
- cotangent: bfloat16 [2, 2, 8192, 768], P(None, 'wsh', 'ctx'), may hold values from -6 to 6
- light_qkv: bfloat16 [768, 1536], P('wsh'), may hold values from -0.21875 to 0.21875
- light_out: bfloat16 [512, 768], P('wsh'), may hold values from -4 to 4
- heavy_qkv: bfloat16 [768, 2304], P('wsh'), may hold values from -0.21875 to 0.21875
- heavy_out: bfloat16 [768, 768], P('wsh'), may hold values from -4 to 4
- light_gu: bfloat16 [768, 2048], P('wsh'), may hold values from -0.21875 to 0.21875
- light_down: bfloat16 [1024, 768], P('wsh'), may hold values from -0.1875 to 0.1875
- heavy_gu: bfloat16 [768, 8192], P('wsh'), may hold values from -0.21875 to 0.21875
- heavy_down: bfloat16 [4096, 768], P('wsh'), may hold values from -0.09375 to 0.09375
- routers: bfloat16 [3, 768], P(None, 'wsh'), may hold values from -0.21875 to 0.21875
- gains: bfloat16 [2, 768], P(None, 'wsh'), may hold values from 0.5 to 1.5
- doc_starts: int32 [2, 2, 5], P(None, 'wsh'), may hold values from 0 to 8191, as said below
- q_index: int32 [2, 2, 1024], P(None, 'wsh', 'ctx'), may hold values from 0 to 8191, as said below
- kv_index: int32 [2, 2, 1024], P(None, 'wsh', 'ctx'), may hold values from 0 to 8191, as said below
- ff_index: int32 [2, 2, 1024], P(None, 'wsh', 'ctx'), may hold values from 0 to 8191, as said below
Outputs:
- out_tokens: bfloat16 [2, 2, 8192, 768], P(None, 'wsh', 'ctx')
- grad_tokens: bfloat16 [2, 2, 8192, 768], P(None, 'wsh', 'ctx')
- grad_light_qkv: float32 [768, 1536], P('wsh')
- grad_light_out: float32 [512, 768], P('wsh')
- grad_heavy_qkv: float32 [768, 2304], P('wsh')
- grad_heavy_out: float32 [768, 768], P('wsh')
- grad_light_gu: float32 [768, 2048], P('wsh')
- grad_light_down: float32 [1024, 768], P('wsh')
- grad_heavy_gu: float32 [768, 8192], P('wsh')
- grad_heavy_down: float32 [4096, 768], P('wsh')
- grad_routers: float32 [3, 768], P(None, 'wsh')
- grad_gains: float32 [2, 768], P(None, 'wsh')
The draws below stay inside these ranges and needn't reach their ends.
Inputs may be any that keep to these rules, and one draw needn't show every extreme that they name: `doc_starts`: per micro-batch and stream the 5 starts rise strictly; the first is 0, the second lies in the first 512 - 128 positions, the third in the last 128 positions of the first 512, the fourth in the first 128 positions of the last 512, the fifth later in the last 512 (512, 8192 as on the slice in use). `q_index`: the entries of the block of 64 that lies on one index of ctx are distinct positions of that index's own 512 positions, rising. `kv_index`: the entries of the block of 64 that lies on one index of ctx are distinct positions of that index's own 512 positions, rising; every document start is among them. `ff_index`: the entries of the block of 64 that lies on one index of ctx are distinct positions of that index's own 512 positions, rising.
All inputs are finite; a program needn't handle non-finite values.
Results may differ from the reference program's by a relative error of at most 0.023.
Values may be sent and summed in bfloat16 or wider, within the bound.
No kernel may reach another device: no remote copies, remote signals or barrier semaphores. Data moves between devices by JAX's collectives and lax.ppermute only.
A program may use at most 320 MiB of HBM per device.

```python
import jax
import jax.numpy as jnp
from jax import lax

D = 768
HD = 64
HL = 8
HH = 12
FL = 1024
FH = 4096
WIN = 128
MB = 2
TOK = 512
LI = 512
ROUTED = 64
SEQ = 8192
STREAMS = 2


def make_starts(key):
    keys = jax.random.split(key, 4)
    shape = (MB, STREAMS)
    first = jax.random.randint(keys[0], shape, 1, TOK - WIN)
    second = jax.random.randint(keys[1], shape, TOK - WIN + 1, TOK)
    third = jax.random.randint(keys[2], shape, SEQ - TOK + 1, SEQ - TOK + WIN)
    fourth = jax.random.randint(keys[3], shape, SEQ - TOK + WIN, SEQ)
    return jnp.stack([jnp.zeros(shape, jnp.int32), first, second, third, fourth], axis=-1).astype(jnp.int32)


def pick_rows(key, forced):
    blocks = SEQ // TOK
    ranks = jax.random.randint(key, (MB, STREAMS, blocks, TOK), 0, 65536)
    local = jnp.arange(TOK, dtype=jnp.int32)
    scores = ranks * TOK + local + forced.reshape(MB, STREAMS, blocks, TOK) * (1 << 28)
    unused, chosen = lax.top_k(scores, TOK // 8)
    chosen = jnp.sort(chosen, axis=-1).astype(jnp.int32)
    offsets = (jnp.arange(blocks, dtype=jnp.int32) * TOK)[:, None]
    return (chosen + offsets).reshape(MB, STREAMS, blocks * (TOK // 8)).astype(jnp.int32)


def draw_doc_starts(key, part):
    return make_starts(jax.random.fold_in(key, 11))


def draw_q_index(key, part):
    return pick_rows(jax.random.fold_in(key, 33), jnp.zeros((MB, STREAMS, SEQ), jnp.int32))


def draw_kv_index(key, part):
    starts = make_starts(jax.random.fold_in(key, 11))
    positions = jnp.arange(SEQ, dtype=jnp.int32)
    forced = jnp.any(positions[None, None, :, None] == starts[:, :, None, :], axis=-1).astype(jnp.int32)
    return pick_rows(jax.random.fold_in(key, 22), forced)


def draw_ff_index(key, part):
    return pick_rows(jax.random.fold_in(key, 44), jnp.zeros((MB, STREAMS, SEQ), jnp.int32))


def block_scale(key, dims, cuts, low, largest):
    loudness, own = 1.0, jax.random.fold_in(key, 6)
    for dim, blocks in cuts:
        draws = jnp.exp(jax.random.uniform(jax.random.fold_in(own, dim), (blocks,), jnp.float32, low / len(cuts), largest / len(cuts)))
        loudness = loudness * jnp.repeat(draws, dims[dim] // blocks).reshape([-1 if axis == dim else 1 for axis in range(len(dims))])
    return loudness


def bell_draw(stream_key, extent, deviation, bound, cuts=(), kind=jnp.bfloat16):
    values = jax.random.normal(stream_key, extent, jnp.float32) * deviation
    if len(cuts) > 0:
        values = block_scale(stream_key, extent, cuts, -0.22, 0.18) * values
    return jnp.clip(values, min=-bound, max=bound).astype(kind)


def setup_inputs(seed: int = 0) -> dict:
    key_of = jax.random.split(jax.random.key(seed), 17)
    return {
        "tokens": bell_draw(key_of[0], (MB, STREAMS, SEQ, D), 1.0, 6.0, ((1, 2), (2, 16))),
        "cotangent": bell_draw(key_of[1], (MB, STREAMS, SEQ, D), 1.0, 6.0, ((1, 2), (2, 16))),
        "light_qkv": bell_draw(key_of[2], (D, 3 * LI), D ** -0.5, 0.21875, ((0, 2),)),
        "light_out": bell_draw(key_of[3], (LI, D), (max(LI // (2 * WIN), 1)) ** -0.5, 4.0, ((0, 2),)),
        "heavy_qkv": bell_draw(key_of[4], (D, 3 * D), D ** -0.5, 0.21875, ((0, 2),)),
        "heavy_out": bell_draw(key_of[5], (D, D), 2 ** -0.5, 4.0, ((0, 2),)),
        "light_gu": bell_draw(key_of[6], (D, 2 * FL), D ** -0.5, 0.21875, ((0, 2),)),
        "light_down": bell_draw(key_of[7], (FL, D), FL ** -0.5, 0.1875, ((0, 2),)),
        "heavy_gu": bell_draw(key_of[8], (D, 2 * FH), D ** -0.5, 0.21875, ((0, 2),)),
        "heavy_down": bell_draw(key_of[9], (FH, D), FH ** -0.5, 0.09375, ((0, 2),)),
        "routers": bell_draw(key_of[10], (3, D), D ** -0.5, 0.21875, ((1, 2),)),
        "gains": jnp.clip(1.0 + 0.1 * jax.random.normal(key_of[11], (2, D), jnp.float32), 0.5, 1.5).astype(jnp.bfloat16),
        "doc_starts": draw_doc_starts(jax.random.fold_in(key_of[16], 71), 0),
        "q_index": draw_q_index(jax.random.fold_in(key_of[16], 71), 0),
        "kv_index": draw_kv_index(jax.random.fold_in(key_of[16], 71), 0),
        "ff_index": draw_ff_index(jax.random.fold_in(key_of[16], 71), 0),
    }


EPS = 1e-06
HIGH = lax.Precision.HIGHEST

@jax.custom_vjp
def low(v):
    return lax.optimization_barrier(v.astype(jnp.bfloat16)).astype(jnp.float32)

@jax.custom_vjp
def low_back(v):
    return v

def low_keep(v):
    return (low(v), None)

def low_pass(kept, grad):
    return (grad,)

def back_keep(v):
    return (v, None)

def back_low(kept, grad):
    return (low(grad),)
low.defvjp(low_keep, low_pass)
low_back.defvjp(back_keep, back_low)

def matrix(left, right):
    return jnp.dot(left, right, precision=HIGH, preferred_element_type=jnp.float32)

def norm_rows(values, gain):
    return values * lax.rsqrt(lax.optimization_barrier(jnp.mean(values * values, axis=-1, keepdims=True)) + EPS) * gain

def gated(gate_up):
    half = gate_up.shape[-1] // 2
    return jax.nn.gelu(gate_up[:, :half], approximate=True) * gate_up[:, half:]

def segment_of(positions, starts):
    return lax.optimization_barrier(jnp.sum((positions[:, None] >= starts[None, :]).astype(jnp.int32), axis=1)) - 1

def split_heads(values, count):
    return values.reshape(values.shape[0], count, HD).transpose(1, 0, 2)

def join_heads(values):
    return values.transpose(1, 0, 2).reshape(values.shape[1], -1)

def attend(query, key, value, allowed):
    scores = low_back(jnp.einsum('hqd,hkd->hqk', query, key, precision=HIGH) * HD ** (-0.5))
    scores = jnp.where(allowed[None], scores, -1e+30)
    probs = low(jax.nn.softmax(scores, axis=-1))
    return jnp.einsum('hqk,hkd->hqd', probs, value, precision=HIGH)

def layer(stream, params, starts, query_pos, key_pos, ffn_pos):
    w_lqkv, w_lout, w_hqkv, w_hout, w_lgu, w_ldown, w_hgu, w_hdown, w_route, w_gain = params
    inner = HL * HD
    positions = jnp.arange(SEQ, dtype=jnp.int32)
    segments = segment_of(positions, starts)
    normed_one = norm_rows(stream, w_gain[0])
    normed_low = low(normed_one)
    light_proj = low_back(low(matrix(normed_low, w_lqkv)))
    light_query = light_proj[:, :inner]
    padded_pair = jnp.pad(light_proj[:, inner:], ((WIN, WIN), (0, 0)))
    padded_seg = jnp.pad(segments, (WIN, WIN), constant_values=-1)

    def light_block(index):
        start = (index * TOK).astype(jnp.int32)
        query = lax.dynamic_slice_in_dim(light_query, start, TOK, 0)
        near = lax.dynamic_slice_in_dim(padded_pair, start, TOK + 2 * WIN, 0)
        near_seg = lax.dynamic_slice_in_dim(padded_seg, start, TOK + 2 * WIN, 0)
        own_seg = lax.dynamic_slice_in_dim(segments, start, TOK, 0)
        offsets = jnp.arange(TOK, dtype=jnp.int32)[:, None] + WIN - jnp.arange(TOK + 2 * WIN, dtype=jnp.int32)[None, :]
        allowed = (jnp.abs(offsets) < WIN) & (own_seg[:, None] == near_seg[None, :])
        mixed = attend(split_heads(query, HL), split_heads(near[:, :inner], HL), split_heads(near[:, inner:], HL), allowed)
        return join_heads(mixed)
    light_blocks = lax.map(jax.checkpoint(light_block), jnp.arange(SEQ // TOK, dtype=jnp.int32))
    light_context = low_back(low(light_blocks.reshape(SEQ, inner)))
    light_branch = low_back(matrix(light_context, w_lout))
    query_rows = normed_low[query_pos]
    key_rows = normed_low[key_pos]
    query_score = matrix(query_rows, w_route[0])
    key_score = matrix(key_rows, w_route[1])
    heavy_query = low_back(low(matrix(query_rows, w_hqkv[:, :D])))
    key_input = low(normed_one[key_pos] * jax.nn.sigmoid(key_score)[:, None])
    heavy_pair = low_back(low(matrix(key_input, w_hqkv[:, D:])))
    query_seg = segments[query_pos]
    key_seg = segments[key_pos]
    key_heads = split_heads(heavy_pair[:, :D], HH)
    value_heads = split_heads(heavy_pair[:, D:], HH)

    def heavy_block(index):
        start = (index * ROUTED).astype(jnp.int32)
        query = lax.dynamic_slice_in_dim(heavy_query, start, ROUTED, 0)
        own_seg = lax.dynamic_slice_in_dim(query_seg, start, ROUTED, 0)
        allowed = own_seg[:, None] == key_seg[None, :]
        return join_heads(attend(split_heads(query, HH), key_heads, value_heads, allowed))
    heavy_blocks = lax.map(jax.checkpoint(heavy_block), jnp.arange(SEQ // TOK, dtype=jnp.int32))
    heavy_context = low_back(low(heavy_blocks.reshape(-1, D)))
    heavy_branch = low_back(matrix(heavy_context, w_hout))
    middle = stream + light_branch + jnp.zeros_like(stream).at[query_pos].add(heavy_branch * jax.nn.sigmoid(query_score)[:, None])
    normed_two = low(norm_rows(middle, w_gain[1]))
    light_gate_up = low_back(matrix(normed_two, w_lgu))
    light_hidden = low(gated(light_gate_up))
    light_ffn = matrix(light_hidden, w_ldown)
    ffn_rows = normed_two[ffn_pos]
    ffn_score = matrix(ffn_rows, w_route[2])
    heavy_gate_up = low_back(matrix(ffn_rows, w_hgu))
    heavy_hidden = low(gated(heavy_gate_up))
    heavy_ffn = low_back(matrix(heavy_hidden, w_hdown))
    return middle + light_ffn + jnp.zeros_like(stream).at[ffn_pos].add(heavy_ffn * jax.nn.sigmoid(ffn_score)[:, None])

def reference(tokens, cotangent, light_qkv, light_out, heavy_qkv, heavy_out, light_gu, light_down, heavy_gu, heavy_down, routers, gains, doc_starts, q_index, kv_index, ff_index):
    params = tuple((w.astype(jnp.float32) for w in (light_qkv, light_out, heavy_qkv, heavy_out, light_gu, light_down, heavy_gu, heavy_down, routers, gains)))

    def flatten(array):
        return array.reshape((MB * STREAMS,) + array.shape[2:])

    def one_stream(totals, item):
        stream, upstream, starts, query_pos, key_pos, ffn_pos = item

        def forward(values, weights):
            return layer(values, weights, starts, query_pos, key_pos, ffn_pos)
        result, pull = jax.vjp(forward, stream.astype(jnp.float32), params)
        grad_stream, grad_params = pull(upstream.astype(jnp.float32))
        totals = tuple((a + b for a, b in zip(totals, grad_params)))
        return (totals, (result.astype(jnp.bfloat16), grad_stream.astype(jnp.bfloat16)))
    initial = tuple((jnp.zeros(w.shape, jnp.float32) for w in params))
    totals, (results, grads) = lax.scan(one_stream, initial, (flatten(tokens), flatten(cotangent), flatten(doc_starts), flatten(q_index), flatten(kv_index), flatten(ff_index)))
    shape = (MB, STREAMS, SEQ, D)
    return (results.reshape(shape), grads.reshape(shape), totals[0], totals[1], totals[2], totals[3], totals[4], totals[5], totals[6], totals[7], totals[8], totals[9])
```

```python
import functools

import jax
import jax.numpy as jnp
from jax import lax
from jax.experimental import pallas as pl
from jax.experimental.pallas import tpu as pltpu
from jax.sharding import PartitionSpec as P

HD = 64
WIN = 128
LANES = 128
COLS = 256
FAR = -1e30
EPS = 1e-06
BF = jnp.bfloat16
F32 = jnp.float32


def mm(left, right):
    return lax.dot_general(left, right, (((1,), (0,)), ((), ())), preferred_element_type=F32)


def mm_t(left, right):
    return lax.dot_general(left, right, (((1,), (1,)), ((), ())), preferred_element_type=F32)


def t_mm(left, right):
    return lax.dot_general(left, right, (((0,), (0,)), ((), ())), preferred_element_type=F32)


def pick(onehot, values):
    high = values.astype(BF)
    low = (values - high.astype(F32)).astype(BF)
    return mm(onehot, high) + mm(onehot, low)


def iota(shape, dim):
    return lax.broadcasted_iota(jnp.int32, shape, dim)


def onehot_cols(positions, base, length):
    return (iota((positions.shape[0], length), 1) == positions - base).astype(F32).astype(BF)


def onehot_rows(positions, base, length):
    return (iota((length, positions.shape[1]), 0) == positions - base).astype(F32).astype(BF)


def segment(info, micro, positions):
    total = jnp.full(positions.shape, -1, jnp.int32)
    for start in range(5):
        total += (positions >= info[4 + micro * 5 + start]).astype(jnp.int32)
    return total


def inverse_rms(values):
    return lax.rsqrt(jnp.mean(values * values, axis=-1, keepdims=True) + EPS)


def halves(info, values):
    half = values.shape[1] // 2
    first, second = (values[:, :half], values[:, half:])
    lower = info[0] == 0
    return (jnp.where(lower, first, second), jnp.where(lower, second, first))


def unhalved(info, own, other):
    lower = info[0] == 0
    return jnp.concatenate([jnp.where(lower, own, other), jnp.where(lower, other, own)], axis=1)


def call(body, outs, grid, in_specs, out_specs, args, scratch=(), flops=0, moved=0, limit=48):
    return pl.pallas_call(
        body,
        out_shape=outs,
        grid_spec=pltpu.PrefetchScalarGridSpec(
            num_scalar_prefetch=1,
            grid=grid,
            in_specs=in_specs,
            out_specs=out_specs,
            scratch_shapes=list(scratch),
        ),
        compiler_params=pltpu.CompilerParams(vmem_limit_bytes=limit * 1024 * 1024),
        cost_estimate=pl.CostEstimate(flops=flops, bytes_accessed=moved, transcendentals=0),
    )(*args)


def whole(shape):
    rank = len(shape)
    return pl.BlockSpec(tuple(shape), lambda *unused: (0,) * rank)


def one_of(shape):
    rank = len(shape)
    return pl.BlockSpec((1,) + tuple(shape[1:]), lambda i, *unused: (i,) + (0,) * (rank - 1))


def sds(shape, dtype):
    return jax.ShapeDtypeStruct(tuple(shape), dtype)


def routed_body(info, x, cols, small, w_own, w_got, q_out, kv_out, hq_out, kin_out, h1k_out, gate_out):
    micros, tok, width = x.shape
    rows = cols.shape[2]
    base = info[1]
    gain = small[3:4].astype(F32)
    taken_q, taken_k = ([], [])
    for m in range(micros):
        both = jnp.concatenate([cols[0, m], cols[1, m]], axis=0)
        got = mm(onehot_cols(both, base, tok), x[m])
        taken_q.append(got[:rows])
        taken_k.append(got[rows:])
    xq, xk = (jnp.concatenate(taken_q, axis=0), jnp.concatenate(taken_k, axis=0))
    low_q = (xq * inverse_rms(xq) * gain).astype(BF)
    h1k = xk * inverse_rms(xk) * gain
    low_k = h1k.astype(BF)
    gate_q = jax.nn.sigmoid(
        jnp.sum(low_q.astype(F32) * small[0:1].astype(F32), axis=-1, keepdims=True)
    )
    gate_k = jax.nn.sigmoid(
        jnp.sum(low_k.astype(F32) * small[1:2].astype(F32), axis=-1, keepdims=True)
    )
    kin = (h1k * gate_k).astype(BF)
    own_q, other_q = halves(info, low_q)
    own_k, other_k = halves(info, kin)
    query = mm(own_q, w_own[:, :width]) + mm(other_q, w_got[:, :width])
    pair = mm(own_k, w_own[:, width:]) + mm(other_k, w_got[:, width:])
    lane = iota((rows, LANES), 1)
    for m in range(micros):
        part = slice(m * rows, (m + 1) * rows)
        q_out[m, :, :width] = query[part].astype(BF)
        kv_out[m, :, : 2 * width] = pair[part].astype(BF)
        seg_q = segment(info, m, cols[0, m])
        seg_k = segment(info, m, cols[1, m])
        q_out[m, :, width:] = (lane == seg_q).astype(F32).astype(BF)
        kv_out[m, :, 2 * width :] = jnp.where((lane < 8) & (lane != seg_k), FAR, 0.0).astype(BF)
        hq_out[m] = low_q[part]
        kin_out[m] = kin[part]
        h1k_out[m] = h1k[part]
        gate_out[m] = jnp.where(lane == 0, gate_q[part], gate_k[part])


def routed_in(info, x, cols, small, w_own, w_got):
    micros, unused, width = x.shape
    rows = cols.shape[2]
    shapes = [
        sds((micros, rows, width + LANES), BF),
        sds((micros, rows, 2 * width + LANES), BF),
        sds((micros, rows, width), BF),
        sds((micros, rows, width), BF),
        sds((micros, rows, width), F32),
        sds((micros, rows, LANES), F32),
    ]
    args = (info, x, cols, small, w_own, w_got)
    return call(
        routed_body,
        shapes,
        (1,),
        [whole(a.shape) for a in args[1:]],
        [whole(s.shape) for s in shapes],
        args,
        flops=2 * micros * rows * width * 3 * width,
        moved=9_000_000,
    )


def light_in_body(info, x, small, w_own, w_got, out):
    values = x[0].astype(F32)
    low = (values * inverse_rms(values) * small[3:4].astype(F32)).astype(BF)
    own, other = halves(info, low)
    out[0] = (mm(own, w_own[...]) + mm(other, w_got[...])).astype(BF)


def light_in(info, x, small, w_own, w_got):
    micros, tok, width = x.shape
    columns = w_own.shape[1]
    split = 2
    rows = tok // split
    spec = lambda n: pl.BlockSpec((1, rows, n), lambda i, *u: (i // split, i % split, 0))
    return call(
        light_in_body,
        sds((micros, tok, columns), BF),
        (micros * split,),
        [spec(width), whole(small.shape), whole(w_own.shape), whole(w_got.shape)],
        spec(columns),
        (info, x, small, w_own, w_got),
        flops=2 * micros * tok * width * columns,
        moved=8_000_000,
    )


def fill_near(near, qkv, before, after):
    tok = qkv.shape[1]
    inner = near.shape[1] // 2
    near[:WIN] = before[0]
    near[WIN : WIN + tok] = qkv[0, :, inner:]
    near[WIN + tok :] = after[0]


def light_bias(info, micro, block):
    start = info[1] + block * WIN
    rows, columns = (WIN, 3 * WIN)
    row_pos = start + iota((rows, 1), 0)
    col_pos = start - WIN + iota((1, columns), 1)
    seg_row = segment(info, micro, row_pos)
    seg_col = jnp.where((col_pos >= 0) & (col_pos < info[2]), segment(info, micro, col_pos), -1)
    shift = iota((rows, columns), 0) + WIN - iota((rows, columns), 1)
    allowed = (jnp.abs(shift) < WIN) & (seg_row == seg_col)
    bias = jnp.where(allowed, 0.0, FAR)
    return jnp.concatenate([bias, bias], axis=0)


def stacked(pair, low_lane):
    zero = jnp.zeros_like(pair)
    return jnp.concatenate(
        [jnp.where(low_lane, pair, zero), jnp.where(low_lane, zero, pair)], axis=0
    )


def merged(values, low_lane):
    rows = values.shape[0] // 2
    return jnp.where(low_lane, values[:rows], values[rows:])


def light_fwd_body(info, qkv, before, after, out, lse_out, near):
    micro = pl.program_id(0)
    tok = qkv.shape[1]
    inner = out.shape[2]
    fill_near(near, qkv, before, after)
    low_lane = iota((WIN, LANES), 1) < HD
    lane = iota((WIN, LANES), 1)

    def block_step(block, carry):
        at = pl.ds(pl.multiple_of(block * WIN, WIN), WIN)
        around = pl.ds(pl.multiple_of(block * WIN, WIN), 3 * WIN)
        bias = light_bias(info, micro, block)
        stats = jnp.zeros((WIN, LANES), F32)
        for pair in range(inner // LANES):
            cut = slice(pair * LANES, (pair + 1) * LANES)
            query = stacked(qkv[0, at, cut] * BF(HD**-0.5), low_lane)
            scores = mm_t(query, near[around, cut]) + bias
            top = jnp.max(scores, axis=-1, keepdims=True)
            weights = jnp.exp(scores - top)
            total = jnp.sum(weights, axis=-1, keepdims=True)
            value = near[around, inner + pair * LANES : inner + (pair + 1) * LANES]
            mixed = mm((weights * (1.0 / total)).astype(BF), value)
            out[0, at, cut] = merged(mixed, low_lane).astype(BF)
            lse = top + jnp.log(total)
            stats = jnp.where(lane == 2 * pair, lse[:WIN], stats)
            stats = jnp.where(lane == 2 * pair + 1, lse[WIN:], stats)
        lse_out[0, at, :] = stats
        return carry

    lax.fori_loop(0, tok // WIN, block_step, 0)


def light_fwd(info, qkv, before, after):
    micros, tok, columns = qkv.shape
    inner = columns // 3
    shapes = [sds((micros, tok, inner), BF), sds((micros, tok, LANES), F32)]
    args = (info, qkv, before, after)
    return call(
        light_fwd_body,
        shapes,
        (micros,),
        [one_of(a.shape) for a in args[1:]],
        [one_of(s.shape) for s in shapes],
        args,
        scratch=[pltpu.VMEM((tok + 2 * WIN, 2 * inner), BF)],
        flops=4_000_000_000,
        moved=6_000_000,
    )


def light_bwd_body(info, qkv, before, after, lse, grad, dq_out, own_out, low_out, high_out, near, dk, dv):
    micro = pl.program_id(0)
    tok = qkv.shape[1]
    inner = grad.shape[2]
    fill_near(near, qkv, before, after)
    dk[...] = jnp.zeros_like(dk)
    dv[...] = jnp.zeros_like(dv)
    low_lane = iota((WIN, LANES), 1) < HD

    def block_step(block, carry):
        at = pl.ds(pl.multiple_of(block * WIN, WIN), WIN)
        around = pl.ds(pl.multiple_of(block * WIN, WIN), 3 * WIN)
        bias = light_bias(info, micro, block)
        stats = lse[0, at, :]
        for pair in range(inner // LANES):
            cut = slice(pair * LANES, (pair + 1) * LANES)
            query = stacked(qkv[0, at, cut] * BF(HD**-0.5), low_lane)
            key = near[around, cut]
            value = near[around, inner + pair * LANES : inner + (pair + 1) * LANES]
            shift = jnp.concatenate(
                [stats[:, 2 * pair : 2 * pair + 1], stats[:, 2 * pair + 1 : 2 * pair + 2]], axis=0
            )
            probs = jnp.exp(mm_t(query, key) + bias - shift)
            upper = stacked(grad[0, at, cut], low_lane)
            grad_probs = mm_t(upper, value)
            center = jnp.sum(probs * grad_probs, axis=-1, keepdims=True)
            slope = (probs * (grad_probs - center)).astype(BF)
            dq_out[0, at, cut] = (merged(mm(slope, key), low_lane) * HD**-0.5).astype(BF)
            dk[around, cut] += t_mm(slope, query)
            dv[around, cut] += t_mm(probs.astype(BF), upper)
        return carry

    lax.fori_loop(0, tok // WIN, block_step, 0)
    own_out[0, :, :inner] = dk[WIN : WIN + tok]
    own_out[0, :, inner:] = dv[WIN : WIN + tok]
    low_out[0, :, :inner] = dk[:WIN].astype(BF)
    low_out[0, :, inner:] = dv[:WIN].astype(BF)
    high_out[0, :, :inner] = dk[WIN + tok :].astype(BF)
    high_out[0, :, inner:] = dv[WIN + tok :].astype(BF)


def light_bwd(info, qkv, before, after, lse, grad):
    micros, tok, columns = qkv.shape
    inner = columns // 3
    shapes = [
        sds((micros, tok, inner), BF),
        sds((micros, tok, 2 * inner), F32),
        sds((micros, WIN, 2 * inner), BF),
        sds((micros, WIN, 2 * inner), BF),
    ]
    args = (info, qkv, before, after, lse, grad)
    return call(
        light_bwd_body,
        shapes,
        (micros,),
        [one_of(a.shape) for a in args[1:]],
        [one_of(s.shape) for s in shapes],
        args,
        scratch=[
            pltpu.VMEM((tok + 2 * WIN, 2 * inner), BF),
            pltpu.VMEM((tok + 2 * WIN, inner), F32),
            pltpu.VMEM((tok + 2 * WIN, inner), F32),
        ],
        flops=10_000_000_000,
        moved=14_000_000,
    )


def heavy_scores(query, parts, bias, cut):
    return [mm_t(query, part[:, cut]) + b for part, b in zip(parts, bias)]


def heavy_fwd_body(info, q, kv_a, kv_b, out, lse_out):
    rows, width = out.shape
    parts = (kv_a, kv_b)
    low_lane = iota((rows, LANES), 1) < HD
    lane = iota((rows, LANES), 1)
    feature = jnp.concatenate([q[:, width:]] * 2, axis=0)
    bias = [mm_t(feature, part[:, 2 * width :]) for part in parts]
    stats = jnp.zeros((rows, LANES), F32)
    for pair in range(width // LANES):
        cut = slice(pair * LANES, (pair + 1) * LANES)
        query = stacked(q[:, cut] * BF(HD**-0.5), low_lane)
        scores = heavy_scores(query, parts, bias, cut)
        top = functools.reduce(
            jnp.maximum, [jnp.max(s, axis=-1, keepdims=True) for s in scores]
        )
        weights = [jnp.exp(s - top) for s in scores]
        total = sum(jnp.sum(w, axis=-1, keepdims=True) for w in weights)
        scale = 1.0 / total
        mixed = sum(
            mm((w * scale).astype(BF), part[:, width + pair * LANES : width + (pair + 1) * LANES])
            for w, part in zip(weights, parts)
        )
        out[:, cut] = merged(mixed, low_lane).astype(BF)
        lse = top + jnp.log(total)
        stats = jnp.where(lane == 2 * pair, lse[:rows], stats)
        stats = jnp.where(lane == 2 * pair + 1, lse[rows:], stats)
    lse_out[...] = stats


def heavy_fwd(info, q, kv_a, kv_b):
    rows = q.shape[0]
    width = q.shape[1] - LANES
    shapes = [sds((rows, width), BF), sds((rows, LANES), F32)]
    args = (info, q, kv_a, kv_b)
    return call(
        heavy_fwd_body,
        shapes,
        (1,),
        [whole(a.shape) for a in args[1:]],
        [whole(s.shape) for s in shapes],
        args,
        flops=1_500_000_000,
        moved=4_000_000,
    )


def heavy_bwd_body(info, q, kv_a, kv_b, lse, grad, dq_out, da_out, db_out):
    rows, width = grad.shape
    parts = (kv_a, kv_b)
    low_lane = iota((rows, LANES), 1) < HD
    feature = jnp.concatenate([q[:, width:]] * 2, axis=0)
    bias = [mm_t(feature, part[:, 2 * width :]) for part in parts]
    for pair in range(width // LANES):
        cut = slice(pair * LANES, (pair + 1) * LANES)
        upcut = slice(width + pair * LANES, width + (pair + 1) * LANES)
        query = stacked(q[:, cut] * BF(HD**-0.5), low_lane)
        shift = jnp.concatenate(
            [lse[:, 2 * pair : 2 * pair + 1], lse[:, 2 * pair + 1 : 2 * pair + 2]], axis=0
        )
        probs = [jnp.exp(s - shift) for s in heavy_scores(query, parts, bias, cut)]
        upper = stacked(grad[:, cut], low_lane)
        grads = [mm_t(upper, part[:, upcut]) for part in parts]
        center = sum(jnp.sum(p * g, axis=-1, keepdims=True) for p, g in zip(probs, grads))
        slopes = [(p * (g - center)).astype(BF) for p, g in zip(probs, grads)]
        dq = sum(mm(s, part[:, cut]) for s, part in zip(slopes, parts))
        dq_out[:, cut] = (merged(dq, low_lane) * HD**-0.5).astype(BF)
        for target, slope, prob in zip((da_out, db_out), slopes, probs):
            target[:, cut] = t_mm(slope, query).astype(BF)
            target[:, upcut] = t_mm(prob.astype(BF), upper).astype(BF)


def heavy_bwd(info, q, kv_a, kv_b, lse, grad):
    rows = q.shape[0]
    width = q.shape[1] - LANES
    shapes = [sds((rows, width), BF)] + [sds((kv.shape[0], 2 * width), BF) for kv in (kv_a, kv_b)]
    args = (info, q, kv_a, kv_b, lse, grad)
    return call(
        heavy_bwd_body,
        shapes,
        (1,),
        [whole(a.shape) for a in args[1:]],
        [whole(s.shape) for s in shapes],
        args,
        flops=4_000_000_000,
        moved=8_000_000,
    )


def middle_body(info, x, up, cols, rows, small, gate, lo, lout, ho, hout, y_out, low_out, ffr_out, dzh_out, hy_out, gf_out):
    tok = x.shape[1]
    base = info[1]
    hy = mm(ho[0], hout[...])
    hy_out[0] = hy
    spread = onehot_rows(rows[0, 0], base, tok)
    y = x[0].astype(F32) + mm(lo[0], lout[...]) + pick(spread, hy * gate[0, :, 0:1])
    y_out[0] = y
    low = (y * inverse_rms(y) * small[4:5].astype(F32)).astype(BF)
    low_out[0] = low
    take = onehot_cols(cols[2, 0], base, tok)
    taken = mm(take, low)
    ffr_out[0] = taken.astype(BF)
    gf = jax.nn.sigmoid(jnp.sum(taken * small[2:3].astype(F32), axis=-1, keepdims=True))
    dzh_out[0] = (mm(take, up[0]) * gf).astype(BF)
    gf_out[0] = jnp.broadcast_to(gf, gf_out.shape[1:])


def second_of(shape):
    rank = len(shape)
    return pl.BlockSpec(
        (shape[0], 1) + tuple(shape[2:]), lambda i, *unused: (0, i) + (0,) * (rank - 2)
    )


def middle(info, x, up, cols, rows, small, gate, lo, lout, ho, hout):
    micros, tok, width = x.shape
    count = cols.shape[2]
    shapes = [
        sds((micros, tok, width), F32),
        sds((micros, tok, width), BF),
        sds((micros, count, width), BF),
        sds((micros, count, width), BF),
        sds((micros, count, width), F32),
        sds((micros, count, LANES), F32),
    ]
    args = (info, x, up, cols, rows, small, gate, lo, lout, ho, hout)
    return call(
        middle_body,
        shapes,
        (micros,),
        [
            one_of(x.shape),
            one_of(up.shape),
            second_of(cols.shape),
            second_of(rows.shape),
            whole(small.shape),
            one_of(gate.shape),
            one_of(lo.shape),
            whole(lout.shape),
            one_of(ho.shape),
            whole(hout.shape),
        ],
        [one_of(s.shape) for s in shapes],
        args,
        flops=2_000_000_000,
        moved=12_000_000,
    )


def pack_rows(target, values):
    step = values.shape[0] // 16
    cuts = values.shape[1] // COLS
    for slot in range(16):
        for cut in range(cuts):
            at = slot * step * cuts + cut * step
            target[0, at : at + step] = values[
                slot * step : (slot + 1) * step, cut * COLS : (cut + 1) * COLS
            ].astype(BF)


def ffn_body(info, a, ct, wg, wu, wd, z_out, dh_out, own_gu, other_gu, own_dn, other_dn):
    step = pl.program_id(0)
    half = pl.num_programs(0) // 2
    width = a.shape[1] // 2
    low, upstream = (a[...], ct[...])
    g, u = (mm(low, wg[...]), mm(low, wu[...]))
    back = mm_t(upstream, wd[...])
    root = (2.0 / 3.141592653589793) ** 0.5
    square = g * g
    tanh = jnp.tanh(root * g * (1.0 + 0.044715 * square))
    bell = 0.5 * (1.0 + tanh)
    gelu = g * bell
    hidden = (gelu * u).astype(BF)
    slope = bell + 0.5 * g * (1.0 - tanh * tanh) * (root * (1.0 + 3 * 0.044715 * square))
    dg = (back * u * slope).astype(BF)
    du = (back * gelu).astype(BF)
    z = mm(hidden, wd[...])
    dh = mm_t(dg, wg[...]) + mm_t(du, wu[...])

    @pl.when(step == 0)
    def first():
        z_out[...] = z
        dh_out[...] = dh

    @pl.when(step > 0)
    def later():
        z_out[...] += z
        dh_out[...] += dh

    down = t_mm(hidden, upstream)

    @pl.when(step < half)
    def send():
        pack_rows(other_dn, down)

    @pl.when(step >= half)
    def keep():
        pack_rows(own_dn, down)

    own = a[:, pl.ds(pl.multiple_of(info[0] * width, width), width)]
    other = a[:, pl.ds(pl.multiple_of((1 - info[0]) * width, width), width)]
    own_gu[0, :width] = t_mm(own, dg).astype(BF)
    own_gu[0, width:] = t_mm(own, du).astype(BF)
    other_gu[0, :width] = t_mm(other, dg).astype(BF)
    other_gu[0, width:] = t_mm(other, du).astype(BF)


def ffn(info, a, ct, w_gu, w_down):
    rows, width = a.shape
    hidden = w_down.shape[0]
    block = COLS
    steps = hidden // block
    half = steps // 2

    def natural(i, info):
        return jnp.where(i < half, (1 - info[0]) * half + i, info[0] * half + i - half)

    unit = (1, width, COLS)
    shapes = [
        sds((rows, width), F32),
        sds((rows, width), F32),
        sds((steps,) + unit[1:], BF),
        sds((steps,) + unit[1:], BF),
        sds((half,) + unit[1:], BF),
        sds((half,) + unit[1:], BF),
    ]
    return call(
        ffn_body,
        shapes,
        (steps,),
        [
            whole(a.shape),
            whole(ct.shape),
            pl.BlockSpec((width, block), lambda i, info: (0, natural(i, info))),
            pl.BlockSpec((width, block), lambda i, info: (0, steps + natural(i, info))),
            pl.BlockSpec((block, width), lambda i, info: (natural(i, info), 0)),
        ],
        [
            whole((rows, width)),
            whole((rows, width)),
            pl.BlockSpec(unit, lambda i, info: (natural(i, info), 0, 0)),
            pl.BlockSpec(unit, lambda i, info: (natural(i, info), 0, 0)),
            pl.BlockSpec(unit, lambda i, info: (jnp.maximum(i - half, 0), 0, 0)),
            pl.BlockSpec(unit, lambda i, info: (jnp.minimum(i, half - 1), 0, 0)),
        ],
        (info, a, ct, w_gu, w_gu, w_down),
        flops=2 * 9 * rows * hidden * width,
        moved=2 * 2 * 3 * hidden * width + rows * width * 12,
    )


def mid_back_body(
    info, y, up, z, dh2, zh, dff, ffr, gf, cols, rows, small, gate, lout, hout, hy, hq,
    out, dy_out, dlo_out, dho_out, dhy_out, dsq_out, part_out,
):
    tok = y.shape[1]
    base = info[1]
    micro = pl.program_id(0)
    spread = onehot_rows(rows[2, 0], base, tok)
    take = onehot_cols(cols[2, 0], base, tok)
    values, top = (y[0], up[0].astype(F32))
    open_f = gf[0, :, 0:1]
    zhv = zh[0]
    out[0] = (values + z[0] + pick(spread, zhv * open_f)).astype(BF)
    taken = mm(take, up[0])
    dsf = jnp.sum(taken * zhv, axis=-1, keepdims=True) * open_f * (1.0 - open_f)
    back = dh2[0] + pick(spread, dff[0] + dsf * small[2:3].astype(F32))
    inv = inverse_rms(values)
    scaled = back * small[4:5].astype(F32)
    mean = jnp.mean(values * scaled, axis=-1, keepdims=True)
    dy = top + inv * scaled - values * (inv * inv * inv * mean)
    dy_out[0] = dy
    dgain = jnp.sum(back * values * inv, axis=0, keepdims=True)
    drf = jnp.sum(dsf * ffr[0].astype(F32), axis=0, keepdims=True)
    dlo_out[0] = mm_t(dy.astype(BF), lout[...]).astype(BF)
    dyq = pick(onehot_cols(cols[0, 0], base, tok), dy)
    open_q = gate[0, :, 0:1]
    dhy = (dyq * open_q).astype(BF)
    dhy_out[0] = dhy
    dsq = jnp.sum(dyq * hy[0], axis=-1, keepdims=True) * open_q * (1.0 - open_q)
    dsq_out[0] = jnp.broadcast_to(dsq, dsq_out.shape[1:])
    drq = jnp.sum(dsq * hq[0].astype(F32), axis=0, keepdims=True)
    dho_out[0] = mm_t(dhy, hout[...]).astype(BF)
    row = iota(part_out.shape, 0)
    part = jnp.where(row == 0, drq, jnp.where(row == 2, drf, jnp.where(row == 4, dgain, 0.0)))

    @pl.when(micro == 0)
    def first():
        part_out[...] = part

    @pl.when(micro > 0)
    def later():
        part_out[...] += part


def mid_back(info, y, up, z, dh2, zh, dff, ffr, gf, cols, rows, small, gate, lout, hout, hy, hq):
    micros, tok, width = y.shape
    count = cols.shape[2]
    shapes = [
        sds((micros, tok, width), BF),
        sds((micros, tok, width), F32),
        sds((micros, tok, lout.shape[0]), BF),
        sds((micros, count, width), BF),
        sds((micros, count, width), BF),
        sds((micros, count, LANES), F32),
        sds((8, width), F32),
    ]
    return call(
        mid_back_body,
        shapes,
        (micros,),
        [
            one_of(y.shape),
            one_of(up.shape),
            one_of(z.shape),
            one_of(dh2.shape),
            one_of(zh.shape),
            one_of(dff.shape),
            one_of(ffr.shape),
            one_of(gf.shape),
            second_of(cols.shape),
            second_of(rows.shape),
            whole(small.shape),
            one_of(gate.shape),
            whole(lout.shape),
            whole(hout.shape),
            one_of(hy.shape),
            one_of(hq.shape),
        ],
        [one_of(s.shape) for s in shapes[:-1]] + [whole(shapes[-1].shape)],
        (info, y, up, z, dh2, zh, dff, ffr, gf, cols, rows, small, gate, lout, hout, hy, hq),
        flops=3_000_000_000,
        moved=22_000_000,
    )


def in_back_body(
    info, x, dy, dq, own, got_low, got_high, dhq, dhkv, dsq, rows, small, gate, hq, kin, h1k, l_own, l_got, h_own, h_got,
    grad_out, dl_out, part_out,
):
    tok, width = x.shape[1:]
    micro = pl.program_id(0)
    base = info[1]
    inner = dq.shape[2]
    dl_out[0, :, :inner] = dq[0]
    dl_out[0, WIN : tok - WIN, inner:] = own[0, WIN : tok - WIN].astype(BF)
    dl_out[0, :WIN, inner:] = (own[0, :WIN] + got_low[0].astype(F32)).astype(BF)
    dl_out[0, tok - WIN :, inner:] = (own[0, tok - WIN :] + got_high[0].astype(F32)).astype(BF)
    light = dl_out[0]
    back = unhalved(info, mm_t(light, l_own[...]), mm_t(light, l_got[...]))
    dkin = unhalved(
        info, mm_t(dhkv[0], h_own[:, width:]), mm_t(dhkv[0], h_got[:, width:])
    )
    open_k = gate[0, :, 1:2]
    source = h1k[0]
    dskv = jnp.sum(dkin * source, axis=-1, keepdims=True) * open_k * (1.0 - open_k)
    to_q = unhalved(info, mm_t(dhq[0], h_own[:, :width]), mm_t(dhq[0], h_got[:, :width]))
    to_q += dsq[0, :, 0:1] * small[0:1].astype(F32)
    to_k = dkin * open_k + dskv * small[1:2].astype(F32)
    back += pick(onehot_rows(rows[0, 0], base, tok), to_q)
    back += pick(onehot_rows(rows[1, 0], base, tok), to_k)
    values = x[0].astype(F32)
    inv = inverse_rms(values)
    scaled = back * small[3:4].astype(F32)
    mean = jnp.mean(values * scaled, axis=-1, keepdims=True)
    grad_out[0] = (dy[0] + inv * scaled - values * (inv * inv * inv * mean)).astype(BF)
    dgain = jnp.sum(back * values * inv, axis=0, keepdims=True)
    drk = jnp.sum(dskv * source.astype(BF).astype(F32), axis=0, keepdims=True)
    row = iota(part_out.shape, 0)
    part = jnp.where(row == 1, drk, jnp.where(row == 3, dgain, 0.0))

    @pl.when(micro == 0)
    def first():
        part_out[...] = part

    @pl.when(micro > 0)
    def later():
        part_out[...] += part


def in_back(info, x, dy, dq, own, got_low, got_high, dhq, dhkv, dsq, rows, small, gate, hq, kin, h1k, l_own, l_got, h_own, h_got):
    micros, tok, width = x.shape
    shapes = [
        sds((micros, tok, width), BF),
        sds((micros, tok, l_own.shape[1]), BF),
        sds((8, width), F32),
    ]
    firsts = (x, dy, dq, own, got_low, got_high, dhq, dhkv, dsq)
    return call(
        in_back_body,
        shapes,
        (micros,),
        [one_of(a.shape) for a in firsts]
        + [second_of(rows.shape), whole(small.shape)]
        + [one_of(a.shape) for a in (gate, hq, kin, h1k)]
        + [whole(a.shape) for a in (l_own, l_got, h_own, h_got)],
        [one_of(s.shape) for s in shapes[:-1]] + [whole(shapes[-1].shape)],
        (info,) + firsts + (rows, small, gate, hq, kin, h1k, l_own, l_got, h_own, h_got),
        flops=4_000_000_000,
        moved=22_000_000,
    )


def grads_body(info, x, small, dl, hq, dhq, kin, dhkv, lo, dy, ho, dhy, own_out, other_out, low):
    micros, tok, width = x.shape
    half = width // 2
    for m in range(micros):
        values = x[m].astype(F32)
        low[m] = (values * inverse_rms(values) * small[3:4].astype(F32)).astype(BF)
    inner = lo.shape[2]
    for target, side in ((other_out, 1 - info[0]), (own_out, info[0])):
        cut = pl.ds(pl.multiple_of(side * half, half), half)

        def put(unit, left, right):
            for block in range(right[0].shape[1] // COLS):
                at = unit + block
                total = sum(
                    t_mm(a, b[:, block * COLS : (block + 1) * COLS]) for a, b in zip(left, right)
                )
                target[at // 2, (at % 2) * half : (at % 2 + 1) * half] = total.astype(BF)
            return unit + right[0].shape[1] // COLS

        every = range(micros)
        unit = put(0, [low[m, :, cut] for m in every], [dl[m] for m in every])
        unit = put(unit, [hq[m, :, cut] for m in every], [dhq[m] for m in every])
        unit = put(unit, [kin[m, :, cut] for m in every], [dhkv[m] for m in every])
        unit = put(unit, [ho[m, :, cut] for m in every], [dhy[m] for m in every])
        part = inner // 2
        small_cut = pl.ds(pl.multiple_of(side * part, part), part)
        total = sum(t_mm(lo[m, :, small_cut], dy[m].astype(BF)) for m in every)
        pack_rows(target.at[pl.ds(unit // 2, 1)], total)


def attention_grads(info, x, small, dl, hq, dhq, kin, dhkv, lo, dy, ho, dhy):
    micros, tok, width = x.shape
    units = (dl.shape[2] + dhq.shape[2] + dhkv.shape[2] + dhy.shape[2]) // COLS
    shapes = [sds((units // 2 + 1, width, COLS), BF)] * 2
    args = (info, x, small, dl, hq, dhq, kin, dhkv, lo, dy, ho, dhy)
    return call(
        grads_body,
        shapes,
        (1,),
        [whole(a.shape) for a in args[1:]],
        [whole(s.shape) for s in shapes],
        args,
        scratch=[pltpu.VMEM(x.shape, BF)],
        flops=2 * micros * tok * width * 2100,
        moved=20_000_000,
    )


def mask_of(slot, order):
    bits = len(order)
    return sum(order[b] for b in range(bits) if (slot >> (bits - 1 - b)) & 1)


def fold_body(order, counts, info, *refs):
    sources = refs[: 2 * len(counts)]
    keep, send = refs[2 * len(counts) :]
    slots = 1 << len(order)
    size = keep.shape[2]
    step = pl.program_id(0)
    start = 0
    for which, count in enumerate(counts):
        own, got = sources[2 * which : 2 * which + 2]

        @pl.when((step >= start) & (step < start + count))
        def part():
            for slot in range(slots):
                owner = jnp.bitwise_xor(info[3], mask_of(slot, order))
                at = pl.ds(pl.multiple_of(owner * size, size), size)
                total = (own[0, at, :].astype(F32) + got[0, at, :].astype(F32)).astype(BF)
                if slot < slots // 2:
                    keep[slot, 0] = total
                else:
                    send[slot - slots // 2, 0] = total

        start += count


def fold(info, order, parts):
    slots = 1 << len(order)
    width = parts[0][0].shape[1]
    counts = [part[3] for part in parts]
    total = sum(counts)
    shape = sds((slots // 2, total, width // slots, COLS), BF)
    args, specs = ([], [])
    start = 0
    for own, got, first, count in parts:
        index = functools.partial(
            lambda first, start, count, i, *u: (
                first + jnp.minimum(jnp.maximum(i - start, 0), count - 1),
                0,
                0,
            ),
            first,
            start,
            count,
        )
        args += [own, got]
        specs += [pl.BlockSpec((1, width, COLS), index)] * 2
        start += count
    spec = pl.BlockSpec((slots // 2, 1, width // slots, COLS), lambda i, *u: (0, i, 0, 0))
    return call(
        functools.partial(fold_body, order, counts),
        [shape, shape],
        (total,),
        specs,
        [spec, spec],
        (info, *args),
        moved=total * width * COLS * 6,
    )


def flipped(value, bit):
    size = lax.axis_size("ctx")
    return lax.ppermute(value, "ctx", [(i, i ^ bit) for i in range(size)])


def scatter_sum(keep, send, order):
    for bit in order:
        got = flipped(send, bit)
        half = keep.shape[0] // 2
        if half == 0:
            return (keep.astype(F32) + got.astype(F32)).astype(BF)
        send = (keep[half:].astype(F32) + got[half:].astype(F32)).astype(BF)
        keep = (keep[:half].astype(F32) + got[:half].astype(F32)).astype(BF)


def gather_pair(value, order):
    for bit in order[:-1]:
        value = jnp.concatenate([value, flipped(value, bit)], axis=0)
    return (value, flipped(value, order[-1]))


def reduced(info, order, parts):
    keep, send = fold(info, order, parts)
    own = scatter_sum(keep, send, order)
    return gather_pair(own, tuple(reversed(order)))


def place(info, order, near, far, block, part, half, write):
    slots = 1 << len(order)
    back = tuple(reversed(order))
    for slot in range(slots):
        mask = sum(back[b] for b in range(len(order)) if (slot >> b) & 1)
        owner = jnp.bitwise_xor(info[3], mask)
        source = near if slot < slots // 2 else far
        value = source[slot % (slots // 2), block].astype(F32)
        write(owner, value)


def unpack_gu_body(order, starts, info, near, far, out):
    side = pl.program_id(1)
    size = near.shape[2]

    def write(owner, value):
        per = out.shape[0] // size

        @pl.when(owner // per == side)
        def hit():
            out[pl.ds(pl.multiple_of((owner % per) * size, size), size), :] = value

    place(info, order, near, far, 0, None, None, write)


def unpack_dn_body(order, info, near, far, out):
    size = near.shape[2]
    cuts = out.shape[1] // COLS
    rows = size // cuts

    def write(owner, value):
        for cut in range(cuts):
            out[
                pl.ds(pl.multiple_of(owner * rows, rows), rows), cut * COLS : (cut + 1) * COLS
            ] = value[cut * rows : (cut + 1) * rows]

    place(info, order, near, far, 0, None, None, write)


def unpack_gu(info, order, pair, first, count, total, base, previous):
    near, far = pair
    slots, unused, size, unused_too = near.shape
    rows = size * slots
    spec = pl.BlockSpec((slots, 1, size, COLS), lambda i, s, *u: (0, first + i, 0, 0))
    out = sds((rows, 2 * total * COLS), F32)
    body = functools.partial(unpack_gu_body, order, None)
    args, specs = ([info, near, far], [spec, spec])
    aliases = {}
    if previous is not None:
        args.append(previous)
        specs.append(pl.BlockSpec(memory_space=pl.ANY))
        aliases = {3: 0}
        inner = body
        body = lambda info, near, far, unused, out: inner(info, near, far, out)
    return pl.pallas_call(
        body,
        out_shape=out,
        grid_spec=pltpu.PrefetchScalarGridSpec(
            num_scalar_prefetch=1,
            grid=(count, 2),
            in_specs=specs,
            out_specs=pl.BlockSpec((rows, COLS), lambda i, s, *u: (0, s * total + base + i)),
        ),
        input_output_aliases=aliases,
        cost_estimate=pl.CostEstimate(flops=0, bytes_accessed=count * rows * COLS * 12, transcendentals=0),
    )(*args)


def unpack_dn(info, order, pair, first, count, total, base, previous):
    near, far = pair
    slots, unused, size, unused_too = near.shape
    width = 2 * slots * size
    cuts = width // COLS
    rows = width * COLS // width
    spec = pl.BlockSpec((slots, 1, size, COLS), lambda i, *u: (0, first + i, 0, 0))
    out = sds((total * rows, width), F32)
    body = functools.partial(unpack_dn_body, order)
    args, specs = ([info, near, far], [spec, spec])
    aliases = {}
    if previous is not None:
        args.append(previous)
        specs.append(pl.BlockSpec(memory_space=pl.ANY))
        aliases = {3: 0}
        inner = body
        body = lambda info, near, far, unused, out: inner(info, near, far, out)
    return pl.pallas_call(
        body,
        out_shape=out,
        grid_spec=pltpu.PrefetchScalarGridSpec(
            num_scalar_prefetch=1,
            grid=(count,),
            in_specs=specs,
            out_specs=pl.BlockSpec((rows, width), lambda i, *u: (base + i, 0)),
        ),
        input_output_aliases=aliases,
        cost_estimate=pl.CostEstimate(flops=0, bytes_accessed=count * rows * width * 6, transcendentals=0),
    )(*args)


def unpack_attention_body(orders, widths, info, *refs):
    pairs, outs = (refs[: 2 * len(orders)], refs[2 * len(orders) :])
    unit = 0
    homes = []
    for which, columns in enumerate(widths):
        for block in range(columns // COLS):
            homes.append((which, block))
    start = 0
    for which, order in enumerate(orders):
        near, far = pairs[2 * which : 2 * which + 2]
        size = near.shape[2]
        for block in range(near.shape[1]):
            at = start + block

            def write(owner, value, at=at):
                if 2 * at >= len(homes):
                    out = outs[len(widths)]
                    cuts = out.shape[1] // COLS
                    rows = size // cuts
                    for cut in range(cuts):
                        out[
                            pl.ds(pl.multiple_of(owner * rows, rows), rows),
                            cut * COLS : (cut + 1) * COLS,
                        ] = value[cut * rows : (cut + 1) * rows]
                    return
                per = outs[0].shape[0] // size
                for side in range(2):
                    which_out, column = homes[2 * at + side]
                    out = outs[which_out]

                    @pl.when(owner // per == side)
                    def hit(out=out, column=column):
                        out[
                            pl.ds(pl.multiple_of((owner % per) * size, size), size),
                            column * COLS : (column + 1) * COLS,
                        ] = value

            place(info, order, near, far, block, None, None, write)
        start += near.shape[1]


def unpack_attention(info, orders, pairs, widths, inner):
    slots, unused, size, unused_too = pairs[0][0].shape
    half = slots * size
    shapes = [sds((half, w), F32) for w in widths] + [sds((inner // 2, 2 * half), F32)]
    args = [info] + [part for pair in pairs for part in pair]
    return call(
        functools.partial(unpack_attention_body, orders, widths),
        shapes,
        (1,),
        [whole(a.shape) for a in args[1:]],
        [whole(s.shape) for s in shapes],
        args,
        moved=14_000_000,
    )


def plain_gu(own, other):
    blocks, width, cols = own.shape

    def rows(part):
        return part.reshape(blocks, 2, width // 2, cols).transpose(2, 1, 0, 3).reshape(width // 2, -1)

    return jnp.concatenate([rows(own), rows(other)], axis=0)


def plain_dn(own, other):
    blocks, width, cols = own.shape
    cuts = width // cols

    def rows(part):
        return (
            part.reshape(blocks, 16, cuts, width // (16 * cuts), cols)
            .transpose(0, 1, 3, 2, 4)
            .reshape(-1, width)
        )

    return jnp.concatenate([rows(own), rows(other)], axis=0)


def plain_units(own, other, widths):
    def unit(part, at):
        half = part.shape[1] // 2
        return part[at // 2, (at % 2) * half : (at % 2 + 1) * half]

    result, at = ([], 0)
    for columns in widths:
        count = columns // COLS
        result.append(
            jnp.concatenate(
                [
                    jnp.concatenate([unit(part, at + i) for i in range(count)], axis=1)
                    for part in (own, other)
                ],
                axis=0,
            )
        )
        at += count
    return result


def plain_sum(grads):
    parts = [lax.psum_scatter(g.astype(BF), "wsh", scatter_dimension=0, tiled=True) for g in grads]
    return tuple(g.astype(F32) for g in lax.psum(parts, "ctx"))


def per_device(
    tokens, cotangent, light_qkv, light_out, heavy_qkv, heavy_out, light_gu, light_down, heavy_gu, heavy_down,
    routers, gains, doc_starts, q_index, kv_index, ff_index,
):
    micros, unused, tok, width = tokens.shape
    count, groups = (lax.axis_size("ctx"), lax.axis_size("wsh"))
    direct = groups == 2 and count == 16
    place_ctx = lax.axis_index("ctx")
    side = lax.axis_index("wsh") if direct else 0
    base = place_ctx * tok
    info = jnp.concatenate(
        [
            jnp.stack([jnp.int32(side), base, jnp.int32(tok * count), place_ctx]).astype(jnp.int32),
            doc_starts[:, 0].reshape(-1),
        ]
    )
    swap = [(0, 1), (1, 0)]

    def pair_of(shard):
        if direct:
            return (shard, lax.ppermute(shard, "wsh", swap))
        full = lax.all_gather(shard, "wsh", axis=0, tiled=True)
        return (full[: full.shape[0] // 2], full[full.shape[0] // 2 :])

    def full_of(shard, axis=0):
        return lax.all_gather(shard, "wsh", axis=axis, tiled=True)

    vectors = jnp.concatenate([routers, gains, jnp.zeros((3, routers.shape[1]), BF)], axis=0)
    if direct:
        got = lax.ppermute(vectors, "wsh", swap)
        small = jnp.concatenate(
            [jnp.where(side == 0, vectors, got), jnp.where(side == 0, got, vectors)], axis=1
        )
    else:
        small = full_of(vectors, 1)
    h_own, h_got = pair_of(heavy_qkv)
    l_own, l_got = pair_of(light_qkv)
    w_lout, w_hout = (full_of(light_out), full_of(heavy_out))
    w_hgu, w_hdown = (full_of(heavy_gu), full_of(heavy_down))
    w_lgu, w_ldown = (full_of(light_gu), full_of(light_down))

    x, up = (tokens[:, 0], cotangent[:, 0])
    index = jnp.stack([q_index[:, 0], kv_index[:, 0], ff_index[:, 0]])
    cols, rows = (index[..., None], index[:, :, None, :])

    q_pay, kv_pay, hq_in, kin, h1k, gate = routed_in(info, x, cols, small, h_own, h_got)
    kv_orders = ((8, 4, 2, 1), (8, 4, 1, 2))
    pairs = []
    for m in range(micros):
        if direct:
            pairs.append(gather_pair(kv_pay[m], kv_orders[m % 2]))
        else:
            every = lax.all_gather(kv_pay[m], "ctx", axis=0, tiled=True)
            pairs.append((every[: every.shape[0] // 2], every[every.shape[0] // 2 :]))
    qkv = light_in(info, x, small, l_own, l_got)
    inner = qkv.shape[2] // 3
    upward = [(i, i + 1) for i in range(count - 1)]
    downward = [(i + 1, i) for i in range(count - 1)]
    before = lax.ppermute(qkv[:, tok - WIN :, inner:], "ctx", upward)
    after = lax.ppermute(qkv[:, :WIN, inner:], "ctx", downward)
    lo, light_lse = light_fwd(info, qkv, before, after)
    heavy = [heavy_fwd(info, q_pay[m], *pairs[m]) for m in range(micros)]
    ho = jnp.stack([h[0] for h in heavy])
    y, low2, ffr, dzh, hy, gf = middle(info, x, up, cols, rows, small, gate, lo, w_lout, ho, w_hout)
    routed = ffr.shape[1]

    def flat(value):
        return value.reshape(-1, value.shape[-1])

    zh, dff, hgu_own, hgu_send, hdn_own, hdn_send = ffn(info, flat(ffr), flat(dzh), w_hgu, w_hdown)
    z, dh2, lgu_own, lgu_send, ldn_own, ldn_send = ffn(info, flat(low2), flat(up), w_lgu, w_ldown)
    if direct:
        hgu_got, hdn_got, lgu_got, ldn_got = (
            lax.ppermute(part, "wsh", swap) for part in (hgu_send, hdn_send, lgu_send, ldn_send)
        )
        orders = ((1, 2, 4, 8), (2, 1, 4, 8), (4, 1, 2, 8))
        chunks = (
            reduced(info, orders[0], [(hgu_own, hgu_got, 0, 8), (lgu_own, lgu_got, 0, 2)]),
            reduced(info, orders[1], [(hgu_own, hgu_got, 8, 8), (lgu_own, lgu_got, 2, 2)]),
            reduced(info, orders[2], [(hdn_own, hdn_got, 0, 8), (ldn_own, ldn_got, 0, 2)]),
        )

    def by_micro(value):
        return value.reshape(micros, -1, value.shape[-1])

    out_tokens, dy, dlo, dho, dhy, dsq, part_two = mid_back(
        info, y, up, by_micro(z), by_micro(dh2), by_micro(zh), by_micro(dff), ffr, gf, cols, rows, small, gate, w_lout,
        w_hout, hy, hq_in,
    )
    dhq, dhkv = ([], [])
    for m in range(micros):
        dq, near, far = heavy_bwd(info, q_pay[m], *pairs[m], heavy[m][1], dho[m])
        dhq.append(dq)
        if direct:
            order = tuple(reversed(kv_orders[m % 2]))
            shape = (count // 2, routed, 2 * width)
            dhkv.append(scatter_sum(near.reshape(shape), far.reshape(shape), order)[0])
        else:
            every = jnp.concatenate([near, far], axis=0)
            dhkv.append(lax.psum_scatter(every, "ctx", scatter_dimension=0, tiled=True))
    dhq, dhkv = (jnp.stack(dhq), jnp.stack(dhkv))
    dlq, dl_own, rim_low, rim_high = light_bwd(info, qkv, before, after, light_lse, dlo)
    got_low = lax.ppermute(rim_high, "ctx", upward)
    got_high = lax.ppermute(rim_low, "ctx", downward)
    grad_tokens, dl, part_one = in_back(
        info, x, dy, dlq, dl_own, got_low, got_high, dhq, dhkv, dsq, rows, small, gate, hq_in, kin, h1k, l_own, l_got,
        h_own, h_got,
    )
    att_own, att_send = attention_grads(info, x, small, dl, hq_in, dhq, kin, dhkv, lo, dy, ho, dhy)
    widths = (light_qkv.shape[1], heavy_qkv.shape[1], heavy_out.shape[1])
    vector = part_one + part_two
    if direct:
        att_got = lax.ppermute(att_send, "wsh", swap)
        pieces = ((0, 4), (4, 3), (7, 3))
        sums = [
            reduced(info, order, [(att_own, att_got, first, size)])
            for order, (first, size) in zip(orders, pieces)
        ]
        half = width // 2
        mine = lax.dynamic_slice_in_dim(vector, side * half, half, 1)
        given = lax.dynamic_slice_in_dim(vector, (1 - side) * half, half, 1)
        mine = mine + lax.ppermute(given, "wsh", swap)
        vector = jnp.sum(lax.all_gather(mine, "ctx", axis=0), axis=0)
        g_lqkv, g_hqkv, g_hout, g_lout = unpack_attention(info, orders, sums, widths, inner)
        first = unpack_gu(info, orders[0], chunks[0], 0, 8, 16, 0, None)
        g_hgu = unpack_gu(info, orders[1], chunks[1], 0, 8, 16, 8, first)
        first = unpack_gu(info, orders[0], chunks[0], 8, 2, 4, 0, None)
        g_lgu = unpack_gu(info, orders[1], chunks[1], 8, 2, 4, 2, first)
        g_hdown = unpack_dn(info, orders[2], chunks[2], 0, 8, 8, 0, None)
        g_ldown = unpack_dn(info, orders[2], chunks[2], 8, 2, 2, 0, None)
    else:
        g_lqkv, g_hqkv, g_hout = plain_units(att_own, att_send, widths)
        last = slice(att_own.shape[0] - 1, att_own.shape[0])
        g_lqkv, g_lout, g_hqkv, g_hout, g_lgu, g_ldown, g_hgu, g_hdown = plain_sum(
            [
                g_lqkv,
                plain_dn(att_own[last], att_send[last]),
                g_hqkv,
                g_hout,
                plain_gu(lgu_own, lgu_send),
                plain_dn(ldn_own, ldn_send),
                plain_gu(hgu_own, hgu_send),
                plain_dn(hdn_own, hdn_send),
            ]
        )
        vector = lax.psum(vector, ("ctx", "wsh"))
        part = width // groups
        vector = lax.dynamic_slice_in_dim(vector, lax.axis_index("wsh") * part, part, 1)
    return (
        out_tokens[:, None],
        grad_tokens[:, None],
        g_lqkv,
        g_lout,
        g_hqkv,
        g_hout,
        g_lgu,
        g_ldown,
        g_hgu,
        g_hdown,
        vector[:3],
        vector[3:5],
    )


def solution(mesh):
    return jax.shard_map(
        per_device,
        mesh=mesh,
        in_specs=(
            P(None, "wsh", "ctx", None),
            P(None, "wsh", "ctx", None),
            P("wsh", None),
            P("wsh", None),
            P("wsh", None),
            P("wsh", None),
            P("wsh", None),
            P("wsh", None),
            P("wsh", None),
            P("wsh", None),
            P(None, "wsh"),
            P(None, "wsh"),
            P(None, "wsh", None),
            P(None, "wsh", "ctx"),
            P(None, "wsh", "ctx"),
            P(None, "wsh", "ctx"),
        ),
        out_specs=(
            P(None, "wsh", "ctx", None),
            P(None, "wsh", "ctx", None),
            P("wsh", None),
            P("wsh", None),
            P("wsh", None),
            P("wsh", None),
            P("wsh", None),
            P("wsh", None),
            P("wsh", None),
            P("wsh", None),
            P(None, "wsh"),
            P(None, "wsh"),
        ),
        check_vma=False,
    )
```

```python
import functools

import jax
import jax.numpy as jnp
from jax import lax
from jax.experimental import pallas as pl
from jax.experimental.pallas import tpu as pltpu
from jax.sharding import PartitionSpec as P

HD = 64
WIN = 128
LANES = 128
COLS = 256
FAR = -1e30
EPS = 1e-06
BF = jnp.bfloat16
F32 = jnp.float32


def mm(left, right):
    return lax.dot_general(left, right, (((1,), (0,)), ((), ())), preferred_element_type=F32)


def mm_t(left, right):
    return lax.dot_general(left, right, (((1,), (1,)), ((), ())), preferred_element_type=F32)


def t_mm(left, right):
    return lax.dot_general(left, right, (((0,), (0,)), ((), ())), preferred_element_type=F32)


def pick(onehot, values):
    high = values.astype(BF)
    low = (values - high.astype(F32)).astype(BF)
    return mm(onehot, high) + mm(onehot, low)


def iota(shape, dim):
    return lax.broadcasted_iota(jnp.int32, shape, dim)


def onehot_cols(positions, base, length):
    return (iota((positions.shape[0], length), 1) == positions - base).astype(F32).astype(BF)


def onehot_rows(positions, base, length):
    return (iota((length, positions.shape[1]), 0) == positions - base).astype(F32).astype(BF)


def segment(info, micro, positions):
    total = jnp.full(positions.shape, -1, jnp.int32)
    for start in range(5):
        total += (positions >= info[4 + micro * 5 + start]).astype(jnp.int32)
    return total


def inverse_rms(values):
    return lax.rsqrt(jnp.mean(values * values, axis=-1, keepdims=True) + EPS)


def halves(info, values):
    half = values.shape[1] // 2
    first, second = (values[:, :half], values[:, half:])
    lower = info[0] == 0
    return (jnp.where(lower, first, second), jnp.where(lower, second, first))


def unhalved(info, own, other):
    lower = info[0] == 0
    return jnp.concatenate([jnp.where(lower, own, other), jnp.where(lower, other, own)], axis=1)


def call(body, outs, grid, in_specs, out_specs, args, scratch=(), flops=0, moved=0, limit=48, name=None):
    return pl.pallas_call(
        body,
        name=name or getattr(body, "__name__", "kernel"),
        out_shape=outs,
        grid_spec=pltpu.PrefetchScalarGridSpec(
            num_scalar_prefetch=1,
            grid=grid,
            in_specs=in_specs,
            out_specs=out_specs,
            scratch_shapes=list(scratch),
        ),
        compiler_params=pltpu.CompilerParams(vmem_limit_bytes=limit * 1024 * 1024),
        cost_estimate=pl.CostEstimate(flops=flops, bytes_accessed=moved, transcendentals=0),
    )(*args)


def whole(shape):
    rank = len(shape)
    return pl.BlockSpec(tuple(shape), lambda *unused: (0,) * rank)


def one_of(shape):
    rank = len(shape)
    return pl.BlockSpec((1,) + tuple(shape[1:]), lambda i, *unused: (i,) + (0,) * (rank - 1))


def sds(shape, dtype):
    return jax.ShapeDtypeStruct(tuple(shape), dtype)


def routed_body(info, x, cols, small, w_own, w_got, q_out, kv_out, hq_out, kin_out, h1k_out, gate_out):
    micros, tok, width = x.shape
    rows = cols.shape[2]
    base = info[1]
    gain = small[3:4].astype(F32)
    taken_q, taken_k = ([], [])
    for m in range(micros):
        both = jnp.concatenate([cols[0, m], cols[1, m]], axis=0)
        got = mm(onehot_cols(both, base, tok), x[m])
        taken_q.append(got[:rows])
        taken_k.append(got[rows:])
    xq, xk = (jnp.concatenate(taken_q, axis=0), jnp.concatenate(taken_k, axis=0))
    low_q = (xq * inverse_rms(xq) * gain).astype(BF)
    h1k = xk * inverse_rms(xk) * gain
    low_k = h1k.astype(BF)
    gate_q = jax.nn.sigmoid(
        jnp.sum(low_q.astype(F32) * small[0:1].astype(F32), axis=-1, keepdims=True)
    )
    gate_k = jax.nn.sigmoid(
        jnp.sum(low_k.astype(F32) * small[1:2].astype(F32), axis=-1, keepdims=True)
    )
    kin = (h1k * gate_k).astype(BF)
    own_q, other_q = halves(info, low_q)
    own_k, other_k = halves(info, kin)
    query = mm(own_q, w_own[:, :width]) + mm(other_q, w_got[:, :width])
    pair = mm(own_k, w_own[:, width:]) + mm(other_k, w_got[:, width:])
    lane = iota((rows, LANES), 1)
    for m in range(micros):
        part = slice(m * rows, (m + 1) * rows)
        q_out[m, :, :width] = query[part].astype(BF)
        kv_out[m, :, : 2 * width] = pair[part].astype(BF)
        seg_q = segment(info, m, cols[0, m])
        seg_k = segment(info, m, cols[1, m])
        q_out[m, :, width:] = (lane == seg_q).astype(F32).astype(BF)
        kv_out[m, :, 2 * width :] = jnp.where((lane < 8) & (lane != seg_k), FAR, 0.0).astype(BF)
        hq_out[m] = low_q[part]
        kin_out[m] = kin[part]
        h1k_out[m] = h1k[part]
        gate_out[m] = jnp.where(lane == 0, gate_q[part], gate_k[part])


def routed_in(info, x, cols, small, w_own, w_got):
    micros, unused, width = x.shape
    rows = cols.shape[2]
    shapes = [
        sds((micros, rows, width + LANES), BF),
        sds((micros, rows, 2 * width + LANES), BF),
        sds((micros, rows, width), BF),
        sds((micros, rows, width), BF),
        sds((micros, rows, width), F32),
        sds((micros, rows, LANES), F32),
    ]
    args = (info, x, cols, small, w_own, w_got)
    return call(
        routed_body,
        shapes,
        (1,),
        [whole(a.shape) for a in args[1:]],
        [whole(s.shape) for s in shapes],
        args,
        flops=2 * micros * rows * width * 3 * width,
        moved=9_000_000,
    )


def light_in_body(info, x, small, w_own, w_got, out):
    values = x[0].astype(F32)
    low = (values * inverse_rms(values) * small[3:4].astype(F32)).astype(BF)
    own, other = halves(info, low)
    out[0] = (mm(own, w_own[...]) + mm(other, w_got[...])).astype(BF)


def light_in(info, x, small, w_own, w_got):
    micros, tok, width = x.shape
    columns = w_own.shape[1]
    split = 2
    rows = tok // split
    spec = lambda n: pl.BlockSpec((1, rows, n), lambda i, *u: (i // split, i % split, 0))
    return call(
        light_in_body,
        sds((micros, tok, columns), BF),
        (micros * split,),
        [spec(width), whole(small.shape), whole(w_own.shape), whole(w_got.shape)],
        spec(columns),
        (info, x, small, w_own, w_got),
        flops=2 * micros * tok * width * columns,
        moved=8_000_000,
    )


def fill_near(near, qkv, before, after):
    tok = qkv.shape[1]
    inner = near.shape[1] // 2
    near[:WIN] = before[0]
    near[WIN : WIN + tok] = qkv[0, :, inner:]
    near[WIN + tok :] = after[0]


def light_bias(info, micro, block):
    start = info[1] + block * WIN
    rows, columns = (WIN, 3 * WIN)
    row_pos = start + iota((rows, 1), 0)
    col_pos = start - WIN + iota((1, columns), 1)
    seg_row = segment(info, micro, row_pos)
    seg_col = jnp.where((col_pos >= 0) & (col_pos < info[2]), segment(info, micro, col_pos), -1)
    shift = iota((rows, columns), 0) + WIN - iota((rows, columns), 1)
    allowed = (jnp.abs(shift) < WIN) & (seg_row == seg_col)
    bias = jnp.where(allowed, 0.0, FAR)
    return jnp.concatenate([bias, bias], axis=0)


def stacked(pair, low_lane):
    zero = jnp.zeros_like(pair)
    return jnp.concatenate(
        [jnp.where(low_lane, pair, zero), jnp.where(low_lane, zero, pair)], axis=0
    )


def merged(values, low_lane):
    rows = values.shape[0] // 2
    return jnp.where(low_lane, values[:rows], values[rows:])


def light_fwd_body(info, qkv, before, after, out, lse_out, near):
    micro = pl.program_id(0)
    tok = qkv.shape[1]
    inner = out.shape[2]
    fill_near(near, qkv, before, after)
    low_lane = iota((WIN, LANES), 1) < HD
    lane = iota((WIN, LANES), 1)

    def block_step(block, carry):
        at = pl.ds(pl.multiple_of(block * WIN, WIN), WIN)
        around = pl.ds(pl.multiple_of(block * WIN, WIN), 3 * WIN)
        bias = light_bias(info, micro, block)
        stats = jnp.zeros((WIN, LANES), F32)
        for pair in range(inner // LANES):
            cut = slice(pair * LANES, (pair + 1) * LANES)
            query = stacked(qkv[0, at, cut] * BF(HD**-0.5), low_lane)
            scores = mm_t(query, near[around, cut]) + bias
            top = jnp.max(scores, axis=-1, keepdims=True)
            weights = jnp.exp(scores - top)
            total = jnp.sum(weights, axis=-1, keepdims=True)
            value = near[around, inner + pair * LANES : inner + (pair + 1) * LANES]
            mixed = mm((weights * (1.0 / total)).astype(BF), value)
            out[0, at, cut] = merged(mixed, low_lane).astype(BF)
            lse = top + jnp.log(total)
            stats = jnp.where(lane == 2 * pair, lse[:WIN], stats)
            stats = jnp.where(lane == 2 * pair + 1, lse[WIN:], stats)
        lse_out[0, at, :] = stats
        return carry

    lax.fori_loop(0, tok // WIN, block_step, 0)


def light_fwd(info, qkv, before, after):
    micros, tok, columns = qkv.shape
    inner = columns // 3
    shapes = [sds((micros, tok, inner), BF), sds((micros, tok, LANES), F32)]
    args = (info, qkv, before, after)
    return call(
        light_fwd_body,
        shapes,
        (micros,),
        [one_of(a.shape) for a in args[1:]],
        [one_of(s.shape) for s in shapes],
        args,
        scratch=[pltpu.VMEM((tok + 2 * WIN, 2 * inner), BF)],
        flops=4_000_000_000,
        moved=6_000_000,
    )


def light_bwd_body(info, qkv, before, after, lse, grad, dq_out, own_out, low_out, high_out, near, dk, dv):
    micro = pl.program_id(0)
    tok = qkv.shape[1]
    inner = grad.shape[2]
    fill_near(near, qkv, before, after)
    dk[...] = jnp.zeros_like(dk)
    dv[...] = jnp.zeros_like(dv)
    low_lane = iota((WIN, LANES), 1) < HD

    def block_step(block, carry):
        at = pl.ds(pl.multiple_of(block * WIN, WIN), WIN)
        around = pl.ds(pl.multiple_of(block * WIN, WIN), 3 * WIN)
        bias = light_bias(info, micro, block)
        stats = lse[0, at, :]
        for pair in range(inner // LANES):
            cut = slice(pair * LANES, (pair + 1) * LANES)
            query = stacked(qkv[0, at, cut] * BF(HD**-0.5), low_lane)
            key = near[around, cut]
            value = near[around, inner + pair * LANES : inner + (pair + 1) * LANES]
            shift = jnp.concatenate(
                [stats[:, 2 * pair : 2 * pair + 1], stats[:, 2 * pair + 1 : 2 * pair + 2]], axis=0
            )
            probs = jnp.exp(mm_t(query, key) + bias - shift)
            upper = stacked(grad[0, at, cut], low_lane)
            grad_probs = mm_t(upper, value)
            center = jnp.sum(probs * grad_probs, axis=-1, keepdims=True)
            slope = (probs * (grad_probs - center)).astype(BF)
            dq_out[0, at, cut] = (merged(mm(slope, key), low_lane) * HD**-0.5).astype(BF)
            dk[around, cut] += t_mm(slope, query)
            dv[around, cut] += t_mm(probs.astype(BF), upper)
        return carry

    lax.fori_loop(0, tok // WIN, block_step, 0)
    own_out[0, :, :inner] = dk[WIN : WIN + tok]
    own_out[0, :, inner:] = dv[WIN : WIN + tok]
    low_out[0, :, :inner] = dk[:WIN].astype(BF)
    low_out[0, :, inner:] = dv[:WIN].astype(BF)
    high_out[0, :, :inner] = dk[WIN + tok :].astype(BF)
    high_out[0, :, inner:] = dv[WIN + tok :].astype(BF)


def light_bwd(info, qkv, before, after, lse, grad):
    micros, tok, columns = qkv.shape
    inner = columns // 3
    shapes = [
        sds((micros, tok, inner), BF),
        sds((micros, tok, 2 * inner), F32),
        sds((micros, WIN, 2 * inner), BF),
        sds((micros, WIN, 2 * inner), BF),
    ]
    args = (info, qkv, before, after, lse, grad)
    return call(
        light_bwd_body,
        shapes,
        (micros,),
        [one_of(a.shape) for a in args[1:]],
        [one_of(s.shape) for s in shapes],
        args,
        scratch=[
            pltpu.VMEM((tok + 2 * WIN, 2 * inner), BF),
            pltpu.VMEM((tok + 2 * WIN, inner), F32),
            pltpu.VMEM((tok + 2 * WIN, inner), F32),
        ],
        flops=10_000_000_000,
        moved=14_000_000,
    )


def heavy_scores(query, parts, bias, cut):
    return [mm_t(query, part[:, cut]) + b for part, b in zip(parts, bias)]


def heavy_fwd_body(info, q, kv_a, kv_b, out, lse_out):
    rows, width = out.shape
    parts = (kv_a, kv_b)
    low_lane = iota((rows, LANES), 1) < HD
    lane = iota((rows, LANES), 1)
    feature = jnp.concatenate([q[:, width:]] * 2, axis=0)
    bias = [mm_t(feature, part[:, 2 * width :]) for part in parts]
    stats = jnp.zeros((rows, LANES), F32)
    for pair in range(width // LANES):
        cut = slice(pair * LANES, (pair + 1) * LANES)
        query = stacked(q[:, cut] * BF(HD**-0.5), low_lane)
        scores = heavy_scores(query, parts, bias, cut)
        top = functools.reduce(
            jnp.maximum, [jnp.max(s, axis=-1, keepdims=True) for s in scores]
        )
        weights = [jnp.exp(s - top) for s in scores]
        total = sum(jnp.sum(w, axis=-1, keepdims=True) for w in weights)
        scale = 1.0 / total
        mixed = sum(
            mm((w * scale).astype(BF), part[:, width + pair * LANES : width + (pair + 1) * LANES])
            for w, part in zip(weights, parts)
        )
        out[:, cut] = merged(mixed, low_lane).astype(BF)
        lse = top + jnp.log(total)
        stats = jnp.where(lane == 2 * pair, lse[:rows], stats)
        stats = jnp.where(lane == 2 * pair + 1, lse[rows:], stats)
    lse_out[...] = stats


def heavy_fwd(info, q, kv_a, kv_b):
    rows = q.shape[0]
    width = q.shape[1] - LANES
    shapes = [sds((rows, width), BF), sds((rows, LANES), F32)]
    args = (info, q, kv_a, kv_b)
    return call(
        heavy_fwd_body,
        shapes,
        (1,),
        [whole(a.shape) for a in args[1:]],
        [whole(s.shape) for s in shapes],
        args,
        flops=1_500_000_000,
        moved=4_000_000,
    )


def heavy_bwd_body(info, q, kv_a, kv_b, lse, grad, dq_out, da_out, db_out):
    rows, width = grad.shape
    parts = (kv_a, kv_b)
    low_lane = iota((rows, LANES), 1) < HD
    feature = jnp.concatenate([q[:, width:]] * 2, axis=0)
    bias = [mm_t(feature, part[:, 2 * width :]) for part in parts]
    for pair in range(width // LANES):
        cut = slice(pair * LANES, (pair + 1) * LANES)
        upcut = slice(width + pair * LANES, width + (pair + 1) * LANES)
        query = stacked(q[:, cut] * BF(HD**-0.5), low_lane)
        shift = jnp.concatenate(
            [lse[:, 2 * pair : 2 * pair + 1], lse[:, 2 * pair + 1 : 2 * pair + 2]], axis=0
        )
        probs = [jnp.exp(s - shift) for s in heavy_scores(query, parts, bias, cut)]
        upper = stacked(grad[:, cut], low_lane)
        grads = [mm_t(upper, part[:, upcut]) for part in parts]
        center = sum(jnp.sum(p * g, axis=-1, keepdims=True) for p, g in zip(probs, grads))
        slopes = [(p * (g - center)).astype(BF) for p, g in zip(probs, grads)]
        dq = sum(mm(s, part[:, cut]) for s, part in zip(slopes, parts))
        dq_out[:, cut] = (merged(dq, low_lane) * HD**-0.5).astype(BF)
        for target, slope, prob in zip((da_out, db_out), slopes, probs):
            target[:, cut] = t_mm(slope, query).astype(BF)
            target[:, upcut] = t_mm(prob.astype(BF), upper).astype(BF)


def heavy_bwd(info, q, kv_a, kv_b, lse, grad):
    rows = q.shape[0]
    width = q.shape[1] - LANES
    shapes = [sds((rows, width), BF)] + [sds((kv.shape[0], 2 * width), BF) for kv in (kv_a, kv_b)]
    args = (info, q, kv_a, kv_b, lse, grad)
    return call(
        heavy_bwd_body,
        shapes,
        (1,),
        [whole(a.shape) for a in args[1:]],
        [whole(s.shape) for s in shapes],
        args,
        flops=4_000_000_000,
        moved=8_000_000,
    )


def middle_body(info, x, up, cols, rows, small, gate, lo, lout, ho, hout, y_out, low_out, ffr_out, dzh_out, hy_out, gf_out):
    tok = x.shape[1]
    base = info[1]
    hy = mm(ho[0], hout[...])
    hy_out[0] = hy
    spread = onehot_rows(rows[0, 0], base, tok)
    y = x[0].astype(F32) + mm(lo[0], lout[...]) + pick(spread, hy * gate[0, :, 0:1])
    y_out[0] = y
    low = (y * inverse_rms(y) * small[4:5].astype(F32)).astype(BF)
    low_out[0] = low
    take = onehot_cols(cols[2, 0], base, tok)
    taken = mm(take, low)
    ffr_out[0] = taken.astype(BF)
    gf = jax.nn.sigmoid(jnp.sum(taken * small[2:3].astype(F32), axis=-1, keepdims=True))
    dzh_out[0] = (mm(take, up[0]) * gf).astype(BF)
    gf_out[0] = jnp.broadcast_to(gf, gf_out.shape[1:])


def second_of(shape):
    rank = len(shape)
    return pl.BlockSpec(
        (shape[0], 1) + tuple(shape[2:]), lambda i, *unused: (0, i) + (0,) * (rank - 2)
    )


def middle(info, x, up, cols, rows, small, gate, lo, lout, ho, hout):
    micros, tok, width = x.shape
    count = cols.shape[2]
    shapes = [
        sds((micros, tok, width), F32),
        sds((micros, tok, width), BF),
        sds((micros, count, width), BF),
        sds((micros, count, width), BF),
        sds((micros, count, width), F32),
        sds((micros, count, LANES), F32),
    ]
    args = (info, x, up, cols, rows, small, gate, lo, lout, ho, hout)
    return call(
        middle_body,
        shapes,
        (micros,),
        [
            one_of(x.shape),
            one_of(up.shape),
            second_of(cols.shape),
            second_of(rows.shape),
            whole(small.shape),
            one_of(gate.shape),
            one_of(lo.shape),
            whole(lout.shape),
            one_of(ho.shape),
            whole(hout.shape),
        ],
        [one_of(s.shape) for s in shapes],
        args,
        flops=2_000_000_000,
        moved=12_000_000,
    )


def pack_rows(target, values):
    step = values.shape[0] // 16
    cuts = values.shape[1] // COLS
    for slot in range(16):
        for cut in range(cuts):
            at = slot * step * cuts + cut * step
            target[0, at : at + step] = values[
                slot * step : (slot + 1) * step, cut * COLS : (cut + 1) * COLS
            ].astype(BF)


def ffn_body(info, a, ct, wg, wu, wd, z_out, dh_out, own_gu, other_gu, own_dn, other_dn):
    step = pl.program_id(0)
    half = pl.num_programs(0) // 2
    width = a.shape[1] // 2
    low, upstream = (a[...], ct[...])
    g, u = (mm(low, wg[...]), mm(low, wu[...]))
    back = mm_t(upstream, wd[...])
    root = (2.0 / 3.141592653589793) ** 0.5
    square = g * g
    tanh = jnp.tanh(root * g * (1.0 + 0.044715 * square))
    bell = 0.5 * (1.0 + tanh)
    gelu = g * bell
    hidden = (gelu * u).astype(BF)
    slope = bell + 0.5 * g * (1.0 - tanh * tanh) * (root * (1.0 + 3 * 0.044715 * square))
    dg = (back * u * slope).astype(BF)
    du = (back * gelu).astype(BF)
    z = mm(hidden, wd[...])
    dh = mm_t(dg, wg[...]) + mm_t(du, wu[...])

    @pl.when(step == 0)
    def first():
        z_out[...] = z
        dh_out[...] = dh

    @pl.when(step > 0)
    def later():
        z_out[...] += z
        dh_out[...] += dh

    down = t_mm(hidden, upstream)

    @pl.when(step < half)
    def send():
        pack_rows(other_dn, down)

    @pl.when(step >= half)
    def keep():
        pack_rows(own_dn, down)

    own = a[:, pl.ds(pl.multiple_of(info[0] * width, width), width)]
    other = a[:, pl.ds(pl.multiple_of((1 - info[0]) * width, width), width)]
    own_gu[0, :width] = t_mm(own, dg).astype(BF)
    own_gu[0, width:] = t_mm(own, du).astype(BF)
    other_gu[0, :width] = t_mm(other, dg).astype(BF)
    other_gu[0, width:] = t_mm(other, du).astype(BF)


def ffn(info, a, ct, w_gu, w_down):
    rows, width = a.shape
    hidden = w_down.shape[0]
    block = COLS
    steps = hidden // block
    half = steps // 2

    def natural(i, info):
        return jnp.where(i < half, (1 - info[0]) * half + i, info[0] * half + i - half)

    unit = (1, width, COLS)
    shapes = [
        sds((rows, width), F32),
        sds((rows, width), F32),
        sds((steps,) + unit[1:], BF),
        sds((steps,) + unit[1:], BF),
        sds((half,) + unit[1:], BF),
        sds((half,) + unit[1:], BF),
    ]
    return call(
        ffn_body,
        shapes,
        (steps,),
        [
            whole(a.shape),
            whole(ct.shape),
            pl.BlockSpec((width, block), lambda i, info: (0, natural(i, info))),
            pl.BlockSpec((width, block), lambda i, info: (0, steps + natural(i, info))),
            pl.BlockSpec((block, width), lambda i, info: (natural(i, info), 0)),
        ],
        [
            whole((rows, width)),
            whole((rows, width)),
            pl.BlockSpec(unit, lambda i, info: (natural(i, info), 0, 0)),
            pl.BlockSpec(unit, lambda i, info: (natural(i, info), 0, 0)),
            pl.BlockSpec(unit, lambda i, info: (jnp.maximum(i - half, 0), 0, 0)),
            pl.BlockSpec(unit, lambda i, info: (jnp.minimum(i, half - 1), 0, 0)),
        ],
        (info, a, ct, w_gu, w_gu, w_down),
        flops=2 * 9 * rows * hidden * width,
        moved=2 * 2 * 3 * hidden * width + rows * width * 12,
    )


def mid_back_body(
    info, y, up, z, dh2, zh, dff, ffr, gf, cols, rows, small, gate, lout, hout, hy, hq,
    out, dy_out, dlo_out, dho_out, dhy_out, dsq_out, part_out,
):
    tok = y.shape[1]
    base = info[1]
    micro = pl.program_id(0)
    spread = onehot_rows(rows[2, 0], base, tok)
    take = onehot_cols(cols[2, 0], base, tok)
    values, top = (y[0], up[0].astype(F32))
    open_f = gf[0, :, 0:1]
    zhv = zh[0]
    out[0] = (values + z[0] + pick(spread, zhv * open_f)).astype(BF)
    taken = mm(take, up[0])
    dsf = jnp.sum(taken * zhv, axis=-1, keepdims=True) * open_f * (1.0 - open_f)
    back = dh2[0] + pick(spread, dff[0] + dsf * small[2:3].astype(F32))
    inv = inverse_rms(values)
    scaled = back * small[4:5].astype(F32)
    mean = jnp.mean(values * scaled, axis=-1, keepdims=True)
    dy = top + inv * scaled - values * (inv * inv * inv * mean)
    dy_out[0] = dy
    dgain = jnp.sum(back * values * inv, axis=0, keepdims=True)
    drf = jnp.sum(dsf * ffr[0].astype(F32), axis=0, keepdims=True)
    dlo_out[0] = mm_t(dy.astype(BF), lout[...]).astype(BF)
    dyq = pick(onehot_cols(cols[0, 0], base, tok), dy)
    open_q = gate[0, :, 0:1]
    dhy = (dyq * open_q).astype(BF)
    dhy_out[0] = dhy
    dsq = jnp.sum(dyq * hy[0], axis=-1, keepdims=True) * open_q * (1.0 - open_q)
    dsq_out[0] = jnp.broadcast_to(dsq, dsq_out.shape[1:])
    drq = jnp.sum(dsq * hq[0].astype(F32), axis=0, keepdims=True)
    dho_out[0] = mm_t(dhy, hout[...]).astype(BF)
    row = iota(part_out.shape, 0)
    part = jnp.where(row == 0, drq, jnp.where(row == 2, drf, jnp.where(row == 4, dgain, 0.0)))

    @pl.when(micro == 0)
    def first():
        part_out[...] = part

    @pl.when(micro > 0)
    def later():
        part_out[...] += part


def mid_back(info, y, up, z, dh2, zh, dff, ffr, gf, cols, rows, small, gate, lout, hout, hy, hq):
    micros, tok, width = y.shape
    count = cols.shape[2]
    shapes = [
        sds((micros, tok, width), BF),
        sds((micros, tok, width), F32),
        sds((micros, tok, lout.shape[0]), BF),
        sds((micros, count, width), BF),
        sds((micros, count, width), BF),
        sds((micros, count, LANES), F32),
        sds((8, width), F32),
    ]
    return call(
        mid_back_body,
        shapes,
        (micros,),
        [
            one_of(y.shape),
            one_of(up.shape),
            one_of(z.shape),
            one_of(dh2.shape),
            one_of(zh.shape),
            one_of(dff.shape),
            one_of(ffr.shape),
            one_of(gf.shape),
            second_of(cols.shape),
            second_of(rows.shape),
            whole(small.shape),
            one_of(gate.shape),
            whole(lout.shape),
            whole(hout.shape),
            one_of(hy.shape),
            one_of(hq.shape),
        ],
        [one_of(s.shape) for s in shapes[:-1]] + [whole(shapes[-1].shape)],
        (info, y, up, z, dh2, zh, dff, ffr, gf, cols, rows, small, gate, lout, hout, hy, hq),
        flops=3_000_000_000,
        moved=22_000_000,
    )


def in_back_body(
    info, x, dy, dq, own, got_low, got_high, dhq, dhkv, dsq, rows, small, gate, hq, kin, h1k, l_own, l_got, h_own, h_got,
    grad_out, dl_out, part_out,
):
    tok, width = x.shape[1:]
    micro = pl.program_id(0)
    base = info[1]
    inner = dq.shape[2]
    dl_out[0, :, :inner] = dq[0]
    dl_out[0, WIN : tok - WIN, inner:] = own[0, WIN : tok - WIN].astype(BF)
    dl_out[0, :WIN, inner:] = (own[0, :WIN] + got_low[0].astype(F32)).astype(BF)
    dl_out[0, tok - WIN :, inner:] = (own[0, tok - WIN :] + got_high[0].astype(F32)).astype(BF)
    light = dl_out[0]
    back = unhalved(info, mm_t(light, l_own[...]), mm_t(light, l_got[...]))
    dkin = unhalved(
        info, mm_t(dhkv[0], h_own[:, width:]), mm_t(dhkv[0], h_got[:, width:])
    )
    open_k = gate[0, :, 1:2]
    source = h1k[0]
    dskv = jnp.sum(dkin * source, axis=-1, keepdims=True) * open_k * (1.0 - open_k)
    to_q = unhalved(info, mm_t(dhq[0], h_own[:, :width]), mm_t(dhq[0], h_got[:, :width]))
    to_q += dsq[0, :, 0:1] * small[0:1].astype(F32)
    to_k = dkin * open_k + dskv * small[1:2].astype(F32)
    back += pick(onehot_rows(rows[0, 0], base, tok), to_q)
    back += pick(onehot_rows(rows[1, 0], base, tok), to_k)
    values = x[0].astype(F32)
    inv = inverse_rms(values)
    scaled = back * small[3:4].astype(F32)
    mean = jnp.mean(values * scaled, axis=-1, keepdims=True)
    grad_out[0] = (dy[0] + inv * scaled - values * (inv * inv * inv * mean)).astype(BF)
    dgain = jnp.sum(back * values * inv, axis=0, keepdims=True)
    drk = jnp.sum(dskv * source.astype(BF).astype(F32), axis=0, keepdims=True)
    row = iota(part_out.shape, 0)
    part = jnp.where(row == 1, drk, jnp.where(row == 3, dgain, 0.0))

    @pl.when(micro == 0)
    def first():
        part_out[...] = part

    @pl.when(micro > 0)
    def later():
        part_out[...] += part


def in_back(info, x, dy, dq, own, got_low, got_high, dhq, dhkv, dsq, rows, small, gate, hq, kin, h1k, l_own, l_got, h_own, h_got):
    micros, tok, width = x.shape
    shapes = [
        sds((micros, tok, width), BF),
        sds((micros, tok, l_own.shape[1]), BF),
        sds((8, width), F32),
    ]
    firsts = (x, dy, dq, own, got_low, got_high, dhq, dhkv, dsq)
    return call(
        in_back_body,
        shapes,
        (micros,),
        [one_of(a.shape) for a in firsts]
        + [second_of(rows.shape), whole(small.shape)]
        + [one_of(a.shape) for a in (gate, hq, kin, h1k)]
        + [whole(a.shape) for a in (l_own, l_got, h_own, h_got)],
        [one_of(s.shape) for s in shapes[:-1]] + [whole(shapes[-1].shape)],
        (info,) + firsts + (rows, small, gate, hq, kin, h1k, l_own, l_got, h_own, h_got),
        flops=4_000_000_000,
        moved=22_000_000,
    )


def grads_body(info, x, small, dl, hq, dhq, kin, dhkv, lo, dy, ho, dhy, own_out, other_out, low):
    micros, tok, width = x.shape
    half = width // 2
    for m in range(micros):
        values = x[m].astype(F32)
        low[m] = (values * inverse_rms(values) * small[3:4].astype(F32)).astype(BF)
    inner = lo.shape[2]
    for target, side in ((other_out, 1 - info[0]), (own_out, info[0])):
        cut = pl.ds(pl.multiple_of(side * half, half), half)

        def put(unit, left, right):
            for block in range(right[0].shape[1] // COLS):
                at = unit + block
                total = sum(
                    t_mm(a, b[:, block * COLS : (block + 1) * COLS]) for a, b in zip(left, right)
                )
                target[at // 2, (at % 2) * half : (at % 2 + 1) * half] = total.astype(BF)
            return unit + right[0].shape[1] // COLS

        every = range(micros)
        unit = put(0, [low[m, :, cut] for m in every], [dl[m] for m in every])
        unit = put(unit, [hq[m, :, cut] for m in every], [dhq[m] for m in every])
        unit = put(unit, [kin[m, :, cut] for m in every], [dhkv[m] for m in every])
        unit = put(unit, [ho[m, :, cut] for m in every], [dhy[m] for m in every])
        part = inner // 2
        small_cut = pl.ds(pl.multiple_of(side * part, part), part)
        total = sum(t_mm(lo[m, :, small_cut], dy[m].astype(BF)) for m in every)
        pack_rows(target.at[pl.ds(unit // 2, 1)], total)


def attention_grads(info, x, small, dl, hq, dhq, kin, dhkv, lo, dy, ho, dhy):
    micros, tok, width = x.shape
    units = (dl.shape[2] + dhq.shape[2] + dhkv.shape[2] + dhy.shape[2]) // COLS
    shapes = [sds((units // 2 + 1, width, COLS), BF)] * 2
    args = (info, x, small, dl, hq, dhq, kin, dhkv, lo, dy, ho, dhy)
    return call(
        grads_body,
        shapes,
        (1,),
        [whole(a.shape) for a in args[1:]],
        [whole(s.shape) for s in shapes],
        args,
        scratch=[pltpu.VMEM(x.shape, BF)],
        flops=2 * micros * tok * width * 2100,
        moved=20_000_000,
    )


def mask_of(slot, order):
    bits = len(order)
    return sum(order[b] for b in range(bits) if (slot >> (bits - 1 - b)) & 1)


def fold_body(order, counts, info, *refs):
    sources = refs[: 2 * len(counts)]
    keep, send = refs[2 * len(counts) :]
    slots = 1 << len(order)
    size = keep.shape[2]
    step = pl.program_id(0)
    start = 0
    for which, count in enumerate(counts):
        own, got = sources[2 * which : 2 * which + 2]

        @pl.when((step >= start) & (step < start + count))
        def part():
            for slot in range(slots):
                owner = jnp.bitwise_xor(info[3], mask_of(slot, order))
                at = pl.ds(pl.multiple_of(owner * size, size), size)
                total = (own[0, at, :].astype(F32) + got[0, at, :].astype(F32)).astype(BF)
                if slot < slots // 2:
                    keep[slot, 0] = total
                else:
                    send[slot - slots // 2, 0] = total

        start += count


def fold(info, order, parts):
    slots = 1 << len(order)
    width = parts[0][0].shape[1]
    counts = [part[3] for part in parts]
    total = sum(counts)
    shape = sds((slots // 2, total, width // slots, COLS), BF)
    args, specs = ([], [])
    start = 0
    for own, got, first, count in parts:
        index = functools.partial(
            lambda first, start, count, i, *u: (
                first + jnp.minimum(jnp.maximum(i - start, 0), count - 1),
                0,
                0,
            ),
            first,
            start,
            count,
        )
        args += [own, got]
        specs += [pl.BlockSpec((1, width, COLS), index)] * 2
        start += count
    spec = pl.BlockSpec((slots // 2, 1, width // slots, COLS), lambda i, *u: (0, i, 0, 0))
    return call(
        functools.partial(fold_body, order, counts),
        [shape, shape],
        (total,),
        specs,
        [spec, spec],
        (info, *args),
        moved=total * width * COLS * 6,
    )


def flipped(value, bit):
    size = lax.axis_size("ctx")
    return lax.ppermute(value, "ctx", [(i, i ^ bit) for i in range(size)])


def tied(*values):
    return lax.optimization_barrier(values)


def scatter_step(keep, got):
    half = keep.shape[0] // 2
    if half == 0:
        return ((keep.astype(F32) + got.astype(F32)).astype(BF), None)
    return (
        (keep[:half].astype(F32) + got[:half].astype(F32)).astype(BF),
        (keep[half:].astype(F32) + got[half:].astype(F32)).astype(BF),
    )


def scatter_start(chunks, orders, stage):
    return [flipped(send, order[stage]) for (keep, send), order in zip(chunks, orders)]


def scatter_end(chunks, got):
    return [scatter_step(keep, g) for (keep, send), g in zip(chunks, got)]


def scatter_sum(keep, send, order):
    for bit in order:
        keep, send = scatter_step(keep, flipped(send, bit))
    return keep


def gather_start(values, orders, stage):
    return [flipped(value, order[-1 - stage]) for value, order in zip(values, orders)]


def gather_end(values, got):
    return [jnp.concatenate([value, g], axis=0) for value, g in zip(values, got)]


def gather_pair(value, order):
    for bit in order[:-1]:
        value = jnp.concatenate([value, flipped(value, bit)], axis=0)
    return (value, flipped(value, order[-1]))


def place(info, order, near, far, block, part, half, write):
    slots = 1 << len(order)
    back = tuple(reversed(order))
    for slot in range(slots):
        mask = sum(back[b] for b in range(len(order)) if (slot >> b) & 1)
        owner = jnp.bitwise_xor(info[3], mask)
        source = near if slot < slots // 2 else far
        value = source[slot % (slots // 2), block].astype(F32)
        write(owner, value)


def unpack_gu_body(order, starts, info, near, far, out):
    side = pl.program_id(1)
    size = near.shape[2]

    def write(owner, value):
        per = out.shape[0] // size

        @pl.when(owner // per == side)
        def hit():
            out[pl.ds(pl.multiple_of((owner % per) * size, size), size), :] = value

    place(info, order, near, far, 0, None, None, write)


def unpack_dn_body(order, info, near, far, out):
    size = near.shape[2]
    cuts = out.shape[1] // COLS
    rows = size // cuts

    def write(owner, value):
        for cut in range(cuts):
            out[
                pl.ds(pl.multiple_of(owner * rows, rows), rows), cut * COLS : (cut + 1) * COLS
            ] = value[cut * rows : (cut + 1) * rows]

    place(info, order, near, far, 0, None, None, write)


def unpack_gu(info, order, pair, first, count, total, base, previous):
    near, far = pair
    slots, unused, size, unused_too = near.shape
    rows = size * slots
    spec = pl.BlockSpec((slots, 1, size, COLS), lambda i, s, *u: (0, first + i, 0, 0))
    out = sds((rows, 2 * total * COLS), F32)
    body = functools.partial(unpack_gu_body, order, None)
    args, specs = ([info, near, far], [spec, spec])
    aliases = {}
    if previous is not None:
        args.append(previous)
        specs.append(pl.BlockSpec(memory_space=pl.ANY))
        aliases = {3: 0}
        inner = body
        body = lambda info, near, far, unused, out: inner(info, near, far, out)
    return pl.pallas_call(
        body,
        out_shape=out,
        grid_spec=pltpu.PrefetchScalarGridSpec(
            num_scalar_prefetch=1,
            grid=(count, 2),
            in_specs=specs,
            out_specs=pl.BlockSpec((rows, COLS), lambda i, s, *u: (0, s * total + base + i)),
        ),
        input_output_aliases=aliases,
        cost_estimate=pl.CostEstimate(flops=0, bytes_accessed=count * rows * COLS * 12, transcendentals=0),
    )(*args)


def unpack_dn(info, order, pair, first, count, total, base, previous):
    near, far = pair
    slots, unused, size, unused_too = near.shape
    width = 2 * slots * size
    cuts = width // COLS
    rows = width * COLS // width
    spec = pl.BlockSpec((slots, 1, size, COLS), lambda i, *u: (0, first + i, 0, 0))
    out = sds((total * rows, width), F32)
    body = functools.partial(unpack_dn_body, order)
    args, specs = ([info, near, far], [spec, spec])
    aliases = {}
    if previous is not None:
        args.append(previous)
        specs.append(pl.BlockSpec(memory_space=pl.ANY))
        aliases = {3: 0}
        inner = body
        body = lambda info, near, far, unused, out: inner(info, near, far, out)
    return pl.pallas_call(
        body,
        out_shape=out,
        grid_spec=pltpu.PrefetchScalarGridSpec(
            num_scalar_prefetch=1,
            grid=(count,),
            in_specs=specs,
            out_specs=pl.BlockSpec((rows, width), lambda i, *u: (base + i, 0)),
        ),
        input_output_aliases=aliases,
        cost_estimate=pl.CostEstimate(flops=0, bytes_accessed=count * rows * width * 6, transcendentals=0),
    )(*args)


def unpack_attention_body(orders, widths, info, *refs):
    pairs, outs = (refs[: 2 * len(orders)], refs[2 * len(orders) :])
    unit = 0
    homes = []
    for which, columns in enumerate(widths):
        for block in range(columns // COLS):
            homes.append((which, block))
    start = 0
    for which, order in enumerate(orders):
        near, far = pairs[2 * which : 2 * which + 2]
        size = near.shape[2]
        for block in range(near.shape[1]):
            at = start + block

            def write(owner, value, at=at):
                if 2 * at >= len(homes):
                    out = outs[len(widths)]
                    cuts = out.shape[1] // COLS
                    rows = size // cuts
                    for cut in range(cuts):
                        out[
                            pl.ds(pl.multiple_of(owner * rows, rows), rows),
                            cut * COLS : (cut + 1) * COLS,
                        ] = value[cut * rows : (cut + 1) * rows]
                    return
                per = outs[0].shape[0] // size
                for side in range(2):
                    which_out, column = homes[2 * at + side]
                    out = outs[which_out]

                    @pl.when(owner // per == side)
                    def hit(out=out, column=column):
                        out[
                            pl.ds(pl.multiple_of((owner % per) * size, size), size),
                            column * COLS : (column + 1) * COLS,
                        ] = value

            place(info, order, near, far, block, None, None, write)
        start += near.shape[1]


def unpack_attention(info, orders, pairs, widths, inner):
    slots, unused, size, unused_too = pairs[0][0].shape
    half = slots * size
    shapes = [sds((half, w), F32) for w in widths] + [sds((inner // 2, 2 * half), F32)]
    args = [info] + [part for pair in pairs for part in pair]
    return call(
        functools.partial(unpack_attention_body, orders, widths),
        shapes,
        (1,),
        [whole(a.shape) for a in args[1:]],
        [whole(s.shape) for s in shapes],
        args,
        moved=14_000_000,
    )


def plain_gu(own, other):
    blocks, width, cols = own.shape

    def rows(part):
        return part.reshape(blocks, 2, width // 2, cols).transpose(2, 1, 0, 3).reshape(width // 2, -1)

    return jnp.concatenate([rows(own), rows(other)], axis=0)


def plain_dn(own, other):
    blocks, width, cols = own.shape
    cuts = width // cols

    def rows(part):
        return (
            part.reshape(blocks, 16, cuts, width // (16 * cuts), cols)
            .transpose(0, 1, 3, 2, 4)
            .reshape(-1, width)
        )

    return jnp.concatenate([rows(own), rows(other)], axis=0)


def plain_units(own, other, widths):
    def unit(part, at):
        half = part.shape[1] // 2
        return part[at // 2, (at % 2) * half : (at % 2 + 1) * half]

    result, at = ([], 0)
    for columns in widths:
        count = columns // COLS
        result.append(
            jnp.concatenate(
                [
                    jnp.concatenate([unit(part, at + i) for i in range(count)], axis=1)
                    for part in (own, other)
                ],
                axis=0,
            )
        )
        at += count
    return result


def plain_sum(grads):
    parts = [lax.psum_scatter(g.astype(BF), "wsh", scatter_dimension=0, tiled=True) for g in grads]
    return tuple(g.astype(F32) for g in lax.psum(parts, "ctx"))


def per_device(
    tokens, cotangent, light_qkv, light_out, heavy_qkv, heavy_out, light_gu, light_down, heavy_gu, heavy_down,
    routers, gains, doc_starts, q_index, kv_index, ff_index,
):
    micros, unused, tok, width = tokens.shape
    count, groups = (lax.axis_size("ctx"), lax.axis_size("wsh"))
    direct = groups == 2 and count == 16
    place_ctx = lax.axis_index("ctx")
    side = lax.axis_index("wsh") if direct else 0
    base = place_ctx * tok
    info = jnp.concatenate(
        [
            jnp.stack([jnp.int32(side), base, jnp.int32(tok * count), place_ctx]).astype(jnp.int32),
            doc_starts[:, 0].reshape(-1),
        ]
    )
    swap = [(0, 1), (1, 0)]

    def pair_of(shard):
        if direct:
            return (shard, lax.ppermute(shard, "wsh", swap))
        full = lax.all_gather(shard, "wsh", axis=0, tiled=True)
        return (full[: full.shape[0] // 2], full[full.shape[0] // 2 :])

    def full_of(shard, axis=0):
        return lax.all_gather(shard, "wsh", axis=axis, tiled=True)

    vectors = jnp.concatenate([routers, gains, jnp.zeros((3, routers.shape[1]), BF)], axis=0)
    if direct:
        got = lax.ppermute(vectors, "wsh", swap)
        small = jnp.concatenate(
            [jnp.where(side == 0, vectors, got), jnp.where(side == 0, got, vectors)], axis=1
        )
    else:
        small = full_of(vectors, 1)
    h_own, h_got = pair_of(heavy_qkv)
    l_own, l_got = pair_of(light_qkv)
    w_lout, w_hout = (full_of(light_out), full_of(heavy_out))
    w_hgu, w_hdown = (full_of(heavy_gu), full_of(heavy_down))
    w_lgu, w_ldown = (full_of(light_gu), full_of(light_down))

    x, up = (tokens[:, 0], cotangent[:, 0])
    index = jnp.stack([q_index[:, 0], kv_index[:, 0], ff_index[:, 0]])
    cols, rows = (index[..., None], index[:, :, None, :])

    q_pay, kv_pay, hq_in, kin, h1k, gate = routed_in(info, x, cols, small, h_own, h_got)
    kv_orders = ((8, 4, 2, 1), (8, 4, 1, 2))
    upward = [(i, i + 1) for i in range(count - 1)]
    downward = [(i + 1, i) for i in range(count - 1)]
    inner = light_qkv.shape[1] // 3

    def rims(qkv):
        return (
            lax.ppermute(qkv[:, tok - WIN :, inner:], "ctx", upward),
            lax.ppermute(qkv[:, :WIN, inner:], "ctx", downward),
        )

    if direct:
        back_orders = [tuple(reversed(order)) for order in kv_orders]
        values = [kv_pay[m] for m in range(micros)]
        got = gather_start(values, back_orders, 0)
        qkv = light_in(info, x, small, l_own, l_got)
        got, qkv, w_lout, w_hout = tied(got, qkv, w_lout, w_hout)
        before, after = rims(qkv)
        values = gather_end(values, got)
        got = gather_start(values, back_orders, 1)
        got, before, after = tied(got, before, after)
        values = gather_end(values, got)
        got = gather_start(values, back_orders, 2)
        lo, light_lse = light_fwd(info, qkv, before, after)
        got, lo, light_lse, w_hgu, w_hdown = tied(got, lo, light_lse, w_hgu, w_hdown)
        values = gather_end(values, got)
        got = gather_start(values, back_orders, 3)
        pairs = list(zip(values, got))
    else:
        pairs = []
        for m in range(micros):
            every = lax.all_gather(kv_pay[m], "ctx", axis=0, tiled=True)
            pairs.append((every[: every.shape[0] // 2], every[every.shape[0] // 2 :]))
        qkv = light_in(info, x, small, l_own, l_got)
        before, after = rims(qkv)
        lo, light_lse = light_fwd(info, qkv, before, after)
    heavy = [heavy_fwd(info, q_pay[m], *pairs[m]) for m in range(micros)]
    heavy, w_lgu, w_ldown = tied(heavy, w_lgu, w_ldown)
    ho = jnp.stack([h[0] for h in heavy])
    y, low2, ffr, dzh, hy, gf = middle(info, x, up, cols, rows, small, gate, lo, w_lout, ho, w_hout)
    routed = ffr.shape[1]

    def flat(value):
        return value.reshape(-1, value.shape[-1])

    zh, dff, hgu_own, hgu_send, hdn_own, hdn_send = ffn(info, flat(ffr), flat(dzh), w_hgu, w_hdown)
    z, dh2, lgu_own, lgu_send, ldn_own, ldn_send = ffn(info, flat(low2), flat(up), w_lgu, w_ldown)
    if direct:
        hgu_got, hdn_got, lgu_got, ldn_got = (
            lax.ppermute(part, "wsh", swap) for part in (hgu_send, hdn_send, lgu_send, ldn_send)
        )
        orders = ((1, 2, 4, 8), (2, 4, 1, 8), (4, 1, 2, 8))
        first = [
            fold(info, orders[0], [(hgu_own, hgu_got, 0, 8), (lgu_own, lgu_got, 0, 2)]),
            fold(info, orders[1], [(hgu_own, hgu_got, 8, 8), (lgu_own, lgu_got, 2, 2)]),
            fold(info, orders[2], [(hdn_own, hdn_got, 0, 8), (ldn_own, ldn_got, 0, 2)]),
        ]
        got = scatter_start(first, orders, 0)

    def by_micro(value):
        return value.reshape(micros, -1, value.shape[-1])

    out_tokens, dy, dlo, dho, dhy, dsq, part_two = mid_back(
        info, y, up, by_micro(z), by_micro(dh2), by_micro(zh), by_micro(dff), ffr, gf, cols, rows, small, gate, w_lout,
        w_hout, hy, hq_in,
    )
    dhq, partial = ([], [])
    for m in range(micros):
        dq, near, far = heavy_bwd(info, q_pay[m], *pairs[m], heavy[m][1], dho[m])
        dhq.append(dq)
        partial.append((near, far))
    dhq = jnp.stack(dhq)
    if direct:
        shape = (count // 2, routed, 2 * width)
        back = [tuple(part.reshape(shape) for part in both) for both in partial]
        got, back, dlo = tied(got, back, dlo)
        first = scatter_end(first, got)
        got = scatter_start(first, orders, 1)
        got_back = scatter_start(back, back_orders, 0)
    else:
        dhkv = jnp.stack(
            [
                lax.psum_scatter(jnp.concatenate(both, axis=0), "ctx", scatter_dimension=0, tiled=True)
                for both in partial
            ]
        )
    dlq, dl_own, rim_low, rim_high = light_bwd(info, qkv, before, after, light_lse, dlo)
    if direct:
        got, got_back, dlq, dl_own, rim_low, rim_high = tied(got, got_back, dlq, dl_own, rim_low, rim_high)
        first, back = (scatter_end(first, got), scatter_end(back, got_back))
        got, got_back = (scatter_start(first, orders, 2), scatter_start(back, back_orders, 1))
    got_low = lax.ppermute(rim_high, "ctx", upward)
    got_high = lax.ppermute(rim_low, "ctx", downward)
    if direct:
        for stage in (2, 3):
            first, back = (scatter_end(first, got), scatter_end(back, got_back))
            if stage == 2:
                got = scatter_start(first, orders, 3)
            else:
                values = [keep for keep, send in first]
                got = gather_start(values, orders, 0)
            got_back = scatter_start(back, back_orders, stage)
            got, got_back, got_low, got_high = tied(got, got_back, got_low, got_high)
        back = scatter_end(back, got_back)
        dhkv = jnp.concatenate([keep for keep, send in back], axis=0)
        values = gather_end(values, got)
        got = gather_start(values, orders, 1)
    grad_tokens, dl, part_one = in_back(
        info, x, dy, dlq, dl_own, got_low, got_high, dhq, dhkv, dsq, rows, small, gate, hq_in, kin, h1k, l_own, l_got,
        h_own, h_got,
    )
    att_own, att_send = attention_grads(info, x, small, dl, hq_in, dhq, kin, dhkv, lo, dy, ho, dhy)
    widths = (light_qkv.shape[1], heavy_qkv.shape[1], heavy_out.shape[1])
    vector = part_one + part_two
    if direct:
        att_got = lax.ppermute(att_send, "wsh", swap)
        half = width // 2
        mine = lax.dynamic_slice_in_dim(vector, side * half, half, 1)
        given = lax.dynamic_slice_in_dim(vector, (1 - side) * half, half, 1)
        vector = mine + lax.ppermute(given, "wsh", swap)
        got, att_got, vector = tied(got, att_got, vector)
        values = gather_end(values, got)
        got = gather_start(values, orders, 2)
        pieces = ((0, 4), (4, 3), (7, 3))
        second = [
            fold(info, order, [(att_own, att_got, start, size)])
            for order, (start, size) in zip(orders, pieces)
        ]
        got, second, vector = tied(got, second, vector)
        values = gather_end(values, got)
        got = gather_start(values, orders, 3)
        got_two = scatter_start(second, orders, 0)
        got_vector = flipped(vector, 1)
        got_two, second, vector, got_vector = tied(got_two, second, vector, got_vector)
        second, vector = (scatter_end(second, got_two), vector + got_vector)
        got_two, got_vector = (scatter_start(second, orders, 1), flipped(vector, 2))
        got, got_two, vector, got_vector = tied(got, got_two, vector, got_vector)
        second, vector = (scatter_end(second, got_two), vector + got_vector)
        chunks = list(zip(values, got))
        got_two, got_vector = (scatter_start(second, orders, 2), flipped(vector, 4))
        g_hdown = unpack_dn(info, orders[2], chunks[2], 0, 8, 8, 0, None)
        got_two, got_vector, vector, g_hdown = tied(got_two, got_vector, vector, g_hdown)
        second, vector = (scatter_end(second, got_two), vector + got_vector)
        got_two, got_vector = (scatter_start(second, orders, 3), flipped(vector, 8))
        part = unpack_gu(info, orders[0], chunks[0], 0, 8, 16, 0, None)
        got_two, got_vector, vector, part = tied(got_two, got_vector, vector, part)
        second, vector = (scatter_end(second, got_two), vector + got_vector)
        values = [keep for keep, send in second]
        got = gather_start(values, orders, 0)
        g_hgu = unpack_gu(info, orders[1], chunks[1], 0, 8, 16, 8, part)
        got, g_hgu = tied(got, g_hgu)
        values = gather_end(values, got)
        got = gather_start(values, orders, 1)
        part = unpack_gu(info, orders[0], chunks[0], 8, 2, 4, 0, None)
        got, part = tied(got, part)
        values = gather_end(values, got)
        got = gather_start(values, orders, 2)
        g_lgu = unpack_gu(info, orders[1], chunks[1], 8, 2, 4, 2, part)
        got, g_lgu = tied(got, g_lgu)
        values = gather_end(values, got)
        got = gather_start(values, orders, 3)
        g_ldown = unpack_dn(info, orders[2], chunks[2], 8, 2, 2, 0, None)
        got, g_ldown = tied(got, g_ldown)
        sums = list(zip(values, got))
        g_lqkv, g_hqkv, g_hout, g_lout = unpack_attention(info, orders, sums, widths, inner)
    else:
        g_lqkv, g_hqkv, g_hout = plain_units(att_own, att_send, widths)
        last = slice(att_own.shape[0] - 1, att_own.shape[0])
        g_lqkv, g_lout, g_hqkv, g_hout, g_lgu, g_ldown, g_hgu, g_hdown = plain_sum(
            [
                g_lqkv,
                plain_dn(att_own[last], att_send[last]),
                g_hqkv,
                g_hout,
                plain_gu(lgu_own, lgu_send),
                plain_dn(ldn_own, ldn_send),
                plain_gu(hgu_own, hgu_send),
                plain_dn(hdn_own, hdn_send),
            ]
        )
        vector = lax.psum(vector, ("ctx", "wsh"))
        part = width // groups
        vector = lax.dynamic_slice_in_dim(vector, lax.axis_index("wsh") * part, part, 1)
    return (
        out_tokens[:, None],
        grad_tokens[:, None],
        g_lqkv,
        g_lout,
        g_hqkv,
        g_hout,
        g_lgu,
        g_ldown,
        g_hgu,
        g_hdown,
        vector[:3],
        vector[3:5],
    )


def solution(mesh):
    return jax.shard_map(
        per_device,
        mesh=mesh,
        in_specs=(
            P(None, "wsh", "ctx", None),
            P(None, "wsh", "ctx", None),
            P("wsh", None),
            P("wsh", None),
            P("wsh", None),
            P("wsh", None),
            P("wsh", None),
            P("wsh", None),
            P("wsh", None),
            P("wsh", None),
            P(None, "wsh"),
            P(None, "wsh"),
            P(None, "wsh", None),
            P(None, "wsh", "ctx"),
            P(None, "wsh", "ctx"),
            P(None, "wsh", "ctx"),
        ),
        out_specs=(
            P(None, "wsh", "ctx", None),
            P(None, "wsh", "ctx", None),
            P("wsh", None),
            P("wsh", None),
            P("wsh", None),
            P("wsh", None),
            P("wsh", None),
            P("wsh", None),
            P("wsh", None),
            P("wsh", None),
            P(None, "wsh"),
            P(None, "wsh"),
        ),
        check_vma=False,
    )
```

```python
import functools

import jax
import jax.numpy as jnp
from jax import lax
from jax.experimental import pallas as pl
from jax.experimental.pallas import tpu as pltpu
from jax.sharding import PartitionSpec as P

HD = 64
WIN = 128
LANES = 128
COLS = 256
FAR = -1e30
EPS = 1e-06
BF = jnp.bfloat16
F32 = jnp.float32


def mm(left, right):
    return lax.dot_general(left, right, (((1,), (0,)), ((), ())), preferred_element_type=F32)


def mm_t(left, right):
    return lax.dot_general(left, right, (((1,), (1,)), ((), ())), preferred_element_type=F32)


def t_mm(left, right):
    return lax.dot_general(left, right, (((0,), (0,)), ((), ())), preferred_element_type=F32)


def pick(onehot, values):
    high = values.astype(BF)
    low = (values - high.astype(F32)).astype(BF)
    return mm(onehot, high) + mm(onehot, low)


def iota(shape, dim):
    return lax.broadcasted_iota(jnp.int32, shape, dim)


def onehot_cols(positions, base, length):
    return (iota((positions.shape[0], length), 1) == positions - base).astype(F32).astype(BF)


def onehot_rows(positions, base, length):
    return (iota((length, positions.shape[1]), 0) == positions - base).astype(F32).astype(BF)


def segment(info, micro, positions):
    total = jnp.full(positions.shape, -1, jnp.int32)
    for start in range(5):
        total += (positions >= info[4 + micro * 5 + start]).astype(jnp.int32)
    return total


def inverse_rms(values):
    return lax.rsqrt(jnp.mean(values * values, axis=-1, keepdims=True) + EPS)


def halves(info, values):
    half = values.shape[1] // 2
    first, second = (values[:, :half], values[:, half:])
    lower = info[0] == 0
    return (jnp.where(lower, first, second), jnp.where(lower, second, first))


def unhalved(info, own, other):
    lower = info[0] == 0
    return jnp.concatenate([jnp.where(lower, own, other), jnp.where(lower, other, own)], axis=1)


def call(body, outs, grid, in_specs, out_specs, args, scratch=(), flops=0, moved=0, limit=48, name=None):
    return pl.pallas_call(
        body,
        name=name or getattr(body, "__name__", "kernel"),
        out_shape=outs,
        grid_spec=pltpu.PrefetchScalarGridSpec(
            num_scalar_prefetch=1,
            grid=grid,
            in_specs=in_specs,
            out_specs=out_specs,
            scratch_shapes=list(scratch),
        ),
        compiler_params=pltpu.CompilerParams(vmem_limit_bytes=limit * 1024 * 1024),
        cost_estimate=pl.CostEstimate(flops=flops, bytes_accessed=moved, transcendentals=0),
    )(*args)


def whole(shape):
    rank = len(shape)
    return pl.BlockSpec(tuple(shape), lambda *unused: (0,) * rank)


def one_of(shape):
    rank = len(shape)
    return pl.BlockSpec((1,) + tuple(shape[1:]), lambda i, *unused: (i,) + (0,) * (rank - 1))


def sds(shape, dtype):
    return jax.ShapeDtypeStruct(tuple(shape), dtype)


def routed_body(info, x, cols, small, w_own, w_got, q_out, kin_out, hq_out, h1k_out, gate_out):
    micros, tok, width = x.shape
    rows = cols.shape[2]
    base = info[1]
    gain = small[3:4].astype(F32)
    taken_q, taken_k = ([], [])
    for m in range(micros):
        both = jnp.concatenate([cols[0, m], cols[1, m]], axis=0)
        got = mm(onehot_cols(both, base, tok), x[m])
        taken_q.append(got[:rows])
        taken_k.append(got[rows:])
    xq, xk = (jnp.concatenate(taken_q, axis=0), jnp.concatenate(taken_k, axis=0))
    low_q = (xq * inverse_rms(xq) * gain).astype(BF)
    h1k = xk * inverse_rms(xk) * gain
    low_k = h1k.astype(BF)
    gate_q = jax.nn.sigmoid(
        jnp.sum(low_q.astype(F32) * small[0:1].astype(F32), axis=-1, keepdims=True)
    )
    gate_k = jax.nn.sigmoid(
        jnp.sum(low_k.astype(F32) * small[1:2].astype(F32), axis=-1, keepdims=True)
    )
    kin = (h1k * gate_k).astype(BF)
    own_q, other_q = halves(info, low_q)
    query = mm(own_q, w_own[...]) + mm(other_q, w_got[...])
    lane = iota((rows, LANES), 1)
    for m in range(micros):
        part = slice(m * rows, (m + 1) * rows)
        q_out[m, :, :width] = query[part].astype(BF)
        kin_out[m, :, :width] = kin[part]
        seg_q = segment(info, m, cols[0, m])
        seg_k = segment(info, m, cols[1, m])
        q_out[m, :, width:] = (lane == seg_q).astype(F32).astype(BF)
        kin_out[m, :, width:] = jnp.where((lane < 8) & (lane != seg_k), FAR, 0.0).astype(BF)
        hq_out[m] = low_q[part]
        h1k_out[m] = h1k[part]
        gate_out[m] = jnp.where(lane == 0, gate_q[part], gate_k[part])


def routed_in(info, x, cols, small, w_own, w_got):
    micros, unused, width = x.shape
    rows = cols.shape[2]
    shapes = [
        sds((micros, rows, width + LANES), BF),
        sds((micros, rows, width + LANES), BF),
        sds((micros, rows, width), BF),
        sds((micros, rows, width), F32),
        sds((micros, rows, LANES), F32),
    ]
    args = (info, x, cols, small, w_own, w_got)
    return call(
        routed_body,
        shapes,
        (1,),
        [whole(a.shape) for a in args[1:4]] + [whole((w_own.shape[0], width))] * 2,
        [whole(s.shape) for s in shapes],
        args,
        flops=2 * micros * rows * width * width,
        moved=5_000_000,
    )


def light_in_body(info, x, small, w_own, w_got, out):
    values = x[0].astype(F32)
    low = (values * inverse_rms(values) * small[3:4].astype(F32)).astype(BF)
    own, other = halves(info, low)
    out[0] = (mm(own, w_own[...]) + mm(other, w_got[...])).astype(BF)


def light_in(info, x, small, w_own, w_got):
    micros, tok, width = x.shape
    columns = w_own.shape[1]
    split = 2
    rows = tok // split
    spec = lambda n: pl.BlockSpec((1, rows, n), lambda i, *u: (i // split, i % split, 0))
    return call(
        light_in_body,
        sds((micros, tok, columns), BF),
        (micros * split,),
        [spec(width), whole(small.shape), whole(w_own.shape), whole(w_got.shape)],
        spec(columns),
        (info, x, small, w_own, w_got),
        flops=2 * micros * tok * width * columns,
        moved=8_000_000,
    )


def fill_near(near, qkv, before, after):
    tok = qkv.shape[1]
    inner = near.shape[1] // 2
    near[:WIN] = before[0]
    near[WIN : WIN + tok] = qkv[0, :, inner:]
    near[WIN + tok :] = after[0]


def light_bias(info, micro, block):
    start = info[1] + block * WIN
    rows, columns = (WIN, 3 * WIN)
    row_pos = start + iota((rows, 1), 0)
    col_pos = start - WIN + iota((1, columns), 1)
    seg_row = segment(info, micro, row_pos)
    seg_col = jnp.where((col_pos >= 0) & (col_pos < info[2]), segment(info, micro, col_pos), -1)
    shift = iota((rows, columns), 0) + WIN - iota((rows, columns), 1)
    allowed = (jnp.abs(shift) < WIN) & (seg_row == seg_col)
    bias = jnp.where(allowed, 0.0, FAR)
    return jnp.concatenate([bias, bias], axis=0)


def stacked(pair, low_lane):
    zero = jnp.zeros_like(pair)
    return jnp.concatenate(
        [jnp.where(low_lane, pair, zero), jnp.where(low_lane, zero, pair)], axis=0
    )


def merged(values, low_lane):
    rows = values.shape[0] // 2
    return jnp.where(low_lane, values[:rows], values[rows:])


def light_fwd_body(info, qkv, before, after, out, lse_out, near):
    micro = pl.program_id(0)
    tok = qkv.shape[1]
    inner = out.shape[2]
    fill_near(near, qkv, before, after)
    low_lane = iota((WIN, LANES), 1) < HD
    lane = iota((WIN, LANES), 1)

    def block_step(block, carry):
        at = pl.ds(pl.multiple_of(block * WIN, WIN), WIN)
        around = pl.ds(pl.multiple_of(block * WIN, WIN), 3 * WIN)
        bias = light_bias(info, micro, block)
        stats = jnp.zeros((WIN, LANES), F32)
        for pair in range(inner // LANES):
            cut = slice(pair * LANES, (pair + 1) * LANES)
            query = stacked(qkv[0, at, cut] * BF(HD**-0.5), low_lane)
            scores = mm_t(query, near[around, cut]) + bias
            top = jnp.max(scores, axis=-1, keepdims=True)
            weights = jnp.exp(scores - top)
            total = jnp.sum(weights, axis=-1, keepdims=True)
            value = near[around, inner + pair * LANES : inner + (pair + 1) * LANES]
            mixed = mm((weights * (1.0 / total)).astype(BF), value)
            out[0, at, cut] = merged(mixed, low_lane).astype(BF)
            lse = top + jnp.log(total)
            stats = jnp.where(lane == 2 * pair, lse[:WIN], stats)
            stats = jnp.where(lane == 2 * pair + 1, lse[WIN:], stats)
        lse_out[0, at, :] = stats
        return carry

    lax.fori_loop(0, tok // WIN, block_step, 0)


def light_fwd(info, qkv, before, after):
    micros, tok, columns = qkv.shape
    inner = columns // 3
    shapes = [sds((micros, tok, inner), BF), sds((micros, tok, LANES), F32)]
    args = (info, qkv, before, after)
    return call(
        light_fwd_body,
        shapes,
        (micros,),
        [one_of(a.shape) for a in args[1:]],
        [one_of(s.shape) for s in shapes],
        args,
        scratch=[pltpu.VMEM((tok + 2 * WIN, 2 * inner), BF)],
        flops=4_000_000_000,
        moved=6_000_000,
    )


def light_bwd_body(info, qkv, before, after, lse, grad, dq_out, own_out, low_out, high_out, near, dk, dv):
    micro = pl.program_id(0)
    tok = qkv.shape[1]
    inner = grad.shape[2]
    fill_near(near, qkv, before, after)
    dk[...] = jnp.zeros_like(dk)
    dv[...] = jnp.zeros_like(dv)
    low_lane = iota((WIN, LANES), 1) < HD

    def block_step(block, carry):
        at = pl.ds(pl.multiple_of(block * WIN, WIN), WIN)
        around = pl.ds(pl.multiple_of(block * WIN, WIN), 3 * WIN)
        bias = light_bias(info, micro, block)
        stats = lse[0, at, :]
        for pair in range(inner // LANES):
            cut = slice(pair * LANES, (pair + 1) * LANES)
            query = stacked(qkv[0, at, cut] * BF(HD**-0.5), low_lane)
            key = near[around, cut]
            value = near[around, inner + pair * LANES : inner + (pair + 1) * LANES]
            shift = jnp.concatenate(
                [stats[:, 2 * pair : 2 * pair + 1], stats[:, 2 * pair + 1 : 2 * pair + 2]], axis=0
            )
            probs = jnp.exp(mm_t(query, key) + bias - shift)
            upper = stacked(grad[0, at, cut], low_lane)
            grad_probs = mm_t(upper, value)
            center = jnp.sum(probs * grad_probs, axis=-1, keepdims=True)
            slope = (probs * (grad_probs - center)).astype(BF)
            dq_out[0, at, cut] = (merged(mm(slope, key), low_lane) * HD**-0.5).astype(BF)
            dk[around, cut] += t_mm(slope, query)
            dv[around, cut] += t_mm(probs.astype(BF), upper)
        return carry

    lax.fori_loop(0, tok // WIN, block_step, 0)
    own_out[0, :, :inner] = dk[WIN : WIN + tok]
    own_out[0, :, inner:] = dv[WIN : WIN + tok]
    low_out[0, :, :inner] = dk[:WIN].astype(BF)
    low_out[0, :, inner:] = dv[:WIN].astype(BF)
    high_out[0, :, :inner] = dk[WIN + tok :].astype(BF)
    high_out[0, :, inner:] = dv[WIN + tok :].astype(BF)


def light_bwd(info, qkv, before, after, lse, grad):
    micros, tok, columns = qkv.shape
    inner = columns // 3
    shapes = [
        sds((micros, tok, inner), BF),
        sds((micros, tok, 2 * inner), F32),
        sds((micros, WIN, 2 * inner), BF),
        sds((micros, WIN, 2 * inner), BF),
    ]
    args = (info, qkv, before, after, lse, grad)
    return call(
        light_bwd_body,
        shapes,
        (micros,),
        [one_of(a.shape) for a in args[1:]],
        [one_of(s.shape) for s in shapes],
        args,
        scratch=[
            pltpu.VMEM((tok + 2 * WIN, 2 * inner), BF),
            pltpu.VMEM((tok + 2 * WIN, inner), F32),
            pltpu.VMEM((tok + 2 * WIN, inner), F32),
        ],
        flops=10_000_000_000,
        moved=14_000_000,
    )


def key_body(info, kin, w_own, w_got, out):
    half = w_own.shape[0]
    width = 2 * half
    own = kin[:, pl.ds(pl.multiple_of(info[0] * half, half), half)]
    other = kin[:, pl.ds(pl.multiple_of((1 - info[0]) * half, half), half)]
    out[...] = (mm(own, w_own[:, width:]) + mm(other, w_got[:, width:])).astype(BF)


def key_project(info, kin, w_own, w_got):
    shape = sds((kin.shape[0], 2 * (kin.shape[1] - LANES)), BF)
    args = (info, kin, w_own, w_got)
    return call(
        key_body,
        shape,
        (1,),
        [whole(a.shape) for a in args[1:]],
        whole(shape.shape),
        args,
        flops=1_200_000_000,
        moved=6_000_000,
    )


def heavy_scores(query, parts, bias, cut):
    return [mm_t(query, part[:, cut]) + b for part, b in zip(parts, bias)]


def heavy_fwd_body(info, q, kin_a, kin_b, kv_a, kv_b, out, lse_out):
    rows, width = out.shape
    parts = (kv_a, kv_b)
    low_lane = iota((rows, LANES), 1) < HD
    lane = iota((rows, LANES), 1)
    feature = jnp.concatenate([q[:, width:]] * 2, axis=0)
    bias = [mm_t(feature, kin[:, width:]) for kin in (kin_a, kin_b)]
    stats = jnp.zeros((rows, LANES), F32)
    for pair in range(width // LANES):
        cut = slice(pair * LANES, (pair + 1) * LANES)
        query = stacked(q[:, cut] * BF(HD**-0.5), low_lane)
        scores = heavy_scores(query, parts, bias, cut)
        top = functools.reduce(
            jnp.maximum, [jnp.max(s, axis=-1, keepdims=True) for s in scores]
        )
        weights = [jnp.exp(s - top) for s in scores]
        total = sum(jnp.sum(w, axis=-1, keepdims=True) for w in weights)
        scale = 1.0 / total
        mixed = sum(
            mm((w * scale).astype(BF), part[:, width + pair * LANES : width + (pair + 1) * LANES])
            for w, part in zip(weights, parts)
        )
        out[:, cut] = merged(mixed, low_lane).astype(BF)
        lse = top + jnp.log(total)
        stats = jnp.where(lane == 2 * pair, lse[:rows], stats)
        stats = jnp.where(lane == 2 * pair + 1, lse[rows:], stats)
    lse_out[...] = stats


def heavy_fwd(info, q, kins, kvs):
    rows = q.shape[0]
    width = q.shape[1] - LANES
    shapes = [sds((rows, width), BF), sds((rows, LANES), F32)]
    args = (info, q, *kins, *kvs)
    return call(
        heavy_fwd_body,
        shapes,
        (1,),
        [whole(a.shape) for a in args[1:]],
        [whole(s.shape) for s in shapes],
        args,
        flops=1_500_000_000,
        moved=5_000_000,
    )


def heavy_bwd_body(info, q, kin_a, kin_b, kv_a, kv_b, lse, grad, w_own, w_got, dq_out, da_out, db_out, ia_out, ib_out):
    rows, width = grad.shape
    parts = (kv_a, kv_b)
    low_lane = iota((rows, LANES), 1) < HD
    feature = jnp.concatenate([q[:, width:]] * 2, axis=0)
    bias = [mm_t(feature, kin[:, width:]) for kin in (kin_a, kin_b)]
    for pair in range(width // LANES):
        cut = slice(pair * LANES, (pair + 1) * LANES)
        upcut = slice(width + pair * LANES, width + (pair + 1) * LANES)
        query = stacked(q[:, cut] * BF(HD**-0.5), low_lane)
        shift = jnp.concatenate(
            [lse[:, 2 * pair : 2 * pair + 1], lse[:, 2 * pair + 1 : 2 * pair + 2]], axis=0
        )
        probs = [jnp.exp(s - shift) for s in heavy_scores(query, parts, bias, cut)]
        upper = stacked(grad[:, cut], low_lane)
        grads = [mm_t(upper, part[:, upcut]) for part in parts]
        center = sum(jnp.sum(p * g, axis=-1, keepdims=True) for p, g in zip(probs, grads))
        slopes = [(p * (g - center)).astype(BF) for p, g in zip(probs, grads)]
        dq = sum(mm(s, part[:, cut]) for s, part in zip(slopes, parts))
        dq_out[:, cut] = (merged(dq, low_lane) * HD**-0.5).astype(BF)
        for target, slope, prob in zip((da_out, db_out), slopes, probs):
            target[:, cut] = t_mm(slope, query).astype(BF)
            target[:, upcut] = t_mm(prob.astype(BF), upper).astype(BF)
    half = width // 2
    for target, source in ((ia_out, da_out), (ib_out, db_out)):
        for weight, side in ((w_own, info[0]), (w_got, 1 - info[0])):
            target[:, pl.ds(pl.multiple_of(side * half, half), half)] = mm_t(
                source[...], weight[:, width:]
            ).astype(BF)


def heavy_bwd(info, q, kins, kvs, lse, grad, w_own, w_got):
    rows = q.shape[0]
    width = q.shape[1] - LANES
    keys = kvs[0].shape[0]
    shapes = [sds((rows, width), BF)] + [sds((keys, 2 * width), BF)] * 2 + [sds((keys, width), BF)] * 2
    args = (info, q, *kins, *kvs, lse, grad, w_own, w_got)
    return call(
        heavy_bwd_body,
        shapes,
        (1,),
        [whole(a.shape) for a in args[1:]],
        [whole(s.shape) for s in shapes],
        args,
        flops=6_500_000_000,
        moved=15_000_000,
    )


def heavy_grads_body(info, *refs):
    micros = (len(refs) - 8) // 4
    hq, dhq, ho, dhy, lo, dy = refs[:6]
    kins, dkvs = (refs[6 : 6 + 2 * micros], refs[6 + 2 * micros : -2])
    other_out, own_out = (refs[-1], refs[-2])
    half = hq.shape[2] // 2
    every = range(micros)
    for target, side in ((other_out, 1 - info[0]), (own_out, info[0])):
        cut = pl.ds(pl.multiple_of(side * half, half), half)

        def put(unit, left, right, columns):
            for block in range(columns // COLS):
                at = unit + block
                total = sum(
                    t_mm(a, b[:, block * COLS : (block + 1) * COLS]) for a, b in zip(left, right)
                )
                target[at // 2, (at % 2) * half : (at % 2 + 1) * half] = total.astype(BF)
            return unit + columns // COLS

        unit = put(0, [hq[m, :, cut] for m in every], [dhq[m] for m in every], dhq.shape[2])
        unit = put(unit, [kin[:, cut] for kin in kins], dkvs, dkvs[0].shape[1])
        unit = put(unit, [ho[m, :, cut] for m in every], [dhy[m] for m in every], dhy.shape[2])
        part = lo.shape[2] // 2
        small_cut = pl.ds(pl.multiple_of(side * part, part), part)
        total = sum(t_mm(lo[m, :, small_cut], dy[m].astype(BF)) for m in every)
        pack_rows(target.at[pl.ds(unit // 2, 1)], total)


def heavy_grads(info, hq, dhq, ho, dhy, lo, dy, kins, dkvs):
    width = hq.shape[2]
    units = (dhq.shape[2] + dkvs[0].shape[1] + dhy.shape[2]) // COLS
    shapes = [sds((units // 2 + 1, width, COLS), BF)] * 2
    args = (info, hq, dhq, ho, dhy, lo, dy, *kins, *dkvs)
    return call(
        heavy_grads_body,
        shapes,
        (1,),
        [whole(a.shape) for a in args[1:]],
        [whole(s.shape) for s in shapes],
        args,
        flops=6_500_000_000,
        moved=28_000_000,
    )


def middle_body(info, x, up, cols, rows, small, gate, lo, lout, ho, hout, y_out, low_out, pay_out, hy_out, gf_out):
    tok = x.shape[1]
    base = info[1]
    hy = mm(ho[0], hout[...])
    hy_out[0] = hy
    spread = onehot_rows(rows[0, 0], base, tok)
    y = x[0].astype(F32) + mm(lo[0], lout[...]) + pick(spread, hy * gate[0, :, 0:1])
    y_out[0] = y
    low = (y * inverse_rms(y) * small[4:5].astype(F32)).astype(BF)
    low_out[0] = low
    take = onehot_cols(cols[2, 0], base, tok)
    taken = mm(take, low)
    width = x.shape[2]
    pay_out[0, :, :width] = taken.astype(BF)
    gf = jax.nn.sigmoid(jnp.sum(taken * small[2:3].astype(F32), axis=-1, keepdims=True))
    pay_out[0, :, width:] = (mm(take, up[0]) * gf).astype(BF)
    gf_out[0] = jnp.broadcast_to(gf, gf_out.shape[1:])


def second_of(shape):
    rank = len(shape)
    return pl.BlockSpec(
        (shape[0], 1) + tuple(shape[2:]), lambda i, *unused: (0, i) + (0,) * (rank - 2)
    )


def middle(info, x, up, cols, rows, small, gate, lo, lout, ho, hout):
    micros, tok, width = x.shape
    count = cols.shape[2]
    shapes = [
        sds((micros, tok, width), F32),
        sds((micros, tok, width), BF),
        sds((micros, count, 2 * width), BF),
        sds((micros, count, width), F32),
        sds((micros, count, LANES), F32),
    ]
    args = (info, x, up, cols, rows, small, gate, lo, lout, ho, hout)
    return call(
        middle_body,
        shapes,
        (micros,),
        [
            one_of(x.shape),
            one_of(up.shape),
            second_of(cols.shape),
            second_of(rows.shape),
            whole(small.shape),
            one_of(gate.shape),
            one_of(lo.shape),
            whole(lout.shape),
            one_of(ho.shape),
            whole(hout.shape),
        ],
        [one_of(s.shape) for s in shapes],
        args,
        flops=2_000_000_000,
        moved=12_000_000,
    )


def pack_rows(target, values):
    step = values.shape[0] // 16
    cuts = values.shape[1] // COLS
    for slot in range(16):
        for cut in range(cuts):
            at = slot * step * cuts + cut * step
            target[0, at : at + step] = values[
                slot * step : (slot + 1) * step, cut * COLS : (cut + 1) * COLS
            ].astype(BF)


def gelu_parts(g):
    root = (2.0 / 3.141592653589793) ** 0.5
    square = g * g
    tanh = jnp.tanh(root * g * (1.0 + 0.044715 * square))
    bell = 0.5 * (1.0 + tanh)
    slope = bell + 0.5 * g * (1.0 - tanh * tanh) * (root * (1.0 + 3 * 0.044715 * square))
    return (g * bell, slope)


def hidden_both_ways(low, upstream, wg, wu, wd):
    g, u = (mm(low, wg), mm(low, wu))
    back = mm_t(upstream, wd)
    gelu, slope = gelu_parts(g)
    return ((gelu * u).astype(BF), (back * u * slope).astype(BF), (back * gelu).astype(BF))


def add_steps(step, pairs):
    @pl.when(step == 0)
    def first():
        for target, value in pairs:
            target[...] = value

    @pl.when(step > 0)
    def later():
        for target, value in pairs:
            target[...] += value


def ffn_local_body(info, a, ct, wg, wu, wd, z_out, dh_out):
    hidden, dg, du = hidden_both_ways(a[...], ct[...], wg[...], wu[...], wd[...])
    z = mm(hidden, wd[...])
    dh = mm_t(dg, wg[...]) + mm_t(du, wu[...])
    add_steps(pl.program_id(0), [(z_out, z), (dh_out, dh)])


def ffn_body(info, a, ct, wg, wu, wd, z_out, dh_out, own_gu, other_gu, own_dn, other_dn):
    step = pl.program_id(0)
    half = pl.num_programs(0) // 2
    width = a.shape[1] // 2
    hidden, dg, du = hidden_both_ways(a[...], ct[...], wg[...], wu[...], wd[...])
    z = mm(hidden, wd[...])
    dh = mm_t(dg, wg[...]) + mm_t(du, wu[...])
    add_steps(step, [(z_out, z), (dh_out, dh)])
    down = t_mm(hidden, ct[...])

    @pl.when(step < half)
    def send():
        pack_rows(other_dn, down)

    @pl.when(step >= half)
    def keep():
        pack_rows(own_dn, down)

    own = a[:, pl.ds(pl.multiple_of(info[0] * width, width), width)]
    other = a[:, pl.ds(pl.multiple_of((1 - info[0]) * width, width), width)]
    own_gu[0, :width] = t_mm(own, dg).astype(BF)
    own_gu[0, width:] = t_mm(own, du).astype(BF)
    other_gu[0, :width] = t_mm(other, dg).astype(BF)
    other_gu[0, width:] = t_mm(other, du).astype(BF)


def ffn_local(info, pay, w_gu, w_down, block):
    rows = pay.shape[0]
    hidden, width = w_down.shape
    steps = hidden // block
    return call(
        ffn_local_body,
        [sds((rows, width), F32)] * 2,
        (steps,),
        [
            pl.BlockSpec((rows, width), lambda i, *u: (0, 0)),
            pl.BlockSpec((rows, width), lambda i, *u: (0, 1)),
            pl.BlockSpec((width, block), lambda i, *u: (0, i)),
            pl.BlockSpec((width, block), lambda i, *u: (0, steps + i)),
            pl.BlockSpec((block, width), lambda i, *u: (i, 0)),
        ],
        [whole((rows, width))] * 2,
        (info, pay, pay, w_gu, w_gu, w_down),
        flops=2 * 6 * rows * hidden * width,
        moved=2 * 3 * hidden * width,
    )


def ffn(info, a, ct, w_gu, w_down):
    rows, width = a.shape
    hidden = w_down.shape[0]
    block = COLS
    steps = hidden // block
    half = steps // 2

    def natural(i, info):
        return jnp.where(i < half, (1 - info[0]) * half + i, info[0] * half + i - half)

    unit = (1, width, COLS)
    shapes = [
        sds((rows, width), F32),
        sds((rows, width), F32),
        sds((steps,) + unit[1:], BF),
        sds((steps,) + unit[1:], BF),
        sds((half,) + unit[1:], BF),
        sds((half,) + unit[1:], BF),
    ]
    return call(
        ffn_body,
        shapes,
        (steps,),
        [
            whole(a.shape),
            whole(ct.shape),
            pl.BlockSpec((width, block), lambda i, info: (0, natural(i, info))),
            pl.BlockSpec((width, block), lambda i, info: (0, steps + natural(i, info))),
            pl.BlockSpec((block, width), lambda i, info: (natural(i, info), 0)),
        ],
        [
            whole((rows, width)),
            whole((rows, width)),
            pl.BlockSpec(unit, lambda i, info: (natural(i, info), 0, 0)),
            pl.BlockSpec(unit, lambda i, info: (natural(i, info), 0, 0)),
            pl.BlockSpec(unit, lambda i, info: (jnp.maximum(i - half, 0), 0, 0)),
            pl.BlockSpec(unit, lambda i, info: (jnp.minimum(i, half - 1), 0, 0)),
        ],
        (info, a, ct, w_gu, w_gu, w_down),
        flops=2 * 9 * rows * hidden * width,
        moved=2 * 2 * 3 * hidden * width + rows * width * 12,
    )


def plane_grads_body(info, near, far, wg, wu, wd, own_gu, other_gu, dn):
    width = wg.shape[0]
    half = width // 2
    sums = None
    for part in (near, far):
        low, upstream = (part[:, :width], part[:, width:])
        hidden, dg, du = hidden_both_ways(low, upstream, wg[...], wu[...], wd[...])
        own = part[:, pl.ds(pl.multiple_of(info[0] * half, half), half)]
        other = part[:, pl.ds(pl.multiple_of((1 - info[0]) * half, half), half)]
        terms = (t_mm(own, dg), t_mm(own, du), t_mm(other, dg), t_mm(other, du), t_mm(hidden, upstream))
        sums = terms if sums is None else tuple(p + q for p, q in zip(sums, terms))
    own_gu[0, :half] = sums[0].astype(BF)
    own_gu[0, half:] = sums[1].astype(BF)
    other_gu[0, :half] = sums[2].astype(BF)
    other_gu[0, half:] = sums[3].astype(BF)
    for cut in range(width // COLS):
        dn[0, cut * COLS : (cut + 1) * COLS] = sums[4][:, cut * COLS : (cut + 1) * COLS].astype(BF)


def plane_grads(info, near, far, w_gu, w_down):
    hidden, width = w_down.shape
    steps = hidden // COLS
    turns = steps // 8

    def block(i, info):
        return info[0] * (steps // 2) + lax.rem(info[3], 4) * turns + i

    unit = (1, width, COLS)
    spec = pl.BlockSpec(unit, lambda i, *u: (i, 0, 0))
    rows = 2 * near.shape[0]
    return call(
        plane_grads_body,
        [sds((turns, width, COLS), BF)] * 3,
        (turns,),
        [
            whole(near.shape),
            whole(far.shape),
            pl.BlockSpec((width, COLS), lambda i, info: (0, block(i, info))),
            pl.BlockSpec((width, COLS), lambda i, info: (0, steps + block(i, info))),
            pl.BlockSpec((COLS, width), lambda i, info: (block(i, info), 0)),
        ],
        [spec] * 3,
        (info, near, far, w_gu, w_gu, w_down),
        flops=2 * 6 * rows * turns * COLS * width,
        moved=9_000_000,
    )


def column_fold_body(order, info, first, second, third, keep, send):
    slots = 1 << len(order)
    size = keep.shape[2]
    place_z = info[3] // 4
    for part, source in enumerate((first, second, third)):
        for block in range(source.shape[0]):
            for slot in range(slots):
                owner = jnp.bitwise_xor(place_z, mask_of(slot, order))
                at = pl.ds(pl.multiple_of(owner * size, size), size)
                target = keep if slot < slots // 2 else send
                target[slot % (slots // 2), part * source.shape[0] + block] = source[block, at, :]


def column_fold(info, order, sources):
    slots = 1 << len(order)
    blocks, width, cols = sources[0].shape
    shape = sds((slots // 2, 3 * blocks, width // slots, cols), BF)
    return call(
        functools.partial(column_fold_body, order),
        [shape, shape],
        (1,),
        [whole(a.shape) for a in sources],
        [whole(shape.shape)] * 2,
        (info, *sources),
        moved=10_000_000,
        name="column_fold",
    )


def mid_back_body(
    info, y, up, z, dh2, zh, dff, ffr, gf, cols, rows, small, gate, lout, hout, hy, hq,
    out, dy_out, dlo_out, dho_out, dhy_out, dsq_out, part_out,
):
    tok = y.shape[1]
    base = info[1]
    micro = pl.program_id(0)
    spread = onehot_rows(rows[2, 0], base, tok)
    take = onehot_cols(cols[2, 0], base, tok)
    values, top = (y[0], up[0].astype(F32))
    open_f = gf[0, :, 0:1]
    zhv = zh[0]
    out[0] = (values + z[0] + pick(spread, zhv * open_f)).astype(BF)
    taken = mm(take, up[0])
    dsf = jnp.sum(taken * zhv, axis=-1, keepdims=True) * open_f * (1.0 - open_f)
    back = dh2[0] + pick(spread, dff[0] + dsf * small[2:3].astype(F32))
    inv = inverse_rms(values)
    scaled = back * small[4:5].astype(F32)
    mean = jnp.mean(values * scaled, axis=-1, keepdims=True)
    dy = top + inv * scaled - values * (inv * inv * inv * mean)
    dy_out[0] = dy
    dgain = jnp.sum(back * values * inv, axis=0, keepdims=True)
    drf = jnp.sum(dsf * ffr[0].astype(F32), axis=0, keepdims=True)
    dlo_out[0] = mm_t(dy.astype(BF), lout[...]).astype(BF)
    dyq = pick(onehot_cols(cols[0, 0], base, tok), dy)
    open_q = gate[0, :, 0:1]
    dhy = (dyq * open_q).astype(BF)
    dhy_out[0] = dhy
    dsq = jnp.sum(dyq * hy[0], axis=-1, keepdims=True) * open_q * (1.0 - open_q)
    dsq_out[0] = jnp.broadcast_to(dsq, dsq_out.shape[1:])
    drq = jnp.sum(dsq * hq[0].astype(F32), axis=0, keepdims=True)
    dho_out[0] = mm_t(dhy, hout[...]).astype(BF)
    row = iota(part_out.shape, 0)
    part = jnp.where(row == 0, drq, jnp.where(row == 2, drf, jnp.where(row == 4, dgain, 0.0)))

    @pl.when(micro == 0)
    def first():
        part_out[...] = part

    @pl.when(micro > 0)
    def later():
        part_out[...] += part


def mid_back(info, y, up, z, dh2, zh, dff, ffr, gf, cols, rows, small, gate, lout, hout, hy, hq):
    micros, tok, width = y.shape
    count = cols.shape[2]
    shapes = [
        sds((micros, tok, width), BF),
        sds((micros, tok, width), F32),
        sds((micros, tok, lout.shape[0]), BF),
        sds((micros, count, width), BF),
        sds((micros, count, width), BF),
        sds((micros, count, LANES), F32),
        sds((8, width), F32),
    ]
    return call(
        mid_back_body,
        shapes,
        (micros,),
        [
            one_of(y.shape),
            one_of(up.shape),
            one_of(z.shape),
            one_of(dh2.shape),
            one_of(zh.shape),
            one_of(dff.shape),
            pl.BlockSpec((1, count, width), lambda i, *u: (i, 0, 0)),
            one_of(gf.shape),
            second_of(cols.shape),
            second_of(rows.shape),
            whole(small.shape),
            one_of(gate.shape),
            whole(lout.shape),
            whole(hout.shape),
            one_of(hy.shape),
            one_of(hq.shape),
        ],
        [one_of(s.shape) for s in shapes[:-1]] + [whole(shapes[-1].shape)],
        (info, y, up, z, dh2, zh, dff, ffr, gf, cols, rows, small, gate, lout, hout, hy, hq),
        flops=3_000_000_000,
        moved=22_000_000,
    )


def light_join_body(info, x, small, dq, own, got_low, got_high, dl_out, own_out, other_out, low):
    tok, width = x.shape[1:]
    micros = x.shape[0]
    half = width // 2
    inner = dq.shape[2]
    for m in range(micros):
        dl_out[m, :, :inner] = dq[m]
        dl_out[m, WIN : tok - WIN, inner:] = own[m, WIN : tok - WIN].astype(BF)
        dl_out[m, :WIN, inner:] = (own[m, :WIN] + got_low[m].astype(F32)).astype(BF)
        dl_out[m, tok - WIN :, inner:] = (own[m, tok - WIN :] + got_high[m].astype(F32)).astype(BF)
        values = x[m].astype(F32)
        low[m] = (values * inverse_rms(values) * small[3:4].astype(F32)).astype(BF)
    for target, side in ((other_out, 1 - info[0]), (own_out, info[0])):
        cut = pl.ds(pl.multiple_of(side * half, half), half)
        for block in range(dl_out.shape[2] // COLS):
            total = sum(
                t_mm(low[m, :, cut], dl_out[m, :, block * COLS : (block + 1) * COLS])
                for m in range(micros)
            )
            target[block // 2, (block % 2) * half : (block % 2 + 1) * half] = total.astype(BF)


def light_join(info, x, small, dq, own, got_low, got_high):
    micros, tok, width = x.shape
    columns = dq.shape[2] + own.shape[2]
    shapes = [sds((micros, tok, columns), BF)] + [sds((columns // (2 * COLS), width, COLS), BF)] * 2
    args = (info, x, small, dq, own, got_low, got_high)
    return call(
        light_join_body,
        shapes,
        (1,),
        [whole(a.shape) for a in args[1:]],
        [whole(s.shape) for s in shapes],
        args,
        scratch=[pltpu.VMEM(x.shape, BF)],
        flops=2 * micros * tok * width * columns,
        moved=20_000_000,
    )


def in_back_body(
    info, x, dy, dl, dhq, dkin, dsq, rows, small, gate, h1k, l_own, l_got, h_own, h_got,
    grad_out, part_out,
):
    tok, width = x.shape[1:]
    micro = pl.program_id(0)
    base = info[1]
    light = dl[0]
    back = unhalved(info, mm_t(light, l_own[...]), mm_t(light, l_got[...]))
    given = dkin[0].astype(F32)
    open_k = gate[0, :, 1:2]
    source = h1k[0]
    dskv = jnp.sum(given * source, axis=-1, keepdims=True) * open_k * (1.0 - open_k)
    to_q = unhalved(info, mm_t(dhq[0], h_own[...]), mm_t(dhq[0], h_got[...]))
    to_q += dsq[0, :, 0:1] * small[0:1].astype(F32)
    to_k = given * open_k + dskv * small[1:2].astype(F32)
    back += pick(onehot_rows(rows[0, 0], base, tok), to_q)
    back += pick(onehot_rows(rows[1, 0], base, tok), to_k)
    values = x[0].astype(F32)
    inv = inverse_rms(values)
    scaled = back * small[3:4].astype(F32)
    mean = jnp.mean(values * scaled, axis=-1, keepdims=True)
    grad_out[0] = (dy[0] + inv * scaled - values * (inv * inv * inv * mean)).astype(BF)
    dgain = jnp.sum(back * values * inv, axis=0, keepdims=True)
    drk = jnp.sum(dskv * source.astype(BF).astype(F32), axis=0, keepdims=True)
    row = iota(part_out.shape, 0)
    part = jnp.where(row == 1, drk, jnp.where(row == 3, dgain, 0.0))

    @pl.when(micro == 0)
    def first():
        part_out[...] = part

    @pl.when(micro > 0)
    def later():
        part_out[...] += part


def in_back(info, x, dy, dl, dhq, dkin, dsq, rows, small, gate, h1k, l_own, l_got, h_own, h_got):
    micros, tok, width = x.shape
    shapes = [sds((micros, tok, width), BF), sds((8, width), F32)]
    firsts = (x, dy, dl, dhq, dkin, dsq)
    return call(
        in_back_body,
        shapes,
        (micros,),
        [one_of(a.shape) for a in firsts]
        + [second_of(rows.shape), whole(small.shape)]
        + [one_of(a.shape) for a in (gate, h1k)]
        + [whole(a.shape) for a in (l_own, l_got)]
        + [whole((h_own.shape[0], width))] * 2,
        [one_of(shapes[0].shape), whole(shapes[1].shape)],
        (info,) + firsts + (rows, small, gate, h1k, l_own, l_got, h_own, h_got),
        flops=2_600_000_000,
        moved=14_000_000,
    )


def mask_of(slot, order):
    bits = len(order)
    return sum(order[b] for b in range(bits) if (slot >> (bits - 1 - b)) & 1)


def fold_body(order, counts, info, *refs):
    sources = refs[: 2 * len(counts)]
    keep, send = refs[2 * len(counts) :]
    slots = 1 << len(order)
    size = keep.shape[2]
    step = pl.program_id(0)
    start = 0
    for which, count in enumerate(counts):
        own, got = sources[2 * which : 2 * which + 2]

        @pl.when((step >= start) & (step < start + count))
        def part():
            for slot in range(slots):
                owner = jnp.bitwise_xor(info[3], mask_of(slot, order))
                at = pl.ds(pl.multiple_of(owner * size, size), size)
                total = (own[0, at, :].astype(F32) + got[0, at, :].astype(F32)).astype(BF)
                if slot < slots // 2:
                    keep[slot, 0] = total
                else:
                    send[slot - slots // 2, 0] = total

        start += count


def fold(info, order, parts):
    slots = 1 << len(order)
    width = parts[0][0].shape[1]
    counts = [part[3] for part in parts]
    total = sum(counts)
    shape = sds((slots // 2, total, width // slots, COLS), BF)
    args, specs = ([], [])
    start = 0
    for own, got, first, count in parts:
        index = functools.partial(
            lambda first, start, count, i, *u: (
                first + jnp.minimum(jnp.maximum(i - start, 0), count - 1),
                0,
                0,
            ),
            first,
            start,
            count,
        )
        args += [own, got]
        specs += [pl.BlockSpec((1, width, COLS), index)] * 2
        start += count
    spec = pl.BlockSpec((slots // 2, 1, width // slots, COLS), lambda i, *u: (0, i, 0, 0))
    return call(
        functools.partial(fold_body, order, counts),
        [shape, shape],
        (total,),
        specs,
        [spec, spec],
        (info, *args),
        moved=total * width * COLS * 6,
    )


def flipped(value, bit):
    size = lax.axis_size("ctx")
    return lax.ppermute(value, "ctx", [(i, i ^ bit) for i in range(size)])


def tied(*values):
    return lax.optimization_barrier(values)


def scatter_step(keep, got):
    half = keep.shape[0] // 2
    if half == 0:
        return ((keep.astype(F32) + got.astype(F32)).astype(BF), None)
    return (
        (keep[:half].astype(F32) + got[:half].astype(F32)).astype(BF),
        (keep[half:].astype(F32) + got[half:].astype(F32)).astype(BF),
    )


def scatter_start(chunks, orders, stage):
    return [flipped(send, order[stage]) for (keep, send), order in zip(chunks, orders)]


def scatter_end(chunks, got):
    return [scatter_step(keep, g) for (keep, send), g in zip(chunks, got)]


def scatter_sum(keep, send, order):
    for bit in order:
        keep, send = scatter_step(keep, flipped(send, bit))
    return keep


def gather_start(values, orders, stage):
    return [flipped(value, order[-1 - stage]) for value, order in zip(values, orders)]


def gather_end(values, got):
    return [jnp.concatenate([value, g], axis=0) for value, g in zip(values, got)]


def gather_pair(value, order):
    for bit in order[:-1]:
        value = jnp.concatenate([value, flipped(value, bit)], axis=0)
    return (value, flipped(value, order[-1]))


def from_owner(info, order, near, far, owner, write):
    slots = 1 << len(order)
    distance = jnp.bitwise_xor(info[3], owner)
    slot = sum(
        jnp.where(jnp.bitwise_and(distance, bit) != 0, 1 << place, 0)
        for place, bit in enumerate(reversed(order))
    )
    inside = lax.rem(slot, slots // 2)

    @pl.when(slot < slots // 2)
    def close():
        write(near.at[inside])

    @pl.when(slot >= slots // 2)
    def distant():
        write(far.at[inside])


def unpack_gu_body(order, info, near, far, *outs):
    out = outs[-1]
    size = near.shape[2]
    per = out.shape[0] // size
    for turn in range(per):

        def write(source, turn=turn):
            for block in range(near.shape[1]):
                out[turn * size : (turn + 1) * size, block * COLS : (block + 1) * COLS] = source[
                    block
                ].astype(F32)

        from_owner(info, order, near, far, pl.program_id(1) * per + turn, write)


def write_dn(out, source, first, size, owner, row):
    cuts = out.shape[1] // COLS
    rows = size // cuts
    value = source[first].astype(F32)
    for cut in range(cuts):
        out[row + owner * rows : row + (owner + 1) * rows, cut * COLS : (cut + 1) * COLS] = value[
            cut * rows : (cut + 1) * rows
        ]


def unpack_dn_body(order, info, near, far, *outs):
    slots, blocks, size = near.shape[:3]
    for owner in range(2 * slots):

        def write(source, owner=owner):
            for block in range(blocks):
                write_dn(outs[-1], source, block, size, owner, block * COLS)

        from_owner(info, order, near, far, owner, write)


def unpack(body, info, order, pair, first, count, step, shape, grid_more, block, index, previous, name):
    near, far = pair
    slots, unused, size, unused_too = near.shape
    spec = pl.BlockSpec((slots, step, size, COLS), lambda i, *u: (0, first // step + i, 0, 0))
    args, specs, aliases = ([info, near, far], [spec, spec], {})
    if previous is not None:
        args.append(previous)
        specs.append(pl.BlockSpec(memory_space=pl.ANY))
        aliases = {3: 0}
    return pl.pallas_call(
        functools.partial(body, order),
        out_shape=sds(shape, F32),
        grid_spec=pltpu.PrefetchScalarGridSpec(
            num_scalar_prefetch=1,
            grid=(count // step,) + grid_more,
            in_specs=specs,
            out_specs=pl.BlockSpec(block, index),
        ),
        input_output_aliases=aliases,
        compiler_params=pltpu.CompilerParams(vmem_limit_bytes=32 * 1024 * 1024),
        cost_estimate=pl.CostEstimate(
            flops=0, bytes_accessed=count * 2 * slots * size * COLS * 6, transcendentals=0
        ),
        name=name,
    )(*args)


def unpack_gu(info, order, pair, first, count, total, base, previous, step):
    rows = pair[0].shape[0] * pair[0].shape[2]
    return unpack(
        unpack_gu_body, info, order, pair, first, count, step, (rows, 2 * total * COLS), (2,), (rows, step * COLS),
        lambda i, s, *u: (0, (s * total + base) // step + i), previous, "unpack_gu",
    )


def unpack_dn(info, order, pair, first, count, total, base, previous, step):
    width = 2 * pair[0].shape[0] * pair[0].shape[2]
    return unpack(
        unpack_dn_body, info, order, pair, first, count, step, (total * COLS, width), (), (step * COLS, width),
        lambda i, *u: (base // step + i, 0), previous, "unpack_dn",
    )


def unpack_plane_gu_body(orders, info, *refs):
    out = refs[-1]
    side, plane = (pl.program_id(0), pl.program_id(2))
    for which, order in enumerate(orders):
        near, far = refs[2 * which : 2 * which + 2]
        blocks, size = near.shape[1:3]
        per = out.shape[0] // 2
        for level in range(2):
            owner = (side * 2 + level) * 4 + plane
            row = level * per + which * size

            def write(source, row=row):
                for block in range(blocks):
                    out[row : row + size, block * COLS : (block + 1) * COLS] = source[block].astype(F32)

            from_owner(info, order, near, far, owner, write)


def unpack_plane_gu(info, orders, pairs, total):
    slots, blocks, size, unused = pairs[0][0].shape
    turns = blocks // 3
    spec = pl.BlockSpec(
        (slots, turns, size, COLS), lambda s, h, q, info: (0, jnp.bitwise_xor(h, info[0]), 0, 0)
    )
    rows = 2 * len(pairs) * size
    args = [info] + [part for pair in pairs for part in pair]
    return call(
        functools.partial(unpack_plane_gu_body, orders),
        sds((rows, 2 * total * COLS), F32),
        (2, 2, 4),
        [spec] * (len(args) - 1),
        pl.BlockSpec((rows, turns * COLS), lambda s, h, q, *u: (0, s * 8 + h * 4 + q)),
        args,
        moved=2 * rows * total * COLS * 6,
        name="unpack_plane_gu",
    )


def unpack_plane_dn_body(orders, info, *refs):
    out = refs[-1]
    plane = pl.program_id(0)
    for which, order in enumerate(orders):
        near, far = refs[2 * which : 2 * which + 2]
        blocks, size = near.shape[1:3]
        for level in range(4):
            owner = level * 4 + plane
            cut, row = divmod((level * len(orders) + which) * size, COLS)

            def write(source, cut=cut, row=row):
                for block in range(blocks):
                    at = block * COLS + row
                    out[at : at + size, cut * COLS : (cut + 1) * COLS] = source[block].astype(F32)

            from_owner(info, order, near, far, owner, write)


def unpack_plane_dn(info, orders, pairs):
    slots, blocks, size, unused = pairs[0][0].shape
    turns = blocks // 3
    width = 4 * len(pairs) * size
    spec = pl.BlockSpec((slots, turns, size, COLS), lambda q, *u: (0, 2, 0, 0))
    args = [info] + [part for pair in pairs for part in pair]
    return call(
        functools.partial(unpack_plane_dn_body, orders),
        sds((4 * turns * COLS, width), F32),
        (4,),
        [spec] * (len(args) - 1),
        pl.BlockSpec((turns * COLS, width), lambda q, *u: (q, 0)),
        args,
        moved=4 * turns * COLS * width * 6,
        name="unpack_plane_dn",
    )


def unpack_units_body(order, first, info, near, far, *outs):
    slots, unused, size = near.shape[:3]
    homes = [
        (out, block * COLS) for out in outs for block in range(out.shape[1] // COLS)
    ]
    for owner in range(2 * slots):
        side, turn = divmod(owner, slots)

        def write(source, side=side, turn=turn):
            for at in range(side, len(homes), 2):
                out, column = homes[at]
                out[turn * size : (turn + 1) * size, column : column + COLS] = source[
                    first + at // 2
                ].astype(F32)

        from_owner(info, order, near, far, owner, write)


def unpack_units(info, order, pair, first, widths):
    slots, unused, size, unused_too = pair[0].shape
    shapes = [sds((slots * size, w), F32) for w in widths]
    args = [info, *pair]
    return call(
        functools.partial(unpack_units_body, order, first),
        shapes,
        (1,),
        [whole(a.shape) for a in args[1:]],
        [whole(s.shape) for s in shapes],
        args,
        moved=sum(widths) * slots * size * 6,
        name="unpack_units",
    )


def plain_gu(own, other):
    blocks, width, cols = own.shape

    def rows(part):
        return part.reshape(blocks, 2, width // 2, cols).transpose(2, 1, 0, 3).reshape(width // 2, -1)

    return jnp.concatenate([rows(own), rows(other)], axis=0)


def plain_dn(own, other):
    blocks, width, cols = own.shape
    cuts = width // cols

    def rows(part):
        return (
            part.reshape(blocks, 16, cuts, width // (16 * cuts), cols)
            .transpose(0, 1, 3, 2, 4)
            .reshape(-1, width)
        )

    return jnp.concatenate([rows(own), rows(other)], axis=0)


def plain_units(own, other, widths):
    def unit(part, at):
        half = part.shape[1] // 2
        return part[at // 2, (at % 2) * half : (at % 2 + 1) * half]

    result, at = ([], 0)
    for columns in widths:
        count = columns // COLS
        result.append(
            jnp.concatenate(
                [
                    jnp.concatenate([unit(part, at + i) for i in range(count)], axis=1)
                    for part in (own, other)
                ],
                axis=0,
            )
        )
        at += count
    return result


def plain_sum(grads):
    parts = [lax.psum_scatter(g.astype(BF), "wsh", scatter_dimension=0, tiled=True) for g in grads]
    return tuple(g.astype(F32) for g in lax.psum(parts, "ctx"))


def per_device(
    tokens, cotangent, light_qkv, light_out, heavy_qkv, heavy_out, light_gu, light_down, heavy_gu, heavy_down,
    routers, gains, doc_starts, q_index, kv_index, ff_index,
):
    micros, unused, tok, width = tokens.shape
    count, groups = (lax.axis_size("ctx"), lax.axis_size("wsh"))
    direct = groups == 2 and count == 16
    place_ctx = lax.axis_index("ctx")
    side = lax.axis_index("wsh") if direct else 0
    base = place_ctx * tok
    info = jnp.concatenate(
        [
            jnp.stack([jnp.int32(side), base, jnp.int32(tok * count), place_ctx]).astype(jnp.int32),
            doc_starts[:, 0].reshape(-1),
        ]
    )
    swap = [(0, 1), (1, 0)]

    def pair_of(shard):
        if direct:
            return (shard, lax.ppermute(shard, "wsh", swap))
        full = lax.all_gather(shard, "wsh", axis=0, tiled=True)
        return (full[: full.shape[0] // 2], full[full.shape[0] // 2 :])

    def full_of(shard, axis=0):
        return lax.all_gather(shard, "wsh", axis=axis, tiled=True)

    vectors = jnp.concatenate([routers, gains, jnp.zeros((3, routers.shape[1]), BF)], axis=0)
    if direct:
        got = lax.ppermute(vectors, "wsh", swap)
        small = jnp.concatenate(
            [jnp.where(side == 0, vectors, got), jnp.where(side == 0, got, vectors)], axis=1
        )
    else:
        small = full_of(vectors, 1)
    h_own, h_got = pair_of(heavy_qkv)
    l_own, l_got = pair_of(light_qkv)
    w_lout, w_hout = (full_of(light_out), full_of(heavy_out))
    w_hgu, w_hdown = (full_of(heavy_gu), full_of(heavy_down))
    w_lgu, w_ldown = (full_of(light_gu), full_of(light_down))

    x, up = (tokens[:, 0], cotangent[:, 0])
    index = jnp.stack([q_index[:, 0], kv_index[:, 0], ff_index[:, 0]])
    cols, rows = (index[..., None], index[:, :, None, :])

    q_pay, kin_pay, hq_in, h1k, gate = routed_in(info, x, cols, small, h_own, h_got)
    kv_orders = ((8, 4, 2, 1), (8, 4, 1, 2))
    back_orders = [tuple(reversed(order)) for order in kv_orders]
    upward = [(i, i + 1) for i in range(count - 1)]
    downward = [(i + 1, i) for i in range(count - 1)]
    inner = light_qkv.shape[1] // 3
    every = range(micros)

    def rims(qkv):
        return (
            lax.ppermute(qkv[:, tok - WIN :, inner:], "ctx", upward),
            lax.ppermute(qkv[:, :WIN, inner:], "ctx", downward),
        )

    def project(kin):
        return key_project(info, kin, h_own, h_got)

    if direct:
        values = [kin_pay[m] for m in every]
        got = gather_start(values, back_orders, 0)
        qkv = light_in(info, x, small, l_own, l_got)
        got, qkv, w_lout, w_hout = tied(got, qkv, w_lout, w_hout)
        before, after = rims(qkv)
        values = gather_end(values, got)
        got = gather_start(values, back_orders, 1)
        got, before, after = tied(got, before, after)
        values = gather_end(values, got)
        got = gather_start(values, back_orders, 2)
        lo, light_lse = light_fwd(info, qkv, before, after)
        got, lo, light_lse, w_hgu, w_hdown = tied(got, lo, light_lse, w_hgu, w_hdown)
        values = gather_end(values, got)
        got = gather_start(values, back_orders, 3)
        near_kv = [project(v) for v in values]
        got, near_kv = tied(got, near_kv)
        kins = list(zip(values, got))
        kvs = [(n, project(f)) for n, f in zip(near_kv, got)]
    else:
        kins = []
        for m in every:
            full = lax.all_gather(kin_pay[m], "ctx", axis=0, tiled=True)
            kins.append((full[: full.shape[0] // 2], full[full.shape[0] // 2 :]))
        kvs = [tuple(project(k) for k in pair) for pair in kins]
        qkv = light_in(info, x, small, l_own, l_got)
        before, after = rims(qkv)
        lo, light_lse = light_fwd(info, qkv, before, after)
    heavy = [heavy_fwd(info, q_pay[m], kins[m], kvs[m]) for m in every]
    heavy, w_lgu, w_ldown = tied(heavy, w_lgu, w_ldown)
    ho = jnp.stack([h[0] for h in heavy])
    y, low2, pay, hy, gf = middle(info, x, up, cols, rows, small, gate, lo, w_lout, ho, w_hout)

    def flat(value):
        return value.reshape(-1, value.shape[-1])

    orders = ((1, 2, 4, 8), (2, 4, 1, 8), (4, 1, 2, 8))
    if direct:
        mine = flat(pay)
        plane = [flipped(mine, bit) for bit in (1, 2, 3)]
        zh, dff = ffn_local(info, mine, w_hgu, w_hdown, 2 * COLS)
        plane, zh, dff = tied(plane, zh, dff)
        near = jnp.concatenate([mine, *plane], axis=0)
        far = lax.ppermute(near, "wsh", swap)
    else:
        zh, dff, hgu_own, hgu_send, hdn_own, hdn_send = ffn(
            info, flat(pay[..., :width]), flat(pay[..., width:]), w_hgu, w_hdown
        )
    z, dh2, lgu_own, lgu_send, ldn_own, ldn_send = ffn(info, flat(low2), flat(up), w_lgu, w_ldown)
    if direct:
        far, z, dh2 = tied(far, z, dh2)
        lgu_got, ldn_got = (lax.ppermute(part, "wsh", swap) for part in (lgu_send, ldn_send))
        plane_own, plane_send, plane_dn = plane_grads(info, near, far, w_hgu, w_hdown)
        plane_got = lax.ppermute(plane_send, "wsh", swap)
        keep, send = column_fold(info, (1, 2), (plane_own, plane_got, plane_dn))
        got = flipped(send, 4)

    def by_micro(value):
        return value.reshape(micros, -1, value.shape[-1])

    out_tokens, dy, dlo, dho, dhy, dsq, part_two = mid_back(
        info, y, up, by_micro(z), by_micro(dh2), by_micro(zh), by_micro(dff), pay, gf, cols, rows, small, gate, w_lout,
        w_hout, hy, hq_in,
    )
    backs = [
        heavy_bwd(info, q_pay[m], kins[m], kvs[m], heavy[m][1], dho[m], h_own, h_got) for m in every
    ]
    dhq = jnp.stack([b[0] for b in backs])
    shape = (count // 2, q_index.shape[2], width)
    back = [tuple(part.reshape(shape) for part in b[3:5]) for b in backs]
    dkvs = [part for b in backs for part in b[1:3]]
    if direct:
        got, back, dlo, dkvs = tied(got, back, dlo, dkvs)
        keep, send = scatter_step(keep, got)
        got = flipped(send, 8)
        got_back = scatter_start(back, back_orders, 0)
    dlq, dl_own, rim_low, rim_high = light_bwd(info, qkv, before, after, light_lse, dlo)
    if direct:
        got, got_back, dlq, dl_own, rim_low, rim_high = tied(got, got_back, dlq, dl_own, rim_low, rim_high)
    got_low = lax.ppermute(rim_high, "ctx", upward)
    got_high = lax.ppermute(rim_low, "ctx", downward)
    if direct:
        keep, send = scatter_step(keep, got)
        third = keep.shape[2] // 3
        values = [keep[:, :, t * third : (t + 1) * third] for t in range(3)]
        back = scatter_end(back, got_back)
        got, got_back = (gather_start(values, orders, 0), scatter_start(back, back_orders, 1))
    kin_all = [part for pair in kins for part in pair]
    ha_own, ha_send = heavy_grads(info, hq_in, dhq, ho, dhy, lo, dy, kin_all, dkvs)
    if direct:
        got, got_back, got_low, got_high, ha_own, ha_send = tied(got, got_back, got_low, got_high, ha_own, ha_send)
        ha_got = lax.ppermute(ha_send, "wsh", swap)
        values, back = (gather_end(values, got), scatter_end(back, got_back))
        got, got_back = (gather_start(values, orders, 1), scatter_start(back, back_orders, 2))
    dl, la_own, la_send = light_join(info, x, small, dlq, dl_own, got_low, got_high)
    if direct:
        la_got = lax.ppermute(la_send, "wsh", swap)
        got, got_back, ha_got, la_got, dl = tied(got, got_back, ha_got, la_got, dl)
        values, back = (gather_end(values, got), scatter_end(back, got_back))
        got, got_back = (gather_start(values, orders, 2), scatter_start(back, back_orders, 3))
        second = [
            fold(info, orders[0], [(ha_own, ha_got, 0, 6)]),
            fold(info, orders[1], [(lgu_own, lgu_got, 0, 4), (ha_own, ha_got, 6, 1)]),
            fold(info, orders[2], [(la_own, la_got, 0, 3), (ldn_own, ldn_got, 0, 2)]),
        ]
        got_two = scatter_start(second, orders, 0)
        got, got_back, got_two = tied(got, got_back, got_two)
        values, second, back = (
            gather_end(values, got), scatter_end(second, got_two), scatter_end(back, got_back)
        )
        dkin = jnp.concatenate([keep for keep, send in back], axis=0)
        got = gather_start(values, orders, 3)
        got_two = scatter_start(second, orders, 1)
    else:
        dkin = jnp.stack(
            [
                lax.psum_scatter(jnp.concatenate(b[3:5], axis=0), "ctx", scatter_dimension=0, tiled=True)
                for b in backs
            ]
        )
    grad_tokens, part_one = in_back(
        info, x, dy, dl, dhq, dkin, dsq, rows, small, gate, h1k, l_own, l_got, h_own, h_got
    )
    widths = (heavy_qkv.shape[1], heavy_out.shape[1])
    vector = part_one + part_two
    if direct:
        half = width // 2
        mine = lax.dynamic_slice_in_dim(vector, side * half, half, 1)
        given = lax.dynamic_slice_in_dim(vector, (1 - side) * half, half, 1)
        vector = mine + lax.ppermute(given, "wsh", swap)
        got_two, vector = tied(got_two, vector)
        second = scatter_end(second, got_two)
        got_two, got_vector = (scatter_start(second, orders, 2), flipped(vector, 1))
        got, got_two, vector, got_vector = tied(got, got_two, vector, got_vector)
        chunks = list(zip(values, got))
        second, vector = (scatter_end(second, got_two), vector + got_vector)
        got_two, got_vector = (scatter_start(second, orders, 3), flipped(vector, 2))
        g_hgu = unpack_plane_gu(info, orders, chunks, heavy_gu.shape[1] // (2 * COLS))
        got_two, vector, got_vector, g_hgu = tied(got_two, vector, got_vector, g_hgu)
        second, vector = (scatter_end(second, got_two), vector + got_vector)
        tails = [keep for keep, send in second]
        got_two, got_vector = (gather_start(tails, orders, 0), flipped(vector, 4))
        g_hdown = unpack_plane_dn(info, orders, chunks)
        got_two, vector, got_vector, g_hdown = tied(got_two, vector, got_vector, g_hdown)
        tails, vector = (gather_end(tails, got_two), vector + got_vector)
        got_two, got_vector = (gather_start(tails, orders, 1), flipped(vector, 8))
        got_two, vector, got_vector = tied(got_two, vector, got_vector)
        tails, vector = (gather_end(tails, got_two), vector + got_vector)
        tails = gather_end(tails, gather_start(tails, orders, 2))
        sums = list(zip(tails, gather_start(tails, orders, 3)))
        g_hqkv, g_hout = unpack_units(info, orders[0], sums[0], 0, widths)
        g_lgu = unpack_gu(info, orders[1], sums[1], 0, 4, 4, 0, None, 4)
        g_lout = unpack_dn(info, orders[1], sums[1], 4, 1, 1, 0, None, 1)
        (g_lqkv,) = unpack_units(info, orders[2], sums[2], 0, (light_qkv.shape[1],))
        g_ldown = unpack_dn(info, orders[2], sums[2], 3, 2, 2, 0, None, 1)
    else:
        g_hqkv, g_hout = plain_units(ha_own, ha_send, widths)
        (g_lqkv,) = plain_units(la_own, la_send, (light_qkv.shape[1],))
        last = slice(ha_own.shape[0] - 1, ha_own.shape[0])
        g_lqkv, g_lout, g_hqkv, g_hout, g_lgu, g_ldown, g_hgu, g_hdown = plain_sum(
            [
                g_lqkv,
                plain_dn(ha_own[last], ha_send[last]),
                g_hqkv,
                g_hout,
                plain_gu(lgu_own, lgu_send),
                plain_dn(ldn_own, ldn_send),
                plain_gu(hgu_own, hgu_send),
                plain_dn(hdn_own, hdn_send),
            ]
        )
        vector = lax.psum(vector, ("ctx", "wsh"))
        part = width // groups
        vector = lax.dynamic_slice_in_dim(vector, lax.axis_index("wsh") * part, part, 1)
    return (
        out_tokens[:, None],
        grad_tokens[:, None],
        g_lqkv,
        g_lout,
        g_hqkv,
        g_hout,
        g_lgu,
        g_ldown,
        g_hgu,
        g_hdown,
        vector[:3],
        vector[3:5],
    )


def solution(mesh):
    return jax.shard_map(
        per_device,
        mesh=mesh,
        in_specs=(
            P(None, "wsh", "ctx", None),
            P(None, "wsh", "ctx", None),
            P("wsh", None),
            P("wsh", None),
            P("wsh", None),
            P("wsh", None),
            P("wsh", None),
            P("wsh", None),
            P("wsh", None),
            P("wsh", None),
            P(None, "wsh"),
            P(None, "wsh"),
            P(None, "wsh", None),
            P(None, "wsh", "ctx"),
            P(None, "wsh", "ctx"),
            P(None, "wsh", "ctx"),
        ),
        out_specs=(
            P(None, "wsh", "ctx", None),
            P(None, "wsh", "ctx", None),
            P("wsh", None),
            P("wsh", None),
            P("wsh", None),
            P("wsh", None),
            P("wsh", None),
            P("wsh", None),
            P("wsh", None),
            P("wsh", None),
            P(None, "wsh"),
            P(None, "wsh"),
        ),
        check_vma=False,
    )
```

```python
import functools

import jax
import jax.numpy as jnp
from jax import lax
from jax.experimental import pallas as pl
from jax.experimental.pallas import tpu as pltpu
from jax.sharding import PartitionSpec as P

HD = 64
WIN = 128
LANES = 128
COLS = 256
FAR = -1e30
EPS = 1e-06
BF = jnp.bfloat16
F32 = jnp.float32


def mm(left, right):
    return lax.dot_general(left, right, (((1,), (0,)), ((), ())), preferred_element_type=F32)


def mm_t(left, right):
    return lax.dot_general(left, right, (((1,), (1,)), ((), ())), preferred_element_type=F32)


def t_mm(left, right):
    return lax.dot_general(left, right, (((0,), (0,)), ((), ())), preferred_element_type=F32)


def pick(onehot, values):
    high = values.astype(BF)
    low = (values - high.astype(F32)).astype(BF)
    return mm(onehot, high) + mm(onehot, low)


def iota(shape, dim):
    return lax.broadcasted_iota(jnp.int32, shape, dim)


def onehot_cols(positions, base, length):
    return (iota((positions.shape[0], length), 1) == positions - base).astype(F32).astype(BF)


def onehot_rows(positions, base, length):
    return (iota((length, positions.shape[1]), 0) == positions - base).astype(F32).astype(BF)


def segment(info, micro, positions):
    total = jnp.full(positions.shape, -1, jnp.int32)
    for start in range(5):
        total += (positions >= info[4 + micro * 5 + start]).astype(jnp.int32)
    return total


def inverse_rms(values):
    return lax.rsqrt(jnp.mean(values * values, axis=-1, keepdims=True) + EPS)


def halves(info, values):
    half = values.shape[1] // 2
    first, second = (values[:, :half], values[:, half:])
    lower = info[0] == 0
    return (jnp.where(lower, first, second), jnp.where(lower, second, first))


def unhalved(info, own, other):
    lower = info[0] == 0
    return jnp.concatenate([jnp.where(lower, own, other), jnp.where(lower, other, own)], axis=1)


def call(body, outs, grid, in_specs, out_specs, args, scratch=(), flops=0, moved=0, limit=48, name=None):
    return pl.pallas_call(
        body,
        name=name or getattr(body, "__name__", "kernel"),
        out_shape=outs,
        grid_spec=pltpu.PrefetchScalarGridSpec(
            num_scalar_prefetch=1,
            grid=grid,
            in_specs=in_specs,
            out_specs=out_specs,
            scratch_shapes=list(scratch),
        ),
        compiler_params=pltpu.CompilerParams(vmem_limit_bytes=limit * 1024 * 1024),
        cost_estimate=pl.CostEstimate(flops=flops, bytes_accessed=moved, transcendentals=0),
    )(*args)


def whole(shape):
    rank = len(shape)
    return pl.BlockSpec(tuple(shape), lambda *unused: (0,) * rank)


def one_of(shape):
    rank = len(shape)
    return pl.BlockSpec((1,) + tuple(shape[1:]), lambda i, *unused: (i,) + (0,) * (rank - 1))


def sds(shape, dtype):
    return jax.ShapeDtypeStruct(tuple(shape), dtype)


def routed_body(info, x, cols, small, q_out, kin_out, h1k_out, gate_out):
    micros, tok, width = x.shape
    rows = cols.shape[2]
    base = info[1]
    gain = small[3:4].astype(F32)
    lane = iota((rows, LANES), 1)
    for m in range(micros):
        both = jnp.concatenate([cols[0, m], cols[1, m]], axis=0)
        got = mm(onehot_cols(both, base, tok), x[m])
        xq, xk = (got[:rows], got[rows:])
        low_q = (xq * inverse_rms(xq) * gain).astype(BF)
        h1k = xk * inverse_rms(xk) * gain
        low_k = h1k.astype(BF)
        gate_q = jax.nn.sigmoid(
            jnp.sum(low_q.astype(F32) * small[0:1].astype(F32), axis=-1, keepdims=True)
        )
        gate_k = jax.nn.sigmoid(
            jnp.sum(low_k.astype(F32) * small[1:2].astype(F32), axis=-1, keepdims=True)
        )
        seg_q = segment(info, m, cols[0, m])
        seg_k = segment(info, m, cols[1, m])
        q_out[m, :, :width] = low_q
        q_out[m, :, width:] = (lane == seg_q).astype(F32).astype(BF)
        kin_out[m, :, :width] = (h1k * gate_k).astype(BF)
        kin_out[m, :, width:] = jnp.where((lane < 8) & (lane != seg_k), FAR, 0.0).astype(BF)
        h1k_out[m] = h1k
        gate_out[m] = jnp.where(lane == 0, gate_q, gate_k)


def routed_in(info, x, cols, small):
    micros, unused, width = x.shape
    rows = cols.shape[2]
    shapes = [
        sds((micros, rows, width + LANES), BF),
        sds((micros, rows, width + LANES), BF),
        sds((micros, rows, width), F32),
        sds((micros, rows, LANES), F32),
    ]
    args = (info, x, cols, small)
    return call(
        routed_body,
        shapes,
        (1,),
        [whole(a.shape) for a in args[1:]],
        [whole(s.shape) for s in shapes],
        args,
        flops=200_000_000,
        moved=3_000_000,
    )


def query_body(info, low, w_own, w_got, out):
    width = 2 * w_own.shape[0]
    for m in range(low.shape[0]):
        own, other = halves(info, low[m, :, :width])
        out[m, :, :width] = (mm(own, w_own[...]) + mm(other, w_got[...])).astype(BF)
        out[m, :, width:] = low[m, :, width:]


def query_project(info, low, w_own, w_got):
    half = w_own.shape[0]
    return call(
        query_body,
        sds(low.shape, BF),
        (1,),
        [whole(low.shape)] + [whole((half, 2 * half))] * 2,
        whole(low.shape),
        (info, low, w_own, w_got),
        flops=2 * low.shape[0] * low.shape[1] * 4 * half * half,
        moved=2_000_000,
    )


def light_in_body(info, x, small, w_own, w_got, out):
    values = x[0].astype(F32)
    low = (values * inverse_rms(values) * small[3:4].astype(F32)).astype(BF)
    own, other = halves(info, low)
    out[0] = (mm(own, w_own[...]) + mm(other, w_got[...])).astype(BF)


def light_in(info, x, small, w_own, w_got):
    micros, tok, width = x.shape
    columns = w_own.shape[1]
    split = 2
    rows = tok // split
    spec = lambda n: pl.BlockSpec((1, rows, n), lambda i, *u: (i // split, i % split, 0))
    return call(
        light_in_body,
        sds((micros, tok, columns), BF),
        (micros * split,),
        [spec(width), whole(small.shape), whole(w_own.shape), whole(w_got.shape)],
        spec(columns),
        (info, x, small, w_own, w_got),
        flops=2 * micros * tok * width * columns,
        moved=8_000_000,
    )


def fill_near(near, qkv, before, after):
    tok = qkv.shape[1]
    inner = near.shape[1] // 2
    near[:WIN] = before[0]
    near[WIN : WIN + tok] = qkv[0, :, inner:]
    near[WIN + tok :] = after[0]


def light_bias(info, micro, block):
    start = info[1] + block * WIN
    rows, columns = (WIN, 3 * WIN)
    row_pos = start + iota((rows, 1), 0)
    col_pos = start - WIN + iota((1, columns), 1)
    seg_row = segment(info, micro, row_pos)
    seg_col = jnp.where((col_pos >= 0) & (col_pos < info[2]), segment(info, micro, col_pos), -1)
    shift = iota((rows, columns), 0) + WIN - iota((rows, columns), 1)
    allowed = (jnp.abs(shift) < WIN) & (seg_row == seg_col)
    bias = jnp.where(allowed, 0.0, FAR)
    return jnp.concatenate([bias, bias], axis=0)


def stacked(pair, low_lane):
    zero = jnp.zeros_like(pair)
    return jnp.concatenate(
        [jnp.where(low_lane, pair, zero), jnp.where(low_lane, zero, pair)], axis=0
    )


def merged(values, low_lane):
    rows = values.shape[0] // 2
    return jnp.where(low_lane, values[:rows], values[rows:])


def light_fwd_body(info, qkv, before, after, out, lse_out, near):
    micro = pl.program_id(0)
    tok = qkv.shape[1]
    inner = out.shape[2]
    fill_near(near, qkv, before, after)
    low_lane = iota((WIN, LANES), 1) < HD
    lane = iota((WIN, LANES), 1)

    def block_step(block, carry):
        at = pl.ds(pl.multiple_of(block * WIN, WIN), WIN)
        around = pl.ds(pl.multiple_of(block * WIN, WIN), 3 * WIN)
        bias = light_bias(info, micro, block)
        stats = jnp.zeros((WIN, LANES), F32)
        for pair in range(inner // LANES):
            cut = slice(pair * LANES, (pair + 1) * LANES)
            query = stacked(qkv[0, at, cut] * BF(HD**-0.5), low_lane)
            scores = mm_t(query, near[around, cut]) + bias
            top = jnp.max(scores, axis=-1, keepdims=True)
            weights = jnp.exp(scores - top)
            total = jnp.sum(weights, axis=-1, keepdims=True)
            value = near[around, inner + pair * LANES : inner + (pair + 1) * LANES]
            mixed = mm((weights * (1.0 / total)).astype(BF), value)
            out[0, at, cut] = merged(mixed, low_lane).astype(BF)
            lse = top + jnp.log(total)
            stats = jnp.where(lane == 2 * pair, lse[:WIN], stats)
            stats = jnp.where(lane == 2 * pair + 1, lse[WIN:], stats)
        lse_out[0, at, :] = stats
        return carry

    [block_step(b, 0) for b in range(tok // WIN)]


def light_fwd(info, qkv, before, after):
    micros, tok, columns = qkv.shape
    inner = columns // 3
    shapes = [sds((micros, tok, inner), BF), sds((micros, tok, LANES), F32)]
    args = (info, qkv, before, after)
    return call(
        light_fwd_body,
        shapes,
        (micros,),
        [one_of(a.shape) for a in args[1:]],
        [one_of(s.shape) for s in shapes],
        args,
        scratch=[pltpu.VMEM((tok + 2 * WIN, 2 * inner), BF)],
        flops=4_000_000_000,
        moved=6_000_000,
    )


def light_bwd_body(info, qkv, before, after, lse, grad, dq_out, own_out, low_out, high_out, near, dk, dv):
    micro = pl.program_id(0)
    tok = qkv.shape[1]
    inner = grad.shape[2]
    fill_near(near, qkv, before, after)
    dk[...] = jnp.zeros_like(dk)
    dv[...] = jnp.zeros_like(dv)
    low_lane = iota((WIN, LANES), 1) < HD

    def block_step(block, carry):
        at = pl.ds(pl.multiple_of(block * WIN, WIN), WIN)
        around = pl.ds(pl.multiple_of(block * WIN, WIN), 3 * WIN)
        bias = light_bias(info, micro, block)
        stats = lse[0, at, :]
        for pair in range(inner // LANES):
            cut = slice(pair * LANES, (pair + 1) * LANES)
            query = stacked(qkv[0, at, cut] * BF(HD**-0.5), low_lane)
            key = near[around, cut]
            value = near[around, inner + pair * LANES : inner + (pair + 1) * LANES]
            shift = jnp.concatenate(
                [stats[:, 2 * pair : 2 * pair + 1], stats[:, 2 * pair + 1 : 2 * pair + 2]], axis=0
            )
            probs = jnp.exp(mm_t(query, key) + bias - shift)
            upper = stacked(grad[0, at, cut], low_lane)
            grad_probs = mm_t(upper, value)
            center = jnp.sum(probs * grad_probs, axis=-1, keepdims=True)
            slope = (probs * (grad_probs - center)).astype(BF)
            dq_out[0, at, cut] = (merged(mm(slope, key), low_lane) * HD**-0.5).astype(BF)
            dk[around, cut] += t_mm(slope, query)
            dv[around, cut] += t_mm(probs.astype(BF), upper)
        return carry

    [block_step(b, 0) for b in range(tok // WIN)]
    own_out[0, :, :inner] = dk[WIN : WIN + tok]
    own_out[0, :, inner:] = dv[WIN : WIN + tok]
    low_out[0, :, :inner] = dk[:WIN].astype(BF)
    low_out[0, :, inner:] = dv[:WIN].astype(BF)
    high_out[0, :, :inner] = dk[WIN + tok :].astype(BF)
    high_out[0, :, inner:] = dv[WIN + tok :].astype(BF)


def light_bwd(info, qkv, before, after, lse, grad):
    micros, tok, columns = qkv.shape
    inner = columns // 3
    shapes = [
        sds((micros, tok, inner), BF),
        sds((micros, tok, 2 * inner), F32),
        sds((micros, WIN, 2 * inner), BF),
        sds((micros, WIN, 2 * inner), BF),
    ]
    args = (info, qkv, before, after, lse, grad)
    return call(
        light_bwd_body,
        shapes,
        (micros,),
        [one_of(a.shape) for a in args[1:]],
        [one_of(s.shape) for s in shapes],
        args,
        scratch=[
            pltpu.VMEM((tok + 2 * WIN, 2 * inner), BF),
            pltpu.VMEM((tok + 2 * WIN, inner), F32),
            pltpu.VMEM((tok + 2 * WIN, inner), F32),
        ],
        flops=10_000_000_000,
        moved=14_000_000,
    )


def key_body(info, kin, w_own, w_got, out):
    half = w_own.shape[0]
    width = 2 * half
    own = kin[:, pl.ds(pl.multiple_of(info[0] * half, half), half)]
    other = kin[:, pl.ds(pl.multiple_of((1 - info[0]) * half, half), half)]
    out[...] = (mm(own, w_own[:, width:]) + mm(other, w_got[:, width:])).astype(BF)


def key_project(info, kin, w_own, w_got):
    shape = sds((kin.shape[0], 2 * (kin.shape[1] - LANES)), BF)
    args = (info, kin, w_own, w_got)
    return call(
        key_body,
        shape,
        (1,),
        [whole(a.shape) for a in args[1:]],
        whole(shape.shape),
        args,
        flops=1_200_000_000,
        moved=6_000_000,
    )


def heavy_scores(query, parts, bias, cut):
    return [mm_t(query, part[:, cut]) + b for part, b in zip(parts, bias)]


def heavy_fwd_body(info, q, kin_a, kin_b, kv_a, kv_b, out, lse_out):
    rows, width = out.shape
    parts = (kv_a, kv_b)
    low_lane = iota((rows, LANES), 1) < HD
    lane = iota((rows, LANES), 1)
    feature = jnp.concatenate([q[:, width:]] * 2, axis=0)
    bias = [mm_t(feature, kin[:, width:]) for kin in (kin_a, kin_b)]
    stats = jnp.zeros((rows, LANES), F32)
    for pair in range(width // LANES):
        cut = slice(pair * LANES, (pair + 1) * LANES)
        query = stacked(q[:, cut] * BF(HD**-0.5), low_lane)
        scores = heavy_scores(query, parts, bias, cut)
        top = functools.reduce(
            jnp.maximum, [jnp.max(s, axis=-1, keepdims=True) for s in scores]
        )
        weights = [jnp.exp(s - top) for s in scores]
        total = sum(jnp.sum(w, axis=-1, keepdims=True) for w in weights)
        scale = 1.0 / total
        mixed = sum(
            mm((w * scale).astype(BF), part[:, width + pair * LANES : width + (pair + 1) * LANES])
            for w, part in zip(weights, parts)
        )
        out[:, cut] = merged(mixed, low_lane).astype(BF)
        lse = top + jnp.log(total)
        stats = jnp.where(lane == 2 * pair, lse[:rows], stats)
        stats = jnp.where(lane == 2 * pair + 1, lse[rows:], stats)
    lse_out[...] = stats


def heavy_fwd(info, q, kins, kvs):
    rows = q.shape[0]
    width = q.shape[1] - LANES
    shapes = [sds((rows, width), BF), sds((rows, LANES), F32)]
    args = (info, q, *kins, *kvs)
    return call(
        heavy_fwd_body,
        shapes,
        (1,),
        [whole(a.shape) for a in args[1:]],
        [whole(s.shape) for s in shapes],
        args,
        flops=1_500_000_000,
        moved=5_000_000,
    )


def heavy_bwd_body(info, q, kin_a, kin_b, kv_a, kv_b, lse, grad, w_own, w_got, dq_out, da_out, db_out, ia_out, ib_out):
    rows, width = grad.shape
    parts = (kv_a, kv_b)
    low_lane = iota((rows, LANES), 1) < HD
    feature = jnp.concatenate([q[:, width:]] * 2, axis=0)
    bias = [mm_t(feature, kin[:, width:]) for kin in (kin_a, kin_b)]
    for pair in range(width // LANES):
        cut = slice(pair * LANES, (pair + 1) * LANES)
        upcut = slice(width + pair * LANES, width + (pair + 1) * LANES)
        query = stacked(q[:, cut] * BF(HD**-0.5), low_lane)
        shift = jnp.concatenate(
            [lse[:, 2 * pair : 2 * pair + 1], lse[:, 2 * pair + 1 : 2 * pair + 2]], axis=0
        )
        probs = [jnp.exp(s - shift) for s in heavy_scores(query, parts, bias, cut)]
        upper = stacked(grad[:, cut], low_lane)
        grads = [mm_t(upper, part[:, upcut]) for part in parts]
        center = sum(jnp.sum(p * g, axis=-1, keepdims=True) for p, g in zip(probs, grads))
        slopes = [(p * (g - center)).astype(BF) for p, g in zip(probs, grads)]
        dq = sum(mm(s, part[:, cut]) for s, part in zip(slopes, parts))
        dq_out[:, cut] = (merged(dq, low_lane) * HD**-0.5).astype(BF)
        for target, slope, prob in zip((da_out, db_out), slopes, probs):
            target[:, cut] = t_mm(slope, query).astype(BF)
            target[:, upcut] = t_mm(prob.astype(BF), upper).astype(BF)
    half = width // 2
    for target, source in ((ia_out, da_out), (ib_out, db_out)):
        for weight, side in ((w_own, info[0]), (w_got, 1 - info[0])):
            target[:, pl.ds(pl.multiple_of(side * half, half), half)] = mm_t(
                source[...], weight[:, width:]
            ).astype(BF)


def heavy_bwd(info, q, kins, kvs, lse, grad, w_own, w_got):
    rows = q.shape[0]
    width = q.shape[1] - LANES
    keys = kvs[0].shape[0]
    shapes = [sds((rows, width), BF)] + [sds((keys, 2 * width), BF)] * 2 + [sds((keys, width), BF)] * 2
    args = (info, q, *kins, *kvs, lse, grad, w_own, w_got)
    return call(
        heavy_bwd_body,
        shapes,
        (1,),
        [whole(a.shape) for a in args[1:]],
        [whole(s.shape) for s in shapes],
        args,
        flops=6_500_000_000,
        moved=15_000_000,
    )


def heavy_grads_body(info, *refs):
    micros = (len(refs) - 8) // 4
    hq, dhq, ho, dhy, lo, dy = refs[:6]
    kins, dkvs = (refs[6 : 6 + 2 * micros], refs[6 + 2 * micros : -2])
    other_out, own_out = (refs[-1], refs[-2])
    half = hq.shape[2] // 2
    every = range(micros)
    for target, side in ((other_out, 1 - info[0]), (own_out, info[0])):
        cut = pl.ds(pl.multiple_of(side * half, half), half)

        def put(unit, left, right, columns):
            for block in range(columns // COLS):
                at = unit + block
                total = sum(
                    t_mm(a, b[:, block * COLS : (block + 1) * COLS]) for a, b in zip(left, right)
                )
                target[at // 2, (at % 2) * half : (at % 2 + 1) * half] = total.astype(BF)
            return unit + columns // COLS

        unit = put(0, [hq[m, :, cut] for m in every], [dhq[m] for m in every], dhq.shape[2])
        unit = put(unit, [kin[:, cut] for kin in kins], dkvs, dkvs[0].shape[1])
        unit = put(unit, [ho[m, :, cut] for m in every], [dhy[m] for m in every], dhy.shape[2])
        part = lo.shape[2] // 2
        small_cut = pl.ds(pl.multiple_of(side * part, part), part)
        total = sum(t_mm(lo[m, :, small_cut], dy[m].astype(BF)) for m in every)
        pack_rows(target.at[pl.ds(unit // 2, 1)], total)


def heavy_grads(info, hq, dhq, ho, dhy, lo, dy, kins, dkvs):
    width = dhq.shape[2]
    units = (dhq.shape[2] + dkvs[0].shape[1] + dhy.shape[2]) // COLS
    shapes = [sds((units // 2 + 1, width, COLS), BF)] * 2
    args = (info, hq, dhq, ho, dhy, lo, dy, *kins, *dkvs)
    return call(
        heavy_grads_body,
        shapes,
        (1,),
        [whole(dhq.shape)] + [whole(a.shape) for a in args[2:]],
        [whole(s.shape) for s in shapes],
        args,
        flops=6_500_000_000,
        moved=28_000_000,
    )


def middle_body(info, x, up, cols, rows, small, gate, lo, lout, lout_got, ho, hout, y_out, low_out, pay_out, hy_out, gf_out):
    tok = x.shape[1]
    base = info[1]
    hy = mm(ho[0], hout[...])
    hy_out[0] = hy
    spread = onehot_rows(rows[0, 0], base, tok)
    part = lout.shape[0]
    own = lo[0, :, pl.ds(pl.multiple_of(info[0] * part, part), part)]
    other = lo[0, :, pl.ds(pl.multiple_of((1 - info[0]) * part, part), part)]
    light = mm(own, lout[...]) + mm(other, lout_got[...])
    y = x[0].astype(F32) + light + pick(spread, hy * gate[0, :, 0:1])
    y_out[0] = y
    low = (y * inverse_rms(y) * small[4:5].astype(F32)).astype(BF)
    low_out[0] = low
    take = onehot_cols(cols[2, 0], base, tok)
    taken = mm(take, low)
    width = x.shape[2]
    pay_out[0, :, :width] = taken.astype(BF)
    gf = jax.nn.sigmoid(jnp.sum(taken * small[2:3].astype(F32), axis=-1, keepdims=True))
    pay_out[0, :, width:] = (mm(take, up[0]) * gf).astype(BF)
    gf_out[0] = jnp.broadcast_to(gf, gf_out.shape[1:])


def second_of(shape):
    rank = len(shape)
    return pl.BlockSpec(
        (shape[0], 1) + tuple(shape[2:]), lambda i, *unused: (0, i) + (0,) * (rank - 2)
    )


def middle(info, x, up, cols, rows, small, gate, lo, lout, lout_got, ho, hout):
    micros, tok, width = x.shape
    count = cols.shape[2]
    shapes = [
        sds((micros, tok, width), F32),
        sds((micros, tok, width), BF),
        sds((micros, count, 2 * width), BF),
        sds((micros, count, width), F32),
        sds((micros, count, LANES), F32),
    ]
    args = (info, x, up, cols, rows, small, gate, lo, lout, lout_got, ho, hout)
    return call(
        middle_body,
        shapes,
        (micros,),
        [
            one_of(x.shape),
            one_of(up.shape),
            second_of(cols.shape),
            second_of(rows.shape),
            whole(small.shape),
            one_of(gate.shape),
            one_of(lo.shape),
            whole(lout.shape),
            whole(lout_got.shape),
            one_of(ho.shape),
            whole(hout.shape),
        ],
        [one_of(s.shape) for s in shapes],
        args,
        flops=2_000_000_000,
        moved=12_000_000,
    )


def pack_rows(target, values):
    step = values.shape[0] // 16
    cuts = values.shape[1] // COLS
    for slot in range(16):
        for cut in range(cuts):
            at = slot * step * cuts + cut * step
            target[0, at : at + step] = values[
                slot * step : (slot + 1) * step, cut * COLS : (cut + 1) * COLS
            ].astype(BF)


def gelu_parts(g):
    root = (2.0 / 3.141592653589793) ** 0.5
    square = g * g
    tanh = jnp.tanh(root * g * (1.0 + 0.044715 * square))
    bell = 0.5 * (1.0 + tanh)
    slope = bell + 0.5 * g * (1.0 - tanh * tanh) * (root * (1.0 + 3 * 0.044715 * square))
    return (g * bell, slope)


def hidden_both_ways(low, upstream, wg, wu, wd):
    g, u = (mm(low, wg), mm(low, wu))
    back = mm_t(upstream, wd)
    gelu, slope = gelu_parts(g)
    return ((gelu * u).astype(BF), (back * u * slope).astype(BF), (back * gelu).astype(BF))


def add_steps(step, pairs):
    @pl.when(step == 0)
    def first():
        for target, value in pairs:
            target[...] = value

    @pl.when(step > 0)
    def later():
        for target, value in pairs:
            target[...] += value


def ffn_local_body(info, a, ct, wg, wu, wd, z_out, dh_out):
    hidden, dg, du = hidden_both_ways(a[...], ct[...], wg[...], wu[...], wd[...])
    z = mm(hidden, wd[...])
    dh = mm_t(dg, wg[...]) + mm_t(du, wu[...])
    add_steps(pl.program_id(0), [(z_out, z), (dh_out, dh)])


def ffn_body(info, a, ct, wg, wu, wd, z_out, dh_out, own_gu, other_gu, own_dn, other_dn):
    step = pl.program_id(0)
    half = pl.num_programs(0) // 2
    width = a.shape[1] // 2
    hidden, dg, du = hidden_both_ways(a[...], ct[...], wg[...], wu[...], wd[...])
    z = mm(hidden, wd[...])
    dh = mm_t(dg, wg[...]) + mm_t(du, wu[...])
    add_steps(step, [(z_out, z), (dh_out, dh)])
    down = t_mm(hidden, ct[...])

    @pl.when(step < half)
    def send():
        pack_rows(other_dn, down)

    @pl.when(step >= half)
    def keep():
        pack_rows(own_dn, down)

    own = a[:, pl.ds(pl.multiple_of(info[0] * width, width), width)]
    other = a[:, pl.ds(pl.multiple_of((1 - info[0]) * width, width), width)]
    own_gu[0, :width] = t_mm(own, dg).astype(BF)
    own_gu[0, width:] = t_mm(own, du).astype(BF)
    other_gu[0, :width] = t_mm(other, dg).astype(BF)
    other_gu[0, width:] = t_mm(other, du).astype(BF)


def ffn_local(info, pay, w_gu, w_down, block):
    rows = pay.shape[0]
    hidden, width = w_down.shape
    steps = hidden // block
    return call(
        ffn_local_body,
        [sds((rows, width), F32)] * 2,
        (steps,),
        [
            pl.BlockSpec((rows, width), lambda i, *u: (0, 0)),
            pl.BlockSpec((rows, width), lambda i, *u: (0, 1)),
            pl.BlockSpec((width, block), lambda i, *u: (0, i)),
            pl.BlockSpec((width, block), lambda i, *u: (0, steps + i)),
            pl.BlockSpec((block, width), lambda i, *u: (i, 0)),
        ],
        [whole((rows, width))] * 2,
        (info, pay, pay, w_gu, w_gu, w_down),
        flops=2 * 6 * rows * hidden * width,
        moved=2 * 3 * hidden * width,
    )


def ffn(info, a, ct, w_gu, w_down):
    rows, width = a.shape
    hidden = w_down.shape[0]
    block = COLS
    steps = hidden // block
    half = steps // 2

    def natural(i, info):
        return jnp.where(i < half, (1 - info[0]) * half + i, info[0] * half + i - half)

    unit = (1, width, COLS)
    shapes = [
        sds((rows, width), F32),
        sds((rows, width), F32),
        sds((steps,) + unit[1:], BF),
        sds((steps,) + unit[1:], BF),
        sds((half,) + unit[1:], BF),
        sds((half,) + unit[1:], BF),
    ]
    return call(
        ffn_body,
        shapes,
        (steps,),
        [
            whole(a.shape),
            whole(ct.shape),
            pl.BlockSpec((width, block), lambda i, info: (0, natural(i, info))),
            pl.BlockSpec((width, block), lambda i, info: (0, steps + natural(i, info))),
            pl.BlockSpec((block, width), lambda i, info: (natural(i, info), 0)),
        ],
        [
            whole((rows, width)),
            whole((rows, width)),
            pl.BlockSpec(unit, lambda i, info: (natural(i, info), 0, 0)),
            pl.BlockSpec(unit, lambda i, info: (natural(i, info), 0, 0)),
            pl.BlockSpec(unit, lambda i, info: (jnp.maximum(i - half, 0), 0, 0)),
            pl.BlockSpec(unit, lambda i, info: (jnp.minimum(i, half - 1), 0, 0)),
        ],
        (info, a, ct, w_gu, w_gu, w_down),
        flops=2 * 9 * rows * hidden * width,
        moved=2 * 2 * 3 * hidden * width + rows * width * 12,
    )


def ffn_all_body(info, a, ct, w_gu, w_down, z_out, dh_out, own_gu, other_gu, own_dn, other_dn, turned, hid, slopes):
    step = pl.program_id(0)
    hidden, whole_width = w_down.shape
    steps = hidden // COLS
    half = steps // 2
    width = whole_width // 2

    @pl.when(step == 0)
    def turn():
        turned[...] = a[...].T

    @pl.when(step < steps)
    def block():
        at = jnp.where(step < half, (1 - info[0]) * half + step, info[0] * half + step - half)
        gate = pl.ds(pl.multiple_of(at * COLS, COLS), COLS)
        upper = pl.ds(pl.multiple_of(hidden + at * COLS, COLS), COLS)
        mixed, dg, du = hidden_both_ways(a[...], ct[...], w_gu[:, gate], w_gu[:, upper], w_down[gate])
        hid[:, gate] = mixed
        slopes[:, gate] = dg
        slopes[:, upper] = du
        down = t_mm(mixed, ct[...])

        @pl.when(step < half)
        def send():
            pack_rows(other_dn, down)

        @pl.when(step >= half)
        def keep():
            pack_rows(own_dn, down)

        for target, side in ((own_gu, info[0]), (other_gu, 1 - info[0])):
            rows = turned[pl.ds(pl.multiple_of(side * width, width), width)]
            target[0, :width] = mm(rows, dg).astype(BF)
            target[0, width:] = mm(rows, du).astype(BF)

    @pl.when(step == steps)
    def last():
        z_out[...] = mm(hid[...], w_down[...]).astype(BF)
        dh_out[...] = mm_t(slopes[...], w_gu[...]).astype(BF)


def ffn_all(info, a, ct, w_gu, w_down):
    rows, width = a.shape
    hidden = w_down.shape[0]
    steps = hidden // COLS
    half = steps // 2

    def natural(i, info):
        return jnp.where(i < half, (1 - info[0]) * half + i, info[0] * half + jnp.minimum(i - half, half - 1))

    unit = (1, width, COLS)
    shapes = [
        sds((rows, width), BF),
        sds((rows, width), BF),
        sds((steps,) + unit[1:], BF),
        sds((steps,) + unit[1:], BF),
        sds((half,) + unit[1:], BF),
        sds((half,) + unit[1:], BF),
    ]
    return call(
        ffn_all_body,
        shapes,
        (steps + 1,),
        [whole(a.shape), whole(ct.shape), whole(w_gu.shape), whole(w_down.shape)],
        [
            whole((rows, width)),
            whole((rows, width)),
            pl.BlockSpec(unit, lambda i, info: (natural(i, info), 0, 0)),
            pl.BlockSpec(unit, lambda i, info: (natural(i, info), 0, 0)),
            pl.BlockSpec(unit, lambda i, info: (jnp.minimum(jnp.maximum(i - half, 0), half - 1), 0, 0)),
            pl.BlockSpec(unit, lambda i, info: (jnp.minimum(i, half - 1), 0, 0)),
        ],
        (info, a, ct, w_gu, w_down),
        scratch=[
            pltpu.VMEM((width, rows), BF),
            pltpu.VMEM((rows, hidden), BF),
            pltpu.VMEM((rows, 2 * hidden), BF),
        ],
        flops=2 * 9 * rows * hidden * width,
        moved=2 * 2 * 3 * hidden * width + rows * width * 12,
    )


def plane_grads_body(info, near, far, wg, wu, wd, own_gu, other_gu, dn):
    width = wg.shape[0]
    half = width // 2
    sums = None
    for part in (near, far):
        low, upstream = (part[:, :width], part[:, width:])
        hidden, dg, du = hidden_both_ways(low, upstream, wg[...], wu[...], wd[...])
        own = part[:, pl.ds(pl.multiple_of(info[0] * half, half), half)]
        other = part[:, pl.ds(pl.multiple_of((1 - info[0]) * half, half), half)]
        terms = (t_mm(own, dg), t_mm(own, du), t_mm(other, dg), t_mm(other, du), t_mm(hidden, upstream))
        sums = terms if sums is None else tuple(p + q for p, q in zip(sums, terms))
    own_gu[0, :half] = sums[0].astype(BF)
    own_gu[0, half:] = sums[1].astype(BF)
    other_gu[0, :half] = sums[2].astype(BF)
    other_gu[0, half:] = sums[3].astype(BF)
    for cut in range(width // COLS):
        dn[0, cut * COLS : (cut + 1) * COLS] = sums[4][:, cut * COLS : (cut + 1) * COLS].astype(BF)


def plane_grads(info, near, far, w_gu, w_down):
    hidden, width = w_down.shape
    steps = hidden // COLS
    turns = steps // 8

    def block(i, info):
        return info[0] * (steps // 2) + lax.rem(info[3], 4) * turns + i

    unit = (1, width, COLS)
    spec = pl.BlockSpec(unit, lambda i, *u: (i, 0, 0))
    rows = 2 * near.shape[0]
    return call(
        plane_grads_body,
        [sds((turns, width, COLS), BF)] * 3,
        (turns,),
        [
            whole(near.shape),
            whole(far.shape),
            pl.BlockSpec((width, COLS), lambda i, info: (0, block(i, info))),
            pl.BlockSpec((width, COLS), lambda i, info: (0, steps + block(i, info))),
            pl.BlockSpec((COLS, width), lambda i, info: (block(i, info), 0)),
        ],
        [spec] * 3,
        (info, near, far, w_gu, w_gu, w_down),
        flops=2 * 6 * rows * turns * COLS * width,
        moved=9_000_000,
    )


def column_fold_body(order, info, first, second, third, keep, send):
    slots = 1 << len(order)
    size = keep.shape[2]
    place_z = info[3] // 4
    for part, source in enumerate((first, second, third)):
        for block in range(source.shape[0]):
            for slot in range(slots):
                owner = jnp.bitwise_xor(place_z, mask_of(slot, order))
                at = pl.ds(pl.multiple_of(owner * size, size), size)
                target = keep if slot < slots // 2 else send
                target[slot % (slots // 2), part * source.shape[0] + block] = source[block, at, :]


def column_fold(info, order, sources):
    slots = 1 << len(order)
    blocks, width, cols = sources[0].shape
    shape = sds((slots // 2, 3 * blocks, width // slots, cols), BF)
    return call(
        functools.partial(column_fold_body, order),
        [shape, shape],
        (1,),
        [whole(a.shape) for a in sources],
        [whole(shape.shape)] * 2,
        (info, *sources),
        moved=10_000_000,
        name="column_fold",
    )


def mid_back_body(
    info, y, up, z, dh2, zh, dff, ffr, gf, cols, rows, small, gate, lout, lout_got, hout, hy, hq,
    out, dy_out, dlo_out, dho_out, dhy_out, dsq_out, part_out,
):
    tok = y.shape[1]
    base = info[1]
    micro = pl.program_id(0)
    spread = onehot_rows(rows[2, 0], base, tok)
    take = onehot_cols(cols[2, 0], base, tok)
    values, top = (y[0], up[0].astype(F32))
    open_f = gf[0, :, 0:1]
    zhv = zh[0]
    out[0] = (values + z[0].astype(F32) + pick(spread, zhv * open_f)).astype(BF)
    taken = mm(take, up[0])
    dsf = jnp.sum(taken * zhv, axis=-1, keepdims=True) * open_f * (1.0 - open_f)
    back = dh2[0].astype(F32) + pick(spread, dff[0] + dsf * small[2:3].astype(F32))
    inv = inverse_rms(values)
    scaled = back * small[4:5].astype(F32)
    mean = jnp.mean(values * scaled, axis=-1, keepdims=True)
    dy = top + inv * scaled - values * (inv * inv * inv * mean)
    dy_out[0] = dy
    dgain = jnp.sum(back * values * inv, axis=0, keepdims=True)
    drf = jnp.sum(dsf * ffr[0].astype(F32), axis=0, keepdims=True)
    part_in = lout.shape[0]
    for weight, side in ((lout, info[0]), (lout_got, 1 - info[0])):
        at = pl.ds(pl.multiple_of(side * part_in, part_in), part_in)
        dlo_out[0, :, at] = mm_t(dy.astype(BF), weight[...]).astype(BF)
    dyq = pick(onehot_cols(cols[0, 0], base, tok), dy)
    open_q = gate[0, :, 0:1]
    dhy = (dyq * open_q).astype(BF)
    dhy_out[0] = dhy
    dsq = jnp.sum(dyq * hy[0], axis=-1, keepdims=True) * open_q * (1.0 - open_q)
    dsq_out[0] = jnp.broadcast_to(dsq, dsq_out.shape[1:])
    drq = jnp.sum(dsq * hq[0].astype(F32), axis=0, keepdims=True)
    dho_out[0] = mm_t(dhy, hout[...]).astype(BF)
    row = iota(part_out.shape, 0)
    part = jnp.where(row == 0, drq, jnp.where(row == 2, drf, jnp.where(row == 4, dgain, 0.0)))

    @pl.when(micro == 0)
    def first():
        part_out[...] = part

    @pl.when(micro > 0)
    def later():
        part_out[...] += part


def mid_back(info, y, up, z, dh2, zh, dff, ffr, gf, cols, rows, small, gate, lout, lout_got, hout, hy, hq):
    micros, tok, width = y.shape
    count = cols.shape[2]
    shapes = [
        sds((micros, tok, width), BF),
        sds((micros, tok, width), F32),
        sds((micros, tok, 2 * lout.shape[0]), BF),
        sds((micros, count, width), BF),
        sds((micros, count, width), BF),
        sds((micros, count, LANES), F32),
        sds((8, width), F32),
    ]
    return call(
        mid_back_body,
        shapes,
        (micros,),
        [
            one_of(y.shape),
            one_of(up.shape),
            one_of(z.shape),
            one_of(dh2.shape),
            one_of(zh.shape),
            one_of(dff.shape),
            pl.BlockSpec((1, count, width), lambda i, *u: (i, 0, 0)),
            one_of(gf.shape),
            second_of(cols.shape),
            second_of(rows.shape),
            whole(small.shape),
            one_of(gate.shape),
            whole(lout.shape),
            whole(lout_got.shape),
            whole(hout.shape),
            one_of(hy.shape),
            pl.BlockSpec((1, count, width), lambda i, *u: (i, 0, 0)),
        ],
        [one_of(s.shape) for s in shapes[:-1]] + [whole(shapes[-1].shape)],
        (info, y, up, z, dh2, zh, dff, ffr, gf, cols, rows, small, gate, lout, lout_got, hout, hy, hq),
        flops=3_000_000_000,
        moved=22_000_000,
    )


def light_join_body(info, x, small, dq, own, got_low, got_high, dl_out, own_out, other_out, low):
    tok, width = x.shape[1:]
    micros = x.shape[0]
    half = width // 2
    inner = dq.shape[2]
    for m in range(micros):
        dl_out[m, :, :inner] = dq[m]
        dl_out[m, WIN : tok - WIN, inner:] = own[m, WIN : tok - WIN].astype(BF)
        dl_out[m, :WIN, inner:] = (own[m, :WIN] + got_low[m].astype(F32)).astype(BF)
        dl_out[m, tok - WIN :, inner:] = (own[m, tok - WIN :] + got_high[m].astype(F32)).astype(BF)
        values = x[m].astype(F32)
        low[m] = (values * inverse_rms(values) * small[3:4].astype(F32)).astype(BF)
    for target, side in ((other_out, 1 - info[0]), (own_out, info[0])):
        cut = pl.ds(pl.multiple_of(side * half, half), half)
        for block in range(dl_out.shape[2] // COLS):
            total = sum(
                t_mm(low[m, :, cut], dl_out[m, :, block * COLS : (block + 1) * COLS])
                for m in range(micros)
            )
            target[block // 2, (block % 2) * half : (block % 2 + 1) * half] = total.astype(BF)


def light_join(info, x, small, dq, own, got_low, got_high):
    micros, tok, width = x.shape
    columns = dq.shape[2] + own.shape[2]
    shapes = [sds((micros, tok, columns), BF)] + [sds((columns // (2 * COLS), width, COLS), BF)] * 2
    args = (info, x, small, dq, own, got_low, got_high)
    return call(
        light_join_body,
        shapes,
        (1,),
        [whole(a.shape) for a in args[1:]],
        [whole(s.shape) for s in shapes],
        args,
        scratch=[pltpu.VMEM(x.shape, BF)],
        flops=2 * micros * tok * width * columns,
        moved=20_000_000,
    )


def in_back_body(
    info, x, dy, dl, dhq, dkin, dsq, rows, small, gate, h1k, l_own, l_got, h_own, h_got,
    grad_out, part_out,
):
    tok, width = x.shape[1:]
    micro = pl.program_id(0)
    base = info[1]
    light = dl[0]
    back = unhalved(info, mm_t(light, l_own[...]), mm_t(light, l_got[...]))
    given = dkin[0].astype(F32)
    open_k = gate[0, :, 1:2]
    source = h1k[0]
    dskv = jnp.sum(given * source, axis=-1, keepdims=True) * open_k * (1.0 - open_k)
    to_q = unhalved(info, mm_t(dhq[0], h_own[...]), mm_t(dhq[0], h_got[...]))
    to_q += dsq[0, :, 0:1] * small[0:1].astype(F32)
    to_k = given * open_k + dskv * small[1:2].astype(F32)
    back += pick(onehot_rows(rows[0, 0], base, tok), to_q)
    back += pick(onehot_rows(rows[1, 0], base, tok), to_k)
    values = x[0].astype(F32)
    inv = inverse_rms(values)
    scaled = back * small[3:4].astype(F32)
    mean = jnp.mean(values * scaled, axis=-1, keepdims=True)
    grad_out[0] = (dy[0] + inv * scaled - values * (inv * inv * inv * mean)).astype(BF)
    dgain = jnp.sum(back * values * inv, axis=0, keepdims=True)
    drk = jnp.sum(dskv * source.astype(BF).astype(F32), axis=0, keepdims=True)
    row = iota(part_out.shape, 0)
    part = jnp.where(row == 1, drk, jnp.where(row == 3, dgain, 0.0))

    @pl.when(micro == 0)
    def first():
        part_out[...] = part

    @pl.when(micro > 0)
    def later():
        part_out[...] += part


def in_back(info, x, dy, dl, dhq, dkin, dsq, rows, small, gate, h1k, l_own, l_got, h_own, h_got):
    micros, tok, width = x.shape
    shapes = [sds((micros, tok, width), BF), sds((8, width), F32)]
    firsts = (x, dy, dl, dhq, dkin, dsq)
    return call(
        in_back_body,
        shapes,
        (micros,),
        [one_of(a.shape) for a in firsts]
        + [second_of(rows.shape), whole(small.shape)]
        + [one_of(a.shape) for a in (gate, h1k)]
        + [whole(a.shape) for a in (l_own, l_got)]
        + [whole((h_own.shape[0], width))] * 2,
        [one_of(shapes[0].shape), whole(shapes[1].shape)],
        (info,) + firsts + (rows, small, gate, h1k, l_own, l_got, h_own, h_got),
        flops=2_600_000_000,
        moved=14_000_000,
    )


def mask_of(slot, order):
    bits = len(order)
    return sum(order[b] for b in range(bits) if (slot >> (bits - 1 - b)) & 1)


def fold_body(order, counts, info, *refs):
    sources = refs[: 2 * len(counts)]
    keep, send = refs[2 * len(counts) :]
    slots = 1 << len(order)
    size = keep.shape[2]
    step = pl.program_id(0)
    start = 0
    for which, count in enumerate(counts):
        own, got = sources[2 * which : 2 * which + 2]

        @pl.when((step >= start) & (step < start + count))
        def part():
            for slot in range(slots):
                owner = jnp.bitwise_xor(info[3], mask_of(slot, order))
                at = pl.ds(pl.multiple_of(owner * size, size), size)
                total = (own[0, at, :].astype(F32) + got[0, at, :].astype(F32)).astype(BF)
                if slot < slots // 2:
                    keep[slot, 0] = total
                else:
                    send[slot - slots // 2, 0] = total

        start += count


def fold(info, order, parts):
    slots = 1 << len(order)
    width = parts[0][0].shape[1]
    counts = [part[3] for part in parts]
    total = sum(counts)
    shape = sds((slots // 2, total, width // slots, COLS), BF)
    args, specs = ([], [])
    start = 0
    for own, got, first, count in parts:
        index = functools.partial(
            lambda first, start, count, i, *u: (
                first + jnp.minimum(jnp.maximum(i - start, 0), count - 1),
                0,
                0,
            ),
            first,
            start,
            count,
        )
        args += [own, got]
        specs += [pl.BlockSpec((1, width, COLS), index)] * 2
        start += count
    spec = pl.BlockSpec((slots // 2, 1, width // slots, COLS), lambda i, *u: (0, i, 0, 0))
    return call(
        functools.partial(fold_body, order, counts),
        [shape, shape],
        (total,),
        specs,
        [spec, spec],
        (info, *args),
        moved=total * width * COLS * 6,
    )


def flipped(value, bit):
    size = lax.axis_size("ctx")
    return lax.ppermute(value, "ctx", [(i, i ^ bit) for i in range(size)])


def tied(*values):
    return lax.optimization_barrier(values)


def scatter_step(keep, got):
    half = keep.shape[0] // 2
    if half == 0:
        return ((keep.astype(F32) + got.astype(F32)).astype(BF), None)
    return (
        (keep[:half].astype(F32) + got[:half].astype(F32)).astype(BF),
        (keep[half:].astype(F32) + got[half:].astype(F32)).astype(BF),
    )


def scatter_start(chunks, orders, stage):
    return [flipped(send, order[stage]) for (keep, send), order in zip(chunks, orders)]


def scatter_end(chunks, got):
    return [scatter_step(keep, g) for (keep, send), g in zip(chunks, got)]


def scatter_sum(keep, send, order):
    for bit in order:
        keep, send = scatter_step(keep, flipped(send, bit))
    return keep


def gather_start(values, orders, stage):
    return [flipped(value, order[-1 - stage]) for value, order in zip(values, orders)]


def gather_end(values, got):
    return [jnp.concatenate([value, g], axis=0) for value, g in zip(values, got)]


def gather_pair(value, order):
    for bit in order[:-1]:
        value = jnp.concatenate([value, flipped(value, bit)], axis=0)
    return (value, flipped(value, order[-1]))


def from_owner(info, order, near, far, owner, write):
    slots = 1 << len(order)
    distance = jnp.bitwise_xor(info[3], owner)
    slot = sum(
        jnp.where(jnp.bitwise_and(distance, bit) != 0, 1 << place, 0)
        for place, bit in enumerate(reversed(order))
    )
    inside = lax.rem(slot, slots // 2)

    @pl.when(slot < slots // 2)
    def close():
        write(near.at[inside])

    @pl.when(slot >= slots // 2)
    def distant():
        write(far.at[inside])


def unpack_gu_body(order, info, near, far, *outs):
    out = outs[-1]
    size = near.shape[2]
    per = out.shape[0] // size
    for turn in range(per):

        def write(source, turn=turn):
            for block in range(near.shape[1]):
                out[turn * size : (turn + 1) * size, block * COLS : (block + 1) * COLS] = source[
                    block
                ].astype(F32)

        from_owner(info, order, near, far, pl.program_id(1) * per + turn, write)


def write_dn(out, source, first, size, owner, row):
    cuts = out.shape[1] // COLS
    rows = size // cuts
    value = source[first].astype(F32)
    for cut in range(cuts):
        out[row + owner * rows : row + (owner + 1) * rows, cut * COLS : (cut + 1) * COLS] = value[
            cut * rows : (cut + 1) * rows
        ]


def unpack_dn_body(order, info, near, far, *outs):
    slots, blocks, size = near.shape[:3]
    for owner in range(2 * slots):

        def write(source, owner=owner):
            for block in range(blocks):
                write_dn(outs[-1], source, block, size, owner, block * COLS)

        from_owner(info, order, near, far, owner, write)


def unpack(body, info, order, pair, first, count, step, shape, grid_more, block, index, previous, name):
    near, far = pair
    slots, unused, size, unused_too = near.shape
    spec = pl.BlockSpec((slots, step, size, COLS), lambda i, *u: (0, first // step + i, 0, 0))
    args, specs, aliases = ([info, near, far], [spec, spec], {})
    if previous is not None:
        args.append(previous)
        specs.append(pl.BlockSpec(memory_space=pl.ANY))
        aliases = {3: 0}
    return pl.pallas_call(
        functools.partial(body, order),
        out_shape=sds(shape, F32),
        grid_spec=pltpu.PrefetchScalarGridSpec(
            num_scalar_prefetch=1,
            grid=(count // step,) + grid_more,
            in_specs=specs,
            out_specs=pl.BlockSpec(block, index),
        ),
        input_output_aliases=aliases,
        compiler_params=pltpu.CompilerParams(vmem_limit_bytes=32 * 1024 * 1024),
        cost_estimate=pl.CostEstimate(
            flops=0, bytes_accessed=count * 2 * slots * size * COLS * 6, transcendentals=0
        ),
        name=name,
    )(*args)


def unpack_gu(info, order, pair, first, count, total, base, previous, step):
    rows = pair[0].shape[0] * pair[0].shape[2]
    return unpack(
        unpack_gu_body, info, order, pair, first, count, step, (rows, 2 * total * COLS), (2,), (rows, step * COLS),
        lambda i, s, *u: (0, (s * total + base) // step + i), previous, "unpack_gu",
    )


def unpack_dn(info, order, pair, first, count, total, base, previous, step):
    width = 2 * pair[0].shape[0] * pair[0].shape[2]
    return unpack(
        unpack_dn_body, info, order, pair, first, count, step, (total * COLS, width), (), (step * COLS, width),
        lambda i, *u: (base // step + i, 0), previous, "unpack_dn",
    )


def unpack_plane_gu_body(info, full, out):
    sides, unused, planes, blocks, size, cols = full.shape
    turns = blocks // 3
    columns = out.shape[1] // sides
    for side in range(sides):
        for half in range(2):
            first = jnp.bitwise_xor(half, info[0]) * turns
            for plane in range(planes):
                for turn in range(turns):
                    at = side * columns + ((half * planes + plane) * turns + turn) * cols
                    out[:, at : at + cols] = full[side, 0, plane, first + turn].astype(F32)


def unpack_plane_gu(info, full, total):
    levels, planes, blocks, size, unused = full.shape
    rows, step = (2 * size, 48)
    turns = size // step
    view = full.reshape((2, levels // 2) + full.shape[1:])
    return call(
        unpack_plane_gu_body,
        sds((rows, 2 * total * COLS), F32),
        (rows // step,),
        [
            pl.BlockSpec(
                (2, 1, planes, blocks, step, COLS), lambda r, *u: (0, r // turns, 0, 0, r % turns, 0)
            )
        ],
        pl.BlockSpec((step, 2 * total * COLS), lambda r, *u: (r, 0)),
        (info, view),
        moved=2 * rows * total * COLS * 6,
        name="unpack_plane_gu",
    )


def unpack_plane_dn_body(info, full, out):
    levels, unused, blocks, size, cols = full.shape
    for level in range(levels):
        for block in range(blocks):
            for part in range(size // 64):
                cut, row = divmod(level * size + part * 64, COLS)
                at = block * COLS + row
                out[at : at + 64, cut * COLS : (cut + 1) * COLS] = full[
                    level, 0, block, part * 64 : (part + 1) * 64
                ].astype(F32)


def unpack_plane_dn(info, full):
    levels, planes, blocks, size, unused = full.shape
    turns = blocks // 3
    width = levels * size
    return call(
        unpack_plane_dn_body,
        sds((planes * turns * COLS, width), F32),
        (planes,),
        [pl.BlockSpec((levels, 1, turns, size, COLS), lambda q, *u: (0, q, 2, 0, 0))],
        pl.BlockSpec((turns * COLS, width), lambda q, *u: (q, 0)),
        (info, full),
        moved=planes * turns * COLS * width * 6,
        name="unpack_plane_dn",
    )


def unpack_units_body(order, first, info, near, far, *outs):
    slots, unused, size = near.shape[:3]
    homes = [
        (out, block * COLS) for out in outs for block in range(out.shape[1] // COLS)
    ]
    for owner in range(2 * slots):
        side, turn = divmod(owner, slots)

        def write(source, side=side, turn=turn):
            for at in range(side, len(homes), 2):
                out, column = homes[at]
                out[turn * size : (turn + 1) * size, column : column + COLS] = source[
                    first + at // 2
                ].astype(F32)

        from_owner(info, order, near, far, owner, write)


def unpack_units(info, order, pair, first, widths):
    slots, unused, size, unused_too = pair[0].shape
    shapes = [sds((slots * size, w), F32) for w in widths]
    args = [info, *pair]
    return call(
        functools.partial(unpack_units_body, order, first),
        shapes,
        (1,),
        [whole(a.shape) for a in args[1:]],
        [whole(s.shape) for s in shapes],
        args,
        moved=sum(widths) * slots * size * 6,
        name="unpack_units",
    )


def plain_gu(own, other):
    blocks, width, cols = own.shape

    def rows(part):
        return part.reshape(blocks, 2, width // 2, cols).transpose(2, 1, 0, 3).reshape(width // 2, -1)

    return jnp.concatenate([rows(own), rows(other)], axis=0)


def plain_dn(own, other):
    blocks, width, cols = own.shape
    cuts = width // cols

    def rows(part):
        return (
            part.reshape(blocks, 16, cuts, width // (16 * cuts), cols)
            .transpose(0, 1, 3, 2, 4)
            .reshape(-1, width)
        )

    return jnp.concatenate([rows(own), rows(other)], axis=0)


def plain_units(own, other, widths):
    def unit(part, at):
        half = part.shape[1] // 2
        return part[at // 2, (at % 2) * half : (at % 2 + 1) * half]

    result, at = ([], 0)
    for columns in widths:
        count = columns // COLS
        result.append(
            jnp.concatenate(
                [
                    jnp.concatenate([unit(part, at + i) for i in range(count)], axis=1)
                    for part in (own, other)
                ],
                axis=0,
            )
        )
        at += count
    return result


def plain_sum(grads):
    parts = [lax.psum_scatter(g.astype(BF), "wsh", scatter_dimension=0, tiled=True) for g in grads]
    return tuple(g.astype(F32) for g in lax.psum(parts, "ctx"))


def per_device(
    tokens, cotangent, light_qkv, light_out, heavy_qkv, heavy_out, light_gu, light_down, heavy_gu, heavy_down,
    routers, gains, doc_starts, q_index, kv_index, ff_index,
):
    micros, unused, tok, width = tokens.shape
    count, groups = (lax.axis_size("ctx"), lax.axis_size("wsh"))
    direct = groups == 2 and count == 16
    place_ctx = lax.axis_index("ctx")
    side = lax.axis_index("wsh") if direct else 0
    base = place_ctx * tok
    info = jnp.concatenate(
        [
            jnp.stack([jnp.int32(side), base, jnp.int32(tok * count), place_ctx]).astype(jnp.int32),
            doc_starts[:, 0].reshape(-1),
        ]
    )
    swap = [(0, 1), (1, 0)]

    def pair_of(shard):
        if direct:
            return (shard, lax.ppermute(shard, "wsh", swap))
        full = lax.all_gather(shard, "wsh", axis=0, tiled=True)
        return (full[: full.shape[0] // 2], full[full.shape[0] // 2 :])

    def full_of(shard, axis=0):
        return lax.all_gather(shard, "wsh", axis=axis, tiled=True)

    vectors = jnp.concatenate([routers, gains, jnp.zeros((3, routers.shape[1]), BF)], axis=0)
    if direct:
        got = lax.ppermute(vectors, "wsh", swap)
        small = jnp.concatenate(
            [jnp.where(side == 0, vectors, got), jnp.where(side == 0, got, vectors)], axis=1
        )
    else:
        small = full_of(vectors, 1)
    x, up = (tokens[:, 0], cotangent[:, 0])
    index = jnp.stack([q_index[:, 0], kv_index[:, 0], ff_index[:, 0]])
    cols, rows = (index[..., None], index[:, :, None, :])
    hq_in, kin_pay, h1k, gate = routed_in(info, x, cols, small)
    l_own, l_got = pair_of(light_qkv)
    h_own, h_got = pair_of(heavy_qkv)
    o_own, o_got = pair_of(light_out)
    w_hout, w_hgu, w_hdown = (full_of(heavy_out), full_of(heavy_gu), full_of(heavy_down))
    w_lgu, w_ldown = (full_of(light_gu), full_of(light_down))
    kv_orders = ((8, 4, 1, 2), (8, 1, 2, 4))
    back_orders = [tuple(reversed(order)) for order in kv_orders]
    upward = [(i, i + 1) for i in range(count - 1)]
    downward = [(i + 1, i) for i in range(count - 1)]
    inner = light_qkv.shape[1] // 3
    every = range(micros)

    def rims(qkv):
        return (
            lax.ppermute(qkv[:, tok - WIN :, inner:], "ctx", upward),
            lax.ppermute(qkv[:, :WIN, inner:], "ctx", downward),
        )

    def project(kin):
        return key_project(info, kin, h_own, h_got)

    if direct:
        values = [kin_pay[m] for m in every]
        got = gather_start(values, back_orders, 0)
        qkv = light_in(info, x, small, l_own, l_got)
        got, qkv = tied(got, qkv)
        before, after = rims(qkv)
        values = gather_end(values, got)
        got = gather_start(values, back_orders, 1)
        q_pay = query_project(info, hq_in, h_own, h_got)
        got, q_pay, w_hout = tied(got, q_pay, w_hout)
        values = gather_end(values, got)
        got = gather_start(values, back_orders, 2)
        got, before, after = tied(got, before, after)
        values = gather_end(values, got)
        got = gather_start(values, back_orders, 3)
        near_kv = [project(v) for v in values]
        lo, light_lse = light_fwd(info, qkv, before, after)
        got, near_kv, lo, light_lse, w_hgu, w_hdown = tied(got, near_kv, lo, light_lse, w_hgu, w_hdown)
        kins = list(zip(values, got))
        kvs = [(n, project(f)) for n, f in zip(near_kv, got)]
    else:
        kins = []
        for m in every:
            full = lax.all_gather(kin_pay[m], "ctx", axis=0, tiled=True)
            kins.append((full[: full.shape[0] // 2], full[full.shape[0] // 2 :]))
        kvs = [tuple(project(k) for k in pair) for pair in kins]
        qkv = light_in(info, x, small, l_own, l_got)
        before, after = rims(qkv)
        lo, light_lse = light_fwd(info, qkv, before, after)
        q_pay = query_project(info, hq_in, h_own, h_got)
    heavy = [heavy_fwd(info, q_pay[m], kins[m], kvs[m]) for m in every]
    heavy, w_lgu, w_ldown = tied(heavy, w_lgu, w_ldown)
    ho = jnp.stack([h[0] for h in heavy])
    y, low2, pay, hy, gf = middle(info, x, up, cols, rows, small, gate, lo, o_own, o_got, ho, w_hout)

    def flat(value):
        return value.reshape(-1, value.shape[-1])

    orders = ((1, 2, 4, 8), (2, 4, 1, 8), (4, 1, 2, 8))
    if direct:
        mine = flat(pay)
        plane = [flipped(mine, bit) for bit in (1, 2, 3)]
        zh, dff = ffn_local(info, mine, w_hgu, w_hdown, 2 * COLS)
        plane, zh, dff = tied(plane, zh, dff)
        near = jnp.concatenate([mine, *plane], axis=0)
        far = lax.ppermute(near, "wsh", swap)
    else:
        zh, dff, hgu_own, hgu_send, hdn_own, hdn_send = ffn(
            info, flat(pay[..., :width]), flat(pay[..., width:]), w_hgu, w_hdown
        )
    z, dh2, lgu_own, lgu_send, ldn_own, ldn_send = ffn_all(info, flat(low2), flat(up), w_lgu, w_ldown)
    if direct:
        far, z, dh2 = tied(far, z, dh2)
        lgu_got, ldn_got = (lax.ppermute(part, "wsh", swap) for part in (lgu_send, ldn_send))
        plane_own, plane_send, plane_dn = plane_grads(info, near, far, w_hgu, w_hdown)
        plane_got = lax.ppermute(plane_send, "wsh", swap)
        keep, send = column_fold(info, (1, 2), (plane_own, plane_got, plane_dn))
        got = flipped(send, 4)

    def by_micro(value):
        return value.reshape(micros, -1, value.shape[-1])

    out_tokens, dy, dlo, dho, dhy, dsq, part_two = mid_back(
        info, y, up, by_micro(z), by_micro(dh2), by_micro(zh), by_micro(dff), pay, gf, cols, rows, small, gate, o_own,
        o_got, w_hout, hy, hq_in,
    )
    backs = [
        heavy_bwd(info, q_pay[m], kins[m], kvs[m], heavy[m][1], dho[m], h_own, h_got) for m in every
    ]
    dhq = jnp.stack([b[0] for b in backs])
    shape = (count // 2, q_index.shape[2], width)
    back = [tuple(part.reshape(shape) for part in b[3:5]) for b in backs]
    dkvs = [part for b in backs for part in b[1:3]]
    if direct:
        got, back, dlo, dkvs = tied(got, back, dlo, dkvs)
        keep, send = scatter_step(keep, got)
        got = flipped(send, 8)
        got_back = scatter_start(back, back_orders, 0)
    dlq, dl_own, rim_low, rim_high = light_bwd(info, qkv, before, after, light_lse, dlo)
    if direct:
        got, got_back, dlq, dl_own, rim_low, rim_high = tied(got, got_back, dlq, dl_own, rim_low, rim_high)
        keep, send = scatter_step(keep, got)
        plane_full = lax.all_gather(keep[0], "ctx", axis=0, tiled=False)
        plane_full = plane_full.reshape((count // 4, 4) + plane_full.shape[1:])
    got_low = lax.ppermute(rim_high, "ctx", upward)
    got_high = lax.ppermute(rim_low, "ctx", downward)
    kin_all = [part for pair in kins for part in pair]
    if direct:
        back = scatter_end(back, got_back)
        got_back = scatter_start(back, back_orders, 1)
    ha_own, ha_send = heavy_grads(info, hq_in, dhq, ho, dhy, lo, dy, kin_all, dkvs)
    if direct:
        got_back, got_low, got_high, ha_own, ha_send = tied(got_back, got_low, got_high, ha_own, ha_send)
        back = scatter_end(back, got_back)
        got_back = scatter_start(back, back_orders, 2)
        ha_got = lax.ppermute(ha_send, "wsh", swap)
    dl, la_own, la_send = light_join(info, x, small, dlq, dl_own, got_low, got_high)
    if direct:
        la_got = lax.ppermute(la_send, "wsh", swap)
        second = [
            fold(info, orders[0], [(ha_own, ha_got, 0, 6)]),
            fold(info, orders[1], [(lgu_own, lgu_got, 0, 4), (ha_own, ha_got, 6, 1)]),
            fold(info, orders[2], [(la_own, la_got, 0, 3), (ldn_own, ldn_got, 0, 2)]),
        ]
        got_back, second, dl = tied(got_back, second, dl)
        got_two = scatter_start(second, orders, 0)
        back = scatter_end(back, got_back)
        got_back = scatter_start(back, back_orders, 3)
        got_two, got_back = tied(got_two, got_back)
        second, back = (scatter_end(second, got_two), scatter_end(back, got_back))
        got_two = scatter_start(second, orders, 1)
        dkin = jnp.concatenate([keep for keep, send in back], axis=0)
    else:
        dkin = jnp.stack(
            [
                lax.psum_scatter(jnp.concatenate(b[3:5], axis=0), "ctx", scatter_dimension=0, tiled=True)
                for b in backs
            ]
        )
    grad_tokens, part_one = in_back(
        info, x, dy, dl, dhq, dkin, dsq, rows, small, gate, h1k, l_own, l_got, h_own, h_got
    )
    widths = (heavy_qkv.shape[1], heavy_out.shape[1])
    vector = part_one + part_two
    if direct:
        half = width // 2
        mine = lax.dynamic_slice_in_dim(vector, side * half, half, 1)
        given = lax.dynamic_slice_in_dim(vector, (1 - side) * half, half, 1)
        got_two, mine, given = tied(got_two, mine, given)
        second = scatter_end(second, got_two)
        got_two = scatter_start(second, orders, 2)
        vector = mine + lax.ppermute(given, "wsh", swap)
        got_two, vector = tied(got_two, vector)
        second = scatter_end(second, got_two)
        got_two, got_vector = (scatter_start(second, orders, 3), flipped(vector, 1))
        got_two, vector, got_vector = tied(got_two, vector, got_vector)
        second, vector = (scatter_end(second, got_two), vector + got_vector)
        tails = [keep for keep, send in second]
        got_two, got_vector = (gather_start(tails, orders, 0), flipped(vector, 2))
        got_two, vector, got_vector = tied(got_two, vector, got_vector)
        tails, vector = (gather_end(tails, got_two), vector + got_vector)
        got_two, got_vector = (gather_start(tails, orders, 1), flipped(vector, 4))
        got_two, vector, got_vector = tied(got_two, vector, got_vector)
        tails, vector = (gather_end(tails, got_two), vector + got_vector)
        got_two, got_vector = (gather_start(tails, orders, 2), flipped(vector, 8))
        g_hdown = unpack_plane_dn(info, plane_full)
        got_two, vector, got_vector, g_hdown, plane_full = tied(got_two, vector, got_vector, g_hdown, plane_full)
        tails, vector = (gather_end(tails, got_two), vector + got_vector)
        got_two = gather_start(tails, orders, 3)
        g_hgu = unpack_plane_gu(info, plane_full, heavy_gu.shape[1] // (2 * COLS))
        got_two, g_hgu = tied(got_two, g_hgu)
        sums = list(zip(tails, got_two))
        g_hqkv, g_hout = unpack_units(info, orders[0], sums[0], 0, widths)
        g_lgu = unpack_gu(info, orders[1], sums[1], 0, 4, 4, 0, None, 4)
        g_lout = unpack_dn(info, orders[1], sums[1], 4, 1, 1, 0, None, 1)
        (g_lqkv,) = unpack_units(info, orders[2], sums[2], 0, (light_qkv.shape[1],))
        g_ldown = unpack_dn(info, orders[2], sums[2], 3, 2, 2, 0, None, 1)
    else:
        g_hqkv, g_hout = plain_units(ha_own, ha_send, widths)
        (g_lqkv,) = plain_units(la_own, la_send, (light_qkv.shape[1],))
        last = slice(ha_own.shape[0] - 1, ha_own.shape[0])
        g_lqkv, g_lout, g_hqkv, g_hout, g_lgu, g_ldown, g_hgu, g_hdown = plain_sum(
            [
                g_lqkv,
                plain_dn(ha_own[last], ha_send[last]),
                g_hqkv,
                g_hout,
                plain_gu(lgu_own, lgu_send),
                plain_dn(ldn_own, ldn_send),
                plain_gu(hgu_own, hgu_send),
                plain_dn(hdn_own, hdn_send),
            ]
        )
        vector = lax.psum(vector, ("ctx", "wsh"))
        part = width // groups
        vector = lax.dynamic_slice_in_dim(vector, lax.axis_index("wsh") * part, part, 1)
    return (
        out_tokens[:, None],
        grad_tokens[:, None],
        g_lqkv,
        g_lout,
        g_hqkv,
        g_hout,
        g_lgu,
        g_ldown,
        g_hgu,
        g_hdown,
        vector[:3],
        vector[3:5],
    )


def solution(mesh):
    return jax.shard_map(
        per_device,
        mesh=mesh,
        in_specs=(
            P(None, "wsh", "ctx", None),
            P(None, "wsh", "ctx", None),
            P("wsh", None),
            P("wsh", None),
            P("wsh", None),
            P("wsh", None),
            P("wsh", None),
            P("wsh", None),
            P("wsh", None),
            P("wsh", None),
            P(None, "wsh"),
            P(None, "wsh"),
            P(None, "wsh", None),
            P(None, "wsh", "ctx"),
            P(None, "wsh", "ctx"),
            P(None, "wsh", "ctx"),
        ),
        out_specs=(
            P(None, "wsh", "ctx", None),
            P(None, "wsh", "ctx", None),
            P("wsh", None),
            P("wsh", None),
            P("wsh", None),
            P("wsh", None),
            P("wsh", None),
            P("wsh", None),
            P("wsh", None),
            P("wsh", None),
            P(None, "wsh"),
            P(None, "wsh"),
        ),
        check_vma=False,
    )
```

```python
import functools

import jax
import jax.numpy as jnp
from jax import lax
from jax.experimental import pallas as pl
from jax.experimental.pallas import tpu as pltpu
from jax.sharding import PartitionSpec as P

HD = 64
WIN = 128
LANES = 128
COLS = 256
FAR = -1e30
EPS = 1e-06
BF = jnp.bfloat16
F32 = jnp.float32


def mm(left, right):
    return lax.dot_general(left, right, (((1,), (0,)), ((), ())), preferred_element_type=F32)


def mm_t(left, right):
    return lax.dot_general(left, right, (((1,), (1,)), ((), ())), preferred_element_type=F32)


def t_mm(left, right):
    return lax.dot_general(left, right, (((0,), (0,)), ((), ())), preferred_element_type=F32)


def pick(onehot, values):
    high = values.astype(BF)
    low = (values - high.astype(F32)).astype(BF)
    return mm(onehot, high) + mm(onehot, low)


def iota(shape, dim):
    return lax.broadcasted_iota(jnp.int32, shape, dim)


def onehot_cols(positions, base, length):
    return (iota((positions.shape[0], length), 1) == positions - base).astype(F32).astype(BF)


def onehot_rows(positions, base, length):
    return (iota((length, positions.shape[1]), 0) == positions - base).astype(F32).astype(BF)


def segment(info, micro, positions):
    total = jnp.full(positions.shape, -1, jnp.int32)
    for start in range(5):
        total += (positions >= info[4 + micro * 5 + start]).astype(jnp.int32)
    return total


def inverse_rms(values):
    return lax.rsqrt(jnp.mean(values * values, axis=-1, keepdims=True) + EPS)


def halves(info, values):
    half = values.shape[1] // 2
    first, second = (values[:, :half], values[:, half:])
    lower = info[0] == 0
    return (jnp.where(lower, first, second), jnp.where(lower, second, first))


def unhalved(info, own, other):
    lower = info[0] == 0
    return jnp.concatenate([jnp.where(lower, own, other), jnp.where(lower, other, own)], axis=1)


def call(body, outs, grid, in_specs, out_specs, args, scratch=(), flops=0, moved=0, limit=48, name=None):
    return pl.pallas_call(
        body,
        name=name or getattr(body, "__name__", "kernel"),
        out_shape=outs,
        grid_spec=pltpu.PrefetchScalarGridSpec(
            num_scalar_prefetch=1,
            grid=grid,
            in_specs=in_specs,
            out_specs=out_specs,
            scratch_shapes=list(scratch),
        ),
        compiler_params=pltpu.CompilerParams(vmem_limit_bytes=limit * 1024 * 1024),
        cost_estimate=pl.CostEstimate(flops=flops, bytes_accessed=moved, transcendentals=0),
    )(*args)


def whole(shape):
    rank = len(shape)
    return pl.BlockSpec(tuple(shape), lambda *unused: (0,) * rank)


def one_of(shape):
    rank = len(shape)
    return pl.BlockSpec((1,) + tuple(shape[1:]), lambda i, *unused: (i,) + (0,) * (rank - 1))


def sds(shape, dtype):
    return jax.ShapeDtypeStruct(tuple(shape), dtype)


def routed_body(info, x, cols, small, q_out, kin_out, h1k_out, gate_out):
    micros, tok, width = x.shape
    rows = cols.shape[2]
    base = info[1]
    gain = small[3:4].astype(F32)
    lane = iota((rows, LANES), 1)
    for m in range(micros):
        both = jnp.concatenate([cols[0, m], cols[1, m]], axis=0)
        got = mm(onehot_cols(both, base, tok), x[m])
        xq, xk = (got[:rows], got[rows:])
        low_q = (xq * inverse_rms(xq) * gain).astype(BF)
        h1k = xk * inverse_rms(xk) * gain
        low_k = h1k.astype(BF)
        gate_q = jax.nn.sigmoid(
            jnp.sum(low_q.astype(F32) * small[0:1].astype(F32), axis=-1, keepdims=True)
        )
        gate_k = jax.nn.sigmoid(
            jnp.sum(low_k.astype(F32) * small[1:2].astype(F32), axis=-1, keepdims=True)
        )
        seg_q = segment(info, m, cols[0, m])
        seg_k = segment(info, m, cols[1, m])
        q_out[m, :, :width] = low_q
        q_out[m, :, width:] = (lane == seg_q).astype(F32).astype(BF)
        kin_out[m, :, :width] = (h1k * gate_k).astype(BF)
        kin_out[m, :, width:] = jnp.where((lane < 8) & (lane != seg_k), FAR, 0.0).astype(BF)
        h1k_out[m] = h1k
        gate_out[m] = jnp.where(lane == 0, gate_q, gate_k)


def routed_in(info, x, cols, small):
    micros, unused, width = x.shape
    rows = cols.shape[2]
    shapes = [
        sds((micros, rows, width + LANES), BF),
        sds((micros, rows, width + LANES), BF),
        sds((micros, rows, width), F32),
        sds((micros, rows, LANES), F32),
    ]
    args = (info, x, cols, small)
    return call(
        routed_body,
        shapes,
        (1,),
        [whole(a.shape) for a in args[1:]],
        [whole(s.shape) for s in shapes],
        args,
        flops=200_000_000,
        moved=3_000_000,
    )


def query_body(info, low, w_own, w_got, out):
    width = 2 * w_own.shape[0]
    for m in range(low.shape[0]):
        own, other = halves(info, low[m, :, :width])
        out[m, :, :width] = (mm(own, w_own[...]) + mm(other, w_got[...])).astype(BF)
        out[m, :, width:] = low[m, :, width:]


def query_project(info, low, w_own, w_got):
    half = w_own.shape[0]
    return call(
        query_body,
        sds(low.shape, BF),
        (1,),
        [whole(low.shape)] + [whole((half, 2 * half))] * 2,
        whole(low.shape),
        (info, low, w_own, w_got),
        flops=2 * low.shape[0] * low.shape[1] * 4 * half * half,
        moved=2_000_000,
    )


def light_in_body(info, x, small, w_own, w_got, out):
    values = x[0].astype(F32)
    low = (values * inverse_rms(values) * small[3:4].astype(F32)).astype(BF)
    own, other = halves(info, low)
    out[0] = (mm(own, w_own[...]) + mm(other, w_got[...])).astype(BF)


def light_in(info, x, small, w_own, w_got):
    micros, tok, width = x.shape
    columns = w_own.shape[1]
    split = 2
    rows = tok // split
    spec = lambda n: pl.BlockSpec((1, rows, n), lambda i, *u: (i // split, i % split, 0))
    return call(
        light_in_body,
        sds((micros, tok, columns), BF),
        (micros * split,),
        [spec(width), whole(small.shape), whole(w_own.shape), whole(w_got.shape)],
        spec(columns),
        (info, x, small, w_own, w_got),
        flops=2 * micros * tok * width * columns,
        moved=8_000_000,
    )


def fill_near(near, qkv, before, after):
    tok = qkv.shape[1]
    inner = near.shape[1] // 2
    near[:WIN] = before[0]
    near[WIN : WIN + tok] = qkv[0, :, inner:]
    near[WIN + tok :] = after[0]


def light_bias(info, micro, block):
    start = info[1] + block * WIN
    rows, columns = (WIN, 3 * WIN)
    row_pos = start + iota((rows, 1), 0)
    col_pos = start - WIN + iota((1, columns), 1)
    seg_row = segment(info, micro, row_pos)
    seg_col = jnp.where((col_pos >= 0) & (col_pos < info[2]), segment(info, micro, col_pos), -1)
    shift = iota((rows, columns), 0) + WIN - iota((rows, columns), 1)
    allowed = (jnp.abs(shift) < WIN) & (seg_row == seg_col)
    bias = jnp.where(allowed, 0.0, FAR)
    return jnp.concatenate([bias, bias], axis=0)


def stacked(pair, low_lane):
    zero = jnp.zeros_like(pair)
    return jnp.concatenate(
        [jnp.where(low_lane, pair, zero), jnp.where(low_lane, zero, pair)], axis=0
    )


def merged(values, low_lane):
    rows = values.shape[0] // 2
    return jnp.where(low_lane, values[:rows], values[rows:])


def light_fwd_blocks(info, qkv, near, blocks, emit):
    micro = pl.program_id(0)
    inner = near.shape[1] // 2
    low_lane = iota((WIN, LANES), 1) < HD
    lane = iota((WIN, LANES), 1)
    for place, block in enumerate(blocks):
        at = slice(block * WIN, (block + 1) * WIN)
        around = slice(block * WIN, (block + 3) * WIN)
        bias = light_bias(info, micro, block)
        stats = jnp.zeros((WIN, LANES), F32)
        for pair in range(inner // LANES):
            cut = slice(pair * LANES, (pair + 1) * LANES)
            query = stacked(qkv[0, at, cut] * BF(HD**-0.5), low_lane)
            scores = mm_t(query, near[around, cut]) + bias
            top = jnp.max(scores, axis=-1, keepdims=True)
            weights = jnp.exp(scores - top)
            total = jnp.sum(weights, axis=-1, keepdims=True)
            value = near[around, inner + pair * LANES : inner + (pair + 1) * LANES]
            mixed = mm((weights * (1.0 / total)).astype(BF), value)
            emit(place, cut, merged(mixed, low_lane).astype(BF))
            lse = top + jnp.log(total)
            stats = jnp.where(lane == 2 * pair, lse[:WIN], stats)
            stats = jnp.where(lane == 2 * pair + 1, lse[WIN:], stats)
        emit(place, None, stats)


def light_inner_body(info, qkv, out, lse_out, near):
    tok = qkv.shape[1]
    inner = out.shape[2]
    near[WIN : WIN + tok] = qkv[0, :, inner:]

    def emit(place, cut, value):
        rows = slice(place * WIN, (place + 1) * WIN)
        if cut is None:
            lse_out[0, rows] = value
        else:
            out[0, rows, cut] = value

    light_fwd_blocks(info, qkv, near, range(1, tok // WIN - 1), emit)


def light_outer_body(info, qkv, before, after, done, lse_done, out, lse_out, near):
    tok = qkv.shape[1]
    fill_near(near, qkv, before, after)
    out[0, WIN : tok - WIN] = done[0]
    lse_out[0, WIN : tok - WIN] = lse_done[0]
    blocks = (0, tok // WIN - 1)

    def emit(place, cut, value):
        rows = slice(blocks[place] * WIN, (blocks[place] + 1) * WIN)
        if cut is None:
            lse_out[0, rows] = value
        else:
            out[0, rows, cut] = value

    light_fwd_blocks(info, qkv, near, blocks, emit)


def light_inner(info, qkv):
    micros, tok, columns = qkv.shape
    inner = columns // 3
    shapes = [sds((micros, tok - 2 * WIN, inner), BF), sds((micros, tok - 2 * WIN, LANES), F32)]
    return call(
        light_inner_body,
        shapes,
        (micros,),
        [one_of(qkv.shape)],
        [one_of(a.shape) for a in shapes],
        (info, qkv),
        scratch=[pltpu.VMEM((tok + 2 * WIN, 2 * inner), BF)],
        flops=2_000_000_000,
        moved=4_000_000,
    )


def light_outer(info, qkv, before, after, done):
    micros, tok, columns = qkv.shape
    inner = columns // 3
    shapes = [sds((micros, tok, inner), BF), sds((micros, tok, LANES), F32)]
    args = (info, qkv, before, after, *done)
    return call(
        light_outer_body,
        shapes,
        (micros,),
        [one_of(a.shape) for a in args[1:]],
        [one_of(a.shape) for a in shapes],
        args,
        scratch=[pltpu.VMEM((tok + 2 * WIN, 2 * inner), BF)],
        flops=2_000_000_000,
        moved=6_000_000,
    )


def light_bwd_blocks(info, qkv, lse, grad, near, dk, dv, blocks, emit):
    micro = pl.program_id(0)
    inner = grad.shape[2]
    low_lane = iota((WIN, LANES), 1) < HD
    for place, block in enumerate(blocks):
        at = slice(block * WIN, (block + 1) * WIN)
        around = slice(block * WIN, (block + 3) * WIN)
        bias = light_bias(info, micro, block)
        stats = lse[0, at, :]
        for pair in range(inner // LANES):
            cut = slice(pair * LANES, (pair + 1) * LANES)
            query = stacked(qkv[0, at, cut] * BF(HD**-0.5), low_lane)
            key = near[around, cut]
            value = near[around, inner + pair * LANES : inner + (pair + 1) * LANES]
            shift = jnp.concatenate(
                [stats[:, 2 * pair : 2 * pair + 1], stats[:, 2 * pair + 1 : 2 * pair + 2]], axis=0
            )
            probs = jnp.exp(mm_t(query, key) + bias - shift)
            upper = stacked(grad[0, at, cut], low_lane)
            grad_probs = mm_t(upper, value)
            center = jnp.sum(probs * grad_probs, axis=-1, keepdims=True)
            slope = (probs * (grad_probs - center)).astype(BF)
            emit(place, cut, (merged(mm(slope, key), low_lane) * HD**-0.5).astype(BF))
            dk[around, cut] += t_mm(slope, query)
            dv[around, cut] += t_mm(probs.astype(BF), upper)


def light_bwd_outer_body(info, qkv, before, after, lse, grad, dq_out, own_out, low_out, high_out, near, dk, dv):
    tok = qkv.shape[1]
    inner = grad.shape[2]
    fill_near(near, qkv, before, after)
    dk[...] = jnp.zeros_like(dk)
    dv[...] = jnp.zeros_like(dv)

    def emit(place, cut, value):
        dq_out[0, place * WIN : (place + 1) * WIN, cut] = value

    light_bwd_blocks(info, qkv, lse, grad, near, dk, dv, (0, tok // WIN - 1), emit)
    for first, source in ((0, dk), (inner, dv)):
        to = slice(first, first + inner)
        own_out[0, :, to] = source[WIN : WIN + tok]
        low_out[0, :, to] = source[:WIN].astype(BF)
        high_out[0, :, to] = source[WIN + tok :].astype(BF)


def light_bwd_inner_body(info, qkv, lse, grad, dq_in, own_in, dq_out, own_out, near, dk, dv):
    tok = qkv.shape[1]
    inner = grad.shape[2]
    near[WIN : WIN + tok] = qkv[0, :, inner:]
    dk[WIN : WIN + tok] = own_in[0, :, :inner]
    dv[WIN : WIN + tok] = own_in[0, :, inner:]
    dq_out[0, :WIN] = dq_in[0, :WIN]
    dq_out[0, tok - WIN :] = dq_in[0, WIN:]
    blocks = range(1, tok // WIN - 1)

    def emit(place, cut, value):
        dq_out[0, blocks[place] * WIN : (blocks[place] + 1) * WIN, cut] = value

    light_bwd_blocks(info, qkv, lse, grad, near, dk, dv, blocks, emit)
    own_out[0, :, :inner] = dk[WIN : WIN + tok]
    own_out[0, :, inner:] = dv[WIN : WIN + tok]


def light_bwd_scratch(tok, inner):
    return [
        pltpu.VMEM((tok + 2 * WIN, 2 * inner), BF),
        pltpu.VMEM((tok + 2 * WIN, inner), F32),
        pltpu.VMEM((tok + 2 * WIN, inner), F32),
    ]


def light_bwd_outer(info, qkv, before, after, lse, grad):
    micros, tok, columns = qkv.shape
    inner = columns // 3
    shapes = [
        sds((micros, 2 * WIN, inner), BF),
        sds((micros, tok, 2 * inner), F32),
        sds((micros, WIN, 2 * inner), BF),
        sds((micros, WIN, 2 * inner), BF),
    ]
    args = (info, qkv, before, after, lse, grad)
    return call(
        light_bwd_outer_body,
        shapes,
        (micros,),
        [one_of(a.shape) for a in args[1:]],
        [one_of(a.shape) for a in shapes],
        args,
        scratch=light_bwd_scratch(tok, inner),
        flops=5_000_000_000,
        moved=12_000_000,
    )


def light_bwd_inner(info, qkv, lse, grad, dq, own):
    micros, tok, columns = qkv.shape
    inner = columns // 3
    shapes = [sds((micros, tok, inner), BF), sds((micros, tok, 2 * inner), F32)]
    args = (info, qkv, lse, grad, dq, own)
    return call(
        light_bwd_inner_body,
        shapes,
        (micros,),
        [one_of(a.shape) for a in args[1:]],
        [one_of(a.shape) for a in shapes],
        args,
        scratch=light_bwd_scratch(tok, inner),
        flops=5_000_000_000,
        moved=14_000_000,
    )


def key_body(info, kin, w_own, w_got, out):
    half = w_own.shape[0]
    width = 2 * half
    own = kin[:, pl.ds(pl.multiple_of(info[0] * half, half), half)]
    other = kin[:, pl.ds(pl.multiple_of((1 - info[0]) * half, half), half)]
    out[...] = (mm(own, w_own[:, width:]) + mm(other, w_got[:, width:])).astype(BF)


def key_project(info, kin, w_own, w_got):
    shape = sds((kin.shape[0], 2 * (kin.shape[1] - LANES)), BF)
    args = (info, kin, w_own, w_got)
    return call(
        key_body,
        shape,
        (1,),
        [whole(a.shape) for a in args[1:]],
        whole(shape.shape),
        args,
        flops=1_200_000_000,
        moved=6_000_000,
    )


def heavy_scores(query, parts, bias, cut):
    return [mm_t(query, part[:, cut]) + b for part, b in zip(parts, bias)]


def heavy_fwd_body(info, q, kin_a, kin_b, kv_a, kv_b, out, lse_out):
    rows, width = out.shape
    parts = (kv_a, kv_b)
    low_lane = iota((rows, LANES), 1) < HD
    lane = iota((rows, LANES), 1)
    feature = jnp.concatenate([q[:, width:]] * 2, axis=0)
    bias = [mm_t(feature, kin[:, width:]) for kin in (kin_a, kin_b)]
    stats = jnp.zeros((rows, LANES), F32)
    for pair in range(width // LANES):
        cut = slice(pair * LANES, (pair + 1) * LANES)
        query = stacked(q[:, cut] * BF(HD**-0.5), low_lane)
        scores = heavy_scores(query, parts, bias, cut)
        top = functools.reduce(
            jnp.maximum, [jnp.max(s, axis=-1, keepdims=True) for s in scores]
        )
        weights = [jnp.exp(s - top) for s in scores]
        total = sum(jnp.sum(w, axis=-1, keepdims=True) for w in weights)
        scale = 1.0 / total
        mixed = sum(
            mm((w * scale).astype(BF), part[:, width + pair * LANES : width + (pair + 1) * LANES])
            for w, part in zip(weights, parts)
        )
        out[:, cut] = merged(mixed, low_lane).astype(BF)
        lse = top + jnp.log(total)
        stats = jnp.where(lane == 2 * pair, lse[:rows], stats)
        stats = jnp.where(lane == 2 * pair + 1, lse[rows:], stats)
    lse_out[...] = stats


def heavy_fwd(info, q, kins, kvs):
    rows = q.shape[0]
    width = q.shape[1] - LANES
    shapes = [sds((rows, width), BF), sds((rows, LANES), F32)]
    args = (info, q, *kins, *kvs)
    return call(
        heavy_fwd_body,
        shapes,
        (1,),
        [whole(a.shape) for a in args[1:]],
        [whole(s.shape) for s in shapes],
        args,
        flops=1_500_000_000,
        moved=5_000_000,
    )


def heavy_bwd_body(info, q, kin_a, kin_b, kv_a, kv_b, lse, grad, w_own, w_got, dq_out, da_out, db_out, ia_out, ib_out):
    rows, width = grad.shape
    parts = (kv_a, kv_b)
    low_lane = iota((rows, LANES), 1) < HD
    feature = jnp.concatenate([q[:, width:]] * 2, axis=0)
    bias = [mm_t(feature, kin[:, width:]) for kin in (kin_a, kin_b)]
    for pair in range(width // LANES):
        cut = slice(pair * LANES, (pair + 1) * LANES)
        upcut = slice(width + pair * LANES, width + (pair + 1) * LANES)
        query = stacked(q[:, cut] * BF(HD**-0.5), low_lane)
        shift = jnp.concatenate(
            [lse[:, 2 * pair : 2 * pair + 1], lse[:, 2 * pair + 1 : 2 * pair + 2]], axis=0
        )
        probs = [jnp.exp(s - shift) for s in heavy_scores(query, parts, bias, cut)]
        upper = stacked(grad[:, cut], low_lane)
        grads = [mm_t(upper, part[:, upcut]) for part in parts]
        center = sum(jnp.sum(p * g, axis=-1, keepdims=True) for p, g in zip(probs, grads))
        slopes = [(p * (g - center)).astype(BF) for p, g in zip(probs, grads)]
        dq = sum(mm(s, part[:, cut]) for s, part in zip(slopes, parts))
        dq_out[:, cut] = (merged(dq, low_lane) * HD**-0.5).astype(BF)
        for target, slope, prob in zip((da_out, db_out), slopes, probs):
            target[:, cut] = t_mm(slope, query).astype(BF)
            target[:, upcut] = t_mm(prob.astype(BF), upper).astype(BF)
    half = width // 2
    for target, source in ((ia_out, da_out), (ib_out, db_out)):
        for weight, side in ((w_own, info[0]), (w_got, 1 - info[0])):
            target[:, pl.ds(pl.multiple_of(side * half, half), half)] = mm_t(
                source[...], weight[:, width:]
            ).astype(BF)


def heavy_bwd(info, q, kins, kvs, lse, grad, w_own, w_got):
    rows = q.shape[0]
    width = q.shape[1] - LANES
    keys = kvs[0].shape[0]
    shapes = [sds((rows, width), BF)] + [sds((keys, 2 * width), BF)] * 2 + [sds((keys, width), BF)] * 2
    args = (info, q, *kins, *kvs, lse, grad, w_own, w_got)
    return call(
        heavy_bwd_body,
        shapes,
        (1,),
        [whole(a.shape) for a in args[1:]],
        [whole(s.shape) for s in shapes],
        args,
        flops=6_500_000_000,
        moved=15_000_000,
    )


def heavy_grads_body(info, *refs):
    micros = (len(refs) - 8) // 4
    hq, dhq, ho, dhy, lo, dy = refs[:6]
    kins, dkvs = (refs[6 : 6 + 2 * micros], refs[6 + 2 * micros : -2])
    other_out, own_out = (refs[-1], refs[-2])
    half = hq.shape[2] // 2
    every = range(micros)
    for target, side in ((other_out, 1 - info[0]), (own_out, info[0])):
        cut = pl.ds(pl.multiple_of(side * half, half), half)

        def put(unit, left, right, columns):
            for block in range(columns // COLS):
                at = unit + block
                total = sum(
                    t_mm(a, b[:, block * COLS : (block + 1) * COLS]) for a, b in zip(left, right)
                )
                target[at // 2, (at % 2) * half : (at % 2 + 1) * half] = total.astype(BF)
            return unit + columns // COLS

        unit = put(0, [hq[m, :, cut] for m in every], [dhq[m] for m in every], dhq.shape[2])
        unit = put(unit, [kin[:, cut] for kin in kins], dkvs, dkvs[0].shape[1])
        unit = put(unit, [ho[m, :, cut] for m in every], [dhy[m] for m in every], dhy.shape[2])
        part = lo.shape[2] // 2
        small_cut = pl.ds(pl.multiple_of(side * part, part), part)
        total = sum(t_mm(lo[m, :, small_cut], dy[m].astype(BF)) for m in every)
        pack_rows(target.at[pl.ds(unit // 2, 1)], total)


def heavy_grads(info, hq, dhq, ho, dhy, lo, dy, kins, dkvs):
    width = dhq.shape[2]
    units = (dhq.shape[2] + dkvs[0].shape[1] + dhy.shape[2]) // COLS
    shapes = [sds((units // 2 + 1, width, COLS), BF)] * 2
    args = (info, hq, dhq, ho, dhy, lo, dy, *kins, *dkvs)
    return call(
        heavy_grads_body,
        shapes,
        (1,),
        [whole(dhq.shape)] + [whole(a.shape) for a in args[2:]],
        [whole(s.shape) for s in shapes],
        args,
        flops=6_500_000_000,
        moved=28_000_000,
    )


def middle_body(info, x, up, cols, rows, small, gate, lo, lout, lout_got, ho, hout, y_out, low_out, pay_out, hy_out, gf_out):
    tok = x.shape[1]
    base = info[1]
    hy = mm(ho[0], hout[...])
    hy_out[0] = hy
    spread = onehot_rows(rows[0, 0], base, tok)
    part = lout.shape[0]
    own = lo[0, :, pl.ds(pl.multiple_of(info[0] * part, part), part)]
    other = lo[0, :, pl.ds(pl.multiple_of((1 - info[0]) * part, part), part)]
    light = mm(own, lout[...]) + mm(other, lout_got[...])
    y = x[0].astype(F32) + light + pick(spread, hy * gate[0, :, 0:1])
    y_out[0] = y
    low = (y * inverse_rms(y) * small[4:5].astype(F32)).astype(BF)
    low_out[0] = low
    take = onehot_cols(cols[2, 0], base, tok)
    taken = mm(take, low)
    width = x.shape[2]
    pay_out[0, :, :width] = taken.astype(BF)
    gf = jax.nn.sigmoid(jnp.sum(taken * small[2:3].astype(F32), axis=-1, keepdims=True))
    pay_out[0, :, width:] = (mm(take, up[0]) * gf).astype(BF)
    gf_out[0] = jnp.broadcast_to(gf, gf_out.shape[1:])


def second_of(shape):
    rank = len(shape)
    return pl.BlockSpec(
        (shape[0], 1) + tuple(shape[2:]), lambda i, *unused: (0, i) + (0,) * (rank - 2)
    )


def middle(info, x, up, cols, rows, small, gate, lo, lout, lout_got, ho, hout):
    micros, tok, width = x.shape
    count = cols.shape[2]
    shapes = [
        sds((micros, tok, width), F32),
        sds((micros, tok, width), BF),
        sds((micros, count, 2 * width), BF),
        sds((micros, count, width), F32),
        sds((micros, count, LANES), F32),
    ]
    args = (info, x, up, cols, rows, small, gate, lo, lout, lout_got, ho, hout)
    return call(
        middle_body,
        shapes,
        (micros,),
        [
            one_of(x.shape),
            one_of(up.shape),
            second_of(cols.shape),
            second_of(rows.shape),
            whole(small.shape),
            one_of(gate.shape),
            one_of(lo.shape),
            whole(lout.shape),
            whole(lout_got.shape),
            one_of(ho.shape),
            whole(hout.shape),
        ],
        [one_of(s.shape) for s in shapes],
        args,
        flops=2_000_000_000,
        moved=12_000_000,
    )


def pack_rows(target, values):
    step = values.shape[0] // 16
    cuts = values.shape[1] // COLS
    for slot in range(16):
        for cut in range(cuts):
            at = slot * step * cuts + cut * step
            target[0, at : at + step] = values[
                slot * step : (slot + 1) * step, cut * COLS : (cut + 1) * COLS
            ].astype(BF)


def gelu_parts(g):
    root = (2.0 / 3.141592653589793) ** 0.5
    square = g * g
    tanh = jnp.tanh(root * g * (1.0 + 0.044715 * square))
    bell = 0.5 * (1.0 + tanh)
    slope = bell + 0.5 * g * (1.0 - tanh * tanh) * (root * (1.0 + 3 * 0.044715 * square))
    return (g * bell, slope)


def hidden_both_ways(low, upstream, wg, wu, wd):
    g, u = (mm(low, wg), mm(low, wu))
    back = mm_t(upstream, wd)
    gelu, slope = gelu_parts(g)
    return ((gelu * u).astype(BF), (back * u * slope).astype(BF), (back * gelu).astype(BF))


def add_steps(step, pairs):
    @pl.when(step == 0)
    def first():
        for target, value in pairs:
            target[...] = value

    @pl.when(step > 0)
    def later():
        for target, value in pairs:
            target[...] += value


def ffn_local_body(info, a, ct, wg, wu, wd, z_out, dh_out):
    hidden, dg, du = hidden_both_ways(a[...], ct[...], wg[...], wu[...], wd[...])
    z = mm(hidden, wd[...])
    dh = mm_t(dg, wg[...]) + mm_t(du, wu[...])
    add_steps(pl.program_id(0), [(z_out, z), (dh_out, dh)])


def ffn_body(info, a, ct, wg, wu, wd, z_out, dh_out, own_gu, other_gu, own_dn, other_dn):
    step = pl.program_id(0)
    half = pl.num_programs(0) // 2
    width = a.shape[1] // 2
    hidden, dg, du = hidden_both_ways(a[...], ct[...], wg[...], wu[...], wd[...])
    z = mm(hidden, wd[...])
    dh = mm_t(dg, wg[...]) + mm_t(du, wu[...])
    add_steps(step, [(z_out, z), (dh_out, dh)])
    down = t_mm(hidden, ct[...])

    @pl.when(step < half)
    def send():
        pack_rows(other_dn, down)

    @pl.when(step >= half)
    def keep():
        pack_rows(own_dn, down)

    own = a[:, pl.ds(pl.multiple_of(info[0] * width, width), width)]
    other = a[:, pl.ds(pl.multiple_of((1 - info[0]) * width, width), width)]
    own_gu[0, :width] = t_mm(own, dg).astype(BF)
    own_gu[0, width:] = t_mm(own, du).astype(BF)
    other_gu[0, :width] = t_mm(other, dg).astype(BF)
    other_gu[0, width:] = t_mm(other, du).astype(BF)


def ffn_local(info, pay, w_gu, w_down, block):
    rows = pay.shape[0]
    hidden, width = w_down.shape
    steps = hidden // block
    return call(
        ffn_local_body,
        [sds((rows, width), F32)] * 2,
        (steps,),
        [
            pl.BlockSpec((rows, width), lambda i, *u: (0, 0)),
            pl.BlockSpec((rows, width), lambda i, *u: (0, 1)),
            pl.BlockSpec((width, block), lambda i, *u: (0, i)),
            pl.BlockSpec((width, block), lambda i, *u: (0, steps + i)),
            pl.BlockSpec((block, width), lambda i, *u: (i, 0)),
        ],
        [whole((rows, width))] * 2,
        (info, pay, pay, w_gu, w_gu, w_down),
        flops=2 * 6 * rows * hidden * width,
        moved=2 * 3 * hidden * width,
    )


def ffn(info, a, ct, w_gu, w_down):
    rows, width = a.shape
    hidden = w_down.shape[0]
    block = COLS
    steps = hidden // block
    half = steps // 2

    def natural(i, info):
        return jnp.where(i < half, (1 - info[0]) * half + i, info[0] * half + i - half)

    unit = (1, width, COLS)
    shapes = [
        sds((rows, width), F32),
        sds((rows, width), F32),
        sds((steps,) + unit[1:], BF),
        sds((steps,) + unit[1:], BF),
        sds((half,) + unit[1:], BF),
        sds((half,) + unit[1:], BF),
    ]
    return call(
        ffn_body,
        shapes,
        (steps,),
        [
            whole(a.shape),
            whole(ct.shape),
            pl.BlockSpec((width, block), lambda i, info: (0, natural(i, info))),
            pl.BlockSpec((width, block), lambda i, info: (0, steps + natural(i, info))),
            pl.BlockSpec((block, width), lambda i, info: (natural(i, info), 0)),
        ],
        [
            whole((rows, width)),
            whole((rows, width)),
            pl.BlockSpec(unit, lambda i, info: (natural(i, info), 0, 0)),
            pl.BlockSpec(unit, lambda i, info: (natural(i, info), 0, 0)),
            pl.BlockSpec(unit, lambda i, info: (jnp.maximum(i - half, 0), 0, 0)),
            pl.BlockSpec(unit, lambda i, info: (jnp.minimum(i, half - 1), 0, 0)),
        ],
        (info, a, ct, w_gu, w_gu, w_down),
        flops=2 * 9 * rows * hidden * width,
        moved=2 * 2 * 3 * hidden * width + rows * width * 12,
    )


def ffn_all_body(info, a, ct, w_gu, w_down, z_out, dh_out, own_gu, other_gu, own_dn, other_dn, turned, hid, slopes):
    step = pl.program_id(0)
    hidden, whole_width = w_down.shape
    steps = hidden // COLS
    half = steps // 2
    width = whole_width // 2

    @pl.when(step == 0)
    def turn():
        turned[...] = a[...].T

    @pl.when(step < steps)
    def block():
        at = jnp.where(step < half, (1 - info[0]) * half + step, info[0] * half + step - half)
        gate = pl.ds(pl.multiple_of(at * COLS, COLS), COLS)
        upper = pl.ds(pl.multiple_of(hidden + at * COLS, COLS), COLS)
        mixed, dg, du = hidden_both_ways(a[...], ct[...], w_gu[:, gate], w_gu[:, upper], w_down[gate])
        hid[:, gate] = mixed
        slopes[:, gate] = dg
        slopes[:, upper] = du
        down = t_mm(mixed, ct[...])

        @pl.when(step < half)
        def send():
            pack_rows(other_dn, down)

        @pl.when(step >= half)
        def keep():
            pack_rows(own_dn, down)

        for target, side in ((own_gu, info[0]), (other_gu, 1 - info[0])):
            rows = turned[pl.ds(pl.multiple_of(side * width, width), width)]
            target[0, :width] = mm(rows, dg).astype(BF)
            target[0, width:] = mm(rows, du).astype(BF)

    @pl.when(step == steps)
    def last():
        z_out[...] = mm(hid[...], w_down[...]).astype(BF)
        dh_out[...] = mm_t(slopes[...], w_gu[...]).astype(BF)


def ffn_all(info, a, ct, w_gu, w_down):
    rows, width = a.shape
    hidden = w_down.shape[0]
    steps = hidden // COLS
    half = steps // 2

    def natural(i, info):
        return jnp.where(i < half, (1 - info[0]) * half + i, info[0] * half + jnp.minimum(i - half, half - 1))

    unit = (1, width, COLS)
    shapes = [
        sds((rows, width), BF),
        sds((rows, width), BF),
        sds((steps,) + unit[1:], BF),
        sds((steps,) + unit[1:], BF),
        sds((half,) + unit[1:], BF),
        sds((half,) + unit[1:], BF),
    ]
    return call(
        ffn_all_body,
        shapes,
        (steps + 1,),
        [whole(a.shape), whole(ct.shape), whole(w_gu.shape), whole(w_down.shape)],
        [
            whole((rows, width)),
            whole((rows, width)),
            pl.BlockSpec(unit, lambda i, info: (natural(i, info), 0, 0)),
            pl.BlockSpec(unit, lambda i, info: (natural(i, info), 0, 0)),
            pl.BlockSpec(unit, lambda i, info: (jnp.minimum(jnp.maximum(i - half, 0), half - 1), 0, 0)),
            pl.BlockSpec(unit, lambda i, info: (jnp.minimum(i, half - 1), 0, 0)),
        ],
        (info, a, ct, w_gu, w_down),
        scratch=[
            pltpu.VMEM((width, rows), BF),
            pltpu.VMEM((rows, hidden), BF),
            pltpu.VMEM((rows, 2 * hidden), BF),
        ],
        flops=2 * 9 * rows * hidden * width,
        moved=2 * 2 * 3 * hidden * width + rows * width * 12,
    )


def plane_grads_body(info, near, far, wg, wu, wd, own_gu, other_gu, dn):
    width = wg.shape[0]
    half = width // 2
    sums = None
    for part in (near, far):
        low, upstream = (part[:, :width], part[:, width:])
        hidden, dg, du = hidden_both_ways(low, upstream, wg[...], wu[...], wd[...])
        own = part[:, pl.ds(pl.multiple_of(info[0] * half, half), half)]
        other = part[:, pl.ds(pl.multiple_of((1 - info[0]) * half, half), half)]
        terms = (t_mm(own, dg), t_mm(own, du), t_mm(other, dg), t_mm(other, du), t_mm(hidden, upstream))
        sums = terms if sums is None else tuple(p + q for p, q in zip(sums, terms))
    own_gu[0, :half] = sums[0].astype(BF)
    own_gu[0, half:] = sums[1].astype(BF)
    other_gu[0, :half] = sums[2].astype(BF)
    other_gu[0, half:] = sums[3].astype(BF)
    for cut in range(width // COLS):
        dn[0, cut * COLS : (cut + 1) * COLS] = sums[4][:, cut * COLS : (cut + 1) * COLS].astype(BF)


def plane_grads(info, near, far, w_gu, w_down):
    hidden, width = w_down.shape
    steps = hidden // COLS
    turns = steps // 8

    def block(i, info):
        return info[0] * (steps // 2) + lax.rem(info[3], 4) * turns + i

    unit = (1, width, COLS)
    spec = pl.BlockSpec(unit, lambda i, *u: (i, 0, 0))
    rows = 2 * near.shape[0]
    return call(
        plane_grads_body,
        [sds((turns, width, COLS), BF)] * 3,
        (turns,),
        [
            whole(near.shape),
            whole(far.shape),
            pl.BlockSpec((width, COLS), lambda i, info: (0, block(i, info))),
            pl.BlockSpec((width, COLS), lambda i, info: (0, steps + block(i, info))),
            pl.BlockSpec((COLS, width), lambda i, info: (block(i, info), 0)),
        ],
        [spec] * 3,
        (info, near, far, w_gu, w_gu, w_down),
        flops=2 * 6 * rows * turns * COLS * width,
        moved=9_000_000,
    )


def column_fold_body(order, info, first, second, third, keep, send):
    slots = 1 << len(order)
    size = keep.shape[2]
    place_z = info[3] // 4
    for part, source in enumerate((first, second, third)):
        for block in range(source.shape[0]):
            for slot in range(slots):
                owner = jnp.bitwise_xor(place_z, mask_of(slot, order))
                at = pl.ds(pl.multiple_of(owner * size, size), size)
                target = keep if slot < slots // 2 else send
                target[slot % (slots // 2), part * source.shape[0] + block] = source[block, at, :]


def column_fold(info, order, sources):
    slots = 1 << len(order)
    blocks, width, cols = sources[0].shape
    shape = sds((slots // 2, 3 * blocks, width // slots, cols), BF)
    return call(
        functools.partial(column_fold_body, order),
        [shape, shape],
        (1,),
        [whole(a.shape) for a in sources],
        [whole(shape.shape)] * 2,
        (info, *sources),
        moved=10_000_000,
        name="column_fold",
    )


def mid_back_body(
    info, y, up, z, dh2, zh, dff, ffr, gf, cols, rows, small, gate, lout, lout_got, hout, hy, hq,
    out, dy_out, dlo_out, dho_out, dhy_out, dsq_out, part_out,
):
    tok = y.shape[1]
    base = info[1]
    micro = pl.program_id(0)
    spread = onehot_rows(rows[2, 0], base, tok)
    take = onehot_cols(cols[2, 0], base, tok)
    values, top = (y[0], up[0].astype(F32))
    open_f = gf[0, :, 0:1]
    zhv = zh[0]
    out[0] = (values + z[0].astype(F32) + pick(spread, zhv * open_f)).astype(BF)
    taken = mm(take, up[0])
    dsf = jnp.sum(taken * zhv, axis=-1, keepdims=True) * open_f * (1.0 - open_f)
    back = dh2[0].astype(F32) + pick(spread, dff[0] + dsf * small[2:3].astype(F32))
    inv = inverse_rms(values)
    scaled = back * small[4:5].astype(F32)
    mean = jnp.mean(values * scaled, axis=-1, keepdims=True)
    dy = top + inv * scaled - values * (inv * inv * inv * mean)
    dy_out[0] = dy
    dgain = jnp.sum(back * values * inv, axis=0, keepdims=True)
    drf = jnp.sum(dsf * ffr[0].astype(F32), axis=0, keepdims=True)
    part_in = lout.shape[0]
    for weight, side in ((lout, info[0]), (lout_got, 1 - info[0])):
        at = pl.ds(pl.multiple_of(side * part_in, part_in), part_in)
        dlo_out[0, :, at] = mm_t(dy.astype(BF), weight[...]).astype(BF)
    dyq = pick(onehot_cols(cols[0, 0], base, tok), dy)
    open_q = gate[0, :, 0:1]
    dhy = (dyq * open_q).astype(BF)
    dhy_out[0] = dhy
    dsq = jnp.sum(dyq * hy[0], axis=-1, keepdims=True) * open_q * (1.0 - open_q)
    dsq_out[0] = jnp.broadcast_to(dsq, dsq_out.shape[1:])
    drq = jnp.sum(dsq * hq[0].astype(F32), axis=0, keepdims=True)
    dho_out[0] = mm_t(dhy, hout[...]).astype(BF)
    row = iota(part_out.shape, 0)
    part = jnp.where(row == 0, drq, jnp.where(row == 2, drf, jnp.where(row == 4, dgain, 0.0)))

    @pl.when(micro == 0)
    def first():
        part_out[...] = part

    @pl.when(micro > 0)
    def later():
        part_out[...] += part


def mid_back(info, y, up, z, dh2, zh, dff, ffr, gf, cols, rows, small, gate, lout, lout_got, hout, hy, hq):
    micros, tok, width = y.shape
    count = cols.shape[2]
    shapes = [
        sds((micros, tok, width), BF),
        sds((micros, tok, width), F32),
        sds((micros, tok, 2 * lout.shape[0]), BF),
        sds((micros, count, width), BF),
        sds((micros, count, width), BF),
        sds((micros, count, LANES), F32),
        sds((8, width), F32),
    ]
    return call(
        mid_back_body,
        shapes,
        (micros,),
        [
            one_of(y.shape),
            one_of(up.shape),
            one_of(z.shape),
            one_of(dh2.shape),
            one_of(zh.shape),
            one_of(dff.shape),
            pl.BlockSpec((1, count, width), lambda i, *u: (i, 0, 0)),
            one_of(gf.shape),
            second_of(cols.shape),
            second_of(rows.shape),
            whole(small.shape),
            one_of(gate.shape),
            whole(lout.shape),
            whole(lout_got.shape),
            whole(hout.shape),
            one_of(hy.shape),
            pl.BlockSpec((1, count, width), lambda i, *u: (i, 0, 0)),
        ],
        [one_of(s.shape) for s in shapes[:-1]] + [whole(shapes[-1].shape)],
        (info, y, up, z, dh2, zh, dff, ffr, gf, cols, rows, small, gate, lout, lout_got, hout, hy, hq),
        flops=3_000_000_000,
        moved=22_000_000,
    )


def light_join_body(info, x, small, dq, own, got_low, got_high, dl_out, own_out, other_out, low):
    tok, width = x.shape[1:]
    micros = x.shape[0]
    half = width // 2
    inner = dq.shape[2]
    for m in range(micros):
        dl_out[m, :, :inner] = dq[m]
        dl_out[m, WIN : tok - WIN, inner:] = own[m, WIN : tok - WIN].astype(BF)
        dl_out[m, :WIN, inner:] = (own[m, :WIN] + got_low[m].astype(F32)).astype(BF)
        dl_out[m, tok - WIN :, inner:] = (own[m, tok - WIN :] + got_high[m].astype(F32)).astype(BF)
        values = x[m].astype(F32)
        low[m] = (values * inverse_rms(values) * small[3:4].astype(F32)).astype(BF)
    for target, side in ((other_out, 1 - info[0]), (own_out, info[0])):
        cut = pl.ds(pl.multiple_of(side * half, half), half)
        for block in range(dl_out.shape[2] // COLS):
            total = sum(
                t_mm(low[m, :, cut], dl_out[m, :, block * COLS : (block + 1) * COLS])
                for m in range(micros)
            )
            target[block // 2, (block % 2) * half : (block % 2 + 1) * half] = total.astype(BF)


def light_join(info, x, small, dq, own, got_low, got_high):
    micros, tok, width = x.shape
    columns = dq.shape[2] + own.shape[2]
    shapes = [sds((micros, tok, columns), BF)] + [sds((columns // (2 * COLS), width, COLS), BF)] * 2
    args = (info, x, small, dq, own, got_low, got_high)
    return call(
        light_join_body,
        shapes,
        (1,),
        [whole(a.shape) for a in args[1:]],
        [whole(s.shape) for s in shapes],
        args,
        scratch=[pltpu.VMEM(x.shape, BF)],
        flops=2 * micros * tok * width * columns,
        moved=20_000_000,
    )


def in_back_body(
    info, x, dy, dl, dhq, dkin, dsq, rows, small, gate, h1k, l_own, l_got, h_own, h_got,
    grad_out, part_out,
):
    tok, width = x.shape[1:]
    micro = pl.program_id(0)
    base = info[1]
    light = dl[0]
    back = unhalved(info, mm_t(light, l_own[...]), mm_t(light, l_got[...]))
    given = dkin[0].astype(F32)
    open_k = gate[0, :, 1:2]
    source = h1k[0]
    dskv = jnp.sum(given * source, axis=-1, keepdims=True) * open_k * (1.0 - open_k)
    to_q = unhalved(info, mm_t(dhq[0], h_own[...]), mm_t(dhq[0], h_got[...]))
    to_q += dsq[0, :, 0:1] * small[0:1].astype(F32)
    to_k = given * open_k + dskv * small[1:2].astype(F32)
    back += pick(onehot_rows(rows[0, 0], base, tok), to_q)
    back += pick(onehot_rows(rows[1, 0], base, tok), to_k)
    values = x[0].astype(F32)
    inv = inverse_rms(values)
    scaled = back * small[3:4].astype(F32)
    mean = jnp.mean(values * scaled, axis=-1, keepdims=True)
    grad_out[0] = (dy[0] + inv * scaled - values * (inv * inv * inv * mean)).astype(BF)
    dgain = jnp.sum(back * values * inv, axis=0, keepdims=True)
    drk = jnp.sum(dskv * source.astype(BF).astype(F32), axis=0, keepdims=True)
    row = iota(part_out.shape, 0)
    part = jnp.where(row == 1, drk, jnp.where(row == 3, dgain, 0.0))

    @pl.when(micro == 0)
    def first():
        part_out[...] = part

    @pl.when(micro > 0)
    def later():
        part_out[...] += part


def in_back(info, x, dy, dl, dhq, dkin, dsq, rows, small, gate, h1k, l_own, l_got, h_own, h_got):
    micros, tok, width = x.shape
    shapes = [sds((micros, tok, width), BF), sds((8, width), F32)]
    firsts = (x, dy, dl, dhq, dkin, dsq)
    return call(
        in_back_body,
        shapes,
        (micros,),
        [one_of(a.shape) for a in firsts]
        + [second_of(rows.shape), whole(small.shape)]
        + [one_of(a.shape) for a in (gate, h1k)]
        + [whole(a.shape) for a in (l_own, l_got)]
        + [whole((h_own.shape[0], width))] * 2,
        [one_of(shapes[0].shape), whole(shapes[1].shape)],
        (info,) + firsts + (rows, small, gate, h1k, l_own, l_got, h_own, h_got),
        flops=2_600_000_000,
        moved=14_000_000,
    )


def mask_of(slot, order):
    bits = len(order)
    return sum(order[b] for b in range(bits) if (slot >> (bits - 1 - b)) & 1)


def fold_body(order, counts, info, *refs):
    sources = refs[: 2 * len(counts)]
    keep, send = refs[2 * len(counts) :]
    slots = 1 << len(order)
    size = keep.shape[2]
    step = pl.program_id(0)
    start = 0
    for which, count in enumerate(counts):
        own, got = sources[2 * which : 2 * which + 2]

        @pl.when((step >= start) & (step < start + count))
        def part():
            for slot in range(slots):
                owner = jnp.bitwise_xor(info[3], mask_of(slot, order))
                at = pl.ds(pl.multiple_of(owner * size, size), size)
                total = (own[0, at, :].astype(F32) + got[0, at, :].astype(F32)).astype(BF)
                if slot < slots // 2:
                    keep[slot, 0] = total
                else:
                    send[slot - slots // 2, 0] = total

        start += count


def fold(info, order, parts):
    slots = 1 << len(order)
    width = parts[0][0].shape[1]
    counts = [part[3] for part in parts]
    total = sum(counts)
    shape = sds((slots // 2, total, width // slots, COLS), BF)
    args, specs = ([], [])
    start = 0
    for own, got, first, count in parts:
        index = functools.partial(
            lambda first, start, count, i, *u: (
                first + jnp.minimum(jnp.maximum(i - start, 0), count - 1),
                0,
                0,
            ),
            first,
            start,
            count,
        )
        args += [own, got]
        specs += [pl.BlockSpec((1, width, COLS), index)] * 2
        start += count
    spec = pl.BlockSpec((slots // 2, 1, width // slots, COLS), lambda i, *u: (0, i, 0, 0))
    return call(
        functools.partial(fold_body, order, counts),
        [shape, shape],
        (total,),
        specs,
        [spec, spec],
        (info, *args),
        moved=total * width * COLS * 6,
    )


def flipped(value, bit):
    size = lax.axis_size("ctx")
    return lax.ppermute(value, "ctx", [(i, i ^ bit) for i in range(size)])


def tied(*values):
    return lax.optimization_barrier(values)


def scatter_step(keep, got):
    half = keep.shape[0] // 2
    if half == 0:
        return ((keep.astype(F32) + got.astype(F32)).astype(BF), None)
    return (
        (keep[:half].astype(F32) + got[:half].astype(F32)).astype(BF),
        (keep[half:].astype(F32) + got[half:].astype(F32)).astype(BF),
    )


def scatter_start(chunks, orders, stage):
    return [flipped(send, order[stage]) for (keep, send), order in zip(chunks, orders)]


def scatter_end(chunks, got):
    return [scatter_step(keep, g) for (keep, send), g in zip(chunks, got)]


def scatter_sum(keep, send, order):
    for bit in order:
        keep, send = scatter_step(keep, flipped(send, bit))
    return keep


def gather_start(values, orders, stage):
    return [flipped(value, order[-1 - stage]) for value, order in zip(values, orders)]


def gather_end(values, got):
    return [jnp.concatenate([value, g], axis=0) for value, g in zip(values, got)]


def gather_pair(value, order):
    for bit in order[:-1]:
        value = jnp.concatenate([value, flipped(value, bit)], axis=0)
    return (value, flipped(value, order[-1]))


def from_owner(info, order, near, far, owner, write):
    slots = 1 << len(order)
    distance = jnp.bitwise_xor(info[3], owner)
    slot = sum(
        jnp.where(jnp.bitwise_and(distance, bit) != 0, 1 << place, 0)
        for place, bit in enumerate(reversed(order))
    )
    inside = lax.rem(slot, slots // 2)

    @pl.when(slot < slots // 2)
    def close():
        write(near.at[inside])

    @pl.when(slot >= slots // 2)
    def distant():
        write(far.at[inside])


def unpack_gu_body(order, info, near, far, *outs):
    out = outs[-1]
    size = near.shape[2]
    per = out.shape[0] // size
    for turn in range(per):

        def write(source, turn=turn):
            for block in range(near.shape[1]):
                out[turn * size : (turn + 1) * size, block * COLS : (block + 1) * COLS] = source[
                    block
                ].astype(F32)

        from_owner(info, order, near, far, pl.program_id(1) * per + turn, write)


def write_dn(out, source, first, size, owner, row):
    cuts = out.shape[1] // COLS
    rows = size // cuts
    value = source[first].astype(F32)
    for cut in range(cuts):
        out[row + owner * rows : row + (owner + 1) * rows, cut * COLS : (cut + 1) * COLS] = value[
            cut * rows : (cut + 1) * rows
        ]


def unpack_dn_body(order, info, near, far, *outs):
    slots, blocks, size = near.shape[:3]
    for owner in range(2 * slots):

        def write(source, owner=owner):
            for block in range(blocks):
                write_dn(outs[-1], source, block, size, owner, block * COLS)

        from_owner(info, order, near, far, owner, write)


def unpack(body, info, order, pair, first, count, step, shape, grid_more, block, index, previous, name):
    near, far = pair
    slots, unused, size, unused_too = near.shape
    spec = pl.BlockSpec((slots, step, size, COLS), lambda i, *u: (0, first // step + i, 0, 0))
    args, specs, aliases = ([info, near, far], [spec, spec], {})
    if previous is not None:
        args.append(previous)
        specs.append(pl.BlockSpec(memory_space=pl.ANY))
        aliases = {3: 0}
    return pl.pallas_call(
        functools.partial(body, order),
        out_shape=sds(shape, F32),
        grid_spec=pltpu.PrefetchScalarGridSpec(
            num_scalar_prefetch=1,
            grid=(count // step,) + grid_more,
            in_specs=specs,
            out_specs=pl.BlockSpec(block, index),
        ),
        input_output_aliases=aliases,
        compiler_params=pltpu.CompilerParams(vmem_limit_bytes=32 * 1024 * 1024),
        cost_estimate=pl.CostEstimate(
            flops=0, bytes_accessed=count * 2 * slots * size * COLS * 6, transcendentals=0
        ),
        name=name,
    )(*args)


def unpack_gu(info, order, pair, first, count, total, base, previous, step):
    rows = pair[0].shape[0] * pair[0].shape[2]
    return unpack(
        unpack_gu_body, info, order, pair, first, count, step, (rows, 2 * total * COLS), (2,), (rows, step * COLS),
        lambda i, s, *u: (0, (s * total + base) // step + i), previous, "unpack_gu",
    )


def unpack_dn(info, order, pair, first, count, total, base, previous, step):
    width = 2 * pair[0].shape[0] * pair[0].shape[2]
    return unpack(
        unpack_dn_body, info, order, pair, first, count, step, (total * COLS, width), (), (step * COLS, width),
        lambda i, *u: (base // step + i, 0), previous, "unpack_dn",
    )


def unpack_plane_gu_body(info, full, out):
    sides, unused, planes, blocks, size, cols = full.shape
    turns = blocks // 3
    columns = out.shape[1] // sides
    for side in range(sides):
        for half in range(2):
            first = jnp.bitwise_xor(half, info[0]) * turns
            for plane in range(planes):
                for turn in range(turns):
                    at = side * columns + ((half * planes + plane) * turns + turn) * cols
                    out[:, at : at + cols] = full[side, 0, plane, first + turn].astype(F32)


def unpack_plane_gu(info, full, total):
    levels, planes, blocks, size, unused = full.shape
    rows, step = (2 * size, 48)
    turns = size // step
    view = full.reshape((2, levels // 2) + full.shape[1:])
    return call(
        unpack_plane_gu_body,
        sds((rows, 2 * total * COLS), F32),
        (rows // step,),
        [
            pl.BlockSpec(
                (2, 1, planes, blocks, step, COLS), lambda r, *u: (0, r // turns, 0, 0, r % turns, 0)
            )
        ],
        pl.BlockSpec((step, 2 * total * COLS), lambda r, *u: (r, 0)),
        (info, view),
        moved=2 * rows * total * COLS * 6,
        name="unpack_plane_gu",
    )


def unpack_plane_dn_body(info, full, out):
    levels, unused, blocks, size, cols = full.shape
    for level in range(levels):
        for block in range(blocks):
            for part in range(size // 64):
                cut, row = divmod(level * size + part * 64, COLS)
                at = block * COLS + row
                out[at : at + 64, cut * COLS : (cut + 1) * COLS] = full[
                    level, 0, block, part * 64 : (part + 1) * 64
                ].astype(F32)


def unpack_plane_dn(info, full):
    levels, planes, blocks, size, unused = full.shape
    turns = blocks // 3
    width = levels * size
    return call(
        unpack_plane_dn_body,
        sds((planes * turns * COLS, width), F32),
        (planes,),
        [pl.BlockSpec((levels, 1, turns, size, COLS), lambda q, *u: (0, q, 2, 0, 0))],
        pl.BlockSpec((turns * COLS, width), lambda q, *u: (q, 0)),
        (info, full),
        moved=planes * turns * COLS * width * 6,
        name="unpack_plane_dn",
    )


def unpack_units_body(order, first, info, near, far, *outs):
    slots, unused, size = near.shape[:3]
    homes = [
        (out, block * COLS) for out in outs for block in range(out.shape[1] // COLS)
    ]
    for owner in range(2 * slots):
        side, turn = divmod(owner, slots)

        def write(source, side=side, turn=turn):
            for at in range(side, len(homes), 2):
                out, column = homes[at]
                out[turn * size : (turn + 1) * size, column : column + COLS] = source[
                    first + at // 2
                ].astype(F32)

        from_owner(info, order, near, far, owner, write)


def unpack_units(info, order, pair, first, widths):
    slots, unused, size, unused_too = pair[0].shape
    shapes = [sds((slots * size, w), F32) for w in widths]
    args = [info, *pair]
    return call(
        functools.partial(unpack_units_body, order, first),
        shapes,
        (1,),
        [whole(a.shape) for a in args[1:]],
        [whole(s.shape) for s in shapes],
        args,
        moved=sum(widths) * slots * size * 6,
        name="unpack_units",
    )


def plain_gu(own, other):
    blocks, width, cols = own.shape

    def rows(part):
        return part.reshape(blocks, 2, width // 2, cols).transpose(2, 1, 0, 3).reshape(width // 2, -1)

    return jnp.concatenate([rows(own), rows(other)], axis=0)


def plain_dn(own, other):
    blocks, width, cols = own.shape
    cuts = width // cols

    def rows(part):
        return (
            part.reshape(blocks, 16, cuts, width // (16 * cuts), cols)
            .transpose(0, 1, 3, 2, 4)
            .reshape(-1, width)
        )

    return jnp.concatenate([rows(own), rows(other)], axis=0)


def plain_units(own, other, widths):
    def unit(part, at):
        half = part.shape[1] // 2
        return part[at // 2, (at % 2) * half : (at % 2 + 1) * half]

    result, at = ([], 0)
    for columns in widths:
        count = columns // COLS
        result.append(
            jnp.concatenate(
                [
                    jnp.concatenate([unit(part, at + i) for i in range(count)], axis=1)
                    for part in (own, other)
                ],
                axis=0,
            )
        )
        at += count
    return result


def plain_sum(grads):
    parts = [lax.psum_scatter(g.astype(BF), "wsh", scatter_dimension=0, tiled=True) for g in grads]
    return tuple(g.astype(F32) for g in lax.psum(parts, "ctx"))


def per_device(
    tokens, cotangent, light_qkv, light_out, heavy_qkv, heavy_out, light_gu, light_down, heavy_gu, heavy_down,
    routers, gains, doc_starts, q_index, kv_index, ff_index,
):
    micros, unused, tok, width = tokens.shape
    count, groups = (lax.axis_size("ctx"), lax.axis_size("wsh"))
    direct = groups == 2 and count == 16
    place_ctx = lax.axis_index("ctx")
    side = lax.axis_index("wsh") if direct else 0
    base = place_ctx * tok
    info = jnp.concatenate(
        [
            jnp.stack([jnp.int32(side), base, jnp.int32(tok * count), place_ctx]).astype(jnp.int32),
            doc_starts[:, 0].reshape(-1),
        ]
    )
    swap = [(0, 1), (1, 0)]

    def pair_of(shard):
        if direct:
            return (shard, lax.ppermute(shard, "wsh", swap))
        full = lax.all_gather(shard, "wsh", axis=0, tiled=True)
        return (full[: full.shape[0] // 2], full[full.shape[0] // 2 :])

    def full_of(shard, axis=0):
        return lax.all_gather(shard, "wsh", axis=axis, tiled=True)

    vectors = jnp.concatenate([routers, gains, jnp.zeros((3, routers.shape[1]), BF)], axis=0)
    if direct:
        got = lax.ppermute(vectors, "wsh", swap)
        small = jnp.concatenate(
            [jnp.where(side == 0, vectors, got), jnp.where(side == 0, got, vectors)], axis=1
        )
    else:
        small = full_of(vectors, 1)
    x, up = (tokens[:, 0], cotangent[:, 0])
    index = jnp.stack([q_index[:, 0], kv_index[:, 0], ff_index[:, 0]])
    cols, rows = (index[..., None], index[:, :, None, :])
    hq_in, kin_pay, h1k, gate = routed_in(info, x, cols, small)
    l_own, l_got = pair_of(light_qkv)
    h_own, h_got = pair_of(heavy_qkv)
    o_own, o_got = pair_of(light_out)
    w_hout, w_hgu, w_hdown = (full_of(heavy_out), full_of(heavy_gu), full_of(heavy_down))
    w_lgu, w_ldown = (full_of(light_gu), full_of(light_down))
    kv_orders = ((8, 4, 2, 1), (8, 1, 4, 2))
    back_orders = [tuple(reversed(order)) for order in kv_orders]
    upward = [(i, i + 1) for i in range(count - 1)]
    downward = [(i + 1, i) for i in range(count - 1)]
    inner = light_qkv.shape[1] // 3
    every = range(micros)

    def rims(qkv):
        return (
            lax.ppermute(qkv[:, tok - WIN :, inner:], "ctx", upward),
            lax.ppermute(qkv[:, :WIN, inner:], "ctx", downward),
        )

    def project(kin):
        return key_project(info, kin, h_own, h_got)

    if direct:
        values = [kin_pay[m] for m in every]
        got = gather_start(values, back_orders, 0)
        qkv = light_in(info, x, small, l_own, l_got)
        got, qkv = tied(got, qkv)
        before, after = rims(qkv)
        values = gather_end(values, got)
        got = gather_start(values, back_orders, 1)
        q_pay = query_project(info, hq_in, h_own, h_got)
        got, q_pay, w_hout = tied(got, q_pay, w_hout)
        values = gather_end(values, got)
        got = gather_start(values, back_orders, 2)
        done = light_inner(info, qkv)
        got, before, after, done = tied(got, before, after, done)
        values = gather_end(values, got)
        got = gather_start(values, back_orders, 3)
        lo, light_lse = light_outer(info, qkv, before, after, done)
        near_kv = [project(v) for v in values]
        got, near_kv, lo, light_lse, w_hgu, w_hdown = tied(got, near_kv, lo, light_lse, w_hgu, w_hdown)
        kins = list(zip(values, got))
        kvs = [(n, project(f)) for n, f in zip(near_kv, got)]
    else:
        kins = []
        for m in every:
            full = lax.all_gather(kin_pay[m], "ctx", axis=0, tiled=True)
            kins.append((full[: full.shape[0] // 2], full[full.shape[0] // 2 :]))
        kvs = [tuple(project(k) for k in pair) for pair in kins]
        qkv = light_in(info, x, small, l_own, l_got)
        before, after = rims(qkv)
        lo, light_lse = light_outer(info, qkv, before, after, light_inner(info, qkv))
        q_pay = query_project(info, hq_in, h_own, h_got)
    heavy = [heavy_fwd(info, q_pay[m], kins[m], kvs[m]) for m in every]
    heavy, w_lgu, w_ldown = tied(heavy, w_lgu, w_ldown)
    ho = jnp.stack([h[0] for h in heavy])
    y, low2, pay, hy, gf = middle(info, x, up, cols, rows, small, gate, lo, o_own, o_got, ho, w_hout)

    def flat(value):
        return value.reshape(-1, value.shape[-1])

    orders = ((1, 2, 4, 8), (2, 4, 1, 8), (4, 1, 2, 8))
    if direct:
        mine = flat(pay)
        plane = [flipped(mine, bit) for bit in (1, 2, 3)]
        zh, dff = ffn_local(info, mine, w_hgu, w_hdown, 2 * COLS)
        plane, zh, dff = tied(plane, zh, dff)
        near = jnp.concatenate([mine, *plane], axis=0)
        far = lax.ppermute(near, "wsh", swap)
    else:
        zh, dff, hgu_own, hgu_send, hdn_own, hdn_send = ffn(
            info, flat(pay[..., :width]), flat(pay[..., width:]), w_hgu, w_hdown
        )
    if direct:
        plane_own, plane_send, plane_dn = plane_grads(info, near, far, w_hgu, w_hdown)
        plane_got = lax.ppermute(plane_send, "wsh", swap)
        keep, send = column_fold(info, (1, 2), (plane_own, plane_got, plane_dn))
        send, low2 = tied(send, low2)
        got = flipped(send, 4)
    z, dh2, lgu_own, lgu_send, ldn_own, ldn_send = ffn_all(info, flat(low2), flat(up), w_lgu, w_ldown)
    if direct:
        got, z, dh2, lgu_send, ldn_send = tied(got, z, dh2, lgu_send, ldn_send)
        keep, send = scatter_step(keep, got)
        got = flipped(send, 8)
        lgu_got, ldn_got = (lax.ppermute(part, "wsh", swap) for part in (lgu_send, ldn_send))

    def by_micro(value):
        return value.reshape(micros, -1, value.shape[-1])

    out_tokens, dy, dlo, dho, dhy, dsq, part_two = mid_back(
        info, y, up, by_micro(z), by_micro(dh2), by_micro(zh), by_micro(dff), pay, gf, cols, rows, small, gate, o_own,
        o_got, w_hout, hy, hq_in,
    )
    backs = []
    for m in every:
        backs.append(heavy_bwd(info, q_pay[m], kins[m], kvs[m], heavy[m][1], dho[m], h_own, h_got))
        if direct and m == 0:
            got, backs[0], dho = tied(got, backs[0], dho)
            keep, send = scatter_step(keep, got)
            plane_full = lax.all_gather(keep[0], "ctx", axis=0, tiled=False)
            plane_full = plane_full.reshape((count // 4, 4) + plane_full.shape[1:])
    dhq = jnp.stack([b[0] for b in backs])
    shape = (count // 2, q_index.shape[2], width)
    back = [tuple(part.reshape(shape) for part in b[3:5]) for b in backs]
    dkvs = [part for b in backs for part in b[1:3]]
    if direct:
        back, dlo, dkvs = tied(back, dlo, dkvs)
        got_back = scatter_start(back, back_orders, 0)
    dlq, dl_own, rim_low, rim_high = light_bwd_outer(info, qkv, before, after, light_lse, dlo)
    got_low = lax.ppermute(rim_high, "ctx", upward)
    got_high = lax.ppermute(rim_low, "ctx", downward)
    dlq, dl_own = light_bwd_inner(info, qkv, light_lse, dlo, dlq, dl_own)
    if direct:
        got_back, dlq, dl_own = tied(got_back, dlq, dl_own)
        back = scatter_end(back, got_back)
        got_back = scatter_start(back, back_orders, 1)
    kin_all = [part for pair in kins for part in pair]
    ha_own, ha_send = heavy_grads(info, hq_in, dhq, ho, dhy, lo, dy, kin_all, dkvs)
    if direct:
        got_back, got_low, got_high, ha_own, ha_send = tied(got_back, got_low, got_high, ha_own, ha_send)
        ha_got = lax.ppermute(ha_send, "wsh", swap)
        back = scatter_end(back, got_back)
        got_back = scatter_start(back, back_orders, 2)
    dl, la_own, la_send = light_join(info, x, small, dlq, dl_own, got_low, got_high)
    if direct:
        la_got = lax.ppermute(la_send, "wsh", swap)
        second = [
            fold(info, orders[0], [(ha_own, ha_got, 0, 6)]),
            fold(info, orders[1], [(lgu_own, lgu_got, 0, 4), (ha_own, ha_got, 6, 1)]),
            fold(info, orders[2], [(la_own, la_got, 0, 3), (ldn_own, ldn_got, 0, 2)]),
        ]
        got_back, second, dl = tied(got_back, second, dl)
        got_two = scatter_start(second, orders, 0)
        back = scatter_end(back, got_back)
        got_back = scatter_start(back, back_orders, 3)
        (got_two,) = tied(got_two)
        second = scatter_end(second, got_two)
        got_two = scatter_start(second, orders, 1)
        back, got_back, second = tied(back, got_back, second)
        back = scatter_end(back, got_back)
        dkin = jnp.concatenate([keep for keep, send in back], axis=0)
    else:
        dkin = jnp.stack(
            [
                lax.psum_scatter(jnp.concatenate(b[3:5], axis=0), "ctx", scatter_dimension=0, tiled=True)
                for b in backs
            ]
        )
    grad_tokens, part_one = in_back(
        info, x, dy, dl, dhq, dkin, dsq, rows, small, gate, h1k, l_own, l_got, h_own, h_got
    )
    widths = (heavy_qkv.shape[1], heavy_out.shape[1])
    vector = part_one + part_two
    if direct:
        half = width // 2
        mine = lax.dynamic_slice_in_dim(vector, side * half, half, 1)
        given = lax.dynamic_slice_in_dim(vector, (1 - side) * half, half, 1)
        got_two, mine, given = tied(got_two, mine, given)
        second = scatter_end(second, got_two)
        got_two = scatter_start(second, orders, 2)
        vector = mine + lax.ppermute(given, "wsh", swap)
        got_two, vector = tied(got_two, vector)
        second = scatter_end(second, got_two)
        got_two, got_vector = (scatter_start(second, orders, 3), flipped(vector, 1))
        got_two, vector, got_vector = tied(got_two, vector, got_vector)
        second, vector = (scatter_end(second, got_two), vector + got_vector)
        tails = [keep for keep, send in second]
        got_two, got_vector = (gather_start(tails, orders, 0), flipped(vector, 2))
        got_two, vector, got_vector = tied(got_two, vector, got_vector)
        tails, vector = (gather_end(tails, got_two), vector + got_vector)
        got_two, got_vector = (gather_start(tails, orders, 1), flipped(vector, 4))
        got_two, vector, got_vector = tied(got_two, vector, got_vector)
        tails, vector = (gather_end(tails, got_two), vector + got_vector)
        got_two, got_vector = (gather_start(tails, orders, 2), flipped(vector, 8))
        g_hdown = unpack_plane_dn(info, plane_full)
        got_two, vector, got_vector, g_hdown, plane_full = tied(got_two, vector, got_vector, g_hdown, plane_full)
        tails, vector = (gather_end(tails, got_two), vector + got_vector)
        got_two = gather_start(tails, orders, 3)
        g_hgu = unpack_plane_gu(info, plane_full, heavy_gu.shape[1] // (2 * COLS))
        got_two, g_hgu = tied(got_two, g_hgu)
        sums = list(zip(tails, got_two))
        g_hqkv, g_hout = unpack_units(info, orders[0], sums[0], 0, widths)
        g_lgu = unpack_gu(info, orders[1], sums[1], 0, 4, 4, 0, None, 4)
        g_lout = unpack_dn(info, orders[1], sums[1], 4, 1, 1, 0, None, 1)
        (g_lqkv,) = unpack_units(info, orders[2], sums[2], 0, (light_qkv.shape[1],))
        g_ldown = unpack_dn(info, orders[2], sums[2], 3, 2, 2, 0, None, 1)
    else:
        g_hqkv, g_hout = plain_units(ha_own, ha_send, widths)
        (g_lqkv,) = plain_units(la_own, la_send, (light_qkv.shape[1],))
        last = slice(ha_own.shape[0] - 1, ha_own.shape[0])
        g_lqkv, g_lout, g_hqkv, g_hout, g_lgu, g_ldown, g_hgu, g_hdown = plain_sum(
            [
                g_lqkv,
                plain_dn(ha_own[last], ha_send[last]),
                g_hqkv,
                g_hout,
                plain_gu(lgu_own, lgu_send),
                plain_dn(ldn_own, ldn_send),
                plain_gu(hgu_own, hgu_send),
                plain_dn(hdn_own, hdn_send),
            ]
        )
        vector = lax.psum(vector, ("ctx", "wsh"))
        part = width // groups
        vector = lax.dynamic_slice_in_dim(vector, lax.axis_index("wsh") * part, part, 1)
    return (
        out_tokens[:, None],
        grad_tokens[:, None],
        g_lqkv,
        g_lout,
        g_hqkv,
        g_hout,
        g_lgu,
        g_ldown,
        g_hgu,
        g_hdown,
        vector[:3],
        vector[3:5],
    )


def solution(mesh):
    return jax.shard_map(
        per_device,
        mesh=mesh,
        in_specs=(
            P(None, "wsh", "ctx", None),
            P(None, "wsh", "ctx", None),
            P("wsh", None),
            P("wsh", None),
            P("wsh", None),
            P("wsh", None),
            P("wsh", None),
            P("wsh", None),
            P("wsh", None),
            P("wsh", None),
            P(None, "wsh"),
            P(None, "wsh"),
            P(None, "wsh", None),
            P(None, "wsh", "ctx"),
            P(None, "wsh", "ctx"),
            P(None, "wsh", "ctx"),
        ),
        out_specs=(
            P(None, "wsh", "ctx", None),
            P(None, "wsh", "ctx", None),
            P("wsh", None),
            P("wsh", None),
            P("wsh", None),
            P("wsh", None),
            P("wsh", None),
            P("wsh", None),
            P("wsh", None),
            P("wsh", None),
            P(None, "wsh"),
            P(None, "wsh"),
        ),
        check_vma=False,
    )
```

```python
import functools

import jax
import jax.numpy as jnp
from jax import lax
from jax.experimental import pallas as pl
from jax.experimental.pallas import tpu as pltpu
from jax.sharding import PartitionSpec as P

HD = 64
WIN = 128
LANES = 128
COLS = 256
FAR = -1e30
EPS = 1e-06
BF = jnp.bfloat16
F32 = jnp.float32


def mm(left, right):
    return lax.dot_general(left, right, (((1,), (0,)), ((), ())), preferred_element_type=F32)


def mm_t(left, right):
    return lax.dot_general(left, right, (((1,), (1,)), ((), ())), preferred_element_type=F32)


def t_mm(left, right):
    return lax.dot_general(left, right, (((0,), (0,)), ((), ())), preferred_element_type=F32)


def pick(onehot, values):
    high = values.astype(BF)
    low = (values - high.astype(F32)).astype(BF)
    return mm(onehot, high) + mm(onehot, low)


def iota(shape, dim):
    return lax.broadcasted_iota(jnp.int32, shape, dim)


def onehot_cols(positions, base, length):
    return (iota((positions.shape[0], length), 1) == positions - base).astype(F32).astype(BF)


def onehot_rows(positions, base, length):
    return (iota((length, positions.shape[1]), 0) == positions - base).astype(F32).astype(BF)


def segment(info, micro, positions):
    total = jnp.full(positions.shape, -1, jnp.int32)
    for start in range(5):
        total += (positions >= info[4 + micro * 5 + start]).astype(jnp.int32)
    return total


def inverse_rms(values):
    return lax.rsqrt(jnp.mean(values * values, axis=-1, keepdims=True) + EPS)


def halves(info, values):
    half = values.shape[1] // 2
    first, second = (values[:, :half], values[:, half:])
    lower = info[0] == 0
    return (jnp.where(lower, first, second), jnp.where(lower, second, first))


def unhalved(info, own, other):
    lower = info[0] == 0
    return jnp.concatenate([jnp.where(lower, own, other), jnp.where(lower, other, own)], axis=1)


def call(body, outs, grid, in_specs, out_specs, args, scratch=(), flops=0, moved=0, limit=48, name=None):
    return pl.pallas_call(
        body,
        name=name or getattr(body, "__name__", "kernel"),
        out_shape=outs,
        grid_spec=pltpu.PrefetchScalarGridSpec(
            num_scalar_prefetch=1,
            grid=grid,
            in_specs=in_specs,
            out_specs=out_specs,
            scratch_shapes=list(scratch),
        ),
        compiler_params=pltpu.CompilerParams(vmem_limit_bytes=limit * 1024 * 1024),
        cost_estimate=pl.CostEstimate(flops=flops, bytes_accessed=moved, transcendentals=0),
    )(*args)


def whole(shape):
    rank = len(shape)
    return pl.BlockSpec(tuple(shape), lambda *unused: (0,) * rank)


def one_of(shape):
    rank = len(shape)
    return pl.BlockSpec((1,) + tuple(shape[1:]), lambda i, *unused: (i,) + (0,) * (rank - 1))


def sds(shape, dtype):
    return jax.ShapeDtypeStruct(tuple(shape), dtype)


def routed_body(info, x, cols, small, q_out, kin_out, h1k_out, gate_out):
    micros, tok, width = x.shape
    rows = cols.shape[2]
    base = info[1]
    gain = small[3:4].astype(F32)
    lane = iota((rows, LANES), 1)
    for m in range(micros):
        both = jnp.concatenate([cols[0, m], cols[1, m]], axis=0)
        got = mm(onehot_cols(both, base, tok), x[m])
        xq, xk = (got[:rows], got[rows:])
        low_q = (xq * inverse_rms(xq) * gain).astype(BF)
        h1k = xk * inverse_rms(xk) * gain
        low_k = h1k.astype(BF)
        gate_q = jax.nn.sigmoid(
            jnp.sum(low_q.astype(F32) * small[0:1].astype(F32), axis=-1, keepdims=True)
        )
        gate_k = jax.nn.sigmoid(
            jnp.sum(low_k.astype(F32) * small[1:2].astype(F32), axis=-1, keepdims=True)
        )
        seg_q = segment(info, m, cols[0, m])
        seg_k = segment(info, m, cols[1, m])
        q_out[m, :, :width] = low_q
        q_out[m, :, width:] = (lane == seg_q).astype(F32).astype(BF)
        kin_out[m, :, :width] = (h1k * gate_k).astype(BF)
        kin_out[m, :, width:] = jnp.where((lane < 8) & (lane != seg_k), FAR, 0.0).astype(BF)
        h1k_out[m] = h1k
        gate_out[m] = jnp.where(lane == 0, gate_q, gate_k)


def routed_in(info, x, cols, small):
    micros, unused, width = x.shape
    rows = cols.shape[2]
    shapes = [
        sds((micros, rows, width + LANES), BF),
        sds((micros, rows, width + LANES), BF),
        sds((micros, rows, width), F32),
        sds((micros, rows, LANES), F32),
    ]
    args = (info, x, cols, small)
    return call(
        routed_body,
        shapes,
        (1,),
        [whole(a.shape) for a in args[1:]],
        [whole(s.shape) for s in shapes],
        args,
        flops=200_000_000,
        moved=3_000_000,
    )


def query_body(info, low, w_own, w_got, out):
    width = 2 * w_own.shape[0]
    for m in range(low.shape[0]):
        own, other = halves(info, low[m, :, :width])
        out[m, :, :width] = (mm(own, w_own[...]) + mm(other, w_got[...])).astype(BF)
        out[m, :, width:] = low[m, :, width:]


def query_project(info, low, w_own, w_got):
    half = w_own.shape[0]
    return call(
        query_body,
        sds(low.shape, BF),
        (1,),
        [whole(low.shape)] + [whole((half, 2 * half))] * 2,
        whole(low.shape),
        (info, low, w_own, w_got),
        flops=2 * low.shape[0] * low.shape[1] * 4 * half * half,
        moved=2_000_000,
    )


def light_in_body(info, x, small, w_own, w_got, out):
    values = x[0].astype(F32)
    low = (values * inverse_rms(values) * small[3:4].astype(F32)).astype(BF)
    own, other = halves(info, low)
    out[0] = (mm(own, w_own[...]) + mm(other, w_got[...])).astype(BF)


def light_in(info, x, small, w_own, w_got):
    micros, tok, width = x.shape
    columns = w_own.shape[1]
    split = 2
    rows = tok // split
    spec = lambda n: pl.BlockSpec((1, rows, n), lambda i, *u: (i // split, i % split, 0))
    return call(
        light_in_body,
        sds((micros, tok, columns), BF),
        (micros * split,),
        [spec(width), whole(small.shape), whole(w_own.shape), whole(w_got.shape)],
        spec(columns),
        (info, x, small, w_own, w_got),
        flops=2 * micros * tok * width * columns,
        moved=8_000_000,
    )


def fill_near(near, qkv, before, after):
    tok = qkv.shape[1]
    inner = near.shape[1] // 2
    near[:WIN] = before[0]
    near[WIN : WIN + tok] = qkv[0, :, inner:]
    near[WIN + tok :] = after[0]


def light_bias(info, micro, block):
    start = info[1] + block * WIN
    rows, columns = (WIN, 3 * WIN)
    row_pos = start + iota((rows, 1), 0)
    col_pos = start - WIN + iota((1, columns), 1)
    seg_row = segment(info, micro, row_pos)
    seg_col = jnp.where((col_pos >= 0) & (col_pos < info[2]), segment(info, micro, col_pos), -1)
    shift = iota((rows, columns), 0) + WIN - iota((rows, columns), 1)
    allowed = (jnp.abs(shift) < WIN) & (seg_row == seg_col)
    bias = jnp.where(allowed, 0.0, FAR)
    return jnp.concatenate([bias, bias], axis=0)


def stacked(pair, low_lane):
    zero = jnp.zeros_like(pair)
    return jnp.concatenate(
        [jnp.where(low_lane, pair, zero), jnp.where(low_lane, zero, pair)], axis=0
    )


def merged(values, low_lane):
    rows = values.shape[0] // 2
    return jnp.where(low_lane, values[:rows], values[rows:])


def light_fwd_blocks(info, qkv, near, blocks, emit):
    micro = pl.program_id(0)
    inner = near.shape[1] // 2
    low_lane = iota((WIN, LANES), 1) < HD
    lane = iota((WIN, LANES), 1)
    for place, block in enumerate(blocks):
        at = slice(block * WIN, (block + 1) * WIN)
        around = slice(block * WIN, (block + 3) * WIN)
        bias = light_bias(info, micro, block)
        stats = jnp.zeros((WIN, LANES), F32)
        for pair in range(inner // LANES):
            cut = slice(pair * LANES, (pair + 1) * LANES)
            query = stacked(qkv[0, at, cut] * BF(HD**-0.5), low_lane)
            scores = mm_t(query, near[around, cut]) + bias
            top = jnp.max(scores, axis=-1, keepdims=True)
            weights = jnp.exp(scores - top)
            total = jnp.sum(weights, axis=-1, keepdims=True)
            value = near[around, inner + pair * LANES : inner + (pair + 1) * LANES]
            mixed = mm((weights * (1.0 / total)).astype(BF), value)
            emit(place, cut, merged(mixed, low_lane).astype(BF))
            lse = top + jnp.log(total)
            stats = jnp.where(lane == 2 * pair, lse[:WIN], stats)
            stats = jnp.where(lane == 2 * pair + 1, lse[WIN:], stats)
        emit(place, None, stats)


def light_inner_body(info, qkv, out, lse_out, near):
    tok = qkv.shape[1]
    inner = out.shape[2]
    near[WIN : WIN + tok] = qkv[0, :, inner:]

    def emit(place, cut, value):
        rows = slice(place * WIN, (place + 1) * WIN)
        if cut is None:
            lse_out[0, rows] = value
        else:
            out[0, rows, cut] = value

    light_fwd_blocks(info, qkv, near, range(1, tok // WIN - 1), emit)


def light_outer_body(info, qkv, before, after, done, lse_done, out, lse_out, near):
    tok = qkv.shape[1]
    fill_near(near, qkv, before, after)
    out[0, WIN : tok - WIN] = done[0]
    lse_out[0, WIN : tok - WIN] = lse_done[0]
    blocks = (0, tok // WIN - 1)

    def emit(place, cut, value):
        rows = slice(blocks[place] * WIN, (blocks[place] + 1) * WIN)
        if cut is None:
            lse_out[0, rows] = value
        else:
            out[0, rows, cut] = value

    light_fwd_blocks(info, qkv, near, blocks, emit)


def light_inner(info, qkv):
    micros, tok, columns = qkv.shape
    inner = columns // 3
    shapes = [sds((micros, tok - 2 * WIN, inner), BF), sds((micros, tok - 2 * WIN, LANES), F32)]
    return call(
        light_inner_body,
        shapes,
        (micros,),
        [one_of(qkv.shape)],
        [one_of(a.shape) for a in shapes],
        (info, qkv),
        scratch=[pltpu.VMEM((tok + 2 * WIN, 2 * inner), BF)],
        flops=2_000_000_000,
        moved=4_000_000,
    )


def light_outer(info, qkv, before, after, done):
    micros, tok, columns = qkv.shape
    inner = columns // 3
    shapes = [sds((micros, tok, inner), BF), sds((micros, tok, LANES), F32)]
    args = (info, qkv, before, after, *done)
    return call(
        light_outer_body,
        shapes,
        (micros,),
        [one_of(a.shape) for a in args[1:]],
        [one_of(a.shape) for a in shapes],
        args,
        scratch=[pltpu.VMEM((tok + 2 * WIN, 2 * inner), BF)],
        flops=2_000_000_000,
        moved=6_000_000,
    )


def light_bwd_blocks(info, qkv, lse, grad, near, dk, dv, blocks, emit):
    micro = pl.program_id(0)
    inner = grad.shape[2]
    low_lane = iota((WIN, LANES), 1) < HD
    for place, block in enumerate(blocks):
        at = slice(block * WIN, (block + 1) * WIN)
        around = slice(block * WIN, (block + 3) * WIN)
        bias = light_bias(info, micro, block)
        stats = lse[0, at, :]
        for pair in range(inner // LANES):
            cut = slice(pair * LANES, (pair + 1) * LANES)
            query = stacked(qkv[0, at, cut] * BF(HD**-0.5), low_lane)
            key = near[around, cut]
            value = near[around, inner + pair * LANES : inner + (pair + 1) * LANES]
            shift = jnp.concatenate(
                [stats[:, 2 * pair : 2 * pair + 1], stats[:, 2 * pair + 1 : 2 * pair + 2]], axis=0
            )
            probs = jnp.exp(mm_t(query, key) + bias - shift)
            upper = stacked(grad[0, at, cut], low_lane)
            grad_probs = mm_t(upper, value)
            center = jnp.sum(probs * grad_probs, axis=-1, keepdims=True)
            slope = (probs * (grad_probs - center)).astype(BF)
            emit(place, cut, (merged(mm(slope, key), low_lane) * HD**-0.5).astype(BF))
            dk[around, cut] += t_mm(slope, query)
            dv[around, cut] += t_mm(probs.astype(BF), upper)


def light_bwd_outer_body(info, qkv, before, after, lse, grad, dq_out, own_out, low_out, high_out, near, dk, dv):
    tok = qkv.shape[1]
    inner = grad.shape[2]
    fill_near(near, qkv, before, after)
    dk[...] = jnp.zeros_like(dk)
    dv[...] = jnp.zeros_like(dv)

    def emit(place, cut, value):
        dq_out[0, place * WIN : (place + 1) * WIN, cut] = value

    light_bwd_blocks(info, qkv, lse, grad, near, dk, dv, (0, tok // WIN - 1), emit)
    for first, source in ((0, dk), (inner, dv)):
        to = slice(first, first + inner)
        own_out[0, :, to] = source[WIN : WIN + tok]
        low_out[0, :, to] = source[:WIN].astype(BF)
        high_out[0, :, to] = source[WIN + tok :].astype(BF)


def light_bwd_inner_body(info, qkv, lse, grad, dq_in, own_in, dq_out, own_out, near, dk, dv):
    tok = qkv.shape[1]
    inner = grad.shape[2]
    near[WIN : WIN + tok] = qkv[0, :, inner:]
    dk[WIN : WIN + tok] = own_in[0, :, :inner]
    dv[WIN : WIN + tok] = own_in[0, :, inner:]
    dq_out[0, :WIN] = dq_in[0, :WIN]
    dq_out[0, tok - WIN :] = dq_in[0, WIN:]
    blocks = range(1, tok // WIN - 1)

    def emit(place, cut, value):
        dq_out[0, blocks[place] * WIN : (blocks[place] + 1) * WIN, cut] = value

    light_bwd_blocks(info, qkv, lse, grad, near, dk, dv, blocks, emit)
    own_out[0, :, :inner] = dk[WIN : WIN + tok]
    own_out[0, :, inner:] = dv[WIN : WIN + tok]


def light_bwd_scratch(tok, inner):
    return [
        pltpu.VMEM((tok + 2 * WIN, 2 * inner), BF),
        pltpu.VMEM((tok + 2 * WIN, inner), F32),
        pltpu.VMEM((tok + 2 * WIN, inner), F32),
    ]


def light_bwd_outer(info, qkv, before, after, lse, grad):
    micros, tok, columns = qkv.shape
    inner = columns // 3
    shapes = [
        sds((micros, 2 * WIN, inner), BF),
        sds((micros, tok, 2 * inner), F32),
        sds((micros, WIN, 2 * inner), BF),
        sds((micros, WIN, 2 * inner), BF),
    ]
    args = (info, qkv, before, after, lse, grad)
    return call(
        light_bwd_outer_body,
        shapes,
        (micros,),
        [one_of(a.shape) for a in args[1:]],
        [one_of(a.shape) for a in shapes],
        args,
        scratch=light_bwd_scratch(tok, inner),
        flops=5_000_000_000,
        moved=12_000_000,
    )


def light_bwd_inner(info, qkv, lse, grad, dq, own):
    micros, tok, columns = qkv.shape
    inner = columns // 3
    shapes = [sds((micros, tok, inner), BF), sds((micros, tok, 2 * inner), F32)]
    args = (info, qkv, lse, grad, dq, own)
    return call(
        light_bwd_inner_body,
        shapes,
        (micros,),
        [one_of(a.shape) for a in args[1:]],
        [one_of(a.shape) for a in shapes],
        args,
        scratch=light_bwd_scratch(tok, inner),
        flops=5_000_000_000,
        moved=14_000_000,
    )


def key_body(info, kin, w_own, w_got, out):
    half = w_own.shape[0]
    width = 2 * half
    own = kin[:, pl.ds(pl.multiple_of(info[0] * half, half), half)]
    other = kin[:, pl.ds(pl.multiple_of((1 - info[0]) * half, half), half)]
    out[...] = (mm(own, w_own[:, width:]) + mm(other, w_got[:, width:])).astype(BF)


def key_project(info, kin, w_own, w_got):
    shape = sds((kin.shape[0], 2 * (kin.shape[1] - LANES)), BF)
    args = (info, kin, w_own, w_got)
    return call(
        key_body,
        shape,
        (1,),
        [whole(a.shape) for a in args[1:]],
        whole(shape.shape),
        args,
        flops=1_200_000_000,
        moved=6_000_000,
    )


def heavy_scores(query, parts, bias, cut):
    return [mm_t(query, part[:, cut]) + b for part, b in zip(parts, bias)]


def heavy_fwd_body(info, q, kin_a, kin_b, kv_a, kv_b, out, lse_out):
    rows, width = out.shape
    parts = (kv_a, kv_b)
    low_lane = iota((rows, LANES), 1) < HD
    lane = iota((rows, LANES), 1)
    feature = jnp.concatenate([q[:, width:]] * 2, axis=0)
    bias = [mm_t(feature, kin[:, width:]) for kin in (kin_a, kin_b)]
    stats = jnp.zeros((rows, LANES), F32)
    for pair in range(width // LANES):
        cut = slice(pair * LANES, (pair + 1) * LANES)
        query = stacked(q[:, cut] * BF(HD**-0.5), low_lane)
        scores = heavy_scores(query, parts, bias, cut)
        top = functools.reduce(
            jnp.maximum, [jnp.max(s, axis=-1, keepdims=True) for s in scores]
        )
        weights = [jnp.exp(s - top) for s in scores]
        total = sum(jnp.sum(w, axis=-1, keepdims=True) for w in weights)
        scale = 1.0 / total
        mixed = sum(
            mm((w * scale).astype(BF), part[:, width + pair * LANES : width + (pair + 1) * LANES])
            for w, part in zip(weights, parts)
        )
        out[:, cut] = merged(mixed, low_lane).astype(BF)
        lse = top + jnp.log(total)
        stats = jnp.where(lane == 2 * pair, lse[:rows], stats)
        stats = jnp.where(lane == 2 * pair + 1, lse[rows:], stats)
    lse_out[...] = stats


def heavy_fwd(info, q, kins, kvs):
    rows = q.shape[0]
    width = q.shape[1] - LANES
    shapes = [sds((rows, width), BF), sds((rows, LANES), F32)]
    args = (info, q, *kins, *kvs)
    return call(
        heavy_fwd_body,
        shapes,
        (1,),
        [whole(a.shape) for a in args[1:]],
        [whole(s.shape) for s in shapes],
        args,
        flops=1_500_000_000,
        moved=5_000_000,
    )


def heavy_bwd_body(info, q, kin_a, kin_b, kv_a, kv_b, lse, grad, w_own, w_got, dq_out, da_out, db_out, ia_out, ib_out):
    rows, width = grad.shape
    parts = (kv_a, kv_b)
    low_lane = iota((rows, LANES), 1) < HD
    feature = jnp.concatenate([q[:, width:]] * 2, axis=0)
    bias = [mm_t(feature, kin[:, width:]) for kin in (kin_a, kin_b)]
    for pair in range(width // LANES):
        cut = slice(pair * LANES, (pair + 1) * LANES)
        upcut = slice(width + pair * LANES, width + (pair + 1) * LANES)
        query = stacked(q[:, cut] * BF(HD**-0.5), low_lane)
        shift = jnp.concatenate(
            [lse[:, 2 * pair : 2 * pair + 1], lse[:, 2 * pair + 1 : 2 * pair + 2]], axis=0
        )
        probs = [jnp.exp(s - shift) for s in heavy_scores(query, parts, bias, cut)]
        upper = stacked(grad[:, cut], low_lane)
        grads = [mm_t(upper, part[:, upcut]) for part in parts]
        center = sum(jnp.sum(p * g, axis=-1, keepdims=True) for p, g in zip(probs, grads))
        slopes = [(p * (g - center)).astype(BF) for p, g in zip(probs, grads)]
        dq = sum(mm(s, part[:, cut]) for s, part in zip(slopes, parts))
        dq_out[:, cut] = (merged(dq, low_lane) * HD**-0.5).astype(BF)
        for target, slope, prob in zip((da_out, db_out), slopes, probs):
            target[:, cut] = t_mm(slope, query).astype(BF)
            target[:, upcut] = t_mm(prob.astype(BF), upper).astype(BF)
    half = width // 2
    for target, source in ((ia_out, da_out), (ib_out, db_out)):
        for weight, side in ((w_own, info[0]), (w_got, 1 - info[0])):
            target[:, pl.ds(pl.multiple_of(side * half, half), half)] = mm_t(
                source[...], weight[:, width:]
            ).astype(BF)


def heavy_bwd(info, q, kins, kvs, lse, grad, w_own, w_got):
    rows = q.shape[0]
    width = q.shape[1] - LANES
    keys = kvs[0].shape[0]
    shapes = [sds((rows, width), BF)] + [sds((keys, 2 * width), BF)] * 2 + [sds((keys, width), BF)] * 2
    args = (info, q, *kins, *kvs, lse, grad, w_own, w_got)
    return call(
        heavy_bwd_body,
        shapes,
        (1,),
        [whole(a.shape) for a in args[1:]],
        [whole(s.shape) for s in shapes],
        args,
        flops=6_500_000_000,
        moved=15_000_000,
    )


def heavy_grads_body(info, *refs):
    micros = (len(refs) - 8) // 4
    hq, dhq, ho, dhy, lo, dy = refs[:6]
    kins, dkvs = (refs[6 : 6 + 2 * micros], refs[6 + 2 * micros : -2])
    other_out, own_out = (refs[-1], refs[-2])
    half = hq.shape[2] // 2
    every = range(micros)
    for target, side in ((other_out, 1 - info[0]), (own_out, info[0])):
        cut = pl.ds(pl.multiple_of(side * half, half), half)

        def put(unit, left, right, columns):
            for block in range(columns // COLS):
                at = unit + block
                total = sum(
                    t_mm(a, b[:, block * COLS : (block + 1) * COLS]) for a, b in zip(left, right)
                )
                target[at // 2, (at % 2) * half : (at % 2 + 1) * half] = total.astype(BF)
            return unit + columns // COLS

        unit = put(0, [hq[m, :, cut] for m in every], [dhq[m] for m in every], dhq.shape[2])
        unit = put(unit, [kin[:, cut] for kin in kins], dkvs, dkvs[0].shape[1])
        unit = put(unit, [ho[m, :, cut] for m in every], [dhy[m] for m in every], dhy.shape[2])
        part = lo.shape[2] // 2
        small_cut = pl.ds(pl.multiple_of(side * part, part), part)
        total = sum(t_mm(lo[m, :, small_cut], dy[m].astype(BF)) for m in every)
        pack_rows(target.at[pl.ds(unit // 2, 1)], total)


def heavy_grads(info, hq, dhq, ho, dhy, lo, dy, kins, dkvs):
    width = dhq.shape[2]
    units = (dhq.shape[2] + dkvs[0].shape[1] + dhy.shape[2]) // COLS
    shapes = [sds((units // 2 + 1, width, COLS), BF)] * 2
    args = (info, hq, dhq, ho, dhy, lo, dy, *kins, *dkvs)
    return call(
        heavy_grads_body,
        shapes,
        (1,),
        [whole(dhq.shape)] + [whole(a.shape) for a in args[2:]],
        [whole(s.shape) for s in shapes],
        args,
        flops=6_500_000_000,
        moved=28_000_000,
    )


def middle_body(info, x, up, cols, rows, small, gate, lo, lout, lout_got, ho, hout, y_out, low_out, pay_out, hy_out, gf_out):
    tok = x.shape[1]
    base = info[1]
    hy = mm(ho[0], hout[...])
    hy_out[0] = hy
    spread = onehot_rows(rows[0, 0], base, tok)
    part = lout.shape[0]
    own = lo[0, :, pl.ds(pl.multiple_of(info[0] * part, part), part)]
    other = lo[0, :, pl.ds(pl.multiple_of((1 - info[0]) * part, part), part)]
    light = mm(own, lout[...]) + mm(other, lout_got[...])
    y = x[0].astype(F32) + light + pick(spread, hy * gate[0, :, 0:1])
    y_out[0] = y
    low = (y * inverse_rms(y) * small[4:5].astype(F32)).astype(BF)
    low_out[0] = low
    take = onehot_cols(cols[2, 0], base, tok)
    taken = mm(take, low)
    width = x.shape[2]
    pay_out[0, :, :width] = taken.astype(BF)
    gf = jax.nn.sigmoid(jnp.sum(taken * small[2:3].astype(F32), axis=-1, keepdims=True))
    pay_out[0, :, width:] = (mm(take, up[0]) * gf).astype(BF)
    gf_out[0] = jnp.broadcast_to(gf, gf_out.shape[1:])


def second_of(shape):
    rank = len(shape)
    return pl.BlockSpec(
        (shape[0], 1) + tuple(shape[2:]), lambda i, *unused: (0, i) + (0,) * (rank - 2)
    )


def middle(info, x, up, cols, rows, small, gate, lo, lout, lout_got, ho, hout):
    micros, tok, width = x.shape
    count = cols.shape[2]
    shapes = [
        sds((micros, tok, width), F32),
        sds((micros, tok, width), BF),
        sds((micros, count, 2 * width), BF),
        sds((micros, count, width), F32),
        sds((micros, count, LANES), F32),
    ]
    args = (info, x, up, cols, rows, small, gate, lo, lout, lout_got, ho, hout)
    return call(
        middle_body,
        shapes,
        (micros,),
        [
            one_of(x.shape),
            one_of(up.shape),
            second_of(cols.shape),
            second_of(rows.shape),
            whole(small.shape),
            one_of(gate.shape),
            one_of(lo.shape),
            whole(lout.shape),
            whole(lout_got.shape),
            one_of(ho.shape),
            whole(hout.shape),
        ],
        [one_of(s.shape) for s in shapes],
        args,
        flops=2_000_000_000,
        moved=12_000_000,
    )


def pack_rows(target, values):
    step = values.shape[0] // 16
    cuts = values.shape[1] // COLS
    for slot in range(16):
        for cut in range(cuts):
            at = slot * step * cuts + cut * step
            target[0, at : at + step] = values[
                slot * step : (slot + 1) * step, cut * COLS : (cut + 1) * COLS
            ].astype(BF)


def gelu_parts(g):
    root = (2.0 / 3.141592653589793) ** 0.5
    square = g * g
    tanh = jnp.tanh(root * g * (1.0 + 0.044715 * square))
    bell = 0.5 * (1.0 + tanh)
    slope = bell + 0.5 * g * (1.0 - tanh * tanh) * (root * (1.0 + 3 * 0.044715 * square))
    return (g * bell, slope)


def hidden_both_ways(low, upstream, wg, wu, wd):
    g, u = (mm(low, wg), mm(low, wu))
    back = mm_t(upstream, wd)
    gelu, slope = gelu_parts(g)
    return ((gelu * u).astype(BF), (back * u * slope).astype(BF), (back * gelu).astype(BF))


def add_steps(step, pairs):
    @pl.when(step == 0)
    def first():
        for target, value in pairs:
            target[...] = value

    @pl.when(step > 0)
    def later():
        for target, value in pairs:
            target[...] += value


def ffn_local_body(info, a, ct, wg, wu, wd, z_out, dh_out):
    hidden, dg, du = hidden_both_ways(a[...], ct[...], wg[...], wu[...], wd[...])
    z = mm(hidden, wd[...])
    dh = mm_t(dg, wg[...]) + mm_t(du, wu[...])
    add_steps(pl.program_id(0), [(z_out, z), (dh_out, dh)])


def ffn_body(info, a, ct, wg, wu, wd, z_out, dh_out, own_gu, other_gu, own_dn, other_dn):
    step = pl.program_id(0)
    half = pl.num_programs(0) // 2
    width = a.shape[1] // 2
    hidden, dg, du = hidden_both_ways(a[...], ct[...], wg[...], wu[...], wd[...])
    z = mm(hidden, wd[...])
    dh = mm_t(dg, wg[...]) + mm_t(du, wu[...])
    add_steps(step, [(z_out, z), (dh_out, dh)])
    down = t_mm(hidden, ct[...])

    @pl.when(step < half)
    def send():
        pack_rows(other_dn, down)

    @pl.when(step >= half)
    def keep():
        pack_rows(own_dn, down)

    own = a[:, pl.ds(pl.multiple_of(info[0] * width, width), width)]
    other = a[:, pl.ds(pl.multiple_of((1 - info[0]) * width, width), width)]
    own_gu[0, :width] = t_mm(own, dg).astype(BF)
    own_gu[0, width:] = t_mm(own, du).astype(BF)
    other_gu[0, :width] = t_mm(other, dg).astype(BF)
    other_gu[0, width:] = t_mm(other, du).astype(BF)


def ffn_local(info, pay, w_gu, w_down, block):
    rows = pay.shape[0]
    hidden, width = w_down.shape
    steps = hidden // block
    return call(
        ffn_local_body,
        [sds((rows, width), F32)] * 2,
        (steps,),
        [
            pl.BlockSpec((rows, width), lambda i, *u: (0, 0)),
            pl.BlockSpec((rows, width), lambda i, *u: (0, 1)),
            pl.BlockSpec((width, block), lambda i, *u: (0, i)),
            pl.BlockSpec((width, block), lambda i, *u: (0, steps + i)),
            pl.BlockSpec((block, width), lambda i, *u: (i, 0)),
        ],
        [whole((rows, width))] * 2,
        (info, pay, pay, w_gu, w_gu, w_down),
        flops=2 * 6 * rows * hidden * width,
        moved=2 * 3 * hidden * width,
    )


def ffn(info, a, ct, w_gu, w_down):
    rows, width = a.shape
    hidden = w_down.shape[0]
    block = COLS
    steps = hidden // block
    half = steps // 2

    def natural(i, info):
        return jnp.where(i < half, (1 - info[0]) * half + i, info[0] * half + i - half)

    unit = (1, width, COLS)
    shapes = [
        sds((rows, width), F32),
        sds((rows, width), F32),
        sds((steps,) + unit[1:], BF),
        sds((steps,) + unit[1:], BF),
        sds((half,) + unit[1:], BF),
        sds((half,) + unit[1:], BF),
    ]
    return call(
        ffn_body,
        shapes,
        (steps,),
        [
            whole(a.shape),
            whole(ct.shape),
            pl.BlockSpec((width, block), lambda i, info: (0, natural(i, info))),
            pl.BlockSpec((width, block), lambda i, info: (0, steps + natural(i, info))),
            pl.BlockSpec((block, width), lambda i, info: (natural(i, info), 0)),
        ],
        [
            whole((rows, width)),
            whole((rows, width)),
            pl.BlockSpec(unit, lambda i, info: (natural(i, info), 0, 0)),
            pl.BlockSpec(unit, lambda i, info: (natural(i, info), 0, 0)),
            pl.BlockSpec(unit, lambda i, info: (jnp.maximum(i - half, 0), 0, 0)),
            pl.BlockSpec(unit, lambda i, info: (jnp.minimum(i, half - 1), 0, 0)),
        ],
        (info, a, ct, w_gu, w_gu, w_down),
        flops=2 * 9 * rows * hidden * width,
        moved=2 * 2 * 3 * hidden * width + rows * width * 12,
    )


def ffn_all_body(info, a, ct, w_gu, w_down, z_out, dh_out, own_gu, other_gu, own_dn, other_dn, turned, hid, slopes):
    step = pl.program_id(0)
    hidden, whole_width = w_down.shape
    steps = hidden // COLS
    half = steps // 2
    width = whole_width // 2

    @pl.when(step == 0)
    def turn():
        turned[...] = a[...].T

    @pl.when(step < steps)
    def block():
        at = jnp.where(step < half, (1 - info[0]) * half + step, info[0] * half + step - half)
        gate = pl.ds(pl.multiple_of(at * COLS, COLS), COLS)
        upper = pl.ds(pl.multiple_of(hidden + at * COLS, COLS), COLS)
        mixed, dg, du = hidden_both_ways(a[...], ct[...], w_gu[:, gate], w_gu[:, upper], w_down[gate])
        hid[:, gate] = mixed
        slopes[:, gate] = dg
        slopes[:, upper] = du
        down = t_mm(mixed, ct[...])

        @pl.when(step < half)
        def send():
            pack_rows(other_dn, down)

        @pl.when(step >= half)
        def keep():
            pack_rows(own_dn, down)

        for target, side in ((own_gu, info[0]), (other_gu, 1 - info[0])):
            rows = turned[pl.ds(pl.multiple_of(side * width, width), width)]
            target[0, :width] = mm(rows, dg).astype(BF)
            target[0, width:] = mm(rows, du).astype(BF)

    @pl.when(step == steps)
    def last():
        z_out[...] = mm(hid[...], w_down[...]).astype(BF)
        dh_out[...] = mm_t(slopes[...], w_gu[...]).astype(BF)


def ffn_all(info, a, ct, w_gu, w_down):
    rows, width = a.shape
    hidden = w_down.shape[0]
    steps = hidden // COLS
    half = steps // 2

    def natural(i, info):
        return jnp.where(i < half, (1 - info[0]) * half + i, info[0] * half + jnp.minimum(i - half, half - 1))

    unit = (1, width, COLS)
    shapes = [
        sds((rows, width), BF),
        sds((rows, width), BF),
        sds((steps,) + unit[1:], BF),
        sds((steps,) + unit[1:], BF),
        sds((half,) + unit[1:], BF),
        sds((half,) + unit[1:], BF),
    ]
    return call(
        ffn_all_body,
        shapes,
        (steps + 1,),
        [whole(a.shape), whole(ct.shape), whole(w_gu.shape), whole(w_down.shape)],
        [
            whole((rows, width)),
            whole((rows, width)),
            pl.BlockSpec(unit, lambda i, info: (natural(i, info), 0, 0)),
            pl.BlockSpec(unit, lambda i, info: (natural(i, info), 0, 0)),
            pl.BlockSpec(unit, lambda i, info: (jnp.minimum(jnp.maximum(i - half, 0), half - 1), 0, 0)),
            pl.BlockSpec(unit, lambda i, info: (jnp.minimum(i, half - 1), 0, 0)),
        ],
        (info, a, ct, w_gu, w_down),
        scratch=[
            pltpu.VMEM((width, rows), BF),
            pltpu.VMEM((rows, hidden), BF),
            pltpu.VMEM((rows, 2 * hidden), BF),
        ],
        flops=2 * 9 * rows * hidden * width,
        moved=2 * 2 * 3 * hidden * width + rows * width * 12,
    )


def plane_grads_body(info, near, far, wg, wu, wd, own_gu, other_gu, dn):
    width = wg.shape[0]
    half = width // 2
    sums = None
    for part in (near, far):
        low, upstream = (part[:, :width], part[:, width:])
        hidden, dg, du = hidden_both_ways(low, upstream, wg[...], wu[...], wd[...])
        own = part[:, pl.ds(pl.multiple_of(info[0] * half, half), half)]
        other = part[:, pl.ds(pl.multiple_of((1 - info[0]) * half, half), half)]
        terms = (t_mm(own, dg), t_mm(own, du), t_mm(other, dg), t_mm(other, du), t_mm(hidden, upstream))
        sums = terms if sums is None else tuple(p + q for p, q in zip(sums, terms))
    own_gu[0, :half] = sums[0].astype(BF)
    own_gu[0, half:] = sums[1].astype(BF)
    other_gu[0, :half] = sums[2].astype(BF)
    other_gu[0, half:] = sums[3].astype(BF)
    for cut in range(width // COLS):
        dn[0, cut * COLS : (cut + 1) * COLS] = sums[4][:, cut * COLS : (cut + 1) * COLS].astype(BF)


def plane_grads(info, near, far, w_gu, w_down):
    hidden, width = w_down.shape
    steps = hidden // COLS
    turns = steps // 8

    def block(i, info):
        return info[0] * (steps // 2) + lax.rem(info[3], 4) * turns + i

    unit = (1, width, COLS)
    spec = pl.BlockSpec(unit, lambda i, *u: (i, 0, 0))
    rows = 2 * near.shape[0]
    return call(
        plane_grads_body,
        [sds((turns, width, COLS), BF)] * 3,
        (turns,),
        [
            whole(near.shape),
            whole(far.shape),
            pl.BlockSpec((width, COLS), lambda i, info: (0, block(i, info))),
            pl.BlockSpec((width, COLS), lambda i, info: (0, steps + block(i, info))),
            pl.BlockSpec((COLS, width), lambda i, info: (block(i, info), 0)),
        ],
        [spec] * 3,
        (info, near, far, w_gu, w_gu, w_down),
        flops=2 * 6 * rows * turns * COLS * width,
        moved=9_000_000,
    )


def column_fold_body(order, info, first, second, third, keep, send):
    slots = 1 << len(order)
    size = keep.shape[2]
    place_z = info[3] // 4
    for part, source in enumerate((first, second, third)):
        for block in range(source.shape[0]):
            for slot in range(slots):
                owner = jnp.bitwise_xor(place_z, mask_of(slot, order))
                at = pl.ds(pl.multiple_of(owner * size, size), size)
                target = keep if slot < slots // 2 else send
                target[slot % (slots // 2), part * source.shape[0] + block] = source[block, at, :]


def column_fold(info, order, sources):
    slots = 1 << len(order)
    blocks, width, cols = sources[0].shape
    shape = sds((slots // 2, 3 * blocks, width // slots, cols), BF)
    return call(
        functools.partial(column_fold_body, order),
        [shape, shape],
        (1,),
        [whole(a.shape) for a in sources],
        [whole(shape.shape)] * 2,
        (info, *sources),
        moved=10_000_000,
        name="column_fold",
    )


def mid_back_body(
    info, y, up, z, dh2, zh, dff, ffr, gf, cols, rows, small, gate, lout, lout_got, hout, hy, hq,
    out, dy_out, dlo_out, dho_out, dhy_out, dsq_out, part_out,
):
    tok = y.shape[1]
    base = info[1]
    micro = pl.program_id(0)
    spread = onehot_rows(rows[2, 0], base, tok)
    take = onehot_cols(cols[2, 0], base, tok)
    values, top = (y[0], up[0].astype(F32))
    open_f = gf[0, :, 0:1]
    zhv = zh[0]
    out[0] = (values + z[0].astype(F32) + pick(spread, zhv * open_f)).astype(BF)
    taken = mm(take, up[0])
    dsf = jnp.sum(taken * zhv, axis=-1, keepdims=True) * open_f * (1.0 - open_f)
    back = dh2[0].astype(F32) + pick(spread, dff[0] + dsf * small[2:3].astype(F32))
    inv = inverse_rms(values)
    scaled = back * small[4:5].astype(F32)
    mean = jnp.mean(values * scaled, axis=-1, keepdims=True)
    dy = top + inv * scaled - values * (inv * inv * inv * mean)
    dy_out[0] = dy
    dgain = jnp.sum(back * values * inv, axis=0, keepdims=True)
    drf = jnp.sum(dsf * ffr[0].astype(F32), axis=0, keepdims=True)
    part_in = lout.shape[0]
    for weight, side in ((lout, info[0]), (lout_got, 1 - info[0])):
        at = pl.ds(pl.multiple_of(side * part_in, part_in), part_in)
        dlo_out[0, :, at] = mm_t(dy.astype(BF), weight[...]).astype(BF)
    dyq = pick(onehot_cols(cols[0, 0], base, tok), dy)
    open_q = gate[0, :, 0:1]
    dhy = (dyq * open_q).astype(BF)
    dhy_out[0] = dhy
    dsq = jnp.sum(dyq * hy[0], axis=-1, keepdims=True) * open_q * (1.0 - open_q)
    dsq_out[0] = jnp.broadcast_to(dsq, dsq_out.shape[1:])
    drq = jnp.sum(dsq * hq[0].astype(F32), axis=0, keepdims=True)
    dho_out[0] = mm_t(dhy, hout[...]).astype(BF)
    row = iota(part_out.shape, 0)
    part = jnp.where(row == 0, drq, jnp.where(row == 2, drf, jnp.where(row == 4, dgain, 0.0)))

    @pl.when(micro == 0)
    def first():
        part_out[...] = part

    @pl.when(micro > 0)
    def later():
        part_out[...] += part


def mid_back(info, y, up, z, dh2, zh, dff, ffr, gf, cols, rows, small, gate, lout, lout_got, hout, hy, hq):
    micros, tok, width = y.shape
    count = cols.shape[2]
    shapes = [
        sds((micros, tok, width), BF),
        sds((micros, tok, width), F32),
        sds((micros, tok, 2 * lout.shape[0]), BF),
        sds((micros, count, width), BF),
        sds((micros, count, width), BF),
        sds((micros, count, LANES), F32),
        sds((8, width), F32),
    ]
    return call(
        mid_back_body,
        shapes,
        (micros,),
        [
            one_of(y.shape),
            one_of(up.shape),
            one_of(z.shape),
            one_of(dh2.shape),
            one_of(zh.shape),
            one_of(dff.shape),
            pl.BlockSpec((1, count, width), lambda i, *u: (i, 0, 0)),
            one_of(gf.shape),
            second_of(cols.shape),
            second_of(rows.shape),
            whole(small.shape),
            one_of(gate.shape),
            whole(lout.shape),
            whole(lout_got.shape),
            whole(hout.shape),
            one_of(hy.shape),
            pl.BlockSpec((1, count, width), lambda i, *u: (i, 0, 0)),
        ],
        [one_of(s.shape) for s in shapes[:-1]] + [whole(shapes[-1].shape)],
        (info, y, up, z, dh2, zh, dff, ffr, gf, cols, rows, small, gate, lout, lout_got, hout, hy, hq),
        flops=3_000_000_000,
        moved=22_000_000,
    )


def light_join_body(info, x, small, dq, own, got_low, got_high, dl_out, own_out, other_out, low):
    tok, width = x.shape[1:]
    micros = x.shape[0]
    half = width // 2
    inner = dq.shape[2]
    for m in range(micros):
        dl_out[m, :, :inner] = dq[m]
        dl_out[m, WIN : tok - WIN, inner:] = own[m, WIN : tok - WIN].astype(BF)
        dl_out[m, :WIN, inner:] = (own[m, :WIN] + got_low[m].astype(F32)).astype(BF)
        dl_out[m, tok - WIN :, inner:] = (own[m, tok - WIN :] + got_high[m].astype(F32)).astype(BF)
        values = x[m].astype(F32)
        low[m] = (values * inverse_rms(values) * small[3:4].astype(F32)).astype(BF)
    for target, side in ((other_out, 1 - info[0]), (own_out, info[0])):
        cut = pl.ds(pl.multiple_of(side * half, half), half)
        for block in range(dl_out.shape[2] // COLS):
            total = sum(
                t_mm(low[m, :, cut], dl_out[m, :, block * COLS : (block + 1) * COLS])
                for m in range(micros)
            )
            target[block // 2, (block % 2) * half : (block % 2 + 1) * half] = total.astype(BF)


def light_join(info, x, small, dq, own, got_low, got_high):
    micros, tok, width = x.shape
    columns = dq.shape[2] + own.shape[2]
    shapes = [sds((micros, tok, columns), BF)] + [sds((columns // (2 * COLS), width, COLS), BF)] * 2
    args = (info, x, small, dq, own, got_low, got_high)
    return call(
        light_join_body,
        shapes,
        (1,),
        [whole(a.shape) for a in args[1:]],
        [whole(s.shape) for s in shapes],
        args,
        scratch=[pltpu.VMEM(x.shape, BF)],
        flops=2 * micros * tok * width * columns,
        moved=20_000_000,
    )


def in_back_body(
    info, x, dy, dl, dhq, dkin, dsq, rows, small, gate, h1k, l_own, l_got, h_own, h_got,
    grad_out, part_out,
):
    tok, width = x.shape[1:]
    micro = pl.program_id(0)
    base = info[1]
    light = dl[0]
    back = unhalved(info, mm_t(light, l_own[...]), mm_t(light, l_got[...]))
    given = dkin[0].astype(F32)
    open_k = gate[0, :, 1:2]
    source = h1k[0]
    dskv = jnp.sum(given * source, axis=-1, keepdims=True) * open_k * (1.0 - open_k)
    to_q = unhalved(info, mm_t(dhq[0], h_own[...]), mm_t(dhq[0], h_got[...]))
    to_q += dsq[0, :, 0:1] * small[0:1].astype(F32)
    to_k = given * open_k + dskv * small[1:2].astype(F32)
    back += pick(onehot_rows(rows[0, 0], base, tok), to_q)
    back += pick(onehot_rows(rows[1, 0], base, tok), to_k)
    values = x[0].astype(F32)
    inv = inverse_rms(values)
    scaled = back * small[3:4].astype(F32)
    mean = jnp.mean(values * scaled, axis=-1, keepdims=True)
    grad_out[0] = (dy[0] + inv * scaled - values * (inv * inv * inv * mean)).astype(BF)
    dgain = jnp.sum(back * values * inv, axis=0, keepdims=True)
    drk = jnp.sum(dskv * source.astype(BF).astype(F32), axis=0, keepdims=True)
    row = iota(part_out.shape, 0)
    part = jnp.where(row == 1, drk, jnp.where(row == 3, dgain, 0.0))

    @pl.when(micro == 0)
    def first():
        part_out[...] = part

    @pl.when(micro > 0)
    def later():
        part_out[...] += part


def in_back(info, x, dy, dl, dhq, dkin, dsq, rows, small, gate, h1k, l_own, l_got, h_own, h_got):
    micros, tok, width = x.shape
    shapes = [sds((micros, tok, width), BF), sds((8, width), F32)]
    firsts = (x, dy, dl, dhq, dkin, dsq)
    return call(
        in_back_body,
        shapes,
        (micros,),
        [one_of(a.shape) for a in firsts]
        + [second_of(rows.shape), whole(small.shape)]
        + [one_of(a.shape) for a in (gate, h1k)]
        + [whole(a.shape) for a in (l_own, l_got)]
        + [whole((h_own.shape[0], width))] * 2,
        [one_of(shapes[0].shape), whole(shapes[1].shape)],
        (info,) + firsts + (rows, small, gate, h1k, l_own, l_got, h_own, h_got),
        flops=2_600_000_000,
        moved=14_000_000,
    )


def mask_of(slot, order):
    bits = len(order)
    return sum(order[b] for b in range(bits) if (slot >> (bits - 1 - b)) & 1)


def fold_body(order, counts, info, *refs):
    sources = refs[: 2 * len(counts)]
    keep, send = refs[2 * len(counts) :]
    slots = 1 << len(order)
    size = keep.shape[2]
    step = pl.program_id(0)
    start = 0
    for which, count in enumerate(counts):
        own, got = sources[2 * which : 2 * which + 2]

        @pl.when((step >= start) & (step < start + count))
        def part():
            for slot in range(slots):
                owner = jnp.bitwise_xor(info[3], mask_of(slot, order))
                at = pl.ds(pl.multiple_of(owner * size, size), size)
                total = (own[0, at, :].astype(F32) + got[0, at, :].astype(F32)).astype(BF)
                if slot < slots // 2:
                    keep[slot, 0] = total
                else:
                    send[slot - slots // 2, 0] = total

        start += count


def fold(info, order, parts):
    slots = 1 << len(order)
    width = parts[0][0].shape[1]
    counts = [part[3] for part in parts]
    total = sum(counts)
    shape = sds((slots // 2, total, width // slots, COLS), BF)
    args, specs = ([], [])
    start = 0
    for own, got, first, count in parts:
        index = functools.partial(
            lambda first, start, count, i, *u: (
                first + jnp.minimum(jnp.maximum(i - start, 0), count - 1),
                0,
                0,
            ),
            first,
            start,
            count,
        )
        args += [own, got]
        specs += [pl.BlockSpec((1, width, COLS), index)] * 2
        start += count
    spec = pl.BlockSpec((slots // 2, 1, width // slots, COLS), lambda i, *u: (0, i, 0, 0))
    return call(
        functools.partial(fold_body, order, counts),
        [shape, shape],
        (total,),
        specs,
        [spec, spec],
        (info, *args),
        moved=total * width * COLS * 6,
    )


def flipped(value, bit):
    size = lax.axis_size("ctx")
    return lax.ppermute(value, "ctx", [(i, i ^ bit) for i in range(size)])


def tied(*values):
    return lax.optimization_barrier(values)


def scatter_step(keep, got):
    half = keep.shape[0] // 2
    if half == 0:
        return ((keep.astype(F32) + got.astype(F32)).astype(BF), None)
    return (
        (keep[:half].astype(F32) + got[:half].astype(F32)).astype(BF),
        (keep[half:].astype(F32) + got[half:].astype(F32)).astype(BF),
    )


def scatter_start(chunks, orders, stage):
    return [flipped(send, order[stage]) for (keep, send), order in zip(chunks, orders)]


def scatter_end(chunks, got):
    return [scatter_step(keep, g) for (keep, send), g in zip(chunks, got)]


def scatter_sum(keep, send, order):
    for bit in order:
        keep, send = scatter_step(keep, flipped(send, bit))
    return keep


def gather_start(values, orders, stage):
    return [flipped(value, order[-1 - stage]) for value, order in zip(values, orders)]


def gather_end(values, got):
    return [jnp.concatenate([value, g], axis=0) for value, g in zip(values, got)]


def gather_pair(value, order):
    for bit in order[:-1]:
        value = jnp.concatenate([value, flipped(value, bit)], axis=0)
    return (value, flipped(value, order[-1]))


def from_owner(info, order, near, far, owner, write):
    slots = 1 << len(order)
    distance = jnp.bitwise_xor(info[3], owner)
    slot = sum(
        jnp.where(jnp.bitwise_and(distance, bit) != 0, 1 << place, 0)
        for place, bit in enumerate(reversed(order))
    )
    inside = lax.rem(slot, slots // 2)

    @pl.when(slot < slots // 2)
    def close():
        write(near.at[inside])

    @pl.when(slot >= slots // 2)
    def distant():
        write(far.at[inside])


def unpack_gu_body(order, info, near, far, *outs):
    out = outs[-1]
    size = near.shape[2]
    per = out.shape[0] // size
    for turn in range(per):

        def write(source, turn=turn):
            for block in range(near.shape[1]):
                out[turn * size : (turn + 1) * size, block * COLS : (block + 1) * COLS] = source[
                    block
                ].astype(F32)

        from_owner(info, order, near, far, pl.program_id(1) * per + turn, write)


def write_dn(out, source, first, size, owner, row):
    cuts = out.shape[1] // COLS
    rows = size // cuts
    value = source[first].astype(F32)
    for cut in range(cuts):
        out[row + owner * rows : row + (owner + 1) * rows, cut * COLS : (cut + 1) * COLS] = value[
            cut * rows : (cut + 1) * rows
        ]


def unpack_dn_body(order, info, near, far, *outs):
    slots, blocks, size = near.shape[:3]
    for owner in range(2 * slots):

        def write(source, owner=owner):
            for block in range(blocks):
                write_dn(outs[-1], source, block, size, owner, block * COLS)

        from_owner(info, order, near, far, owner, write)


def unpack(body, info, order, pair, first, count, step, shape, grid_more, block, index, previous, name):
    near, far = pair
    slots, unused, size, unused_too = near.shape
    spec = pl.BlockSpec((slots, step, size, COLS), lambda i, *u: (0, first // step + i, 0, 0))
    args, specs, aliases = ([info, near, far], [spec, spec], {})
    if previous is not None:
        args.append(previous)
        specs.append(pl.BlockSpec(memory_space=pl.ANY))
        aliases = {3: 0}
    return pl.pallas_call(
        functools.partial(body, order),
        out_shape=sds(shape, F32),
        grid_spec=pltpu.PrefetchScalarGridSpec(
            num_scalar_prefetch=1,
            grid=(count // step,) + grid_more,
            in_specs=specs,
            out_specs=pl.BlockSpec(block, index),
        ),
        input_output_aliases=aliases,
        compiler_params=pltpu.CompilerParams(vmem_limit_bytes=32 * 1024 * 1024),
        cost_estimate=pl.CostEstimate(
            flops=0, bytes_accessed=count * 2 * slots * size * COLS * 6, transcendentals=0
        ),
        name=name,
    )(*args)


def unpack_gu(info, order, pair, first, count, total, base, previous, step):
    rows = pair[0].shape[0] * pair[0].shape[2]
    return unpack(
        unpack_gu_body, info, order, pair, first, count, step, (rows, 2 * total * COLS), (2,), (rows, step * COLS),
        lambda i, s, *u: (0, (s * total + base) // step + i), previous, "unpack_gu",
    )


def unpack_dn(info, order, pair, first, count, total, base, previous, step):
    width = 2 * pair[0].shape[0] * pair[0].shape[2]
    return unpack(
        unpack_dn_body, info, order, pair, first, count, step, (total * COLS, width), (), (step * COLS, width),
        lambda i, *u: (base // step + i, 0), previous, "unpack_dn",
    )


def unpack_plane_gu_body(info, full, out):
    sides, unused, planes, blocks, size, cols = full.shape
    turns = blocks // 3
    columns = out.shape[1] // sides
    for side in range(sides):
        for half in range(2):
            first = jnp.bitwise_xor(half, info[0]) * turns
            for plane in range(planes):
                for turn in range(turns):
                    at = side * columns + ((half * planes + plane) * turns + turn) * cols
                    out[:, at : at + cols] = full[side, 0, plane, first + turn].astype(F32)


def unpack_plane_gu(info, full, total):
    levels, planes, blocks, size, unused = full.shape
    rows, step = (2 * size, 48)
    turns = size // step
    view = full.reshape((2, levels // 2) + full.shape[1:])
    return call(
        unpack_plane_gu_body,
        sds((rows, 2 * total * COLS), F32),
        (rows // step,),
        [
            pl.BlockSpec(
                (2, 1, planes, blocks, step, COLS), lambda r, *u: (0, r // turns, 0, 0, r % turns, 0)
            )
        ],
        pl.BlockSpec((step, 2 * total * COLS), lambda r, *u: (r, 0)),
        (info, view),
        moved=2 * rows * total * COLS * 6,
        name="unpack_plane_gu",
    )


def unpack_plane_dn_body(info, full, out):
    levels, unused, blocks, size, cols = full.shape
    for level in range(levels):
        for block in range(blocks):
            for part in range(size // 64):
                cut, row = divmod(level * size + part * 64, COLS)
                at = block * COLS + row
                out[at : at + 64, cut * COLS : (cut + 1) * COLS] = full[
                    level, 0, block, part * 64 : (part + 1) * 64
                ].astype(F32)


def unpack_plane_dn(info, full):
    levels, planes, blocks, size, unused = full.shape
    turns = blocks // 3
    width = levels * size
    return call(
        unpack_plane_dn_body,
        sds((planes * turns * COLS, width), F32),
        (planes,),
        [pl.BlockSpec((levels, 1, turns, size, COLS), lambda q, *u: (0, q, 2, 0, 0))],
        pl.BlockSpec((turns * COLS, width), lambda q, *u: (q, 0)),
        (info, full),
        moved=planes * turns * COLS * width * 6,
        name="unpack_plane_dn",
    )


def unpack_units_body(order, first, info, near, far, *outs):
    slots, unused, size = near.shape[:3]
    homes = [
        (out, block * COLS) for out in outs for block in range(out.shape[1] // COLS)
    ]
    for owner in range(2 * slots):
        side, turn = divmod(owner, slots)

        def write(source, side=side, turn=turn):
            for at in range(side, len(homes), 2):
                out, column = homes[at]
                out[turn * size : (turn + 1) * size, column : column + COLS] = source[
                    first + at // 2
                ].astype(F32)

        from_owner(info, order, near, far, owner, write)


def unpack_units(info, order, pair, first, widths):
    slots, unused, size, unused_too = pair[0].shape
    shapes = [sds((slots * size, w), F32) for w in widths]
    args = [info, *pair]
    return call(
        functools.partial(unpack_units_body, order, first),
        shapes,
        (1,),
        [whole(a.shape) for a in args[1:]],
        [whole(s.shape) for s in shapes],
        args,
        moved=sum(widths) * slots * size * 6,
        name="unpack_units",
    )


def plain_gu(own, other):
    blocks, width, cols = own.shape

    def rows(part):
        return part.reshape(blocks, 2, width // 2, cols).transpose(2, 1, 0, 3).reshape(width // 2, -1)

    return jnp.concatenate([rows(own), rows(other)], axis=0)


def plain_dn(own, other):
    blocks, width, cols = own.shape
    cuts = width // cols

    def rows(part):
        return (
            part.reshape(blocks, 16, cuts, width // (16 * cuts), cols)
            .transpose(0, 1, 3, 2, 4)
            .reshape(-1, width)
        )

    return jnp.concatenate([rows(own), rows(other)], axis=0)


def plain_units(own, other, widths):
    def unit(part, at):
        half = part.shape[1] // 2
        return part[at // 2, (at % 2) * half : (at % 2 + 1) * half]

    result, at = ([], 0)
    for columns in widths:
        count = columns // COLS
        result.append(
            jnp.concatenate(
                [
                    jnp.concatenate([unit(part, at + i) for i in range(count)], axis=1)
                    for part in (own, other)
                ],
                axis=0,
            )
        )
        at += count
    return result


def plain_sum(grads):
    parts = [lax.psum_scatter(g.astype(BF), "wsh", scatter_dimension=0, tiled=True) for g in grads]
    return tuple(g.astype(F32) for g in lax.psum(parts, "ctx"))


def per_device(
    tokens, cotangent, light_qkv, light_out, heavy_qkv, heavy_out, light_gu, light_down, heavy_gu, heavy_down,
    routers, gains, doc_starts, q_index, kv_index, ff_index,
):
    micros, unused, tok, width = tokens.shape
    count, groups = (lax.axis_size("ctx"), lax.axis_size("wsh"))
    direct = groups == 2 and count == 16
    place_ctx = lax.axis_index("ctx")
    side = lax.axis_index("wsh") if direct else 0
    base = place_ctx * tok
    info = jnp.concatenate(
        [
            jnp.stack([jnp.int32(side), base, jnp.int32(tok * count), place_ctx]).astype(jnp.int32),
            doc_starts[:, 0].reshape(-1),
        ]
    )
    swap = [(0, 1), (1, 0)]

    def pair_of(shard):
        if direct:
            return (shard, lax.ppermute(shard, "wsh", swap))
        full = lax.all_gather(shard, "wsh", axis=0, tiled=True)
        return (full[: full.shape[0] // 2], full[full.shape[0] // 2 :])

    def full_of(shard, axis=0):
        return lax.all_gather(shard, "wsh", axis=axis, tiled=True)

    vectors = jnp.concatenate([routers, gains, jnp.zeros((3, routers.shape[1]), BF)], axis=0)
    if direct:
        got = lax.ppermute(vectors, "wsh", swap)
        small = jnp.concatenate(
            [jnp.where(side == 0, vectors, got), jnp.where(side == 0, got, vectors)], axis=1
        )
    else:
        small = full_of(vectors, 1)
    x, up = (tokens[:, 0], cotangent[:, 0])
    index = jnp.stack([q_index[:, 0], kv_index[:, 0], ff_index[:, 0]])
    cols, rows = (index[..., None], index[:, :, None, :])
    hq_in, kin_pay, h1k, gate = routed_in(info, x, cols, small)
    l_own, l_got = pair_of(light_qkv)
    h_own, h_got = pair_of(heavy_qkv)
    o_own, o_got = pair_of(light_out)
    w_hout, w_hgu, w_hdown = (full_of(heavy_out), full_of(heavy_gu), full_of(heavy_down))
    w_lgu, w_ldown = (full_of(light_gu), full_of(light_down))
    kv_orders = ((8, 4, 2, 1), (8, 1, 4, 2))
    back_orders = [tuple(reversed(order)) for order in kv_orders]
    upward = [(i, i + 1) for i in range(count - 1)]
    downward = [(i + 1, i) for i in range(count - 1)]
    inner = light_qkv.shape[1] // 3
    every = range(micros)

    def rims(qkv):
        return (
            lax.ppermute(qkv[:, tok - WIN :, inner:], "ctx", upward),
            lax.ppermute(qkv[:, :WIN, inner:], "ctx", downward),
        )

    def project(kin):
        return key_project(info, kin, h_own, h_got)

    if direct:
        values = [kin_pay[m] for m in every]
        got = gather_start(values, back_orders, 0)
        qkv = light_in(info, x, small, l_own, l_got)
        got, qkv = tied(got, qkv)
        before, after = rims(qkv)
        values = gather_end(values, got)
        got = gather_start(values, back_orders, 1)
        q_pay = query_project(info, hq_in, h_own, h_got)
        got, q_pay, w_hout = tied(got, q_pay, w_hout)
        values = gather_end(values, got)
        got = gather_start(values, back_orders, 2)
        done = light_inner(info, qkv)
        got, before, after, done = tied(got, before, after, done)
        values = gather_end(values, got)
        got = gather_start(values, back_orders, 3)
        lo, light_lse = light_outer(info, qkv, before, after, done)
        near_kv = [project(v) for v in values]
        got, near_kv, lo, light_lse, w_hgu, w_hdown = tied(got, near_kv, lo, light_lse, w_hgu, w_hdown)
        kins = list(zip(values, got))
        kvs = [(n, project(f)) for n, f in zip(near_kv, got)]
    else:
        kins = []
        for m in every:
            full = lax.all_gather(kin_pay[m], "ctx", axis=0, tiled=True)
            kins.append((full[: full.shape[0] // 2], full[full.shape[0] // 2 :]))
        kvs = [tuple(project(k) for k in pair) for pair in kins]
        qkv = light_in(info, x, small, l_own, l_got)
        before, after = rims(qkv)
        lo, light_lse = light_outer(info, qkv, before, after, light_inner(info, qkv))
        q_pay = query_project(info, hq_in, h_own, h_got)
    heavy = [heavy_fwd(info, q_pay[m], kins[m], kvs[m]) for m in every]
    heavy, w_lgu, w_ldown = tied(heavy, w_lgu, w_ldown)
    ho = jnp.stack([h[0] for h in heavy])
    y, low2, pay, hy, gf = middle(info, x, up, cols, rows, small, gate, lo, o_own, o_got, ho, w_hout)

    def flat(value):
        return value.reshape(-1, value.shape[-1])

    orders = ((1, 2, 4, 8), (2, 4, 1, 8), (4, 1, 2, 8))
    back_two = ((1, 2, 4, 8), (2, 1, 4, 8), (4, 1, 2, 8))
    if direct:
        mine = flat(pay)
        plane = [flipped(mine, bit) for bit in (1, 2, 3)]
        zh, dff = ffn_local(info, mine, w_hgu, w_hdown, 2 * COLS)
        plane, zh, dff = tied(plane, zh, dff)
        near = jnp.concatenate([mine, *plane], axis=0)
        far = lax.ppermute(near, "wsh", swap)
    else:
        zh, dff, hgu_own, hgu_send, hdn_own, hdn_send = ffn(
            info, flat(pay[..., :width]), flat(pay[..., width:]), w_hgu, w_hdown
        )
    if direct:
        plane_own, plane_send, plane_dn = plane_grads(info, near, far, w_hgu, w_hdown)
        plane_got = lax.ppermute(plane_send, "wsh", swap)
        keep, send = column_fold(info, (1, 2), (plane_own, plane_got, plane_dn))
        send, low2 = tied(send, low2)
        got = flipped(send, 4)
    z, dh2, lgu_own, lgu_send, ldn_own, ldn_send = ffn_all(info, flat(low2), flat(up), w_lgu, w_ldown)
    if direct:
        got, z, dh2, lgu_send, ldn_send = tied(got, z, dh2, lgu_send, ldn_send)
        keep, send = scatter_step(keep, got)
        got = flipped(send, 8)
        lgu_got, ldn_got = (lax.ppermute(part, "wsh", swap) for part in (lgu_send, ldn_send))

    def by_micro(value):
        return value.reshape(micros, -1, value.shape[-1])

    out_tokens, dy, dlo, dho, dhy, dsq, part_two = mid_back(
        info, y, up, by_micro(z), by_micro(dh2), by_micro(zh), by_micro(dff), pay, gf, cols, rows, small, gate, o_own,
        o_got, w_hout, hy, hq_in,
    )
    dlq, dl_own, rim_low, rim_high = light_bwd_outer(info, qkv, before, after, light_lse, dlo)
    if direct:
        got, dlq, dl_own, rim_low, rim_high, dho = tied(got, dlq, dl_own, rim_low, rim_high, dho)
        keep, send = scatter_step(keep, got)
        plane_full = lax.all_gather(keep[0], "ctx", axis=0, tiled=False)
        plane_full = plane_full.reshape((count // 4, 4) + plane_full.shape[1:])
    got_low = lax.ppermute(rim_high, "ctx", upward)
    got_high = lax.ppermute(rim_low, "ctx", downward)
    backs = [
        heavy_bwd(info, q_pay[m], kins[m], kvs[m], heavy[m][1], dho[m], h_own, h_got) for m in every
    ]
    dhq = jnp.stack([b[0] for b in backs])
    shape = (count // 2, q_index.shape[2], width)
    back = [tuple(part.reshape(shape) for part in b[3:5]) for b in backs]
    dkvs = [part for b in backs for part in b[1:3]]
    if direct:
        back, dlo, dkvs, got_low, got_high = tied(back, dlo, dkvs, got_low, got_high)
        got_back = scatter_start(back, back_orders, 0)
    dlq, dl_own = light_bwd_inner(info, qkv, light_lse, dlo, dlq, dl_own)
    if direct:
        got_back, dlq, dl_own = tied(got_back, dlq, dl_own)
        back = scatter_end(back, got_back)
        got_back = scatter_start(back, back_orders, 1)
    kin_all = [part for pair in kins for part in pair]
    dl, la_own, la_send = light_join(info, x, small, dlq, dl_own, got_low, got_high)
    if direct:
        la_got = lax.ppermute(la_send, "wsh", swap)
    ha_own, ha_send = heavy_grads(info, hq_in, dhq, ho, dhy, lo, dy, kin_all, dkvs)
    if direct:
        got_back, ha_own, ha_send, la_got, dl = tied(got_back, ha_own, ha_send, la_got, dl)
        ha_got = lax.ppermute(ha_send, "wsh", swap)
        back = scatter_end(back, got_back)
        got_back = scatter_start(back, back_orders, 2)
        second = [
            fold(info, orders[0], [(ha_own, ha_got, 0, 6)]),
            fold(info, back_two[1], [(lgu_own, lgu_got, 0, 4), (ha_own, ha_got, 6, 1)]),
            fold(info, orders[2], [(la_own, la_got, 0, 3), (ldn_own, ldn_got, 0, 2)]),
        ]
        got_back, second, dl = tied(got_back, second, dl)
        *got_two, got_last = scatter_start(second, back_two, 0)
        back = scatter_end(back, got_back)
        got_back = scatter_start(back, back_orders, 3)
        (got_two,) = tied(got_two)
        *second, last = second
        second = scatter_end(second, got_two)
        got_two = scatter_start(second, back_two, 1)
        back, got_back, second = tied(back, got_back, second)
        back = scatter_end(back, got_back)
        dkin = jnp.concatenate([keep for keep, send in back], axis=0)
    else:
        dkin = jnp.stack(
            [
                lax.psum_scatter(jnp.concatenate(b[3:5], axis=0), "ctx", scatter_dimension=0, tiled=True)
                for b in backs
            ]
        )
    grad_tokens, part_one = in_back(
        info, x, dy, dl, dhq, dkin, dsq, rows, small, gate, h1k, l_own, l_got, h_own, h_got
    )
    widths = (heavy_qkv.shape[1], heavy_out.shape[1])
    vector = part_one + part_two
    if direct:
        half = width // 2
        mine = lax.dynamic_slice_in_dim(vector, side * half, half, 1)
        given = lax.dynamic_slice_in_dim(vector, (1 - side) * half, half, 1)
        got_two, got_last, mine, given = tied(got_two, got_last, mine, given)
        second, last = (scatter_end(second, got_two), scatter_step(last[0], got_last))
        got_two, got_last = (scatter_start(second, back_two, 2), flipped(last[1], back_two[2][1]))
        vector = mine + lax.ppermute(given, "wsh", swap)
        got_two, got_last, vector = tied(got_two, got_last, vector)
        second, last = (scatter_end(second, got_two), scatter_step(last[0], got_last))
        got_two, got_last = (scatter_start(second, back_two, 3), flipped(last[1], back_two[2][2]))
        got_vector = flipped(vector, 1)
        got_two, got_last, vector, got_vector = tied(got_two, got_last, vector, got_vector)
        second, last = (scatter_end(second, got_two), scatter_step(last[0], got_last))
        got_last = flipped(last[1], back_two[2][3])
        second, got_last, got_vector = tied(second, got_last, got_vector)
        vector = vector + got_vector
        second = [*second, scatter_step(last[0], got_last)]
        tails = [keep for keep, send in second]
        got_two, got_vector = (gather_start(tails, orders, 0), flipped(vector, 2))
        got_two, vector, got_vector = tied(got_two, vector, got_vector)
        tails, vector = (gather_end(tails, got_two), vector + got_vector)
        got_two, got_vector = (gather_start(tails, orders, 1), flipped(vector, 4))
        got_two, vector, got_vector = tied(got_two, vector, got_vector)
        tails, vector = (gather_end(tails, got_two), vector + got_vector)
        got_two, got_vector = (gather_start(tails, orders, 2), flipped(vector, 8))
        g_hdown = unpack_plane_dn(info, plane_full)
        got_two, vector, got_vector, g_hdown, plane_full = tied(got_two, vector, got_vector, g_hdown, plane_full)
        tails, vector = (gather_end(tails, got_two), vector + got_vector)
        got_two = gather_start(tails, orders, 3)
        g_hgu = unpack_plane_gu(info, plane_full, heavy_gu.shape[1] // (2 * COLS))
        got_two, g_hgu = tied(got_two, g_hgu)
        sums = list(zip(tails, got_two))
        g_hqkv, g_hout = unpack_units(info, orders[0], sums[0], 0, widths)
        g_lgu = unpack_gu(info, orders[1], sums[1], 0, 4, 4, 0, None, 4)
        g_lout = unpack_dn(info, orders[1], sums[1], 4, 1, 1, 0, None, 1)
        (g_lqkv,) = unpack_units(info, orders[2], sums[2], 0, (light_qkv.shape[1],))
        g_ldown = unpack_dn(info, orders[2], sums[2], 3, 2, 2, 0, None, 1)
    else:
        g_hqkv, g_hout = plain_units(ha_own, ha_send, widths)
        (g_lqkv,) = plain_units(la_own, la_send, (light_qkv.shape[1],))
        last = slice(ha_own.shape[0] - 1, ha_own.shape[0])
        g_lqkv, g_lout, g_hqkv, g_hout, g_lgu, g_ldown, g_hgu, g_hdown = plain_sum(
            [
                g_lqkv,
                plain_dn(ha_own[last], ha_send[last]),
                g_hqkv,
                g_hout,
                plain_gu(lgu_own, lgu_send),
                plain_dn(ldn_own, ldn_send),
                plain_gu(hgu_own, hgu_send),
                plain_dn(hdn_own, hdn_send),
            ]
        )
        vector = lax.psum(vector, ("ctx", "wsh"))
        part = width // groups
        vector = lax.dynamic_slice_in_dim(vector, lax.axis_index("wsh") * part, part, 1)
    return (
        out_tokens[:, None],
        grad_tokens[:, None],
        g_lqkv,
        g_lout,
        g_hqkv,
        g_hout,
        g_lgu,
        g_ldown,
        g_hgu,
        g_hdown,
        vector[:3],
        vector[3:5],
    )


def solution(mesh):
    return jax.shard_map(
        per_device,
        mesh=mesh,
        in_specs=(
            P(None, "wsh", "ctx", None),
            P(None, "wsh", "ctx", None),
            P("wsh", None),
            P("wsh", None),
            P("wsh", None),
            P("wsh", None),
            P("wsh", None),
            P("wsh", None),
            P("wsh", None),
            P("wsh", None),
            P(None, "wsh"),
            P(None, "wsh"),
            P(None, "wsh", None),
            P(None, "wsh", "ctx"),
            P(None, "wsh", "ctx"),
            P(None, "wsh", "ctx"),
        ),
        out_specs=(
            P(None, "wsh", "ctx", None),
            P(None, "wsh", "ctx", None),
            P("wsh", None),
            P("wsh", None),
            P("wsh", None),
            P("wsh", None),
            P("wsh", None),
            P("wsh", None),
            P("wsh", None),
            P("wsh", None),
            P(None, "wsh"),
            P(None, "wsh"),
        ),
        check_vma=False,
    )
```

```python
import functools

import jax
import jax.numpy as jnp
from jax import lax
from jax.experimental import pallas as pl
from jax.experimental.pallas import tpu as pltpu
from jax.sharding import PartitionSpec as P

HD = 64
WIN = 128
LANES = 128
COLS = 256
FAR = -1e30
EPS = 1e-06
BF = jnp.bfloat16
F32 = jnp.float32


def mm(left, right):
    return lax.dot_general(left, right, (((1,), (0,)), ((), ())), preferred_element_type=F32)


def mm_t(left, right):
    return lax.dot_general(left, right, (((1,), (1,)), ((), ())), preferred_element_type=F32)


def t_mm(left, right):
    return lax.dot_general(left, right, (((0,), (0,)), ((), ())), preferred_element_type=F32)


def pick(onehot, values):
    high = values.astype(BF)
    low = (values - high.astype(F32)).astype(BF)
    return mm(onehot, high) + mm(onehot, low)


def iota(shape, dim):
    return lax.broadcasted_iota(jnp.int32, shape, dim)


def onehot_cols(positions, base, length):
    return (iota((positions.shape[0], length), 1) == positions - base).astype(F32).astype(BF)


def onehot_rows(positions, base, length):
    return (iota((length, positions.shape[1]), 0) == positions - base).astype(F32).astype(BF)


def segment(info, micro, positions):
    total = jnp.full(positions.shape, -1, jnp.int32)
    for start in range(5):
        total += (positions >= info[4 + micro * 5 + start]).astype(jnp.int32)
    return total


def inverse_rms(values):
    return lax.rsqrt(jnp.mean(values * values, axis=-1, keepdims=True) + EPS)


def halves(info, values):
    half = values.shape[1] // 2
    first, second = (values[:, :half], values[:, half:])
    lower = info[0] == 0
    return (jnp.where(lower, first, second), jnp.where(lower, second, first))


def unhalved(info, own, other):
    lower = info[0] == 0
    return jnp.concatenate([jnp.where(lower, own, other), jnp.where(lower, other, own)], axis=1)


def call(body, outs, grid, in_specs, out_specs, args, scratch=(), flops=0, moved=0, limit=48, name=None):
    return pl.pallas_call(
        body,
        name=name or getattr(body, "__name__", "kernel"),
        out_shape=outs,
        grid_spec=pltpu.PrefetchScalarGridSpec(
            num_scalar_prefetch=1,
            grid=grid,
            in_specs=in_specs,
            out_specs=out_specs,
            scratch_shapes=list(scratch),
        ),
        compiler_params=pltpu.CompilerParams(vmem_limit_bytes=limit * 1024 * 1024),
        cost_estimate=pl.CostEstimate(flops=flops, bytes_accessed=moved, transcendentals=0),
    )(*args)


def whole(shape):
    rank = len(shape)
    return pl.BlockSpec(tuple(shape), lambda *unused: (0,) * rank)


def one_of(shape):
    rank = len(shape)
    return pl.BlockSpec((1,) + tuple(shape[1:]), lambda i, *unused: (i,) + (0,) * (rank - 1))


def sds(shape, dtype):
    return jax.ShapeDtypeStruct(tuple(shape), dtype)


def routed_body(info, x, cols, small, q_out, kin_out, h1k_out, gate_out):
    micros, tok, width = x.shape
    rows = cols.shape[2]
    base = info[1]
    gain = small[3:4].astype(F32)
    lane = iota((rows, LANES), 1)
    for m in range(micros):
        both = jnp.concatenate([cols[0, m], cols[1, m]], axis=0)
        got = mm(onehot_cols(both, base, tok), x[m])
        xq, xk = (got[:rows], got[rows:])
        low_q = (xq * inverse_rms(xq) * gain).astype(BF)
        h1k = xk * inverse_rms(xk) * gain
        low_k = h1k.astype(BF)
        gate_q = jax.nn.sigmoid(
            jnp.sum(low_q.astype(F32) * small[0:1].astype(F32), axis=-1, keepdims=True)
        )
        gate_k = jax.nn.sigmoid(
            jnp.sum(low_k.astype(F32) * small[1:2].astype(F32), axis=-1, keepdims=True)
        )
        seg_q = segment(info, m, cols[0, m])
        seg_k = segment(info, m, cols[1, m])
        q_out[m, :, :width] = low_q
        q_out[m, :, width:] = (lane == seg_q).astype(F32).astype(BF)
        kin_out[m, :, :width] = (h1k * gate_k).astype(BF)
        kin_out[m, :, width:] = jnp.where((lane < 8) & (lane != seg_k), FAR, 0.0).astype(BF)
        h1k_out[m] = h1k
        gate_out[m] = jnp.where(lane == 0, gate_q, gate_k)


def routed_in(info, x, cols, small):
    micros, unused, width = x.shape
    rows = cols.shape[2]
    shapes = [
        sds((micros, rows, width + LANES), BF),
        sds((micros, rows, width + LANES), BF),
        sds((micros, rows, width), F32),
        sds((micros, rows, LANES), F32),
    ]
    args = (info, x, cols, small)
    return call(
        routed_body,
        shapes,
        (1,),
        [whole(a.shape) for a in args[1:]],
        [whole(s.shape) for s in shapes],
        args,
        flops=200_000_000,
        moved=3_000_000,
    )


def query_body(info, low, w_own, w_got, out):
    width = 2 * w_own.shape[0]
    for m in range(low.shape[0]):
        own, other = halves(info, low[m, :, :width])
        out[m, :, :width] = (mm(own, w_own[...]) + mm(other, w_got[...])).astype(BF)
        out[m, :, width:] = low[m, :, width:]


def query_project(info, low, w_own, w_got):
    half = w_own.shape[0]
    return call(
        query_body,
        sds(low.shape, BF),
        (1,),
        [whole(low.shape)] + [whole((half, 2 * half))] * 2,
        whole(low.shape),
        (info, low, w_own, w_got),
        flops=2 * low.shape[0] * low.shape[1] * 4 * half * half,
        moved=2_000_000,
    )


def light_in_body(info, x, small, w_own, w_got, out):
    values = x[0].astype(F32)
    low = (values * inverse_rms(values) * small[3:4].astype(F32)).astype(BF)
    own, other = halves(info, low)
    out[0] = (mm(own, w_own[...]) + mm(other, w_got[...])).astype(BF)


def light_in(info, x, small, w_own, w_got):
    micros, tok, width = x.shape
    columns = w_own.shape[1]
    split = 2
    rows = tok // split
    spec = lambda n: pl.BlockSpec((1, rows, n), lambda i, *u: (i // split, i % split, 0))
    return call(
        light_in_body,
        sds((micros, tok, columns), BF),
        (micros * split,),
        [spec(width), whole(small.shape), whole(w_own.shape), whole(w_got.shape)],
        spec(columns),
        (info, x, small, w_own, w_got),
        flops=2 * micros * tok * width * columns,
        moved=8_000_000,
    )


def fill_near(near, qkv, before, after):
    tok = qkv.shape[1]
    inner = near.shape[1] // 2
    near[:WIN] = before[0]
    near[WIN : WIN + tok] = qkv[0, :, inner:]
    near[WIN + tok :] = after[0]


def light_bias(info, micro, block):
    start = info[1] + block * WIN
    rows, columns = (WIN, 3 * WIN)
    row_pos = start + iota((rows, 1), 0)
    col_pos = start - WIN + iota((1, columns), 1)
    seg_row = segment(info, micro, row_pos)
    seg_col = jnp.where((col_pos >= 0) & (col_pos < info[2]), segment(info, micro, col_pos), -1)
    shift = iota((rows, columns), 0) + WIN - iota((rows, columns), 1)
    allowed = (jnp.abs(shift) < WIN) & (seg_row == seg_col)
    bias = jnp.where(allowed, 0.0, FAR)
    return jnp.concatenate([bias, bias], axis=0)


def stacked(pair, low_lane):
    zero = jnp.zeros_like(pair)
    return jnp.concatenate(
        [jnp.where(low_lane, pair, zero), jnp.where(low_lane, zero, pair)], axis=0
    )


def merged(values, low_lane):
    rows = values.shape[0] // 2
    return jnp.where(low_lane, values[:rows], values[rows:])


def light_fwd_blocks(info, qkv, near, blocks, emit):
    micro = pl.program_id(0)
    inner = near.shape[1] // 2
    low_lane = iota((WIN, LANES), 1) < HD
    lane = iota((WIN, LANES), 1)
    for place, block in enumerate(blocks):
        at = slice(block * WIN, (block + 1) * WIN)
        around = slice(block * WIN, (block + 3) * WIN)
        bias = light_bias(info, micro, block)
        stats = jnp.zeros((WIN, LANES), F32)
        for pair in range(inner // LANES):
            cut = slice(pair * LANES, (pair + 1) * LANES)
            query = stacked(qkv[0, at, cut] * BF(HD**-0.5), low_lane)
            scores = mm_t(query, near[around, cut]) + bias
            top = jnp.max(scores, axis=-1, keepdims=True)
            weights = jnp.exp(scores - top)
            total = jnp.sum(weights, axis=-1, keepdims=True)
            value = near[around, inner + pair * LANES : inner + (pair + 1) * LANES]
            mixed = mm((weights * (1.0 / total)).astype(BF), value)
            emit(place, cut, merged(mixed, low_lane).astype(BF))
            lse = top + jnp.log(total)
            stats = jnp.where(lane == 2 * pair, lse[:WIN], stats)
            stats = jnp.where(lane == 2 * pair + 1, lse[WIN:], stats)
        emit(place, None, stats)


def light_inner_body(info, qkv, out, lse_out, near):
    tok = qkv.shape[1]
    inner = out.shape[2]
    near[WIN : WIN + tok] = qkv[0, :, inner:]

    def emit(place, cut, value):
        rows = slice(place * WIN, (place + 1) * WIN)
        if cut is None:
            lse_out[0, rows] = value
        else:
            out[0, rows, cut] = value

    light_fwd_blocks(info, qkv, near, range(1, tok // WIN - 1), emit)


def light_outer_body(info, qkv, before, after, done, lse_done, out, lse_out, near):
    tok = qkv.shape[1]
    fill_near(near, qkv, before, after)
    out[0, WIN : tok - WIN] = done[0]
    lse_out[0, WIN : tok - WIN] = lse_done[0]
    blocks = (0, tok // WIN - 1)

    def emit(place, cut, value):
        rows = slice(blocks[place] * WIN, (blocks[place] + 1) * WIN)
        if cut is None:
            lse_out[0, rows] = value
        else:
            out[0, rows, cut] = value

    light_fwd_blocks(info, qkv, near, blocks, emit)


def light_inner(info, qkv):
    micros, tok, columns = qkv.shape
    inner = columns // 3
    shapes = [sds((micros, tok - 2 * WIN, inner), BF), sds((micros, tok - 2 * WIN, LANES), F32)]
    return call(
        light_inner_body,
        shapes,
        (micros,),
        [one_of(qkv.shape)],
        [one_of(a.shape) for a in shapes],
        (info, qkv),
        scratch=[pltpu.VMEM((tok + 2 * WIN, 2 * inner), BF)],
        flops=2_000_000_000,
        moved=4_000_000,
    )


def light_outer(info, qkv, before, after, done):
    micros, tok, columns = qkv.shape
    inner = columns // 3
    shapes = [sds((micros, tok, inner), BF), sds((micros, tok, LANES), F32)]
    args = (info, qkv, before, after, *done)
    return call(
        light_outer_body,
        shapes,
        (micros,),
        [one_of(a.shape) for a in args[1:]],
        [one_of(a.shape) for a in shapes],
        args,
        scratch=[pltpu.VMEM((tok + 2 * WIN, 2 * inner), BF)],
        flops=2_000_000_000,
        moved=6_000_000,
    )


def light_bwd_blocks(info, qkv, lse, grad, near, dk, dv, blocks, emit):
    micro = pl.program_id(0)
    inner = grad.shape[2]
    low_lane = iota((WIN, LANES), 1) < HD
    for place, block in enumerate(blocks):
        at = slice(block * WIN, (block + 1) * WIN)
        around = slice(block * WIN, (block + 3) * WIN)
        bias = light_bias(info, micro, block)
        stats = lse[0, at, :]
        for pair in range(inner // LANES):
            cut = slice(pair * LANES, (pair + 1) * LANES)
            query = stacked(qkv[0, at, cut] * BF(HD**-0.5), low_lane)
            key = near[around, cut]
            value = near[around, inner + pair * LANES : inner + (pair + 1) * LANES]
            shift = jnp.concatenate(
                [stats[:, 2 * pair : 2 * pair + 1], stats[:, 2 * pair + 1 : 2 * pair + 2]], axis=0
            )
            probs = jnp.exp(mm_t(query, key) + bias - shift)
            upper = stacked(grad[0, at, cut], low_lane)
            grad_probs = mm_t(upper, value)
            center = jnp.sum(probs * grad_probs, axis=-1, keepdims=True)
            slope = (probs * (grad_probs - center)).astype(BF)
            emit(place, cut, (merged(mm(slope, key), low_lane) * HD**-0.5).astype(BF))
            dk[around, cut] += t_mm(slope, query)
            dv[around, cut] += t_mm(probs.astype(BF), upper)


def light_bwd_outer_body(info, qkv, before, after, lse, grad, dq_out, own_out, low_out, high_out, near, dk, dv):
    tok = qkv.shape[1]
    inner = grad.shape[2]
    fill_near(near, qkv, before, after)
    dk[...] = jnp.zeros_like(dk)
    dv[...] = jnp.zeros_like(dv)

    def emit(place, cut, value):
        dq_out[0, place * WIN : (place + 1) * WIN, cut] = value

    light_bwd_blocks(info, qkv, lse, grad, near, dk, dv, (0, tok // WIN - 1), emit)
    for first, source in ((0, dk), (inner, dv)):
        to = slice(first, first + inner)
        own_out[0, :, to] = source[WIN : WIN + tok]
        low_out[0, :, to] = source[:WIN].astype(BF)
        high_out[0, :, to] = source[WIN + tok :].astype(BF)


def light_bwd_inner_body(info, qkv, lse, grad, dq_in, own_in, dq_out, own_out, near, dk, dv):
    tok = qkv.shape[1]
    inner = grad.shape[2]
    near[WIN : WIN + tok] = qkv[0, :, inner:]
    dk[WIN : WIN + tok] = own_in[0, :, :inner]
    dv[WIN : WIN + tok] = own_in[0, :, inner:]
    dq_out[0, :WIN] = dq_in[0, :WIN]
    dq_out[0, tok - WIN :] = dq_in[0, WIN:]
    blocks = range(1, tok // WIN - 1)

    def emit(place, cut, value):
        dq_out[0, blocks[place] * WIN : (blocks[place] + 1) * WIN, cut] = value

    light_bwd_blocks(info, qkv, lse, grad, near, dk, dv, blocks, emit)
    own_out[0, :, :inner] = dk[WIN : WIN + tok]
    own_out[0, :, inner:] = dv[WIN : WIN + tok]


def light_bwd_scratch(tok, inner):
    return [
        pltpu.VMEM((tok + 2 * WIN, 2 * inner), BF),
        pltpu.VMEM((tok + 2 * WIN, inner), F32),
        pltpu.VMEM((tok + 2 * WIN, inner), F32),
    ]


def light_bwd_outer(info, qkv, before, after, lse, grad):
    micros, tok, columns = qkv.shape
    inner = columns // 3
    shapes = [
        sds((micros, 2 * WIN, inner), BF),
        sds((micros, tok, 2 * inner), F32),
        sds((micros, WIN, 2 * inner), BF),
        sds((micros, WIN, 2 * inner), BF),
    ]
    args = (info, qkv, before, after, lse, grad)
    return call(
        light_bwd_outer_body,
        shapes,
        (micros,),
        [one_of(a.shape) for a in args[1:]],
        [one_of(a.shape) for a in shapes],
        args,
        scratch=light_bwd_scratch(tok, inner),
        flops=5_000_000_000,
        moved=12_000_000,
    )


def light_bwd_inner(info, qkv, lse, grad, dq, own):
    micros, tok, columns = qkv.shape
    inner = columns // 3
    shapes = [sds((micros, tok, inner), BF), sds((micros, tok, 2 * inner), F32)]
    args = (info, qkv, lse, grad, dq, own)
    return call(
        light_bwd_inner_body,
        shapes,
        (micros,),
        [one_of(a.shape) for a in args[1:]],
        [one_of(a.shape) for a in shapes],
        args,
        scratch=light_bwd_scratch(tok, inner),
        flops=5_000_000_000,
        moved=14_000_000,
    )


def key_body(info, kin, w_own, w_got, out):
    half = w_own.shape[0]
    width = 2 * half
    own = kin[:, pl.ds(pl.multiple_of(info[0] * half, half), half)]
    other = kin[:, pl.ds(pl.multiple_of((1 - info[0]) * half, half), half)]
    out[...] = (mm(own, w_own[:, width:]) + mm(other, w_got[:, width:])).astype(BF)


def key_project(info, kin, w_own, w_got):
    shape = sds((kin.shape[0], 2 * (kin.shape[1] - LANES)), BF)
    args = (info, kin, w_own, w_got)
    return call(
        key_body,
        shape,
        (1,),
        [whole(a.shape) for a in args[1:]],
        whole(shape.shape),
        args,
        flops=1_200_000_000,
        moved=6_000_000,
    )


def heavy_scores(query, parts, bias, cut):
    return [mm_t(query, part[:, cut]) + b for part, b in zip(parts, bias)]


def heavy_fwd_body(info, q, kin_a, kin_b, kv_a, kv_b, out, lse_out):
    rows, width = out.shape
    parts = (kv_a, kv_b)
    low_lane = iota((rows, LANES), 1) < HD
    lane = iota((rows, LANES), 1)
    feature = jnp.concatenate([q[:, width:]] * 2, axis=0)
    bias = [mm_t(feature, kin[:, width:]) for kin in (kin_a, kin_b)]
    stats = jnp.zeros((rows, LANES), F32)
    for pair in range(width // LANES):
        cut = slice(pair * LANES, (pair + 1) * LANES)
        query = stacked(q[:, cut] * BF(HD**-0.5), low_lane)
        scores = heavy_scores(query, parts, bias, cut)
        top = functools.reduce(
            jnp.maximum, [jnp.max(s, axis=-1, keepdims=True) for s in scores]
        )
        weights = [jnp.exp(s - top) for s in scores]
        total = sum(jnp.sum(w, axis=-1, keepdims=True) for w in weights)
        scale = 1.0 / total
        mixed = sum(
            mm((w * scale).astype(BF), part[:, width + pair * LANES : width + (pair + 1) * LANES])
            for w, part in zip(weights, parts)
        )
        out[:, cut] = merged(mixed, low_lane).astype(BF)
        lse = top + jnp.log(total)
        stats = jnp.where(lane == 2 * pair, lse[:rows], stats)
        stats = jnp.where(lane == 2 * pair + 1, lse[rows:], stats)
    lse_out[...] = stats


def heavy_fwd(info, q, kins, kvs):
    rows = q.shape[0]
    width = q.shape[1] - LANES
    shapes = [sds((rows, width), BF), sds((rows, LANES), F32)]
    args = (info, q, *kins, *kvs)
    return call(
        heavy_fwd_body,
        shapes,
        (1,),
        [whole(a.shape) for a in args[1:]],
        [whole(s.shape) for s in shapes],
        args,
        flops=1_500_000_000,
        moved=5_000_000,
    )


def heavy_bwd_body(info, q, kin_a, kin_b, kv_a, kv_b, lse, grad, w_own, w_got, dq_out, da_out, db_out, ia_out, ib_out):
    rows, width = grad.shape
    parts = (kv_a, kv_b)
    low_lane = iota((rows, LANES), 1) < HD
    feature = jnp.concatenate([q[:, width:]] * 2, axis=0)
    bias = [mm_t(feature, kin[:, width:]) for kin in (kin_a, kin_b)]
    for pair in range(width // LANES):
        cut = slice(pair * LANES, (pair + 1) * LANES)
        upcut = slice(width + pair * LANES, width + (pair + 1) * LANES)
        query = stacked(q[:, cut] * BF(HD**-0.5), low_lane)
        shift = jnp.concatenate(
            [lse[:, 2 * pair : 2 * pair + 1], lse[:, 2 * pair + 1 : 2 * pair + 2]], axis=0
        )
        probs = [jnp.exp(s - shift) for s in heavy_scores(query, parts, bias, cut)]
        upper = stacked(grad[:, cut], low_lane)
        grads = [mm_t(upper, part[:, upcut]) for part in parts]
        center = sum(jnp.sum(p * g, axis=-1, keepdims=True) for p, g in zip(probs, grads))
        slopes = [(p * (g - center)).astype(BF) for p, g in zip(probs, grads)]
        dq = sum(mm(s, part[:, cut]) for s, part in zip(slopes, parts))
        dq_out[:, cut] = (merged(dq, low_lane) * HD**-0.5).astype(BF)
        for target, slope, prob in zip((da_out, db_out), slopes, probs):
            target[:, cut] = t_mm(slope, query).astype(BF)
            target[:, upcut] = t_mm(prob.astype(BF), upper).astype(BF)
    half = width // 2
    for target, source in ((ia_out, da_out), (ib_out, db_out)):
        for weight, side in ((w_own, info[0]), (w_got, 1 - info[0])):
            target[:, pl.ds(pl.multiple_of(side * half, half), half)] = mm_t(
                source[...], weight[:, width:]
            ).astype(BF)


def heavy_bwd(info, q, kins, kvs, lse, grad, w_own, w_got):
    rows = q.shape[0]
    width = q.shape[1] - LANES
    keys = kvs[0].shape[0]
    shapes = [sds((rows, width), BF)] + [sds((keys, 2 * width), BF)] * 2 + [sds((keys, width), BF)] * 2
    args = (info, q, *kins, *kvs, lse, grad, w_own, w_got)
    return call(
        heavy_bwd_body,
        shapes,
        (1,),
        [whole(a.shape) for a in args[1:]],
        [whole(s.shape) for s in shapes],
        args,
        flops=6_500_000_000,
        moved=15_000_000,
    )


def heavy_grads_body(info, *refs):
    micros = (len(refs) - 8) // 4
    hq, dhq, ho, dhy, lo, dy = refs[:6]
    kins, dkvs = (refs[6 : 6 + 2 * micros], refs[6 + 2 * micros : -2])
    other_out, own_out = (refs[-1], refs[-2])
    half = hq.shape[2] // 2
    every = range(micros)
    for target, side in ((other_out, 1 - info[0]), (own_out, info[0])):
        cut = pl.ds(pl.multiple_of(side * half, half), half)

        def put(unit, left, right, columns):
            for block in range(columns // COLS):
                at = unit + block
                total = sum(
                    t_mm(a, b[:, block * COLS : (block + 1) * COLS]) for a, b in zip(left, right)
                )
                target[at // 2, (at % 2) * half : (at % 2 + 1) * half] = total.astype(BF)
            return unit + columns // COLS

        unit = put(0, [hq[m, :, cut] for m in every], [dhq[m] for m in every], dhq.shape[2])
        unit = put(unit, [kin[:, cut] for kin in kins], dkvs, dkvs[0].shape[1])
        unit = put(unit, [ho[m, :, cut] for m in every], [dhy[m] for m in every], dhy.shape[2])
        part = lo.shape[2] // 2
        small_cut = pl.ds(pl.multiple_of(side * part, part), part)
        total = sum(t_mm(lo[m, :, small_cut], dy[m].astype(BF)) for m in every)
        pack_rows(target.at[pl.ds(unit // 2, 1)], total)


def heavy_grads(info, hq, dhq, ho, dhy, lo, dy, kins, dkvs):
    width = dhq.shape[2]
    units = (dhq.shape[2] + dkvs[0].shape[1] + dhy.shape[2]) // COLS
    shapes = [sds((units // 2 + 1, width, COLS), BF)] * 2
    args = (info, hq, dhq, ho, dhy, lo, dy, *kins, *dkvs)
    return call(
        heavy_grads_body,
        shapes,
        (1,),
        [whole(dhq.shape)] + [whole(a.shape) for a in args[2:]],
        [whole(s.shape) for s in shapes],
        args,
        flops=6_500_000_000,
        moved=28_000_000,
    )


def middle_body(info, x, up, cols, rows, small, gate, lo, lout, lout_got, ho, hout, y_out, low_out, pay_out, hy_out, gf_out):
    tok = x.shape[1]
    base = info[1]
    hy = mm(ho[0], hout[...])
    hy_out[0] = hy
    spread = onehot_rows(rows[0, 0], base, tok)
    part = lout.shape[0]
    own = lo[0, :, pl.ds(pl.multiple_of(info[0] * part, part), part)]
    other = lo[0, :, pl.ds(pl.multiple_of((1 - info[0]) * part, part), part)]
    light = mm(own, lout[...]) + mm(other, lout_got[...])
    y = x[0].astype(F32) + light + pick(spread, hy * gate[0, :, 0:1])
    y_out[0] = y
    low = (y * inverse_rms(y) * small[4:5].astype(F32)).astype(BF)
    low_out[0] = low
    take = onehot_cols(cols[2, 0], base, tok)
    taken = mm(take, low)
    width = x.shape[2]
    pay_out[0, :, :width] = taken.astype(BF)
    gf = jax.nn.sigmoid(jnp.sum(taken * small[2:3].astype(F32), axis=-1, keepdims=True))
    pay_out[0, :, width:] = (mm(take, up[0]) * gf).astype(BF)
    gf_out[0] = jnp.broadcast_to(gf, gf_out.shape[1:])


def second_of(shape):
    rank = len(shape)
    return pl.BlockSpec(
        (shape[0], 1) + tuple(shape[2:]), lambda i, *unused: (0, i) + (0,) * (rank - 2)
    )


def middle(info, x, up, cols, rows, small, gate, lo, lout, lout_got, ho, hout):
    micros, tok, width = x.shape
    count = cols.shape[2]
    shapes = [
        sds((micros, tok, width), F32),
        sds((micros, tok, width), BF),
        sds((micros, count, 2 * width), BF),
        sds((micros, count, width), F32),
        sds((micros, count, LANES), F32),
    ]
    args = (info, x, up, cols, rows, small, gate, lo, lout, lout_got, ho, hout)
    return call(
        middle_body,
        shapes,
        (micros,),
        [
            one_of(x.shape),
            one_of(up.shape),
            second_of(cols.shape),
            second_of(rows.shape),
            whole(small.shape),
            one_of(gate.shape),
            one_of(lo.shape),
            whole(lout.shape),
            whole(lout_got.shape),
            one_of(ho.shape),
            whole(hout.shape),
        ],
        [one_of(s.shape) for s in shapes],
        args,
        flops=2_000_000_000,
        moved=12_000_000,
    )


def pack_rows(target, values):
    step = values.shape[0] // 16
    cuts = values.shape[1] // COLS
    for slot in range(16):
        for cut in range(cuts):
            at = slot * step * cuts + cut * step
            target[0, at : at + step] = values[
                slot * step : (slot + 1) * step, cut * COLS : (cut + 1) * COLS
            ].astype(BF)


def gelu_parts(g):
    root = (2.0 / 3.141592653589793) ** 0.5
    square = g * g
    tanh = jnp.tanh(root * g * (1.0 + 0.044715 * square))
    bell = 0.5 * (1.0 + tanh)
    slope = bell + 0.5 * g * (1.0 - tanh * tanh) * (root * (1.0 + 3 * 0.044715 * square))
    return (g * bell, slope)


def hidden_both_ways(low, upstream, wg, wu, wd):
    g, u = (mm(low, wg), mm(low, wu))
    back = mm_t(upstream, wd)
    gelu, slope = gelu_parts(g)
    return ((gelu * u).astype(BF), (back * u * slope).astype(BF), (back * gelu).astype(BF))


def add_steps(step, pairs):
    @pl.when(step == 0)
    def first():
        for target, value in pairs:
            target[...] = value

    @pl.when(step > 0)
    def later():
        for target, value in pairs:
            target[...] += value


def ffn_local_body(info, a, ct, wg, wu, wd, z_out, dh_out):
    hidden, dg, du = hidden_both_ways(a[...], ct[...], wg[...], wu[...], wd[...])
    z = mm(hidden, wd[...])
    dh = mm_t(dg, wg[...]) + mm_t(du, wu[...])
    add_steps(pl.program_id(0), [(z_out, z), (dh_out, dh)])


def ffn_body(info, a, ct, wg, wu, wd, z_out, dh_out, own_gu, other_gu, own_dn, other_dn):
    step = pl.program_id(0)
    half = pl.num_programs(0) // 2
    width = a.shape[1] // 2
    hidden, dg, du = hidden_both_ways(a[...], ct[...], wg[...], wu[...], wd[...])
    z = mm(hidden, wd[...])
    dh = mm_t(dg, wg[...]) + mm_t(du, wu[...])
    add_steps(step, [(z_out, z), (dh_out, dh)])
    down = t_mm(hidden, ct[...])

    @pl.when(step < half)
    def send():
        pack_rows(other_dn, down)

    @pl.when(step >= half)
    def keep():
        pack_rows(own_dn, down)

    own = a[:, pl.ds(pl.multiple_of(info[0] * width, width), width)]
    other = a[:, pl.ds(pl.multiple_of((1 - info[0]) * width, width), width)]
    own_gu[0, :width] = t_mm(own, dg).astype(BF)
    own_gu[0, width:] = t_mm(own, du).astype(BF)
    other_gu[0, :width] = t_mm(other, dg).astype(BF)
    other_gu[0, width:] = t_mm(other, du).astype(BF)


def ffn_local(info, pay, w_gu, w_down, block):
    rows = pay.shape[0]
    hidden, width = w_down.shape
    steps = hidden // block
    return call(
        ffn_local_body,
        [sds((rows, width), F32)] * 2,
        (steps,),
        [
            pl.BlockSpec((rows, width), lambda i, *u: (0, 0)),
            pl.BlockSpec((rows, width), lambda i, *u: (0, 1)),
            pl.BlockSpec((width, block), lambda i, *u: (0, i)),
            pl.BlockSpec((width, block), lambda i, *u: (0, steps + i)),
            pl.BlockSpec((block, width), lambda i, *u: (i, 0)),
        ],
        [whole((rows, width))] * 2,
        (info, pay, pay, w_gu, w_gu, w_down),
        flops=2 * 6 * rows * hidden * width,
        moved=2 * 3 * hidden * width,
    )


def ffn(info, a, ct, w_gu, w_down):
    rows, width = a.shape
    hidden = w_down.shape[0]
    block = COLS
    steps = hidden // block
    half = steps // 2

    def natural(i, info):
        return jnp.where(i < half, (1 - info[0]) * half + i, info[0] * half + i - half)

    unit = (1, width, COLS)
    shapes = [
        sds((rows, width), F32),
        sds((rows, width), F32),
        sds((steps,) + unit[1:], BF),
        sds((steps,) + unit[1:], BF),
        sds((half,) + unit[1:], BF),
        sds((half,) + unit[1:], BF),
    ]
    return call(
        ffn_body,
        shapes,
        (steps,),
        [
            whole(a.shape),
            whole(ct.shape),
            pl.BlockSpec((width, block), lambda i, info: (0, natural(i, info))),
            pl.BlockSpec((width, block), lambda i, info: (0, steps + natural(i, info))),
            pl.BlockSpec((block, width), lambda i, info: (natural(i, info), 0)),
        ],
        [
            whole((rows, width)),
            whole((rows, width)),
            pl.BlockSpec(unit, lambda i, info: (natural(i, info), 0, 0)),
            pl.BlockSpec(unit, lambda i, info: (natural(i, info), 0, 0)),
            pl.BlockSpec(unit, lambda i, info: (jnp.maximum(i - half, 0), 0, 0)),
            pl.BlockSpec(unit, lambda i, info: (jnp.minimum(i, half - 1), 0, 0)),
        ],
        (info, a, ct, w_gu, w_gu, w_down),
        flops=2 * 9 * rows * hidden * width,
        moved=2 * 2 * 3 * hidden * width + rows * width * 12,
    )


def ffn_all_body(info, a, ct, w_gu, w_down, z_out, dh_out, own_gu, other_gu, own_dn, other_dn, turned, hid, slopes):
    step = pl.program_id(0)
    hidden, whole_width = w_down.shape
    steps = hidden // COLS
    half = steps // 2
    width = whole_width // 2

    @pl.when(step == 0)
    def turn():
        turned[...] = a[...].T

    @pl.when(step < steps)
    def block():
        at = jnp.where(step < half, (1 - info[0]) * half + step, info[0] * half + step - half)
        gate = pl.ds(pl.multiple_of(at * COLS, COLS), COLS)
        upper = pl.ds(pl.multiple_of(hidden + at * COLS, COLS), COLS)
        mixed, dg, du = hidden_both_ways(a[...], ct[...], w_gu[:, gate], w_gu[:, upper], w_down[gate])
        hid[:, gate] = mixed
        slopes[:, gate] = dg
        slopes[:, upper] = du
        down = t_mm(mixed, ct[...])

        @pl.when(step < half)
        def send():
            pack_rows(other_dn, down)

        @pl.when(step >= half)
        def keep():
            pack_rows(own_dn, down)

        for target, side in ((own_gu, info[0]), (other_gu, 1 - info[0])):
            rows = turned[pl.ds(pl.multiple_of(side * width, width), width)]
            target[0, :width] = mm(rows, dg).astype(BF)
            target[0, width:] = mm(rows, du).astype(BF)

    @pl.when(step == steps)
    def last():
        z_out[...] = mm(hid[...], w_down[...]).astype(BF)
        dh_out[...] = mm_t(slopes[...], w_gu[...]).astype(BF)


def ffn_all(info, a, ct, w_gu, w_down):
    rows, width = a.shape
    hidden = w_down.shape[0]
    steps = hidden // COLS
    half = steps // 2

    def natural(i, info):
        return jnp.where(i < half, (1 - info[0]) * half + i, info[0] * half + jnp.minimum(i - half, half - 1))

    unit = (1, width, COLS)
    shapes = [
        sds((rows, width), BF),
        sds((rows, width), BF),
        sds((steps,) + unit[1:], BF),
        sds((steps,) + unit[1:], BF),
        sds((half,) + unit[1:], BF),
        sds((half,) + unit[1:], BF),
    ]
    return call(
        ffn_all_body,
        shapes,
        (steps + 1,),
        [whole(a.shape), whole(ct.shape), whole(w_gu.shape), whole(w_down.shape)],
        [
            whole((rows, width)),
            whole((rows, width)),
            pl.BlockSpec(unit, lambda i, info: (natural(i, info), 0, 0)),
            pl.BlockSpec(unit, lambda i, info: (natural(i, info), 0, 0)),
            pl.BlockSpec(unit, lambda i, info: (jnp.minimum(jnp.maximum(i - half, 0), half - 1), 0, 0)),
            pl.BlockSpec(unit, lambda i, info: (jnp.minimum(i, half - 1), 0, 0)),
        ],
        (info, a, ct, w_gu, w_down),
        scratch=[
            pltpu.VMEM((width, rows), BF),
            pltpu.VMEM((rows, hidden), BF),
            pltpu.VMEM((rows, 2 * hidden), BF),
        ],
        flops=2 * 9 * rows * hidden * width,
        moved=2 * 2 * 3 * hidden * width + rows * width * 12,
    )


def plane_grads_body(info, near, far, wg, wu, wd, own_gu, other_gu, dn):
    width = wg.shape[0]
    half = width // 2
    sums = None
    for part in (near, far):
        low, upstream = (part[:, :width], part[:, width:])
        hidden, dg, du = hidden_both_ways(low, upstream, wg[...], wu[...], wd[...])
        own = part[:, pl.ds(pl.multiple_of(info[0] * half, half), half)]
        other = part[:, pl.ds(pl.multiple_of((1 - info[0]) * half, half), half)]
        terms = (t_mm(own, dg), t_mm(own, du), t_mm(other, dg), t_mm(other, du), t_mm(hidden, upstream))
        sums = terms if sums is None else tuple(p + q for p, q in zip(sums, terms))
    own_gu[0, :half] = sums[0].astype(BF)
    own_gu[0, half:] = sums[1].astype(BF)
    other_gu[0, :half] = sums[2].astype(BF)
    other_gu[0, half:] = sums[3].astype(BF)
    for cut in range(width // COLS):
        dn[0, cut * COLS : (cut + 1) * COLS] = sums[4][:, cut * COLS : (cut + 1) * COLS].astype(BF)


def plane_grads(info, near, far, w_gu, w_down):
    hidden, width = w_down.shape
    steps = hidden // COLS
    turns = steps // 8

    def block(i, info):
        return info[0] * (steps // 2) + lax.rem(info[3], 4) * turns + i

    unit = (1, width, COLS)
    spec = pl.BlockSpec(unit, lambda i, *u: (i, 0, 0))
    rows = 2 * near.shape[0]
    return call(
        plane_grads_body,
        [sds((turns, width, COLS), BF)] * 3,
        (turns,),
        [
            whole(near.shape),
            whole(far.shape),
            pl.BlockSpec((width, COLS), lambda i, info: (0, block(i, info))),
            pl.BlockSpec((width, COLS), lambda i, info: (0, steps + block(i, info))),
            pl.BlockSpec((COLS, width), lambda i, info: (block(i, info), 0)),
        ],
        [spec] * 3,
        (info, near, far, w_gu, w_gu, w_down),
        flops=2 * 6 * rows * turns * COLS * width,
        moved=9_000_000,
    )


def column_fold_body(order, info, first, second, third, keep, send):
    slots = 1 << len(order)
    size = keep.shape[2]
    place_z = info[3] // 4
    for part, source in enumerate((first, second, third)):
        for block in range(source.shape[0]):
            for slot in range(slots):
                owner = jnp.bitwise_xor(place_z, mask_of(slot, order))
                at = pl.ds(pl.multiple_of(owner * size, size), size)
                target = keep if slot < slots // 2 else send
                target[slot % (slots // 2), part * source.shape[0] + block] = source[block, at, :]


def column_fold(info, order, sources):
    slots = 1 << len(order)
    blocks, width, cols = sources[0].shape
    shape = sds((slots // 2, 3 * blocks, width // slots, cols), BF)
    return call(
        functools.partial(column_fold_body, order),
        [shape, shape],
        (1,),
        [whole(a.shape) for a in sources],
        [whole(shape.shape)] * 2,
        (info, *sources),
        moved=10_000_000,
        name="column_fold",
    )


def mid_back_body(
    info, y, up, z, dh2, zh, dff, ffr, gf, cols, rows, small, gate, lout, lout_got, hout, hy, hq,
    out, dy_out, dlo_out, dho_out, dhy_out, dsq_out, part_out,
):
    tok = y.shape[1]
    base = info[1]
    micro = pl.program_id(0)
    spread = onehot_rows(rows[2, 0], base, tok)
    take = onehot_cols(cols[2, 0], base, tok)
    values, top = (y[0], up[0].astype(F32))
    open_f = gf[0, :, 0:1]
    zhv = zh[0]
    out[0] = (values + z[0].astype(F32) + pick(spread, zhv * open_f)).astype(BF)
    taken = mm(take, up[0])
    dsf = jnp.sum(taken * zhv, axis=-1, keepdims=True) * open_f * (1.0 - open_f)
    back = dh2[0].astype(F32) + pick(spread, dff[0] + dsf * small[2:3].astype(F32))
    inv = inverse_rms(values)
    scaled = back * small[4:5].astype(F32)
    mean = jnp.mean(values * scaled, axis=-1, keepdims=True)
    dy = top + inv * scaled - values * (inv * inv * inv * mean)
    dy_out[0] = dy
    dgain = jnp.sum(back * values * inv, axis=0, keepdims=True)
    drf = jnp.sum(dsf * ffr[0].astype(F32), axis=0, keepdims=True)
    part_in = lout.shape[0]
    for weight, side in ((lout, info[0]), (lout_got, 1 - info[0])):
        at = pl.ds(pl.multiple_of(side * part_in, part_in), part_in)
        dlo_out[0, :, at] = mm_t(dy.astype(BF), weight[...]).astype(BF)
    dyq = pick(onehot_cols(cols[0, 0], base, tok), dy)
    open_q = gate[0, :, 0:1]
    dhy = (dyq * open_q).astype(BF)
    dhy_out[0] = dhy
    dsq = jnp.sum(dyq * hy[0], axis=-1, keepdims=True) * open_q * (1.0 - open_q)
    dsq_out[0] = jnp.broadcast_to(dsq, dsq_out.shape[1:])
    drq = jnp.sum(dsq * hq[0].astype(F32), axis=0, keepdims=True)
    dho_out[0] = mm_t(dhy, hout[...]).astype(BF)
    row = iota(part_out.shape, 0)
    part = jnp.where(row == 0, drq, jnp.where(row == 2, drf, jnp.where(row == 4, dgain, 0.0)))

    @pl.when(micro == 0)
    def first():
        part_out[...] = part

    @pl.when(micro > 0)
    def later():
        part_out[...] += part


def mid_back(info, y, up, z, dh2, zh, dff, ffr, gf, cols, rows, small, gate, lout, lout_got, hout, hy, hq):
    micros, tok, width = y.shape
    count = cols.shape[2]
    shapes = [
        sds((micros, tok, width), BF),
        sds((micros, tok, width), F32),
        sds((micros, tok, 2 * lout.shape[0]), BF),
        sds((micros, count, width), BF),
        sds((micros, count, width), BF),
        sds((micros, count, LANES), F32),
        sds((8, width), F32),
    ]
    return call(
        mid_back_body,
        shapes,
        (micros,),
        [
            one_of(y.shape),
            one_of(up.shape),
            one_of(z.shape),
            one_of(dh2.shape),
            one_of(zh.shape),
            one_of(dff.shape),
            pl.BlockSpec((1, count, width), lambda i, *u: (i, 0, 0)),
            one_of(gf.shape),
            second_of(cols.shape),
            second_of(rows.shape),
            whole(small.shape),
            one_of(gate.shape),
            whole(lout.shape),
            whole(lout_got.shape),
            whole(hout.shape),
            one_of(hy.shape),
            pl.BlockSpec((1, count, width), lambda i, *u: (i, 0, 0)),
        ],
        [one_of(s.shape) for s in shapes[:-1]] + [whole(shapes[-1].shape)],
        (info, y, up, z, dh2, zh, dff, ffr, gf, cols, rows, small, gate, lout, lout_got, hout, hy, hq),
        flops=3_000_000_000,
        moved=22_000_000,
    )


def light_join_body(info, x, small, dq, own, got_low, got_high, dl_out, own_out, other_out, low):
    tok, width = x.shape[1:]
    micros = x.shape[0]
    half = width // 2
    inner = dq.shape[2]
    for m in range(micros):
        dl_out[m, :, :inner] = dq[m]
        dl_out[m, WIN : tok - WIN, inner:] = own[m, WIN : tok - WIN].astype(BF)
        dl_out[m, :WIN, inner:] = (own[m, :WIN] + got_low[m].astype(F32)).astype(BF)
        dl_out[m, tok - WIN :, inner:] = (own[m, tok - WIN :] + got_high[m].astype(F32)).astype(BF)
        values = x[m].astype(F32)
        low[m] = (values * inverse_rms(values) * small[3:4].astype(F32)).astype(BF)
    for target, side in ((other_out, 1 - info[0]), (own_out, info[0])):
        cut = pl.ds(pl.multiple_of(side * half, half), half)
        for block in range(dl_out.shape[2] // COLS):
            total = sum(
                t_mm(low[m, :, cut], dl_out[m, :, block * COLS : (block + 1) * COLS])
                for m in range(micros)
            )
            target[block // 2, (block % 2) * half : (block % 2 + 1) * half] = total.astype(BF)


def light_join(info, x, small, dq, own, got_low, got_high):
    micros, tok, width = x.shape
    columns = dq.shape[2] + own.shape[2]
    shapes = [sds((micros, tok, columns), BF)] + [sds((columns // (2 * COLS), width, COLS), BF)] * 2
    args = (info, x, small, dq, own, got_low, got_high)
    return call(
        light_join_body,
        shapes,
        (1,),
        [whole(a.shape) for a in args[1:]],
        [whole(s.shape) for s in shapes],
        args,
        scratch=[pltpu.VMEM(x.shape, BF)],
        flops=2 * micros * tok * width * columns,
        moved=20_000_000,
    )


def in_back_body(
    info, x, dy, dl, dhq, dkin, dsq, rows, small, gate, h1k, l_own, l_got, h_own, h_got,
    grad_out, part_out,
):
    tok, width = x.shape[1:]
    micro = pl.program_id(0)
    base = info[1]
    light = dl[0]
    back = unhalved(info, mm_t(light, l_own[...]), mm_t(light, l_got[...]))
    given = dkin[0].astype(F32)
    open_k = gate[0, :, 1:2]
    source = h1k[0]
    dskv = jnp.sum(given * source, axis=-1, keepdims=True) * open_k * (1.0 - open_k)
    to_q = unhalved(info, mm_t(dhq[0], h_own[...]), mm_t(dhq[0], h_got[...]))
    to_q += dsq[0, :, 0:1] * small[0:1].astype(F32)
    to_k = given * open_k + dskv * small[1:2].astype(F32)
    back += pick(onehot_rows(rows[0, 0], base, tok), to_q)
    back += pick(onehot_rows(rows[1, 0], base, tok), to_k)
    values = x[0].astype(F32)
    inv = inverse_rms(values)
    scaled = back * small[3:4].astype(F32)
    mean = jnp.mean(values * scaled, axis=-1, keepdims=True)
    grad_out[0] = (dy[0] + inv * scaled - values * (inv * inv * inv * mean)).astype(BF)
    dgain = jnp.sum(back * values * inv, axis=0, keepdims=True)
    drk = jnp.sum(dskv * source.astype(BF).astype(F32), axis=0, keepdims=True)
    row = iota(part_out.shape, 0)
    part = jnp.where(row == 1, drk, jnp.where(row == 3, dgain, 0.0))

    @pl.when(micro == 0)
    def first():
        part_out[...] = part

    @pl.when(micro > 0)
    def later():
        part_out[...] += part


def in_back(info, x, dy, dl, dhq, dkin, dsq, rows, small, gate, h1k, l_own, l_got, h_own, h_got):
    micros, tok, width = x.shape
    shapes = [sds((micros, tok, width), BF), sds((8, width), F32)]
    firsts = (x, dy, dl, dhq, dkin, dsq)
    return call(
        in_back_body,
        shapes,
        (micros,),
        [one_of(a.shape) for a in firsts]
        + [second_of(rows.shape), whole(small.shape)]
        + [one_of(a.shape) for a in (gate, h1k)]
        + [whole(a.shape) for a in (l_own, l_got)]
        + [whole((h_own.shape[0], width))] * 2,
        [one_of(shapes[0].shape), whole(shapes[1].shape)],
        (info,) + firsts + (rows, small, gate, h1k, l_own, l_got, h_own, h_got),
        flops=2_600_000_000,
        moved=14_000_000,
    )


def mask_of(slot, order):
    bits = len(order)
    return sum(order[b] for b in range(bits) if (slot >> (bits - 1 - b)) & 1)


def fold_body(order, counts, info, *refs):
    sources = refs[: 2 * len(counts)]
    keep, send = refs[2 * len(counts) :]
    slots = 1 << len(order)
    size = keep.shape[2]
    step = pl.program_id(0)
    start = 0
    for which, count in enumerate(counts):
        own, got = sources[2 * which : 2 * which + 2]

        @pl.when((step >= start) & (step < start + count))
        def part():
            for slot in range(slots):
                owner = jnp.bitwise_xor(info[3], mask_of(slot, order))
                at = pl.ds(pl.multiple_of(owner * size, size), size)
                total = (own[0, at, :].astype(F32) + got[0, at, :].astype(F32)).astype(BF)
                if slot < slots // 2:
                    keep[slot, 0] = total
                else:
                    send[slot - slots // 2, 0] = total

        start += count


def fold(info, order, parts):
    slots = 1 << len(order)
    width = parts[0][0].shape[1]
    counts = [part[3] for part in parts]
    total = sum(counts)
    shape = sds((slots // 2, total, width // slots, COLS), BF)
    args, specs = ([], [])
    start = 0
    for own, got, first, count in parts:
        index = functools.partial(
            lambda first, start, count, i, *u: (
                first + jnp.minimum(jnp.maximum(i - start, 0), count - 1),
                0,
                0,
            ),
            first,
            start,
            count,
        )
        args += [own, got]
        specs += [pl.BlockSpec((1, width, COLS), index)] * 2
        start += count
    spec = pl.BlockSpec((slots // 2, 1, width // slots, COLS), lambda i, *u: (0, i, 0, 0))
    return call(
        functools.partial(fold_body, order, counts),
        [shape, shape],
        (total,),
        specs,
        [spec, spec],
        (info, *args),
        moved=total * width * COLS * 6,
    )


def flipped(value, bit):
    size = lax.axis_size("ctx")
    return lax.ppermute(value, "ctx", [(i, i ^ bit) for i in range(size)])


def tied(*values):
    return lax.optimization_barrier(values)


def scatter_step(keep, got):
    half = keep.shape[0] // 2
    if half == 0:
        return ((keep.astype(F32) + got.astype(F32)).astype(BF), None)
    return (
        (keep[:half].astype(F32) + got[:half].astype(F32)).astype(BF),
        (keep[half:].astype(F32) + got[half:].astype(F32)).astype(BF),
    )


def scatter_start(chunks, orders, stage):
    return [flipped(send, order[stage]) for (keep, send), order in zip(chunks, orders)]


def scatter_end(chunks, got):
    return [scatter_step(keep, g) for (keep, send), g in zip(chunks, got)]


def scatter_sum(keep, send, order):
    for bit in order:
        keep, send = scatter_step(keep, flipped(send, bit))
    return keep


def gather_start(values, orders, stage):
    return [flipped(value, order[-1 - stage]) for value, order in zip(values, orders)]


def gather_end(values, got):
    return [jnp.concatenate([value, g], axis=0) for value, g in zip(values, got)]


def gather_pair(value, order):
    for bit in order[:-1]:
        value = jnp.concatenate([value, flipped(value, bit)], axis=0)
    return (value, flipped(value, order[-1]))


def from_owner(info, order, near, far, owner, write):
    slots = 1 << len(order)
    distance = jnp.bitwise_xor(info[3], owner)
    slot = sum(
        jnp.where(jnp.bitwise_and(distance, bit) != 0, 1 << place, 0)
        for place, bit in enumerate(reversed(order))
    )
    inside = lax.rem(slot, slots // 2)

    @pl.when(slot < slots // 2)
    def close():
        write(near.at[inside])

    @pl.when(slot >= slots // 2)
    def distant():
        write(far.at[inside])


def unpack_gu_body(order, info, near, far, *outs):
    out = outs[-1]
    size = near.shape[2]
    per = out.shape[0] // size
    for turn in range(per):

        def write(source, turn=turn):
            for block in range(near.shape[1]):
                out[turn * size : (turn + 1) * size, block * COLS : (block + 1) * COLS] = source[
                    block
                ].astype(F32)

        from_owner(info, order, near, far, pl.program_id(1) * per + turn, write)


def write_dn(out, source, first, size, owner, row):
    cuts = out.shape[1] // COLS
    rows = size // cuts
    value = source[first].astype(F32)
    for cut in range(cuts):
        out[row + owner * rows : row + (owner + 1) * rows, cut * COLS : (cut + 1) * COLS] = value[
            cut * rows : (cut + 1) * rows
        ]


def unpack_dn_body(order, info, near, far, *outs):
    slots, blocks, size = near.shape[:3]
    for owner in range(2 * slots):

        def write(source, owner=owner):
            for block in range(blocks):
                write_dn(outs[-1], source, block, size, owner, block * COLS)

        from_owner(info, order, near, far, owner, write)


def unpack(body, info, order, pair, first, count, step, shape, grid_more, block, index, previous, name):
    near, far = pair
    slots, unused, size, unused_too = near.shape
    spec = pl.BlockSpec((slots, step, size, COLS), lambda i, *u: (0, first // step + i, 0, 0))
    args, specs, aliases = ([info, near, far], [spec, spec], {})
    if previous is not None:
        args.append(previous)
        specs.append(pl.BlockSpec(memory_space=pl.ANY))
        aliases = {3: 0}
    return pl.pallas_call(
        functools.partial(body, order),
        out_shape=sds(shape, F32),
        grid_spec=pltpu.PrefetchScalarGridSpec(
            num_scalar_prefetch=1,
            grid=(count // step,) + grid_more,
            in_specs=specs,
            out_specs=pl.BlockSpec(block, index),
        ),
        input_output_aliases=aliases,
        compiler_params=pltpu.CompilerParams(vmem_limit_bytes=32 * 1024 * 1024),
        cost_estimate=pl.CostEstimate(
            flops=0, bytes_accessed=count * 2 * slots * size * COLS * 6, transcendentals=0
        ),
        name=name,
    )(*args)


def unpack_gu(info, order, pair, first, count, total, base, previous, step):
    rows = pair[0].shape[0] * pair[0].shape[2]
    return unpack(
        unpack_gu_body, info, order, pair, first, count, step, (rows, 2 * total * COLS), (2,), (rows, step * COLS),
        lambda i, s, *u: (0, (s * total + base) // step + i), previous, "unpack_gu",
    )


def unpack_dn(info, order, pair, first, count, total, base, previous, step):
    width = 2 * pair[0].shape[0] * pair[0].shape[2]
    return unpack(
        unpack_dn_body, info, order, pair, first, count, step, (total * COLS, width), (), (step * COLS, width),
        lambda i, *u: (base // step + i, 0), previous, "unpack_dn",
    )


def unpack_plane_gu_body(info, full, out):
    sides, unused, planes, blocks, size, cols = full.shape
    turns = blocks // 3
    columns = out.shape[1] // sides
    for side in range(sides):
        for half in range(2):
            first = jnp.bitwise_xor(half, info[0]) * turns
            for plane in range(planes):
                for turn in range(turns):
                    at = side * columns + ((half * planes + plane) * turns + turn) * cols
                    out[:, at : at + cols] = full[side, 0, plane, first + turn].astype(F32)


def unpack_plane_gu(info, full, total):
    levels, planes, blocks, size, unused = full.shape
    rows, step = (2 * size, 48)
    turns = size // step
    view = full.reshape((2, levels // 2) + full.shape[1:])
    return call(
        unpack_plane_gu_body,
        sds((rows, 2 * total * COLS), F32),
        (rows // step,),
        [
            pl.BlockSpec(
                (2, 1, planes, blocks, step, COLS), lambda r, *u: (0, r // turns, 0, 0, r % turns, 0)
            )
        ],
        pl.BlockSpec((step, 2 * total * COLS), lambda r, *u: (r, 0)),
        (info, view),
        moved=2 * rows * total * COLS * 6,
        name="unpack_plane_gu",
    )


def unpack_plane_dn_body(info, full, out):
    levels, unused, blocks, size, cols = full.shape
    for level in range(levels):
        for block in range(blocks):
            for part in range(size // 64):
                cut, row = divmod(level * size + part * 64, COLS)
                at = block * COLS + row
                out[at : at + 64, cut * COLS : (cut + 1) * COLS] = full[
                    level, 0, block, part * 64 : (part + 1) * 64
                ].astype(F32)


def unpack_plane_dn(info, full):
    levels, planes, blocks, size, unused = full.shape
    turns = blocks // 3
    width = levels * size
    return call(
        unpack_plane_dn_body,
        sds((planes * turns * COLS, width), F32),
        (planes,),
        [pl.BlockSpec((levels, 1, turns, size, COLS), lambda q, *u: (0, q, 2, 0, 0))],
        pl.BlockSpec((turns * COLS, width), lambda q, *u: (q, 0)),
        (info, full),
        moved=planes * turns * COLS * width * 6,
        name="unpack_plane_dn",
    )


def unpack_units_body(order, first, info, near, far, *outs):
    slots, unused, size = near.shape[:3]
    homes = [
        (out, block * COLS) for out in outs for block in range(out.shape[1] // COLS)
    ]
    for owner in range(2 * slots):
        side, turn = divmod(owner, slots)

        def write(source, side=side, turn=turn):
            for at in range(side, len(homes), 2):
                out, column = homes[at]
                out[turn * size : (turn + 1) * size, column : column + COLS] = source[
                    first + at // 2
                ].astype(F32)

        from_owner(info, order, near, far, owner, write)


def unpack_units(info, order, pair, first, widths):
    slots, unused, size, unused_too = pair[0].shape
    shapes = [sds((slots * size, w), F32) for w in widths]
    args = [info, *pair]
    return call(
        functools.partial(unpack_units_body, order, first),
        shapes,
        (1,),
        [whole(a.shape) for a in args[1:]],
        [whole(s.shape) for s in shapes],
        args,
        moved=sum(widths) * slots * size * 6,
        name="unpack_units",
    )


def unpack_second_body(orders, info, *refs):
    pairs, outs = ([refs[i : i + 2] for i in (0, 2, 4)], refs[6:])
    qkv_out, hout_out, gu_out, lout_out, light_out, dn_out = outs
    slots, unused, size = refs[0].shape[:3]
    half = gu_out.shape[1] // 2
    blocks = half // COLS

    def homes(targets):
        return [(out, block * COLS) for out in targets for block in range(out.shape[1] // COLS)]

    def put_units(source, targets, side, rows):
        every = homes(targets)
        for at in range(side, len(every), 2):
            out, column = every[at]
            out[rows, column : column + COLS] = source[at // 2].astype(F32)

    for owner in range(2 * slots):
        side, turn = divmod(owner, slots)
        rows = slice(turn * size, (turn + 1) * size)

        def first(source, side=side, rows=rows):
            put_units(source, (qkv_out, hout_out), side, rows)

        def second(source, side=side, rows=rows, owner=owner):
            for block in range(blocks):
                at = side * half + block * COLS
                gu_out[rows, at : at + COLS] = source[block].astype(F32)
            write_dn(lout_out, source, blocks, size, owner, 0)

        def third(source, side=side, rows=rows, owner=owner):
            put_units(source, (light_out,), side, rows)
            used = light_out.shape[1] // (2 * COLS)
            for block in range(dn_out.shape[0] // COLS):
                write_dn(dn_out, source, used + block, size, owner, block * COLS)

        for order, (near, far), write in zip(orders, pairs, (first, second, third)):
            from_owner(info, order, near, far, owner, write)


def unpack_second(info, orders, pairs, shapes):
    args = [info] + [part for pair in pairs for part in pair]
    outs = [sds(shape, F32) for shape in shapes]
    return call(
        functools.partial(unpack_second_body, orders),
        outs,
        (1,),
        [whole(a.shape) for a in args[1:]],
        [whole(out.shape) for out in outs],
        args,
        moved=20_000_000,
        name="unpack_second",
    )


def plain_gu(own, other):
    blocks, width, cols = own.shape

    def rows(part):
        return part.reshape(blocks, 2, width // 2, cols).transpose(2, 1, 0, 3).reshape(width // 2, -1)

    return jnp.concatenate([rows(own), rows(other)], axis=0)


def plain_dn(own, other):
    blocks, width, cols = own.shape
    cuts = width // cols

    def rows(part):
        return (
            part.reshape(blocks, 16, cuts, width // (16 * cuts), cols)
            .transpose(0, 1, 3, 2, 4)
            .reshape(-1, width)
        )

    return jnp.concatenate([rows(own), rows(other)], axis=0)


def plain_units(own, other, widths):
    def unit(part, at):
        half = part.shape[1] // 2
        return part[at // 2, (at % 2) * half : (at % 2 + 1) * half]

    result, at = ([], 0)
    for columns in widths:
        count = columns // COLS
        result.append(
            jnp.concatenate(
                [
                    jnp.concatenate([unit(part, at + i) for i in range(count)], axis=1)
                    for part in (own, other)
                ],
                axis=0,
            )
        )
        at += count
    return result


def plain_sum(grads):
    parts = [lax.psum_scatter(g.astype(BF), "wsh", scatter_dimension=0, tiled=True) for g in grads]
    return tuple(g.astype(F32) for g in lax.psum(parts, "ctx"))


def per_device(
    tokens, cotangent, light_qkv, light_out, heavy_qkv, heavy_out, light_gu, light_down, heavy_gu, heavy_down,
    routers, gains, doc_starts, q_index, kv_index, ff_index,
):
    micros, unused, tok, width = tokens.shape
    count, groups = (lax.axis_size("ctx"), lax.axis_size("wsh"))
    direct = groups == 2 and count == 16
    place_ctx = lax.axis_index("ctx")
    side = lax.axis_index("wsh") if direct else 0
    base = place_ctx * tok
    info = jnp.concatenate(
        [
            jnp.stack([jnp.int32(side), base, jnp.int32(tok * count), place_ctx]).astype(jnp.int32),
            doc_starts[:, 0].reshape(-1),
        ]
    )
    swap = [(0, 1), (1, 0)]

    def pair_of(shard):
        if direct:
            return (shard, lax.ppermute(shard, "wsh", swap))
        full = lax.all_gather(shard, "wsh", axis=0, tiled=True)
        return (full[: full.shape[0] // 2], full[full.shape[0] // 2 :])

    def full_of(shard, axis=0):
        return lax.all_gather(shard, "wsh", axis=axis, tiled=True)

    vectors = jnp.concatenate([routers, gains, jnp.zeros((3, routers.shape[1]), BF)], axis=0)
    if direct:
        got = lax.ppermute(vectors, "wsh", swap)
        small = jnp.concatenate(
            [jnp.where(side == 0, vectors, got), jnp.where(side == 0, got, vectors)], axis=1
        )
    else:
        small = full_of(vectors, 1)
    x, up = (tokens[:, 0], cotangent[:, 0])
    index = jnp.stack([q_index[:, 0], kv_index[:, 0], ff_index[:, 0]])
    cols, rows = (index[..., None], index[:, :, None, :])
    hq_in, kin_pay, h1k, gate = routed_in(info, x, cols, small)
    l_own, l_got = pair_of(light_qkv)
    h_own, h_got = pair_of(heavy_qkv)
    o_own, o_got = pair_of(light_out)
    w_hout, w_hgu, w_hdown = (full_of(heavy_out), full_of(heavy_gu), full_of(heavy_down))
    w_lgu, w_ldown = (full_of(light_gu), full_of(light_down))
    kv_orders = ((8, 4, 2, 1), (8, 1, 4, 2))
    back_orders = [tuple(reversed(order)) for order in kv_orders]
    upward = [(i, i + 1) for i in range(count - 1)]
    downward = [(i + 1, i) for i in range(count - 1)]
    inner = light_qkv.shape[1] // 3
    every = range(micros)

    def rims(qkv):
        return (
            lax.ppermute(qkv[:, tok - WIN :, inner:], "ctx", upward),
            lax.ppermute(qkv[:, :WIN, inner:], "ctx", downward),
        )

    def project(kin):
        return key_project(info, kin, h_own, h_got)

    if direct:
        values = [kin_pay[m] for m in every]
        got = gather_start(values, back_orders, 0)
        qkv = light_in(info, x, small, l_own, l_got)
        got, qkv = tied(got, qkv)
        before, after = rims(qkv)
        values = gather_end(values, got)
        got = gather_start(values, back_orders, 1)
        q_pay = query_project(info, hq_in, h_own, h_got)
        got, q_pay, w_hout = tied(got, q_pay, w_hout)
        values = gather_end(values, got)
        got = gather_start(values, back_orders, 2)
        done = light_inner(info, qkv)
        got, before, after, done = tied(got, before, after, done)
        values = gather_end(values, got)
        got = gather_start(values, back_orders, 3)
        lo, light_lse = light_outer(info, qkv, before, after, done)
        near_kv = [project(v) for v in values]
        got, near_kv, lo, light_lse, w_hgu, w_hdown = tied(got, near_kv, lo, light_lse, w_hgu, w_hdown)
        kins = list(zip(values, got))
        kvs = [(n, project(f)) for n, f in zip(near_kv, got)]
    else:
        kins = []
        for m in every:
            full = lax.all_gather(kin_pay[m], "ctx", axis=0, tiled=True)
            kins.append((full[: full.shape[0] // 2], full[full.shape[0] // 2 :]))
        kvs = [tuple(project(k) for k in pair) for pair in kins]
        qkv = light_in(info, x, small, l_own, l_got)
        before, after = rims(qkv)
        lo, light_lse = light_outer(info, qkv, before, after, light_inner(info, qkv))
        q_pay = query_project(info, hq_in, h_own, h_got)
    heavy = [heavy_fwd(info, q_pay[m], kins[m], kvs[m]) for m in every]
    heavy, w_lgu, w_ldown = tied(heavy, w_lgu, w_ldown)
    ho = jnp.stack([h[0] for h in heavy])
    y, low2, pay, hy, gf = middle(info, x, up, cols, rows, small, gate, lo, o_own, o_got, ho, w_hout)

    def flat(value):
        return value.reshape(-1, value.shape[-1])

    orders = ((1, 2, 4, 8), (2, 4, 1, 8), (4, 1, 2, 8))
    back_two = ((1, 2, 4, 8), (2, 1, 4, 8), (4, 1, 2, 8))
    if direct:
        mine = flat(pay)
        plane = [flipped(mine, bit) for bit in (1, 2, 3)]
        zh, dff = ffn_local(info, mine, w_hgu, w_hdown, 2 * COLS)
        plane, zh, dff = tied(plane, zh, dff)
        near = jnp.concatenate([mine, *plane], axis=0)
        far = lax.ppermute(near, "wsh", swap)
    else:
        zh, dff, hgu_own, hgu_send, hdn_own, hdn_send = ffn(
            info, flat(pay[..., :width]), flat(pay[..., width:]), w_hgu, w_hdown
        )
    if direct:
        plane_own, plane_send, plane_dn = plane_grads(info, near, far, w_hgu, w_hdown)
        plane_got = lax.ppermute(plane_send, "wsh", swap)
        keep, send = column_fold(info, (1, 2), (plane_own, plane_got, plane_dn))
        send, low2 = tied(send, low2)
        got = flipped(send, 4)
    z, dh2, lgu_own, lgu_send, ldn_own, ldn_send = ffn_all(info, flat(low2), flat(up), w_lgu, w_ldown)
    if direct:
        got, z, dh2, lgu_send, ldn_send = tied(got, z, dh2, lgu_send, ldn_send)
        keep, send = scatter_step(keep, got)
        got = flipped(send, 8)
        lgu_got, ldn_got = (lax.ppermute(part, "wsh", swap) for part in (lgu_send, ldn_send))

    def by_micro(value):
        return value.reshape(micros, -1, value.shape[-1])

    out_tokens, dy, dlo, dho, dhy, dsq, part_two = mid_back(
        info, y, up, by_micro(z), by_micro(dh2), by_micro(zh), by_micro(dff), pay, gf, cols, rows, small, gate, o_own,
        o_got, w_hout, hy, hq_in,
    )
    dlq, dl_own, rim_low, rim_high = light_bwd_outer(info, qkv, before, after, light_lse, dlo)
    if direct:
        got, dlq, dl_own, rim_low, rim_high, dho = tied(got, dlq, dl_own, rim_low, rim_high, dho)
        keep, send = scatter_step(keep, got)
        plane_full = lax.all_gather(keep[0], "ctx", axis=0, tiled=False)
        plane_full = plane_full.reshape((count // 4, 4) + plane_full.shape[1:])
    got_low = lax.ppermute(rim_high, "ctx", upward)
    got_high = lax.ppermute(rim_low, "ctx", downward)
    backs = [
        heavy_bwd(info, q_pay[m], kins[m], kvs[m], heavy[m][1], dho[m], h_own, h_got) for m in every
    ]
    dhq = jnp.stack([b[0] for b in backs])
    shape = (count // 2, q_index.shape[2], width)
    back = [tuple(part.reshape(shape) for part in b[3:5]) for b in backs]
    dkvs = [part for b in backs for part in b[1:3]]
    if direct:
        back, dlo, dkvs, got_low, got_high = tied(back, dlo, dkvs, got_low, got_high)
        got_back = scatter_start(back, back_orders, 0)
    dlq, dl_own = light_bwd_inner(info, qkv, light_lse, dlo, dlq, dl_own)
    if direct:
        got_back, dlq, dl_own = tied(got_back, dlq, dl_own)
        back = scatter_end(back, got_back)
        got_back = scatter_start(back, back_orders, 1)
    kin_all = [part for pair in kins for part in pair]
    dl, la_own, la_send = light_join(info, x, small, dlq, dl_own, got_low, got_high)
    if direct:
        la_got = lax.ppermute(la_send, "wsh", swap)
    ha_own, ha_send = heavy_grads(info, hq_in, dhq, ho, dhy, lo, dy, kin_all, dkvs)
    if direct:
        got_back, ha_own, ha_send, la_got, dl = tied(got_back, ha_own, ha_send, la_got, dl)
        ha_got = lax.ppermute(ha_send, "wsh", swap)
        back = scatter_end(back, got_back)
        got_back = scatter_start(back, back_orders, 2)
        second = [
            fold(info, orders[0], [(ha_own, ha_got, 0, 6)]),
            fold(info, back_two[1], [(lgu_own, lgu_got, 0, 4), (ha_own, ha_got, 6, 1)]),
            fold(info, orders[2], [(la_own, la_got, 0, 3), (ldn_own, ldn_got, 0, 2)]),
        ]
        got_back, second, dl = tied(got_back, second, dl)
        *got_two, got_last = scatter_start(second, back_two, 0)
        back = scatter_end(back, got_back)
        got_back = scatter_start(back, back_orders, 3)
        (got_two,) = tied(got_two)
        *second, last = second
        second = scatter_end(second, got_two)
        got_two = scatter_start(second, back_two, 1)
        back, got_back, second = tied(back, got_back, second)
        back = scatter_end(back, got_back)
        dkin = jnp.concatenate([keep for keep, send in back], axis=0)
    else:
        dkin = jnp.stack(
            [
                lax.psum_scatter(jnp.concatenate(b[3:5], axis=0), "ctx", scatter_dimension=0, tiled=True)
                for b in backs
            ]
        )
    grad_tokens, part_one = in_back(
        info, x, dy, dl, dhq, dkin, dsq, rows, small, gate, h1k, l_own, l_got, h_own, h_got
    )
    widths = (heavy_qkv.shape[1], heavy_out.shape[1])
    vector = part_one + part_two
    if direct:
        half = width // 2
        mine = lax.dynamic_slice_in_dim(vector, side * half, half, 1)
        given = lax.dynamic_slice_in_dim(vector, (1 - side) * half, half, 1)
        got_two, got_last, mine, given = tied(got_two, got_last, mine, given)
        second, last = (scatter_end(second, got_two), scatter_step(last[0], got_last))
        got_two, got_last = (scatter_start(second, back_two, 2), flipped(last[1], back_two[2][1]))
        vector = mine + lax.ppermute(given, "wsh", swap)
        got_two, got_last, vector = tied(got_two, got_last, vector)
        second, last = (scatter_end(second, got_two), scatter_step(last[0], got_last))
        got_two, got_last = (scatter_start(second, back_two, 3), flipped(last[1], back_two[2][2]))
        got_vector = flipped(vector, 1)
        got_two, got_last, vector, got_vector = tied(got_two, got_last, vector, got_vector)
        second, last = (scatter_end(second, got_two), scatter_step(last[0], got_last))
        got_last = flipped(last[1], back_two[2][3])
        second, got_last, got_vector = tied(second, got_last, got_vector)
        vector = vector + got_vector
        second = [*second, scatter_step(last[0], got_last)]
        tails = [keep for keep, send in second]
        got_two, got_vector = (gather_start(tails, orders, 0), flipped(vector, 2))
        got_two, vector, got_vector = tied(got_two, vector, got_vector)
        tails, vector = (gather_end(tails, got_two), vector + got_vector)
        got_two, got_vector = (gather_start(tails, orders, 1), flipped(vector, 4))
        got_two, vector, got_vector = tied(got_two, vector, got_vector)
        tails, vector = (gather_end(tails, got_two), vector + got_vector)
        got_two, got_vector = (gather_start(tails, orders, 2), flipped(vector, 8))
        g_hdown = unpack_plane_dn(info, plane_full)
        got_two, vector, got_vector, g_hdown, plane_full = tied(got_two, vector, got_vector, g_hdown, plane_full)
        tails, vector = (gather_end(tails, got_two), vector + got_vector)
        got_two = gather_start(tails, orders, 3)
        g_hgu = unpack_plane_gu(info, plane_full, heavy_gu.shape[1] // (2 * COLS))
        got_two, g_hgu = tied(got_two, g_hgu)
        sums = list(zip(tails, got_two))
        g_hqkv, g_hout, g_lgu, g_lout, g_lqkv, g_ldown = unpack_second(
            info,
            orders,
            sums,
            [
                weight.shape
                for weight in (heavy_qkv, heavy_out, light_gu, light_out, light_qkv, light_down)
            ],
        )
    else:
        g_hqkv, g_hout = plain_units(ha_own, ha_send, widths)
        (g_lqkv,) = plain_units(la_own, la_send, (light_qkv.shape[1],))
        last = slice(ha_own.shape[0] - 1, ha_own.shape[0])
        g_lqkv, g_lout, g_hqkv, g_hout, g_lgu, g_ldown, g_hgu, g_hdown = plain_sum(
            [
                g_lqkv,
                plain_dn(ha_own[last], ha_send[last]),
                g_hqkv,
                g_hout,
                plain_gu(lgu_own, lgu_send),
                plain_dn(ldn_own, ldn_send),
                plain_gu(hgu_own, hgu_send),
                plain_dn(hdn_own, hdn_send),
            ]
        )
        vector = lax.psum(vector, ("ctx", "wsh"))
        part = width // groups
        vector = lax.dynamic_slice_in_dim(vector, lax.axis_index("wsh") * part, part, 1)
    return (
        out_tokens[:, None],
        grad_tokens[:, None],
        g_lqkv,
        g_lout,
        g_hqkv,
        g_hout,
        g_lgu,
        g_ldown,
        g_hgu,
        g_hdown,
        vector[:3],
        vector[3:5],
    )


def solution(mesh):
    return jax.shard_map(
        per_device,
        mesh=mesh,
        in_specs=(
            P(None, "wsh", "ctx", None),
            P(None, "wsh", "ctx", None),
            P("wsh", None),
            P("wsh", None),
            P("wsh", None),
            P("wsh", None),
            P("wsh", None),
            P("wsh", None),
            P("wsh", None),
            P("wsh", None),
            P(None, "wsh"),
            P(None, "wsh"),
            P(None, "wsh", None),
            P(None, "wsh", "ctx"),
            P(None, "wsh", "ctx"),
            P(None, "wsh", "ctx"),
        ),
        out_specs=(
            P(None, "wsh", "ctx", None),
            P(None, "wsh", "ctx", None),
            P("wsh", None),
            P("wsh", None),
            P("wsh", None),
            P("wsh", None),
            P("wsh", None),
            P("wsh", None),
            P("wsh", None),
            P("wsh", None),
            P(None, "wsh"),
            P(None, "wsh"),
        ),
        check_vma=False,
    )
```

```python
import functools

import jax
import jax.numpy as jnp
from jax import lax
from jax.experimental import pallas as pl
from jax.experimental.pallas import tpu as pltpu
from jax.sharding import PartitionSpec as P

HD = 64
WIN = 128
LANES = 128
COLS = 256
FAR = -1e30
EPS = 1e-06
BF = jnp.bfloat16
F32 = jnp.float32


def mm(left, right):
    return lax.dot_general(left, right, (((1,), (0,)), ((), ())), preferred_element_type=F32)


def mm_t(left, right):
    return lax.dot_general(left, right, (((1,), (1,)), ((), ())), preferred_element_type=F32)


def t_mm(left, right):
    return lax.dot_general(left, right, (((0,), (0,)), ((), ())), preferred_element_type=F32)


def pick(onehot, values):
    high = values.astype(BF)
    low = (values - high.astype(F32)).astype(BF)
    return mm(onehot, high) + mm(onehot, low)


def iota(shape, dim):
    return lax.broadcasted_iota(jnp.int32, shape, dim)


def onehot_cols(positions, base, length):
    return (iota((positions.shape[0], length), 1) == positions - base).astype(F32).astype(BF)


def onehot_rows(positions, base, length):
    return (iota((length, positions.shape[1]), 0) == positions - base).astype(F32).astype(BF)


def segment(info, micro, positions):
    total = jnp.full(positions.shape, -1, jnp.int32)
    for start in range(5):
        total += (positions >= info[4 + micro * 5 + start]).astype(jnp.int32)
    return total


def inverse_rms(values):
    return lax.rsqrt(jnp.mean(values * values, axis=-1, keepdims=True) + EPS)


def halves(info, values):
    half = values.shape[1] // 2
    first, second = (values[:, :half], values[:, half:])
    lower = info[0] == 0
    return (jnp.where(lower, first, second), jnp.where(lower, second, first))


def unhalved(info, own, other):
    lower = info[0] == 0
    return jnp.concatenate([jnp.where(lower, own, other), jnp.where(lower, other, own)], axis=1)


def call(body, outs, grid, in_specs, out_specs, args, scratch=(), flops=0, moved=0, limit=48, name=None):
    return pl.pallas_call(
        body,
        name=name or getattr(body, "__name__", "kernel"),
        out_shape=outs,
        grid_spec=pltpu.PrefetchScalarGridSpec(
            num_scalar_prefetch=1,
            grid=grid,
            in_specs=in_specs,
            out_specs=out_specs,
            scratch_shapes=list(scratch),
        ),
        compiler_params=pltpu.CompilerParams(vmem_limit_bytes=limit * 1024 * 1024),
        cost_estimate=pl.CostEstimate(flops=flops, bytes_accessed=moved, transcendentals=0),
    )(*args)


def whole(shape):
    rank = len(shape)
    return pl.BlockSpec(tuple(shape), lambda *unused: (0,) * rank)


def one_of(shape):
    rank = len(shape)
    return pl.BlockSpec((1,) + tuple(shape[1:]), lambda i, *unused: (i,) + (0,) * (rank - 1))


def sds(shape, dtype):
    return jax.ShapeDtypeStruct(tuple(shape), dtype)


def routed_body(info, x, cols, small, q_out, kin_out, h1k_out, gate_out):
    micros, tok, width = x.shape
    rows = cols.shape[2]
    base = info[1]
    gain = small[3:4].astype(F32)
    lane = iota((rows, LANES), 1)
    for m in range(micros):
        both = jnp.concatenate([cols[0, m], cols[1, m]], axis=0)
        got = mm(onehot_cols(both, base, tok), x[m])
        xq, xk = (got[:rows], got[rows:])
        low_q = (xq * inverse_rms(xq) * gain).astype(BF)
        h1k = xk * inverse_rms(xk) * gain
        low_k = h1k.astype(BF)
        gate_q = jax.nn.sigmoid(
            jnp.sum(low_q.astype(F32) * small[0:1].astype(F32), axis=-1, keepdims=True)
        )
        gate_k = jax.nn.sigmoid(
            jnp.sum(low_k.astype(F32) * small[1:2].astype(F32), axis=-1, keepdims=True)
        )
        seg_q = segment(info, m, cols[0, m])
        seg_k = segment(info, m, cols[1, m])
        q_out[m, :, :width] = low_q
        q_out[m, :, width:] = (lane == seg_q).astype(F32).astype(BF)
        kin_out[m, :, :width] = (h1k * gate_k).astype(BF)
        kin_out[m, :, width:] = jnp.where((lane < 8) & (lane != seg_k), FAR, 0.0).astype(BF)
        h1k_out[m] = h1k
        gate_out[m] = jnp.where(lane == 0, gate_q, gate_k)


def routed_in(info, x, cols, small):
    micros, unused, width = x.shape
    rows = cols.shape[2]
    shapes = [
        sds((micros, rows, width + LANES), BF),
        sds((micros, rows, width + LANES), BF),
        sds((micros, rows, width), F32),
        sds((micros, rows, LANES), F32),
    ]
    args = (info, x, cols, small)
    return call(
        routed_body,
        shapes,
        (1,),
        [whole(a.shape) for a in args[1:]],
        [whole(s.shape) for s in shapes],
        args,
        flops=200_000_000,
        moved=3_000_000,
    )


def query_body(info, low, w_own, w_got, out):
    width = 2 * w_own.shape[0]
    for m in range(low.shape[0]):
        own, other = halves(info, low[m, :, :width])
        out[m, :, :width] = (mm(own, w_own[...]) + mm(other, w_got[...])).astype(BF)
        out[m, :, width:] = low[m, :, width:]


def query_project(info, low, w_own, w_got):
    half = w_own.shape[0]
    return call(
        query_body,
        sds(low.shape, BF),
        (1,),
        [whole(low.shape)] + [whole((half, 2 * half))] * 2,
        whole(low.shape),
        (info, low, w_own, w_got),
        flops=2 * low.shape[0] * low.shape[1] * 4 * half * half,
        moved=2_000_000,
    )


def light_in_body(info, x, small, w_own, w_got, out):
    values = x[0].astype(F32)
    low = (values * inverse_rms(values) * small[3:4].astype(F32)).astype(BF)
    own, other = halves(info, low)
    out[0] = (mm(own, w_own[...]) + mm(other, w_got[...])).astype(BF)


def light_in(info, x, small, w_own, w_got):
    micros, tok, width = x.shape
    columns = w_own.shape[1]
    split = 2
    rows = tok // split
    spec = lambda n: pl.BlockSpec((1, rows, n), lambda i, *u: (i // split, i % split, 0))
    return call(
        light_in_body,
        sds((micros, tok, columns), BF),
        (micros * split,),
        [spec(width), whole(small.shape), whole(w_own.shape), whole(w_got.shape)],
        spec(columns),
        (info, x, small, w_own, w_got),
        flops=2 * micros * tok * width * columns,
        moved=8_000_000,
    )


def fill_near(near, qkv, before, after):
    tok = qkv.shape[1]
    inner = near.shape[1] // 2
    near[:WIN] = before[0]
    near[WIN : WIN + tok] = qkv[0, :, inner:]
    near[WIN + tok :] = after[0]


def light_bias(info, micro, block):
    start = info[1] + block * WIN
    rows, columns = (WIN, 3 * WIN)
    row_pos = start + iota((rows, 1), 0)
    col_pos = start - WIN + iota((1, columns), 1)
    seg_row = segment(info, micro, row_pos)
    seg_col = jnp.where((col_pos >= 0) & (col_pos < info[2]), segment(info, micro, col_pos), -1)
    shift = iota((rows, columns), 0) + WIN - iota((rows, columns), 1)
    allowed = (jnp.abs(shift) < WIN) & (seg_row == seg_col)
    bias = jnp.where(allowed, 0.0, FAR)
    return jnp.concatenate([bias, bias], axis=0)


def stacked(pair, low_lane):
    zero = jnp.zeros_like(pair)
    return jnp.concatenate(
        [jnp.where(low_lane, pair, zero), jnp.where(low_lane, zero, pair)], axis=0
    )


def merged(values, low_lane):
    rows = values.shape[0] // 2
    return jnp.where(low_lane, values[:rows], values[rows:])


def light_fwd_blocks(info, qkv, near, blocks, emit):
    micro = pl.program_id(0)
    inner = near.shape[1] // 2
    low_lane = iota((WIN, LANES), 1) < HD
    lane = iota((WIN, LANES), 1)
    for place, block in enumerate(blocks):
        at = slice(block * WIN, (block + 1) * WIN)
        around = slice(block * WIN, (block + 3) * WIN)
        bias = light_bias(info, micro, block)
        stats = jnp.zeros((WIN, LANES), F32)
        for pair in range(inner // LANES):
            cut = slice(pair * LANES, (pair + 1) * LANES)
            query = stacked(qkv[0, at, cut] * BF(HD**-0.5), low_lane)
            scores = mm_t(query, near[around, cut]) + bias
            top = jnp.max(scores, axis=-1, keepdims=True)
            weights = jnp.exp(scores - top)
            total = jnp.sum(weights, axis=-1, keepdims=True)
            value = near[around, inner + pair * LANES : inner + (pair + 1) * LANES]
            mixed = mm((weights * (1.0 / total)).astype(BF), value)
            emit(place, cut, merged(mixed, low_lane).astype(BF))
            lse = top + jnp.log(total)
            stats = jnp.where(lane == 2 * pair, lse[:WIN], stats)
            stats = jnp.where(lane == 2 * pair + 1, lse[WIN:], stats)
        emit(place, None, stats)


def light_inner_body(info, qkv, out, lse_out, near):
    tok = qkv.shape[1]
    inner = out.shape[2]
    near[WIN : WIN + tok] = qkv[0, :, inner:]

    def emit(place, cut, value):
        rows = slice(place * WIN, (place + 1) * WIN)
        if cut is None:
            lse_out[0, rows] = value
        else:
            out[0, rows, cut] = value

    light_fwd_blocks(info, qkv, near, range(1, tok // WIN - 1), emit)


def light_outer_body(info, qkv, before, after, done, lse_done, out, lse_out, near):
    tok = qkv.shape[1]
    fill_near(near, qkv, before, after)
    out[0, WIN : tok - WIN] = done[0]
    lse_out[0, WIN : tok - WIN] = lse_done[0]
    blocks = (0, tok // WIN - 1)

    def emit(place, cut, value):
        rows = slice(blocks[place] * WIN, (blocks[place] + 1) * WIN)
        if cut is None:
            lse_out[0, rows] = value
        else:
            out[0, rows, cut] = value

    light_fwd_blocks(info, qkv, near, blocks, emit)


def light_inner(info, qkv):
    micros, tok, columns = qkv.shape
    inner = columns // 3
    shapes = [sds((micros, tok - 2 * WIN, inner), BF), sds((micros, tok - 2 * WIN, LANES), F32)]
    return call(
        light_inner_body,
        shapes,
        (micros,),
        [one_of(qkv.shape)],
        [one_of(a.shape) for a in shapes],
        (info, qkv),
        scratch=[pltpu.VMEM((tok + 2 * WIN, 2 * inner), BF)],
        flops=2_000_000_000,
        moved=4_000_000,
    )


def light_outer(info, qkv, before, after, done):
    micros, tok, columns = qkv.shape
    inner = columns // 3
    shapes = [sds((micros, tok, inner), BF), sds((micros, tok, LANES), F32)]
    args = (info, qkv, before, after, *done)
    return call(
        light_outer_body,
        shapes,
        (micros,),
        [one_of(a.shape) for a in args[1:]],
        [one_of(a.shape) for a in shapes],
        args,
        scratch=[pltpu.VMEM((tok + 2 * WIN, 2 * inner), BF)],
        flops=2_000_000_000,
        moved=6_000_000,
    )


def light_bwd_blocks(info, qkv, lse, grad, near, dk, dv, blocks, emit):
    micro = pl.program_id(0)
    inner = grad.shape[2]
    low_lane = iota((WIN, LANES), 1) < HD
    for place, block in enumerate(blocks):
        at = slice(block * WIN, (block + 1) * WIN)
        around = slice(block * WIN, (block + 3) * WIN)
        bias = light_bias(info, micro, block)
        stats = lse[0, at, :]
        for pair in range(inner // LANES):
            cut = slice(pair * LANES, (pair + 1) * LANES)
            query = stacked(qkv[0, at, cut] * BF(HD**-0.5), low_lane)
            key = near[around, cut]
            value = near[around, inner + pair * LANES : inner + (pair + 1) * LANES]
            shift = jnp.concatenate(
                [stats[:, 2 * pair : 2 * pair + 1], stats[:, 2 * pair + 1 : 2 * pair + 2]], axis=0
            )
            probs = jnp.exp(mm_t(query, key) + bias - shift)
            upper = stacked(grad[0, at, cut], low_lane)
            grad_probs = mm_t(upper, value)
            center = jnp.sum(probs * grad_probs, axis=-1, keepdims=True)
            slope = (probs * (grad_probs - center)).astype(BF)
            emit(place, cut, (merged(mm(slope, key), low_lane) * HD**-0.5).astype(BF))
            dk[around, cut] += t_mm(slope, query)
            dv[around, cut] += t_mm(probs.astype(BF), upper)


def light_bwd_outer_body(info, qkv, before, after, lse, grad, dq_out, own_out, low_out, high_out, near, dk, dv):
    tok = qkv.shape[1]
    inner = grad.shape[2]
    fill_near(near, qkv, before, after)
    dk[...] = jnp.zeros_like(dk)
    dv[...] = jnp.zeros_like(dv)

    def emit(place, cut, value):
        dq_out[0, place * WIN : (place + 1) * WIN, cut] = value

    light_bwd_blocks(info, qkv, lse, grad, near, dk, dv, (0, tok // WIN - 1), emit)
    for first, source in ((0, dk), (inner, dv)):
        to = slice(first, first + inner)
        own_out[0, :, to] = source[WIN : WIN + tok]
        low_out[0, :, to] = source[:WIN].astype(BF)
        high_out[0, :, to] = source[WIN + tok :].astype(BF)


def light_bwd_inner_body(info, qkv, lse, grad, dq_in, own_in, dq_out, own_out, near, dk, dv):
    tok = qkv.shape[1]
    inner = grad.shape[2]
    near[WIN : WIN + tok] = qkv[0, :, inner:]
    dk[WIN : WIN + tok] = own_in[0, :, :inner]
    dv[WIN : WIN + tok] = own_in[0, :, inner:]
    dq_out[0, :WIN] = dq_in[0, :WIN]
    dq_out[0, tok - WIN :] = dq_in[0, WIN:]
    blocks = range(1, tok // WIN - 1)

    def emit(place, cut, value):
        dq_out[0, blocks[place] * WIN : (blocks[place] + 1) * WIN, cut] = value

    light_bwd_blocks(info, qkv, lse, grad, near, dk, dv, blocks, emit)
    own_out[0, :, :inner] = dk[WIN : WIN + tok]
    own_out[0, :, inner:] = dv[WIN : WIN + tok]


def light_bwd_scratch(tok, inner):
    return [
        pltpu.VMEM((tok + 2 * WIN, 2 * inner), BF),
        pltpu.VMEM((tok + 2 * WIN, inner), F32),
        pltpu.VMEM((tok + 2 * WIN, inner), F32),
    ]


def light_bwd_outer(info, qkv, before, after, lse, grad):
    micros, tok, columns = qkv.shape
    inner = columns // 3
    shapes = [
        sds((micros, 2 * WIN, inner), BF),
        sds((micros, tok, 2 * inner), F32),
        sds((micros, WIN, 2 * inner), BF),
        sds((micros, WIN, 2 * inner), BF),
    ]
    args = (info, qkv, before, after, lse, grad)
    return call(
        light_bwd_outer_body,
        shapes,
        (micros,),
        [one_of(a.shape) for a in args[1:]],
        [one_of(a.shape) for a in shapes],
        args,
        scratch=light_bwd_scratch(tok, inner),
        flops=5_000_000_000,
        moved=12_000_000,
    )


def light_bwd_inner(info, qkv, lse, grad, dq, own):
    micros, tok, columns = qkv.shape
    inner = columns // 3
    shapes = [sds((micros, tok, inner), BF), sds((micros, tok, 2 * inner), F32)]
    args = (info, qkv, lse, grad, dq, own)
    return call(
        light_bwd_inner_body,
        shapes,
        (micros,),
        [one_of(a.shape) for a in args[1:]],
        [one_of(a.shape) for a in shapes],
        args,
        scratch=light_bwd_scratch(tok, inner),
        flops=5_000_000_000,
        moved=14_000_000,
    )


def key_body(info, kin, w_own, w_got, out):
    half = w_own.shape[0]
    width = 2 * half
    own = kin[:, pl.ds(pl.multiple_of(info[0] * half, half), half)]
    other = kin[:, pl.ds(pl.multiple_of((1 - info[0]) * half, half), half)]
    out[...] = (mm(own, w_own[:, width:]) + mm(other, w_got[:, width:])).astype(BF)


def key_project(info, kin, w_own, w_got):
    shape = sds((kin.shape[0], 2 * (kin.shape[1] - LANES)), BF)
    args = (info, kin, w_own, w_got)
    return call(
        key_body,
        shape,
        (1,),
        [whole(a.shape) for a in args[1:]],
        whole(shape.shape),
        args,
        flops=1_200_000_000,
        moved=6_000_000,
    )


def heavy_scores(query, parts, bias, cut):
    return [mm_t(query, part[:, cut]) + b for part, b in zip(parts, bias)]


def heavy_fwd_body(info, q, kin_a, kin_b, kv_a, kv_b, out, lse_out):
    rows, width = out.shape
    parts = (kv_a, kv_b)
    low_lane = iota((rows, LANES), 1) < HD
    lane = iota((rows, LANES), 1)
    feature = jnp.concatenate([q[:, width:]] * 2, axis=0)
    bias = [mm_t(feature, kin[:, width:]) for kin in (kin_a, kin_b)]
    stats = jnp.zeros((rows, LANES), F32)
    for pair in range(width // LANES):
        cut = slice(pair * LANES, (pair + 1) * LANES)
        query = stacked(q[:, cut] * BF(HD**-0.5), low_lane)
        scores = heavy_scores(query, parts, bias, cut)
        top = functools.reduce(
            jnp.maximum, [jnp.max(s, axis=-1, keepdims=True) for s in scores]
        )
        weights = [jnp.exp(s - top) for s in scores]
        total = sum(jnp.sum(w, axis=-1, keepdims=True) for w in weights)
        scale = 1.0 / total
        mixed = sum(
            mm((w * scale).astype(BF), part[:, width + pair * LANES : width + (pair + 1) * LANES])
            for w, part in zip(weights, parts)
        )
        out[:, cut] = merged(mixed, low_lane).astype(BF)
        lse = top + jnp.log(total)
        stats = jnp.where(lane == 2 * pair, lse[:rows], stats)
        stats = jnp.where(lane == 2 * pair + 1, lse[rows:], stats)
    lse_out[...] = stats


def heavy_fwd(info, q, kins, kvs):
    rows = q.shape[0]
    width = q.shape[1] - LANES
    shapes = [sds((rows, width), BF), sds((rows, LANES), F32)]
    args = (info, q, *kins, *kvs)
    return call(
        heavy_fwd_body,
        shapes,
        (1,),
        [whole(a.shape) for a in args[1:]],
        [whole(s.shape) for s in shapes],
        args,
        flops=1_500_000_000,
        moved=5_000_000,
    )


def heavy_bwd_body(info, q, kin_a, kin_b, kv_a, kv_b, lse, grad, w_own, w_got, dq_out, da_out, db_out, ia_out, ib_out):
    rows, width = grad.shape
    parts = (kv_a, kv_b)
    low_lane = iota((rows, LANES), 1) < HD
    feature = jnp.concatenate([q[:, width:]] * 2, axis=0)
    bias = [mm_t(feature, kin[:, width:]) for kin in (kin_a, kin_b)]
    for pair in range(width // LANES):
        cut = slice(pair * LANES, (pair + 1) * LANES)
        upcut = slice(width + pair * LANES, width + (pair + 1) * LANES)
        query = stacked(q[:, cut] * BF(HD**-0.5), low_lane)
        shift = jnp.concatenate(
            [lse[:, 2 * pair : 2 * pair + 1], lse[:, 2 * pair + 1 : 2 * pair + 2]], axis=0
        )
        probs = [jnp.exp(s - shift) for s in heavy_scores(query, parts, bias, cut)]
        upper = stacked(grad[:, cut], low_lane)
        grads = [mm_t(upper, part[:, upcut]) for part in parts]
        center = sum(jnp.sum(p * g, axis=-1, keepdims=True) for p, g in zip(probs, grads))
        slopes = [(p * (g - center)).astype(BF) for p, g in zip(probs, grads)]
        dq = sum(mm(s, part[:, cut]) for s, part in zip(slopes, parts))
        dq_out[:, cut] = (merged(dq, low_lane) * HD**-0.5).astype(BF)
        for target, slope, prob in zip((da_out, db_out), slopes, probs):
            target[:, cut] = t_mm(slope, query).astype(BF)
            target[:, upcut] = t_mm(prob.astype(BF), upper).astype(BF)
    half = width // 2
    for target, source in ((ia_out, da_out), (ib_out, db_out)):
        for weight, side in ((w_own, info[0]), (w_got, 1 - info[0])):
            target[:, pl.ds(pl.multiple_of(side * half, half), half)] = mm_t(
                source[...], weight[:, width:]
            ).astype(BF)


def heavy_bwd(info, q, kins, kvs, lse, grad, w_own, w_got):
    rows = q.shape[0]
    width = q.shape[1] - LANES
    keys = kvs[0].shape[0]
    shapes = [sds((rows, width), BF)] + [sds((keys, 2 * width), BF)] * 2 + [sds((keys, width), BF)] * 2
    args = (info, q, *kins, *kvs, lse, grad, w_own, w_got)
    return call(
        heavy_bwd_body,
        shapes,
        (1,),
        [whole(a.shape) for a in args[1:]],
        [whole(s.shape) for s in shapes],
        args,
        flops=6_500_000_000,
        moved=15_000_000,
    )


def heavy_grads_body(info, *refs):
    micros = (len(refs) - 8) // 4
    hq, dhq, ho, dhy, lo, dy = refs[:6]
    kins, dkvs = (refs[6 : 6 + 2 * micros], refs[6 + 2 * micros : -2])
    other_out, own_out = (refs[-1], refs[-2])
    half = hq.shape[2] // 2
    every = range(micros)
    for target, side in ((other_out, 1 - info[0]), (own_out, info[0])):
        cut = pl.ds(pl.multiple_of(side * half, half), half)

        def put(unit, left, right, columns):
            for block in range(columns // COLS):
                at = unit + block
                total = sum(
                    t_mm(a, b[:, block * COLS : (block + 1) * COLS]) for a, b in zip(left, right)
                )
                target[at // 2, (at % 2) * half : (at % 2 + 1) * half] = total.astype(BF)
            return unit + columns // COLS

        unit = put(0, [hq[m, :, cut] for m in every], [dhq[m] for m in every], dhq.shape[2])
        unit = put(unit, [kin[:, cut] for kin in kins], dkvs, dkvs[0].shape[1])
        unit = put(unit, [ho[m, :, cut] for m in every], [dhy[m] for m in every], dhy.shape[2])
        part = lo.shape[2] // 2
        small_cut = pl.ds(pl.multiple_of(side * part, part), part)
        total = sum(t_mm(lo[m, :, small_cut], dy[m].astype(BF)) for m in every)
        pack_rows(target.at[pl.ds(unit // 2, 1)], total)


def heavy_grads(info, hq, dhq, ho, dhy, lo, dy, kins, dkvs):
    width = dhq.shape[2]
    units = (dhq.shape[2] + dkvs[0].shape[1] + dhy.shape[2]) // COLS
    shapes = [sds((units // 2 + 1, width, COLS), BF)] * 2
    args = (info, hq, dhq, ho, dhy, lo, dy, *kins, *dkvs)
    return call(
        heavy_grads_body,
        shapes,
        (1,),
        [whole(dhq.shape)] + [whole(a.shape) for a in args[2:]],
        [whole(s.shape) for s in shapes],
        args,
        flops=6_500_000_000,
        moved=28_000_000,
    )


def middle_body(info, x, up, cols, rows, small, gate, lo, lout, lout_got, ho, hout, y_out, low_out, pay_out, hy_out, gf_out):
    tok = x.shape[1]
    base = info[1]
    hy = mm(ho[0], hout[...])
    hy_out[0] = hy
    spread = onehot_rows(rows[0, 0], base, tok)
    part = lout.shape[0]
    own = lo[0, :, pl.ds(pl.multiple_of(info[0] * part, part), part)]
    other = lo[0, :, pl.ds(pl.multiple_of((1 - info[0]) * part, part), part)]
    light = mm(own, lout[...]) + mm(other, lout_got[...])
    y = x[0].astype(F32) + light + pick(spread, hy * gate[0, :, 0:1])
    y_out[0] = y
    low = (y * inverse_rms(y) * small[4:5].astype(F32)).astype(BF)
    low_out[0] = low
    take = onehot_cols(cols[2, 0], base, tok)
    taken = mm(take, low)
    width = x.shape[2]
    pay_out[0, :, :width] = taken.astype(BF)
    gf = jax.nn.sigmoid(jnp.sum(taken * small[2:3].astype(F32), axis=-1, keepdims=True))
    pay_out[0, :, width:] = (mm(take, up[0]) * gf).astype(BF)
    gf_out[0] = jnp.broadcast_to(gf, gf_out.shape[1:])


def second_of(shape):
    rank = len(shape)
    return pl.BlockSpec(
        (shape[0], 1) + tuple(shape[2:]), lambda i, *unused: (0, i) + (0,) * (rank - 2)
    )


def middle(info, x, up, cols, rows, small, gate, lo, lout, lout_got, ho, hout):
    micros, tok, width = x.shape
    count = cols.shape[2]
    shapes = [
        sds((micros, tok, width), F32),
        sds((micros, tok, width), BF),
        sds((micros, count, 2 * width), BF),
        sds((micros, count, width), F32),
        sds((micros, count, LANES), F32),
    ]
    args = (info, x, up, cols, rows, small, gate, lo, lout, lout_got, ho, hout)
    return call(
        middle_body,
        shapes,
        (micros,),
        [
            one_of(x.shape),
            one_of(up.shape),
            second_of(cols.shape),
            second_of(rows.shape),
            whole(small.shape),
            one_of(gate.shape),
            one_of(lo.shape),
            whole(lout.shape),
            whole(lout_got.shape),
            one_of(ho.shape),
            whole(hout.shape),
        ],
        [one_of(s.shape) for s in shapes],
        args,
        flops=2_000_000_000,
        moved=12_000_000,
    )


def pack_rows(target, values):
    step = values.shape[0] // 16
    cuts = values.shape[1] // COLS
    for slot in range(16):
        for cut in range(cuts):
            at = slot * step * cuts + cut * step
            target[0, at : at + step] = values[
                slot * step : (slot + 1) * step, cut * COLS : (cut + 1) * COLS
            ].astype(BF)


def gelu_parts(g):
    root = (2.0 / 3.141592653589793) ** 0.5
    square = g * g
    tanh = jnp.tanh(root * g * (1.0 + 0.044715 * square))
    bell = 0.5 * (1.0 + tanh)
    slope = bell + 0.5 * g * (1.0 - tanh * tanh) * (root * (1.0 + 3 * 0.044715 * square))
    return (g * bell, slope)


def hidden_both_ways(low, upstream, wg, wu, wd):
    g, u = (mm(low, wg), mm(low, wu))
    back = mm_t(upstream, wd)
    gelu, slope = gelu_parts(g)
    return ((gelu * u).astype(BF), (back * u * slope).astype(BF), (back * gelu).astype(BF))


def add_steps(step, pairs):
    @pl.when(step == 0)
    def first():
        for target, value in pairs:
            target[...] = value

    @pl.when(step > 0)
    def later():
        for target, value in pairs:
            target[...] += value


def ffn_local_body(info, a, ct, wg, wu, wd, z_out, dh_out):
    hidden, dg, du = hidden_both_ways(a[...], ct[...], wg[...], wu[...], wd[...])
    z = mm(hidden, wd[...])
    dh = mm_t(dg, wg[...]) + mm_t(du, wu[...])
    add_steps(pl.program_id(0), [(z_out, z), (dh_out, dh)])


def ffn_body(info, a, ct, wg, wu, wd, z_out, dh_out, own_gu, other_gu, own_dn, other_dn):
    step = pl.program_id(0)
    half = pl.num_programs(0) // 2
    width = a.shape[1] // 2
    hidden, dg, du = hidden_both_ways(a[...], ct[...], wg[...], wu[...], wd[...])
    z = mm(hidden, wd[...])
    dh = mm_t(dg, wg[...]) + mm_t(du, wu[...])
    add_steps(step, [(z_out, z), (dh_out, dh)])
    down = t_mm(hidden, ct[...])

    @pl.when(step < half)
    def send():
        pack_rows(other_dn, down)

    @pl.when(step >= half)
    def keep():
        pack_rows(own_dn, down)

    own = a[:, pl.ds(pl.multiple_of(info[0] * width, width), width)]
    other = a[:, pl.ds(pl.multiple_of((1 - info[0]) * width, width), width)]
    own_gu[0, :width] = t_mm(own, dg).astype(BF)
    own_gu[0, width:] = t_mm(own, du).astype(BF)
    other_gu[0, :width] = t_mm(other, dg).astype(BF)
    other_gu[0, width:] = t_mm(other, du).astype(BF)


def ffn_local(info, pay, w_gu, w_down, block):
    rows = pay.shape[0]
    hidden, width = w_down.shape
    steps = hidden // block
    return call(
        ffn_local_body,
        [sds((rows, width), F32)] * 2,
        (steps,),
        [
            pl.BlockSpec((rows, width), lambda i, *u: (0, 0)),
            pl.BlockSpec((rows, width), lambda i, *u: (0, 1)),
            pl.BlockSpec((width, block), lambda i, *u: (0, i)),
            pl.BlockSpec((width, block), lambda i, *u: (0, steps + i)),
            pl.BlockSpec((block, width), lambda i, *u: (i, 0)),
        ],
        [whole((rows, width))] * 2,
        (info, pay, pay, w_gu, w_gu, w_down),
        flops=2 * 6 * rows * hidden * width,
        moved=2 * 3 * hidden * width,
    )


def ffn(info, a, ct, w_gu, w_down):
    rows, width = a.shape
    hidden = w_down.shape[0]
    block = COLS
    steps = hidden // block
    half = steps // 2

    def natural(i, info):
        return jnp.where(i < half, (1 - info[0]) * half + i, info[0] * half + i - half)

    unit = (1, width, COLS)
    shapes = [
        sds((rows, width), F32),
        sds((rows, width), F32),
        sds((steps,) + unit[1:], BF),
        sds((steps,) + unit[1:], BF),
        sds((half,) + unit[1:], BF),
        sds((half,) + unit[1:], BF),
    ]
    return call(
        ffn_body,
        shapes,
        (steps,),
        [
            whole(a.shape),
            whole(ct.shape),
            pl.BlockSpec((width, block), lambda i, info: (0, natural(i, info))),
            pl.BlockSpec((width, block), lambda i, info: (0, steps + natural(i, info))),
            pl.BlockSpec((block, width), lambda i, info: (natural(i, info), 0)),
        ],
        [
            whole((rows, width)),
            whole((rows, width)),
            pl.BlockSpec(unit, lambda i, info: (natural(i, info), 0, 0)),
            pl.BlockSpec(unit, lambda i, info: (natural(i, info), 0, 0)),
            pl.BlockSpec(unit, lambda i, info: (jnp.maximum(i - half, 0), 0, 0)),
            pl.BlockSpec(unit, lambda i, info: (jnp.minimum(i, half - 1), 0, 0)),
        ],
        (info, a, ct, w_gu, w_gu, w_down),
        flops=2 * 9 * rows * hidden * width,
        moved=2 * 2 * 3 * hidden * width + rows * width * 12,
    )


def ffn_all_body(info, a, ct, w_gu, w_down, z_out, dh_out, own_gu, other_gu, own_dn, other_dn, turned, hid, slopes):
    step = pl.program_id(0)
    hidden, whole_width = w_down.shape
    steps = hidden // COLS
    half = steps // 2
    width = whole_width // 2

    @pl.when(step == 0)
    def turn():
        turned[...] = a[...].T

    @pl.when(step < steps)
    def block():
        at = jnp.where(step < half, (1 - info[0]) * half + step, info[0] * half + step - half)
        gate = pl.ds(pl.multiple_of(at * COLS, COLS), COLS)
        upper = pl.ds(pl.multiple_of(hidden + at * COLS, COLS), COLS)
        mixed, dg, du = hidden_both_ways(a[...], ct[...], w_gu[:, gate], w_gu[:, upper], w_down[gate])
        hid[:, gate] = mixed
        slopes[:, gate] = dg
        slopes[:, upper] = du
        down = t_mm(mixed, ct[...])

        @pl.when(step < half)
        def send():
            pack_rows(other_dn, down)

        @pl.when(step >= half)
        def keep():
            pack_rows(own_dn, down)

        for target, side in ((own_gu, info[0]), (other_gu, 1 - info[0])):
            rows = turned[pl.ds(pl.multiple_of(side * width, width), width)]
            target[0, :width] = mm(rows, dg).astype(BF)
            target[0, width:] = mm(rows, du).astype(BF)

    @pl.when(step == steps)
    def last():
        z_out[...] = mm(hid[...], w_down[...]).astype(BF)
        dh_out[...] = mm_t(slopes[...], w_gu[...]).astype(BF)


def ffn_all(info, a, ct, w_gu, w_down):
    rows, width = a.shape
    hidden = w_down.shape[0]
    steps = hidden // COLS
    half = steps // 2

    def natural(i, info):
        return jnp.where(i < half, (1 - info[0]) * half + i, info[0] * half + jnp.minimum(i - half, half - 1))

    unit = (1, width, COLS)
    shapes = [
        sds((rows, width), BF),
        sds((rows, width), BF),
        sds((steps,) + unit[1:], BF),
        sds((steps,) + unit[1:], BF),
        sds((half,) + unit[1:], BF),
        sds((half,) + unit[1:], BF),
    ]
    return call(
        ffn_all_body,
        shapes,
        (steps + 1,),
        [whole(a.shape), whole(ct.shape), whole(w_gu.shape), whole(w_down.shape)],
        [
            whole((rows, width)),
            whole((rows, width)),
            pl.BlockSpec(unit, lambda i, info: (natural(i, info), 0, 0)),
            pl.BlockSpec(unit, lambda i, info: (natural(i, info), 0, 0)),
            pl.BlockSpec(unit, lambda i, info: (jnp.minimum(jnp.maximum(i - half, 0), half - 1), 0, 0)),
            pl.BlockSpec(unit, lambda i, info: (jnp.minimum(i, half - 1), 0, 0)),
        ],
        (info, a, ct, w_gu, w_down),
        scratch=[
            pltpu.VMEM((width, rows), BF),
            pltpu.VMEM((rows, hidden), BF),
            pltpu.VMEM((rows, 2 * hidden), BF),
        ],
        flops=2 * 9 * rows * hidden * width,
        moved=2 * 2 * 3 * hidden * width + rows * width * 12,
    )


def plane_grads_body(info, near, far, wg, wu, wd, own_gu, other_gu, dn):
    width = wg.shape[0]
    half = width // 2
    sums = None
    for part in (near, far):
        low, upstream = (part[:, :width], part[:, width:])
        hidden, dg, du = hidden_both_ways(low, upstream, wg[...], wu[...], wd[...])
        own = part[:, pl.ds(pl.multiple_of(info[0] * half, half), half)]
        other = part[:, pl.ds(pl.multiple_of((1 - info[0]) * half, half), half)]
        terms = (t_mm(own, dg), t_mm(own, du), t_mm(other, dg), t_mm(other, du), t_mm(hidden, upstream))
        sums = terms if sums is None else tuple(p + q for p, q in zip(sums, terms))
    own_gu[0, :half] = sums[0].astype(BF)
    own_gu[0, half:] = sums[1].astype(BF)
    other_gu[0, :half] = sums[2].astype(BF)
    other_gu[0, half:] = sums[3].astype(BF)
    for cut in range(width // COLS):
        dn[0, cut * COLS : (cut + 1) * COLS] = sums[4][:, cut * COLS : (cut + 1) * COLS].astype(BF)


def plane_grads(info, near, far, w_gu, w_down):
    hidden, width = w_down.shape
    steps = hidden // COLS
    turns = steps // 8

    def block(i, info):
        return info[0] * (steps // 2) + lax.rem(info[3], 4) * turns + i

    unit = (1, width, COLS)
    spec = pl.BlockSpec(unit, lambda i, *u: (i, 0, 0))
    rows = 2 * near.shape[0]
    return call(
        plane_grads_body,
        [sds((turns, width, COLS), BF)] * 3,
        (turns,),
        [
            whole(near.shape),
            whole(far.shape),
            pl.BlockSpec((width, COLS), lambda i, info: (0, block(i, info))),
            pl.BlockSpec((width, COLS), lambda i, info: (0, steps + block(i, info))),
            pl.BlockSpec((COLS, width), lambda i, info: (block(i, info), 0)),
        ],
        [spec] * 3,
        (info, near, far, w_gu, w_gu, w_down),
        flops=2 * 6 * rows * turns * COLS * width,
        moved=9_000_000,
    )


def column_fold_body(order, info, first, second, third, keep, send):
    slots = 1 << len(order)
    size = keep.shape[2]
    place_z = info[3] // 4
    for part, source in enumerate((first, second, third)):
        for block in range(source.shape[0]):
            for slot in range(slots):
                owner = jnp.bitwise_xor(place_z, mask_of(slot, order))
                at = pl.ds(pl.multiple_of(owner * size, size), size)
                target = keep if slot < slots // 2 else send
                target[slot % (slots // 2), part * source.shape[0] + block] = source[block, at, :]


def column_fold(info, order, sources):
    slots = 1 << len(order)
    blocks, width, cols = sources[0].shape
    shape = sds((slots // 2, 3 * blocks, width // slots, cols), BF)
    return call(
        functools.partial(column_fold_body, order),
        [shape, shape],
        (1,),
        [whole(a.shape) for a in sources],
        [whole(shape.shape)] * 2,
        (info, *sources),
        moved=10_000_000,
        name="column_fold",
    )


def mid_back_body(
    info, y, up, z, dh2, zh, dff, ffr, gf, cols, rows, small, gate, lout, lout_got, hout, hy, hq,
    out, dy_out, dlo_out, dho_out, dhy_out, dsq_out, part_out,
):
    tok = y.shape[1]
    base = info[1]
    micro = pl.program_id(0)
    spread = onehot_rows(rows[2, 0], base, tok)
    take = onehot_cols(cols[2, 0], base, tok)
    values, top = (y[0], up[0].astype(F32))
    open_f = gf[0, :, 0:1]
    zhv = zh[0]
    out[0] = (values + z[0].astype(F32) + pick(spread, zhv * open_f)).astype(BF)
    taken = mm(take, up[0])
    dsf = jnp.sum(taken * zhv, axis=-1, keepdims=True) * open_f * (1.0 - open_f)
    back = dh2[0].astype(F32) + pick(spread, dff[0] + dsf * small[2:3].astype(F32))
    inv = inverse_rms(values)
    scaled = back * small[4:5].astype(F32)
    mean = jnp.mean(values * scaled, axis=-1, keepdims=True)
    dy = top + inv * scaled - values * (inv * inv * inv * mean)
    dy_out[0] = dy
    dgain = jnp.sum(back * values * inv, axis=0, keepdims=True)
    drf = jnp.sum(dsf * ffr[0].astype(F32), axis=0, keepdims=True)
    part_in = lout.shape[0]
    for weight, side in ((lout, info[0]), (lout_got, 1 - info[0])):
        at = pl.ds(pl.multiple_of(side * part_in, part_in), part_in)
        dlo_out[0, :, at] = mm_t(dy.astype(BF), weight[...]).astype(BF)
    dyq = pick(onehot_cols(cols[0, 0], base, tok), dy)
    open_q = gate[0, :, 0:1]
    dhy = (dyq * open_q).astype(BF)
    dhy_out[0] = dhy
    dsq = jnp.sum(dyq * hy[0], axis=-1, keepdims=True) * open_q * (1.0 - open_q)
    dsq_out[0] = jnp.broadcast_to(dsq, dsq_out.shape[1:])
    drq = jnp.sum(dsq * hq[0].astype(F32), axis=0, keepdims=True)
    dho_out[0] = mm_t(dhy, hout[...]).astype(BF)
    row = iota(part_out.shape, 0)
    part = jnp.where(row == 0, drq, jnp.where(row == 2, drf, jnp.where(row == 4, dgain, 0.0)))

    @pl.when(micro == 0)
    def first():
        part_out[...] = part

    @pl.when(micro > 0)
    def later():
        part_out[...] += part


def mid_back(info, y, up, z, dh2, zh, dff, ffr, gf, cols, rows, small, gate, lout, lout_got, hout, hy, hq):
    micros, tok, width = y.shape
    count = cols.shape[2]
    shapes = [
        sds((micros, tok, width), BF),
        sds((micros, tok, width), F32),
        sds((micros, tok, 2 * lout.shape[0]), BF),
        sds((micros, count, width), BF),
        sds((micros, count, width), BF),
        sds((micros, count, LANES), F32),
        sds((8, width), F32),
    ]
    return call(
        mid_back_body,
        shapes,
        (micros,),
        [
            one_of(y.shape),
            one_of(up.shape),
            one_of(z.shape),
            one_of(dh2.shape),
            one_of(zh.shape),
            one_of(dff.shape),
            pl.BlockSpec((1, count, width), lambda i, *u: (i, 0, 0)),
            one_of(gf.shape),
            second_of(cols.shape),
            second_of(rows.shape),
            whole(small.shape),
            one_of(gate.shape),
            whole(lout.shape),
            whole(lout_got.shape),
            whole(hout.shape),
            one_of(hy.shape),
            pl.BlockSpec((1, count, width), lambda i, *u: (i, 0, 0)),
        ],
        [one_of(s.shape) for s in shapes[:-1]] + [whole(shapes[-1].shape)],
        (info, y, up, z, dh2, zh, dff, ffr, gf, cols, rows, small, gate, lout, lout_got, hout, hy, hq),
        flops=3_000_000_000,
        moved=22_000_000,
    )


def light_join_body(info, x, small, dq, own, got_low, got_high, dl_out, own_out, other_out, low):
    tok, width = x.shape[1:]
    micros = x.shape[0]
    half = width // 2
    inner = dq.shape[2]
    for m in range(micros):
        dl_out[m, :, :inner] = dq[m]
        dl_out[m, WIN : tok - WIN, inner:] = own[m, WIN : tok - WIN].astype(BF)
        dl_out[m, :WIN, inner:] = (own[m, :WIN] + got_low[m].astype(F32)).astype(BF)
        dl_out[m, tok - WIN :, inner:] = (own[m, tok - WIN :] + got_high[m].astype(F32)).astype(BF)
        values = x[m].astype(F32)
        low[m] = (values * inverse_rms(values) * small[3:4].astype(F32)).astype(BF)
    for target, side in ((other_out, 1 - info[0]), (own_out, info[0])):
        cut = pl.ds(pl.multiple_of(side * half, half), half)
        for block in range(dl_out.shape[2] // COLS):
            total = sum(
                t_mm(low[m, :, cut], dl_out[m, :, block * COLS : (block + 1) * COLS])
                for m in range(micros)
            )
            target[block // 2, (block % 2) * half : (block % 2 + 1) * half] = total.astype(BF)


def light_join(info, x, small, dq, own, got_low, got_high):
    micros, tok, width = x.shape
    columns = dq.shape[2] + own.shape[2]
    shapes = [sds((micros, tok, columns), BF)] + [sds((columns // (2 * COLS), width, COLS), BF)] * 2
    args = (info, x, small, dq, own, got_low, got_high)
    return call(
        light_join_body,
        shapes,
        (1,),
        [whole(a.shape) for a in args[1:]],
        [whole(s.shape) for s in shapes],
        args,
        scratch=[pltpu.VMEM(x.shape, BF)],
        flops=2 * micros * tok * width * columns,
        moved=20_000_000,
    )


def in_back_body(
    info, x, dy, dl, dhq, dkin, dsq, rows, small, gate, h1k, l_own, l_got, h_own, h_got,
    grad_out, part_out,
):
    tok, width = x.shape[1:]
    micro = pl.program_id(0)
    base = info[1]
    light = dl[0]
    back = unhalved(info, mm_t(light, l_own[...]), mm_t(light, l_got[...]))
    given = dkin[0].astype(F32)
    open_k = gate[0, :, 1:2]
    source = h1k[0]
    dskv = jnp.sum(given * source, axis=-1, keepdims=True) * open_k * (1.0 - open_k)
    to_q = unhalved(info, mm_t(dhq[0], h_own[...]), mm_t(dhq[0], h_got[...]))
    to_q += dsq[0, :, 0:1] * small[0:1].astype(F32)
    to_k = given * open_k + dskv * small[1:2].astype(F32)
    back += pick(onehot_rows(rows[0, 0], base, tok), to_q)
    back += pick(onehot_rows(rows[1, 0], base, tok), to_k)
    values = x[0].astype(F32)
    inv = inverse_rms(values)
    scaled = back * small[3:4].astype(F32)
    mean = jnp.mean(values * scaled, axis=-1, keepdims=True)
    grad_out[0] = (dy[0] + inv * scaled - values * (inv * inv * inv * mean)).astype(BF)
    dgain = jnp.sum(back * values * inv, axis=0, keepdims=True)
    drk = jnp.sum(dskv * source.astype(BF).astype(F32), axis=0, keepdims=True)
    row = iota(part_out.shape, 0)
    part = jnp.where(row == 1, drk, jnp.where(row == 3, dgain, 0.0))

    @pl.when(micro == 0)
    def first():
        part_out[...] = part

    @pl.when(micro > 0)
    def later():
        part_out[...] += part


def in_back(info, x, dy, dl, dhq, dkin, dsq, rows, small, gate, h1k, l_own, l_got, h_own, h_got):
    micros, tok, width = x.shape
    shapes = [sds((micros, tok, width), BF), sds((8, width), F32)]
    firsts = (x, dy, dl, dhq, dkin, dsq)
    return call(
        in_back_body,
        shapes,
        (micros,),
        [one_of(a.shape) for a in firsts]
        + [second_of(rows.shape), whole(small.shape)]
        + [one_of(a.shape) for a in (gate, h1k)]
        + [whole(a.shape) for a in (l_own, l_got)]
        + [whole((h_own.shape[0], width))] * 2,
        [one_of(shapes[0].shape), whole(shapes[1].shape)],
        (info,) + firsts + (rows, small, gate, h1k, l_own, l_got, h_own, h_got),
        flops=2_600_000_000,
        moved=14_000_000,
    )


def mask_of(slot, order):
    bits = len(order)
    return sum(order[b] for b in range(bits) if (slot >> (bits - 1 - b)) & 1)


def fold_body(order, counts, info, *refs):
    sources = refs[: 2 * len(counts)]
    keep, send = refs[2 * len(counts) :]
    slots = 1 << len(order)
    size = keep.shape[2]
    step = pl.program_id(0)
    start = 0
    for which, count in enumerate(counts):
        own, got = sources[2 * which : 2 * which + 2]

        @pl.when((step >= start) & (step < start + count))
        def part():
            for slot in range(slots):
                owner = jnp.bitwise_xor(info[3], mask_of(slot, order))
                at = pl.ds(pl.multiple_of(owner * size, size), size)
                total = (own[0, at, :].astype(F32) + got[0, at, :].astype(F32)).astype(BF)
                if slot < slots // 2:
                    keep[slot, 0] = total
                else:
                    send[slot - slots // 2, 0] = total

        start += count


def fold(info, order, parts):
    slots = 1 << len(order)
    width = parts[0][0].shape[1]
    counts = [part[3] for part in parts]
    total = sum(counts)
    shape = sds((slots // 2, total, width // slots, COLS), BF)
    args, specs = ([], [])
    start = 0
    for own, got, first, count in parts:
        index = functools.partial(
            lambda first, start, count, i, *u: (
                first + jnp.minimum(jnp.maximum(i - start, 0), count - 1),
                0,
                0,
            ),
            first,
            start,
            count,
        )
        args += [own, got]
        specs += [pl.BlockSpec((1, width, COLS), index)] * 2
        start += count
    spec = pl.BlockSpec((slots // 2, 1, width // slots, COLS), lambda i, *u: (0, i, 0, 0))
    return call(
        functools.partial(fold_body, order, counts),
        [shape, shape],
        (total,),
        specs,
        [spec, spec],
        (info, *args),
        moved=total * width * COLS * 6,
    )


def flipped(value, bit):
    size = lax.axis_size("ctx")
    return lax.ppermute(value, "ctx", [(i, i ^ bit) for i in range(size)])


def tied(*values):
    return lax.optimization_barrier(values)


def scatter_step(keep, got):
    half = keep.shape[0] // 2
    if half == 0:
        return ((keep.astype(F32) + got.astype(F32)).astype(BF), None)
    return (
        (keep[:half].astype(F32) + got[:half].astype(F32)).astype(BF),
        (keep[half:].astype(F32) + got[half:].astype(F32)).astype(BF),
    )


def scatter_start(chunks, orders, stage):
    return [flipped(send, order[stage]) for (keep, send), order in zip(chunks, orders)]


def scatter_end(chunks, got):
    return [scatter_step(keep, g) for (keep, send), g in zip(chunks, got)]


def scatter_sum(keep, send, order):
    for bit in order:
        keep, send = scatter_step(keep, flipped(send, bit))
    return keep


def gather_start(values, orders, stage):
    return [flipped(value, order[-1 - stage]) for value, order in zip(values, orders)]


def gather_end(values, got):
    return [jnp.concatenate([value, g], axis=0) for value, g in zip(values, got)]


def gather_pair(value, order):
    for bit in order[:-1]:
        value = jnp.concatenate([value, flipped(value, bit)], axis=0)
    return (value, flipped(value, order[-1]))


def from_owner(info, order, near, far, owner, write):
    slots = 1 << len(order)
    distance = jnp.bitwise_xor(info[3], owner)
    slot = sum(
        jnp.where(jnp.bitwise_and(distance, bit) != 0, 1 << place, 0)
        for place, bit in enumerate(reversed(order))
    )
    inside = lax.rem(slot, slots // 2)

    @pl.when(slot < slots // 2)
    def close():
        write(near.at[inside])

    @pl.when(slot >= slots // 2)
    def distant():
        write(far.at[inside])


def unpack_gu_body(order, info, near, far, *outs):
    out = outs[-1]
    size = near.shape[2]
    per = out.shape[0] // size
    for turn in range(per):

        def write(source, turn=turn):
            for block in range(near.shape[1]):
                out[turn * size : (turn + 1) * size, block * COLS : (block + 1) * COLS] = source[
                    block
                ].astype(F32)

        from_owner(info, order, near, far, pl.program_id(1) * per + turn, write)


def write_dn(out, source, first, size, owner, row):
    cuts = out.shape[1] // COLS
    rows = size // cuts
    value = source[first].astype(F32)
    for cut in range(cuts):
        out[row + owner * rows : row + (owner + 1) * rows, cut * COLS : (cut + 1) * COLS] = value[
            cut * rows : (cut + 1) * rows
        ]


def unpack_dn_body(order, info, near, far, *outs):
    slots, blocks, size = near.shape[:3]
    for owner in range(2 * slots):

        def write(source, owner=owner):
            for block in range(blocks):
                write_dn(outs[-1], source, block, size, owner, block * COLS)

        from_owner(info, order, near, far, owner, write)


def unpack(body, info, order, pair, first, count, step, shape, grid_more, block, index, previous, name):
    near, far = pair
    slots, unused, size, unused_too = near.shape
    spec = pl.BlockSpec((slots, step, size, COLS), lambda i, *u: (0, first // step + i, 0, 0))
    args, specs, aliases = ([info, near, far], [spec, spec], {})
    if previous is not None:
        args.append(previous)
        specs.append(pl.BlockSpec(memory_space=pl.ANY))
        aliases = {3: 0}
    return pl.pallas_call(
        functools.partial(body, order),
        out_shape=sds(shape, F32),
        grid_spec=pltpu.PrefetchScalarGridSpec(
            num_scalar_prefetch=1,
            grid=(count // step,) + grid_more,
            in_specs=specs,
            out_specs=pl.BlockSpec(block, index),
        ),
        input_output_aliases=aliases,
        compiler_params=pltpu.CompilerParams(vmem_limit_bytes=32 * 1024 * 1024),
        cost_estimate=pl.CostEstimate(
            flops=0, bytes_accessed=count * 2 * slots * size * COLS * 6, transcendentals=0
        ),
        name=name,
    )(*args)


def unpack_gu(info, order, pair, first, count, total, base, previous, step):
    rows = pair[0].shape[0] * pair[0].shape[2]
    return unpack(
        unpack_gu_body, info, order, pair, first, count, step, (rows, 2 * total * COLS), (2,), (rows, step * COLS),
        lambda i, s, *u: (0, (s * total + base) // step + i), previous, "unpack_gu",
    )


def unpack_dn(info, order, pair, first, count, total, base, previous, step):
    width = 2 * pair[0].shape[0] * pair[0].shape[2]
    return unpack(
        unpack_dn_body, info, order, pair, first, count, step, (total * COLS, width), (), (step * COLS, width),
        lambda i, *u: (base // step + i, 0), previous, "unpack_dn",
    )


def unpack_plane_gu_body(info, full, out):
    sides, unused, planes, blocks, size, cols = full.shape
    turns = blocks // 3
    columns = out.shape[1] // sides
    for side in range(sides):
        for half in range(2):
            first = jnp.bitwise_xor(half, info[0]) * turns
            for plane in range(planes):
                for turn in range(turns):
                    at = side * columns + ((half * planes + plane) * turns + turn) * cols
                    out[:, at : at + cols] = full[side, 0, plane, first + turn].astype(F32)


def unpack_plane_gu(info, full, total):
    levels, planes, blocks, size, unused = full.shape
    rows, step = (2 * size, 48)
    turns = size // step
    view = full.reshape((2, levels // 2) + full.shape[1:])
    return call(
        unpack_plane_gu_body,
        sds((rows, 2 * total * COLS), F32),
        (rows // step,),
        [
            pl.BlockSpec(
                (2, 1, planes, blocks, step, COLS), lambda r, *u: (0, r // turns, 0, 0, r % turns, 0)
            )
        ],
        pl.BlockSpec((step, 2 * total * COLS), lambda r, *u: (r, 0)),
        (info, view),
        moved=2 * rows * total * COLS * 6,
        name="unpack_plane_gu",
    )


def unpack_plane_dn_body(info, full, out):
    levels, unused, blocks, size, cols = full.shape
    for level in range(levels):
        for block in range(blocks):
            for part in range(size // 64):
                cut, row = divmod(level * size + part * 64, COLS)
                at = block * COLS + row
                out[at : at + 64, cut * COLS : (cut + 1) * COLS] = full[
                    level, 0, block, part * 64 : (part + 1) * 64
                ].astype(F32)


def unpack_plane_dn(info, full):
    levels, planes, blocks, size, unused = full.shape
    turns = blocks // 3
    width = levels * size
    return call(
        unpack_plane_dn_body,
        sds((planes * turns * COLS, width), F32),
        (planes,),
        [pl.BlockSpec((levels, 1, turns, size, COLS), lambda q, *u: (0, q, 2, 0, 0))],
        pl.BlockSpec((turns * COLS, width), lambda q, *u: (q, 0)),
        (info, full),
        moved=planes * turns * COLS * width * 6,
        name="unpack_plane_dn",
    )


def unpack_units_body(order, first, info, near, far, *outs):
    slots, unused, size = near.shape[:3]
    homes = [
        (out, block * COLS) for out in outs for block in range(out.shape[1] // COLS)
    ]
    for owner in range(2 * slots):
        side, turn = divmod(owner, slots)

        def write(source, side=side, turn=turn):
            for at in range(side, len(homes), 2):
                out, column = homes[at]
                out[turn * size : (turn + 1) * size, column : column + COLS] = source[
                    first + at // 2
                ].astype(F32)

        from_owner(info, order, near, far, owner, write)


def unpack_units(info, order, pair, first, widths):
    slots, unused, size, unused_too = pair[0].shape
    shapes = [sds((slots * size, w), F32) for w in widths]
    args = [info, *pair]
    return call(
        functools.partial(unpack_units_body, order, first),
        shapes,
        (1,),
        [whole(a.shape) for a in args[1:]],
        [whole(s.shape) for s in shapes],
        args,
        moved=sum(widths) * slots * size * 6,
        name="unpack_units",
    )


def unpack_second_body(orders, info, *refs):
    pairs, outs = ([refs[i : i + 2] for i in (0, 2, 4)], refs[6:])
    qkv_out, hout_out, gu_out, lout_out, light_out, dn_out = outs
    slots, unused, size = refs[0].shape[:3]
    half = gu_out.shape[1] // 2
    blocks = half // COLS

    def homes(targets):
        return [(out, block * COLS) for out in targets for block in range(out.shape[1] // COLS)]

    def put_units(source, targets, side, rows):
        every = homes(targets)
        for at in range(side, len(every), 2):
            out, column = every[at]
            out[rows, column : column + COLS] = source[at // 2].astype(F32)

    for owner in range(2 * slots):
        side, turn = divmod(owner, slots)
        rows = slice(turn * size, (turn + 1) * size)

        def first(source, side=side, rows=rows):
            put_units(source, (qkv_out, hout_out), side, rows)

        def second(source, side=side, rows=rows, owner=owner):
            for block in range(blocks):
                at = side * half + block * COLS
                gu_out[rows, at : at + COLS] = source[block].astype(F32)
            write_dn(lout_out, source, blocks, size, owner, 0)

        def third(source, side=side, rows=rows, owner=owner):
            put_units(source, (light_out,), side, rows)
            used = light_out.shape[1] // (2 * COLS)
            for block in range(dn_out.shape[0] // COLS):
                write_dn(dn_out, source, used + block, size, owner, block * COLS)

        for order, (near, far), write in zip(orders, pairs, (first, second, third)):
            from_owner(info, order, near, far, owner, write)


def unpack_second(info, orders, pairs, shapes):
    args = [info] + [part for pair in pairs for part in pair]
    outs = [sds(shape, F32) for shape in shapes]
    return call(
        functools.partial(unpack_second_body, orders),
        outs,
        (1,),
        [whole(a.shape) for a in args[1:]],
        [whole(out.shape) for out in outs],
        args,
        moved=20_000_000,
        name="unpack_second",
    )


def plain_gu(own, other):
    blocks, width, cols = own.shape

    def rows(part):
        return part.reshape(blocks, 2, width // 2, cols).transpose(2, 1, 0, 3).reshape(width // 2, -1)

    return jnp.concatenate([rows(own), rows(other)], axis=0)


def plain_dn(own, other):
    blocks, width, cols = own.shape
    cuts = width // cols

    def rows(part):
        return (
            part.reshape(blocks, 16, cuts, width // (16 * cuts), cols)
            .transpose(0, 1, 3, 2, 4)
            .reshape(-1, width)
        )

    return jnp.concatenate([rows(own), rows(other)], axis=0)


def plain_units(own, other, widths):
    def unit(part, at):
        half = part.shape[1] // 2
        return part[at // 2, (at % 2) * half : (at % 2 + 1) * half]

    result, at = ([], 0)
    for columns in widths:
        count = columns // COLS
        result.append(
            jnp.concatenate(
                [
                    jnp.concatenate([unit(part, at + i) for i in range(count)], axis=1)
                    for part in (own, other)
                ],
                axis=0,
            )
        )
        at += count
    return result


def plain_sum(grads):
    parts = [lax.psum_scatter(g.astype(BF), "wsh", scatter_dimension=0, tiled=True) for g in grads]
    return tuple(g.astype(F32) for g in lax.psum(parts, "ctx"))


def per_device(
    tokens, cotangent, light_qkv, light_out, heavy_qkv, heavy_out, light_gu, light_down, heavy_gu, heavy_down,
    routers, gains, doc_starts, q_index, kv_index, ff_index,
):
    micros, unused, tok, width = tokens.shape
    count, groups = (lax.axis_size("ctx"), lax.axis_size("wsh"))
    direct = groups == 2 and count == 16
    place_ctx = lax.axis_index("ctx")
    side = lax.axis_index("wsh") if direct else 0
    base = place_ctx * tok
    info = jnp.concatenate(
        [
            jnp.stack([jnp.int32(side), base, jnp.int32(tok * count), place_ctx]).astype(jnp.int32),
            doc_starts[:, 0].reshape(-1),
        ]
    )
    swap = [(0, 1), (1, 0)]

    def pair_of(shard):
        if direct:
            return (shard, lax.ppermute(shard, "wsh", swap))
        full = lax.all_gather(shard, "wsh", axis=0, tiled=True)
        return (full[: full.shape[0] // 2], full[full.shape[0] // 2 :])

    def full_of(shard, axis=0):
        return lax.all_gather(shard, "wsh", axis=axis, tiled=True)

    vectors = jnp.concatenate([routers, gains, jnp.zeros((3, routers.shape[1]), BF)], axis=0)
    if direct:
        got = lax.ppermute(vectors, "wsh", swap)
        small = jnp.concatenate(
            [jnp.where(side == 0, vectors, got), jnp.where(side == 0, got, vectors)], axis=1
        )
    else:
        small = full_of(vectors, 1)
    x, up = (tokens[:, 0], cotangent[:, 0])
    index = jnp.stack([q_index[:, 0], kv_index[:, 0], ff_index[:, 0]])
    cols, rows = (index[..., None], index[:, :, None, :])
    hq_in, kin_pay, h1k, gate = routed_in(info, x, cols, small)
    l_own, l_got = pair_of(light_qkv)
    h_own, h_got = pair_of(heavy_qkv)
    o_own, o_got = pair_of(light_out)
    w_hout, w_hgu, w_hdown = (full_of(heavy_out), full_of(heavy_gu), full_of(heavy_down))
    w_lgu, w_ldown = (full_of(light_gu), full_of(light_down))
    kv_orders = ((8, 4, 2, 1), (8, 1, 4, 2))
    back_orders = [tuple(reversed(order)) for order in kv_orders]
    upward = [(i, i + 1) for i in range(count - 1)]
    downward = [(i + 1, i) for i in range(count - 1)]
    inner = light_qkv.shape[1] // 3
    every = range(micros)

    def rims(qkv):
        return (
            lax.ppermute(qkv[:, tok - WIN :, inner:], "ctx", upward),
            lax.ppermute(qkv[:, :WIN, inner:], "ctx", downward),
        )

    def project(kin):
        return key_project(info, kin, h_own, h_got)

    if direct:
        values = [kin_pay[m] for m in every]
        got = gather_start(values, back_orders, 0)
        qkv = light_in(info, x, small, l_own, l_got)
        got, qkv = tied(got, qkv)
        before, after = rims(qkv)
        values = gather_end(values, got)
        got = gather_start(values, back_orders, 1)
        q_pay = query_project(info, hq_in, h_own, h_got)
        got, q_pay, w_hout = tied(got, q_pay, w_hout)
        values = gather_end(values, got)
        got = gather_start(values, back_orders, 2)
        done = light_inner(info, qkv)
        got, before, after, done = tied(got, before, after, done)
        values = gather_end(values, got)
        got = gather_start(values, back_orders, 3)
        lo, light_lse = light_outer(info, qkv, before, after, done)
        near_kv = [project(v) for v in values]
        got, near_kv, lo, light_lse, w_hgu, w_hdown = tied(got, near_kv, lo, light_lse, w_hgu, w_hdown)
        kins = list(zip(values, got))
        kvs = [(n, project(f)) for n, f in zip(near_kv, got)]
    else:
        kins = []
        for m in every:
            full = lax.all_gather(kin_pay[m], "ctx", axis=0, tiled=True)
            kins.append((full[: full.shape[0] // 2], full[full.shape[0] // 2 :]))
        kvs = [tuple(project(k) for k in pair) for pair in kins]
        qkv = light_in(info, x, small, l_own, l_got)
        before, after = rims(qkv)
        lo, light_lse = light_outer(info, qkv, before, after, light_inner(info, qkv))
        q_pay = query_project(info, hq_in, h_own, h_got)
    heavy = [heavy_fwd(info, q_pay[m], kins[m], kvs[m]) for m in every]
    heavy, w_lgu, w_ldown = tied(heavy, w_lgu, w_ldown)
    ho = jnp.stack([h[0] for h in heavy])
    y, low2, pay, hy, gf = middle(info, x, up, cols, rows, small, gate, lo, o_own, o_got, ho, w_hout)

    def flat(value):
        return value.reshape(-1, value.shape[-1])

    orders = ((1, 2, 4, 8), (2, 4, 1, 8), (4, 1, 2, 8))
    back_two = ((1, 2, 4, 8), (2, 1, 4, 8), (4, 1, 2, 8))
    if direct:
        mine = flat(pay)
        plane = [flipped(mine, bit) for bit in (1, 2, 3)]
        zh, dff = ffn_local(info, mine, w_hgu, w_hdown, 4 * COLS)
        plane, zh, dff = tied(plane, zh, dff)
        near = jnp.concatenate([mine, *plane], axis=0)
        far = lax.ppermute(near, "wsh", swap)
    else:
        zh, dff, hgu_own, hgu_send, hdn_own, hdn_send = ffn(
            info, flat(pay[..., :width]), flat(pay[..., width:]), w_hgu, w_hdown
        )
    if direct:
        plane_own, plane_send, plane_dn = plane_grads(info, near, far, w_hgu, w_hdown)
        plane_got = lax.ppermute(plane_send, "wsh", swap)
        keep, send = column_fold(info, (1, 2), (plane_own, plane_got, plane_dn))
        send, low2 = tied(send, low2)
        got = flipped(send, 4)
    z, dh2, lgu_own, lgu_send, ldn_own, ldn_send = ffn_all(info, flat(low2), flat(up), w_lgu, w_ldown)
    if direct:
        got, z, dh2, lgu_send, ldn_send = tied(got, z, dh2, lgu_send, ldn_send)
        keep, send = scatter_step(keep, got)
        got = flipped(send, 8)
        lgu_got, ldn_got = (lax.ppermute(part, "wsh", swap) for part in (lgu_send, ldn_send))

    def by_micro(value):
        return value.reshape(micros, -1, value.shape[-1])

    out_tokens, dy, dlo, dho, dhy, dsq, part_two = mid_back(
        info, y, up, by_micro(z), by_micro(dh2), by_micro(zh), by_micro(dff), pay, gf, cols, rows, small, gate, o_own,
        o_got, w_hout, hy, hq_in,
    )
    dlq, dl_own, rim_low, rim_high = light_bwd_outer(info, qkv, before, after, light_lse, dlo)
    if direct:
        got, dlq, dl_own, rim_low, rim_high, dho = tied(got, dlq, dl_own, rim_low, rim_high, dho)
        keep, send = scatter_step(keep, got)
        plane_full = lax.all_gather(keep[0], "ctx", axis=0, tiled=False)
        plane_full = plane_full.reshape((count // 4, 4) + plane_full.shape[1:])
    got_low = lax.ppermute(rim_high, "ctx", upward)
    got_high = lax.ppermute(rim_low, "ctx", downward)
    backs = [
        heavy_bwd(info, q_pay[m], kins[m], kvs[m], heavy[m][1], dho[m], h_own, h_got) for m in every
    ]
    dhq = jnp.stack([b[0] for b in backs])
    shape = (count // 2, q_index.shape[2], width)
    back = [tuple(part.reshape(shape) for part in b[3:5]) for b in backs]
    dkvs = [part for b in backs for part in b[1:3]]
    if direct:
        back, dlo, dkvs, got_low, got_high = tied(back, dlo, dkvs, got_low, got_high)
        got_back = scatter_start(back, back_orders, 0)
    dlq, dl_own = light_bwd_inner(info, qkv, light_lse, dlo, dlq, dl_own)
    if direct:
        got_back, dlq, dl_own = tied(got_back, dlq, dl_own)
        back = scatter_end(back, got_back)
        got_back = scatter_start(back, back_orders, 1)
    kin_all = [part for pair in kins for part in pair]
    dl, la_own, la_send = light_join(info, x, small, dlq, dl_own, got_low, got_high)
    if direct:
        la_got = lax.ppermute(la_send, "wsh", swap)
    ha_own, ha_send = heavy_grads(info, hq_in, dhq, ho, dhy, lo, dy, kin_all, dkvs)
    if direct:
        got_back, ha_own, ha_send, la_got, dl = tied(got_back, ha_own, ha_send, la_got, dl)
        ha_got = lax.ppermute(ha_send, "wsh", swap)
        back = scatter_end(back, got_back)
        got_back = scatter_start(back, back_orders, 2)
        second = [
            fold(info, orders[0], [(ha_own, ha_got, 0, 6)]),
            fold(info, back_two[1], [(lgu_own, lgu_got, 0, 4), (ha_own, ha_got, 6, 1)]),
            fold(info, orders[2], [(la_own, la_got, 0, 3), (ldn_own, ldn_got, 0, 2)]),
        ]
        got_back, second, dl = tied(got_back, second, dl)
        *got_two, got_last = scatter_start(second, back_two, 0)
        back = scatter_end(back, got_back)
        got_back = scatter_start(back, back_orders, 3)
        (got_two,) = tied(got_two)
        *second, last = second
        second = scatter_end(second, got_two)
        got_two = scatter_start(second, back_two, 1)
        back, got_back, second = tied(back, got_back, second)
        back = scatter_end(back, got_back)
        dkin = jnp.concatenate([keep for keep, send in back], axis=0)
    else:
        dkin = jnp.stack(
            [
                lax.psum_scatter(jnp.concatenate(b[3:5], axis=0), "ctx", scatter_dimension=0, tiled=True)
                for b in backs
            ]
        )
    grad_tokens, part_one = in_back(
        info, x, dy, dl, dhq, dkin, dsq, rows, small, gate, h1k, l_own, l_got, h_own, h_got
    )
    widths = (heavy_qkv.shape[1], heavy_out.shape[1])
    vector = part_one + part_two
    if direct:
        half = width // 2
        mine = lax.dynamic_slice_in_dim(vector, side * half, half, 1)
        given = lax.dynamic_slice_in_dim(vector, (1 - side) * half, half, 1)
        got_two, got_last, mine, given = tied(got_two, got_last, mine, given)
        second, last = (scatter_end(second, got_two), scatter_step(last[0], got_last))
        got_two, got_last = (scatter_start(second, back_two, 2), flipped(last[1], back_two[2][1]))
        vector = mine + lax.ppermute(given, "wsh", swap)
        got_two, got_last, vector = tied(got_two, got_last, vector)
        second, last = (scatter_end(second, got_two), scatter_step(last[0], got_last))
        got_two, got_last = (scatter_start(second, back_two, 3), flipped(last[1], back_two[2][2]))
        got_vector = flipped(vector, 1)
        got_two, got_last, vector, got_vector = tied(got_two, got_last, vector, got_vector)
        second, last = (scatter_end(second, got_two), scatter_step(last[0], got_last))
        got_last = flipped(last[1], back_two[2][3])
        second, got_last, got_vector = tied(second, got_last, got_vector)
        vector = vector + got_vector
        second = [*second, scatter_step(last[0], got_last)]
        tails = [keep for keep, send in second]
        got_two, got_vector = (gather_start(tails, orders, 0), flipped(vector, 2))
        got_two, vector, got_vector = tied(got_two, vector, got_vector)
        tails, vector = (gather_end(tails, got_two), vector + got_vector)
        got_two, got_vector = (gather_start(tails, orders, 1), flipped(vector, 4))
        got_two, vector, got_vector = tied(got_two, vector, got_vector)
        tails, vector = (gather_end(tails, got_two), vector + got_vector)
        got_two, got_vector = (gather_start(tails, orders, 2), flipped(vector, 8))
        g_hdown = unpack_plane_dn(info, plane_full)
        got_two, vector, got_vector, g_hdown, plane_full = tied(got_two, vector, got_vector, g_hdown, plane_full)
        tails, vector = (gather_end(tails, got_two), vector + got_vector)
        got_two = gather_start(tails, orders, 3)
        g_hgu = unpack_plane_gu(info, plane_full, heavy_gu.shape[1] // (2 * COLS))
        got_two, g_hgu = tied(got_two, g_hgu)
        sums = list(zip(tails, got_two))
        g_hqkv, g_hout, g_lgu, g_lout, g_lqkv, g_ldown = unpack_second(
            info,
            orders,
            sums,
            [
                weight.shape
                for weight in (heavy_qkv, heavy_out, light_gu, light_out, light_qkv, light_down)
            ],
        )
    else:
        g_hqkv, g_hout = plain_units(ha_own, ha_send, widths)
        (g_lqkv,) = plain_units(la_own, la_send, (light_qkv.shape[1],))
        last = slice(ha_own.shape[0] - 1, ha_own.shape[0])
        g_lqkv, g_lout, g_hqkv, g_hout, g_lgu, g_ldown, g_hgu, g_hdown = plain_sum(
            [
                g_lqkv,
                plain_dn(ha_own[last], ha_send[last]),
                g_hqkv,
                g_hout,
                plain_gu(lgu_own, lgu_send),
                plain_dn(ldn_own, ldn_send),
                plain_gu(hgu_own, hgu_send),
                plain_dn(hdn_own, hdn_send),
            ]
        )
        vector = lax.psum(vector, ("ctx", "wsh"))
        part = width // groups
        vector = lax.dynamic_slice_in_dim(vector, lax.axis_index("wsh") * part, part, 1)
    return (
        out_tokens[:, None],
        grad_tokens[:, None],
        g_lqkv,
        g_lout,
        g_hqkv,
        g_hout,
        g_lgu,
        g_ldown,
        g_hgu,
        g_hdown,
        vector[:3],
        vector[3:5],
    )


def solution(mesh):
    return jax.shard_map(
        per_device,
        mesh=mesh,
        in_specs=(
            P(None, "wsh", "ctx", None),
            P(None, "wsh", "ctx", None),
            P("wsh", None),
            P("wsh", None),
            P("wsh", None),
            P("wsh", None),
            P("wsh", None),
            P("wsh", None),
            P("wsh", None),
            P("wsh", None),
            P(None, "wsh"),
            P(None, "wsh"),
            P(None, "wsh", None),
            P(None, "wsh", "ctx"),
            P(None, "wsh", "ctx"),
            P(None, "wsh", "ctx"),
        ),
        out_specs=(
            P(None, "wsh", "ctx", None),
            P(None, "wsh", "ctx", None),
            P("wsh", None),
            P("wsh", None),
            P("wsh", None),
            P("wsh", None),
            P("wsh", None),
            P("wsh", None),
            P("wsh", None),
            P("wsh", None),
            P(None, "wsh"),
            P(None, "wsh"),
        ),
        check_vma=False,
    )
```
